32 devices in a mesh: batch: 16 (over z, y, x), stream: 2 (over core).
Axes of the slice: x: 2, y: 2, z: 4, core: 2. Of those that a mesh axis runs over, the one named last changes fastest.
Arguments:
- tokens: bfloat16 [16384, 1024], P('batch'), may hold values from -6 to 6
- cotangent: bfloat16 [16384, 1024], P('batch'), may hold values from -6 to 6
- branch_weight: bfloat16 [2, 2, 4096, 1024], P('stream')
- branch_bias: bfloat16 [2, 2, 4096], P('stream'), may hold values from -1.1953125 to 1.1953125
- up_weight: bfloat16 [2, 4096, 1024], replicated, may hold values from -0.1875 to 0.1875
- down_bias: bfloat16 [2, 1024], replicated, may hold values from -3 to 3
- norm_gain: bfloat16 [2, 1024], replicated, may hold values from 0.5 to 1.5
- norm_bias: bfloat16 [2, 1024], replicated, may hold values from -2 to 2
- freq_seeds: int32 [2, 16, 64], replicated, may hold values from 1 to 63
- doc_starts: int32 [16, 4], P('batch'), may hold values from 0 to 1023, as said below
Outputs:
- result: float32 [16384, 1024], P('batch')
- input_grad: float32 [16384, 1024], P('batch')
- branch_weight_grad: float32 [2, 2, 4096, 1024], P('stream', None, 'batch')
- branch_bias_grad: float32 [2, 2, 4096], P('stream', None, 'batch')
- up_weight_grad: float32 [2, 4096, 1024], P(None, ('batch', 'stream'))
- down_bias_grad: float32 [2, 1024], P(None, 'batch')
- norm_gain_grad: float32 [2, 1024], P(None, 'batch')
- norm_bias_grad: float32 [2, 1024], P(None, 'batch')
The draws below stay inside these ranges and needn't reach their ends.
Inputs may be any that keep to these rules, and one draw needn't show every extreme that they name: `doc_starts`: row s lists the first positions of the 4 documents of sequence s, strictly increasing, the first being 0.
All inputs are finite; a program needn't handle non-finite values.
Results may differ from the reference program's by a relative error of at most 0.038.
Values sent between devices are 32-bit elements; how exact they have to be, the bound alone decides.
A program may use at most 384 MiB of HBM per device.

```python
import math
import jax
import jax.numpy as jnp
from jax import lax

D = 1024
HEADS = 16
DH = 64
FF = 4096
ROT = 16
FEAT = 64
LAYERS = 2
NDOC = 4
LEN = 1024
SEQS = 16
TOKENS = 16384


def draw_branch_weight(key, part):
    key = jax.random.fold_in(key, 5)
    normals = jax.random.truncated_normal(key, -6.0, 6.0, (2, LAYERS, 4 * D, D), jnp.float32)
    stream_rows = jnp.arange(2)[:, None, None, None]
    weight_rows = jnp.arange(4 * D)[None, None, :, None]
    attention_scale = jnp.where(weight_rows < 2 * D, 0.5 * D ** (-0.5), jnp.where(weight_rows < 3 * D, D ** (-0.5), 4.0 * D ** (-0.5)))
    scale_all = jnp.where(stream_rows == 0, attention_scale, FF ** (-0.5))
    return (normals * scale_all).astype(jnp.bfloat16)


def draw_doc_starts(key, part):
    key = jax.random.fold_in(key, 11)
    row_keys = jax.random.split(key, SEQS)

    def one_row(row_key):
        shuffled = jax.random.permutation(row_key, LEN - 1).astype(jnp.int32) + 1
        picked = jnp.sort(shuffled[:NDOC - 1])
        return jnp.concatenate([jnp.zeros((1,), jnp.int32), picked])
    return jax.vmap(one_row)(row_keys)


def place_ends(entries, key, least, largest):
    longest = entries.shape.index(max(entries.shape))
    spots = []
    for shift in (0, 1):
        where = [jax.random.randint(jax.random.fold_in(key, axis), (), 0, length) for axis, length in enumerate(entries.shape)]
        where[longest] = (where[longest] + shift) % entries.shape[longest]
        spots.append(tuple(where))
    return entries.at[spots[0]].set(least).at[spots[1]].set(largest)


def level_of(own_key, dims, cuts, low, largest):
    def one(axis_at, parts):
        steps = jax.random.uniform(jax.random.fold_in(jax.random.fold_in(own_key, 6), axis_at), (parts,), jnp.float32, low / len(cuts), largest / len(cuts))
        return jnp.repeat(jnp.exp(steps), dims[axis_at] // parts).reshape((-1,) + (1,) * (len(dims) - axis_at - 1))

    level = one(*cuts[0])
    for cut in cuts[1:]:
        level = level * one(*cut)
    return level


def scatter_about(stream_key, shape, width, most, cuts=(), kind=jnp.bfloat16):
    drawn = jax.random.normal(stream_key, shape, jnp.float32) * width
    if len(cuts) > 0:
        drawn = level_of(stream_key, shape, cuts, -0.22, 0.18) * drawn
    return jnp.clip(drawn, min=-most, max=most).astype(kind)


def setup_inputs(seed: int = 0) -> dict:
    key_of = jax.random.split(jax.random.key(seed), 11)
    return {
        "tokens": scatter_about(key_of[0], (TOKENS, D), 1.0, 6.0, ((0, 16),)),
        "cotangent": scatter_about(key_of[1], (TOKENS, D), 1.0, 6.0, ((0, 16),)),
        "branch_weight": draw_branch_weight(jax.random.fold_in(key_of[10], 71), 0),
        "branch_bias": scatter_about(key_of[3], (2, LAYERS, 4 * D), 0.2, 1.1953125, ((0, 2),)),
        "up_weight": scatter_about(key_of[4], (LAYERS, FF, D), D ** -0.5, 0.1875),
        "down_bias": scatter_about(key_of[5], (LAYERS, D), 0.5, 3.0),
        "norm_gain": jnp.clip(1.0 + 0.1 * jax.random.normal(key_of[6], (LAYERS, D), jnp.float32), 0.5, 1.5).astype(jnp.bfloat16),
        "norm_bias": scatter_about(key_of[7], (LAYERS, D), 0.3, 2.0),
        "freq_seeds": place_ends(jax.random.randint(key_of[8], (LAYERS, HEADS, DH), 1, FEAT), jax.random.fold_in(key_of[8], 1), 1, FEAT - 1).astype(jnp.int32),
        "doc_starts": draw_doc_starts(jax.random.fold_in(key_of[10], 71), 0),
    }


EPSILON = 1e-05
HIGH = lax.Precision.HIGHEST

@jax.custom_vjp
def low(v):
    return lax.optimization_barrier(v.astype(jnp.bfloat16)).astype(jnp.float32)

@jax.custom_vjp
def low_back(v):
    return v

def low_keep(v):
    return (low(v), None)

def low_pass(kept, grad):
    return (grad,)

def back_keep(v):
    return (v, None)

def back_low(kept, grad):
    return (low(grad),)
low.defvjp(low_keep, low_pass)
low_back.defvjp(back_keep, back_low)

def matmul(left, right):
    return jnp.dot(left, right, precision=HIGH, preferred_element_type=jnp.float32)

def layer_norm(values, scale_gain, offset):
    average = lax.optimization_barrier(jnp.mean(values, -1, keepdims=True))
    centered = values - average
    variance = lax.optimization_barrier(jnp.mean(centered * centered, -1, keepdims=True))
    return centered * lax.rsqrt(variance + EPSILON) * scale_gain + offset

def normal_quantile(prob):
    nearer = jnp.minimum(prob, 1.0 - prob)
    radius = jnp.sqrt(-2.0 * jnp.log(nearer))
    upper = 2.515517 + 0.802853 * radius + 0.010328 * radius * radius
    lower = 1.0 + 1.432788 * radius + 0.189269 * radius * radius + 0.001308 * radius * radius * radius
    magnitude = radius - upper / lower
    return jnp.where(prob > 0.5, magnitude, -magnitude)

def cosine_table(head_size):
    samples = jnp.arange(head_size, dtype=jnp.float32)
    freqs = samples[:, None]
    angles = math.pi * (samples[None, :] + 0.5) * freqs / head_size
    cosine_rows = jnp.cos(angles) * math.sqrt(2.0 / head_size)
    return jnp.where(freqs == 0.0, cosine_rows * math.sqrt(0.5), cosine_rows)

def feature_tables(seeds):
    indices = jnp.arange(FEAT, dtype=jnp.int32)
    lattice = indices[None, :, None] * seeds[:, None, :] % FEAT
    frequency = normal_quantile((lattice.astype(jnp.float32) + 0.5) / FEAT)
    cosine_rows = cosine_table(DH)
    project = jnp.einsum('kn,hmk->hnm', cosine_rows, frequency, precision=HIGH) * DH ** (-0.25)
    weights = FEAT * jax.nn.softmax(-0.5 / DH * lax.optimization_barrier(jnp.sum(frequency * frequency, -1)), axis=-1)
    return (project, weights)

def rotary_tables(length):
    position = jnp.arange(length, dtype=jnp.float32)
    inverse = 10000.0 ** (-jnp.arange(0, ROT, 2, dtype=jnp.float32) / ROT)
    angles = position[:, None] * inverse[None, :]
    angles = jnp.concatenate([angles, angles], axis=1)
    return (jnp.cos(angles), jnp.sin(angles))

def rotate(head_values, cosine_rows, sine_rows):
    turned_part = head_values[..., :ROT]
    halfway = ROT // 2
    swapped = jnp.concatenate([-turned_part[..., halfway:], turned_part[..., :halfway]], axis=-1)
    rotated = turned_part * cosine_rows[:, None, :] + swapped * sine_rows[:, None, :]
    return jnp.concatenate([rotated, head_values[..., ROT:]], axis=-1)

def feature_maps(queries, keys_in, cosine_rows, sine_rows, project, weights):
    length = queries.shape[0]
    query_heads = queries.reshape(length, HEADS, DH)
    key_heads = keys_in.reshape(length, HEADS, DH)
    query_z = jnp.einsum('thd,hdm->thm', rotate(query_heads, cosine_rows, sine_rows), project, precision=HIGH)
    key_z = jnp.einsum('thd,hdm->thm', rotate(key_heads, cosine_rows, sine_rows), project, precision=HIGH)
    key_z = key_z - 0.5 / math.sqrt(DH) * lax.optimization_barrier(jnp.sum(key_heads * key_heads, -1, keepdims=True))
    return (jnp.exp(query_z), weights[None, :, :] * jnp.exp(key_z))

def attention_branch(hidden, block_weight, block_bias, project, weights, cosine_rows, sine_rows, allowed):
    length = hidden.shape[0]
    projected = low_back(matmul(hidden, jnp.transpose(block_weight[:3 * D])) + block_bias[:3 * D])
    query_feat, key_feat = feature_maps(projected[:, :D], projected[:, D:2 * D], cosine_rows, sine_rows, project, weights)
    query_feat = low(query_feat)
    key_feat = low(key_feat)
    value_heads = low(projected[:, 2 * D:]).reshape(length, HEADS, DH)
    scores = jnp.einsum('qhm,khm->hqk', query_feat, key_feat, precision=HIGH)
    scores = low_back(jnp.where(allowed[None], scores, 0.0))
    totals = lax.optimization_barrier(jnp.sum(scores, -1))
    numerator = low_back(jnp.einsum('hqk,khd->qhd', low(scores), value_heads, precision=HIGH))
    mixed_heads = numerator / jnp.transpose(totals)[:, :, None]
    mixed_heads = low(low_back(mixed_heads.reshape(length, D)))
    return matmul(mixed_heads, block_weight[3 * D:]) + block_bias[3 * D:]

def mlp_branch(hidden, block_weight, block_bias, up_block, down_block):
    hidden_units = low_back(matmul(hidden, jnp.transpose(up_block)) + block_bias)
    active = low(jax.nn.gelu(hidden_units, approximate=False))
    return matmul(active, block_weight) + down_block

def sequence_forward(values, starts, weights_all, biases_all, up_all, down_all, gains_all, offsets_all, tables, cosine_rows, sine_rows):
    length = values.shape[0]
    position = jnp.arange(length, dtype=jnp.int32)
    doc_ids = lax.optimization_barrier(jnp.sum((starts[None, :] <= position[:, None]).astype(jnp.int32), axis=1))
    allowed = (doc_ids[:, None] == doc_ids[None, :]) & (position[None, :] <= position[:, None])
    for layer_idx in range(LAYERS):
        hidden = low(layer_norm(values, gains_all[layer_idx], offsets_all[layer_idx]))
        project, weights = tables[layer_idx]
        attn_out = attention_branch(hidden, weights_all[0, layer_idx], biases_all[0, layer_idx], project, weights, cosine_rows, sine_rows, allowed)
        mlp_out = mlp_branch(hidden, weights_all[1, layer_idx], biases_all[1, layer_idx], up_all[layer_idx], down_all[layer_idx])
        values = low_back(values + attn_out + mlp_out)
    return values

def reference(tokens, cotangent, branch_weight, branch_bias, up_weight, down_bias, norm_gain, norm_bias, freq_seeds, doc_starts):
    cosine_rows, sine_rows = rotary_tables(LEN)
    tables = [feature_tables(freq_seeds[layer_idx]) for layer_idx in range(LAYERS)]
    primals = tuple((entry.astype(jnp.float32) for entry in (tokens, branch_weight, branch_bias, up_weight, down_bias, norm_gain, norm_bias)))

    def forward(values, weights_all, biases_all, up_all, down_all, gains_all, offsets_all):

        def one_sequence(values_seq, starts):
            return sequence_forward(values_seq, starts, weights_all, biases_all, up_all, down_all, gains_all, offsets_all, tables, cosine_rows, sine_rows)
        checked = jax.checkpoint(one_sequence)

        def advance(carried, element):
            return (carried, checked(element[0], element[1]))
        _, outputs = lax.scan(advance, jnp.zeros((), jnp.float32), (values.reshape(SEQS, LEN, D), doc_starts))
        return outputs.reshape(TOKENS, D)
    result, backward = jax.vjp(forward, *primals)
    gradients = backward(cotangent.astype(jnp.float32))
    return (result, gradients[0], gradients[1], gradients[2], gradients[3], gradients[4], gradients[5], gradients[6])
```

```python
import functools
import math

import jax
import jax.numpy as jnp
import numpy as np
from jax import lax
from jax.experimental import pallas as pl
from jax.experimental.pallas import tpu as pltpu
from jax.sharding import PartitionSpec as P

HEADS = 16
DH = 64
ROT = 16
FEAT = 64
LAYERS = 2
EPSILON = 1e-05
HIGH = lax.Precision.HIGHEST
F32 = jnp.float32
BF16 = jnp.bfloat16
WIDE = 256
PAIR = 128
QUADS = HEADS * DH // WIDE
PAIRS = HEADS * DH // PAIR
ROWS = 256
VMEM_LIMIT = 56 * 1024 * 1024


def params():
    return pltpu.CompilerParams(vmem_limit_bytes=VMEM_LIMIT)


def whole(shape):
    zeros = (0,) * len(shape)
    return pl.BlockSpec(shape, lambda *_: zeros, pipeline_mode=pl.Buffered(1))


def dot_nn(left, right):
    return lax.dot_general(left, right, (((1,), (0,)), ((), ())), preferred_element_type=F32)


def dot_nt(left, right):
    return lax.dot_general(left, right, (((1,), (1,)), ((), ())), preferred_element_type=F32)


def split(values):
    upper = values.astype(BF16)
    return upper, (values - upper.astype(F32)).astype(BF16)


def lane_index(rows, lanes):
    return lax.broadcasted_iota(jnp.int32, (rows, lanes), 1)


def row_index(rows, lanes):
    return lax.broadcasted_iota(jnp.int32, (rows, lanes), 0)


def cosine_block():
    samples = np.arange(DH, dtype=np.float64)
    angles = math.pi * (samples[None, :] + 0.5) * samples[:, None] / DH
    table = np.cos(angles) * math.sqrt(2.0 / DH)
    table[0] *= math.sqrt(0.5)
    return np.kron(np.eye(WIDE // DH), table.T * DH ** (-0.25)).astype(np.float32)


def rotary_rows(length):
    position = np.arange(length, dtype=np.float32)
    inverse = (10000.0 ** (-np.arange(0, ROT, 2, dtype=np.float32) / ROT)).astype(np.float32)
    angles = position[:, None] * inverse[None, :]
    cosine, sine = np.cos(angles), np.sin(angles)
    rest = DH - ROT
    cosine_head = np.concatenate([cosine, cosine, np.ones((length, rest))], 1)
    sine_head = np.concatenate([-sine, sine, np.zeros((length, rest))], 1)
    repeat = PAIR // DH
    return (
        np.tile(cosine_head, (1, repeat)).astype(np.float32),
        np.tile(sine_head, (1, repeat)).astype(np.float32),
    )


def tables_kernel(seeds_ref, cosine_ref, upper_ref, lower_ref, weight_ref):
    feature = lane_index(WIDE, WIDE)
    lattice = (feature % FEAT) * seeds_ref[0] % FEAT
    prob = (lattice.astype(F32) + 0.5) / FEAT
    radius = jnp.sqrt(-2.0 * jnp.log(jnp.minimum(prob, 1.0 - prob)))
    above = 2.515517 + 0.802853 * radius + 0.010328 * radius * radius
    below = (
        1.0 + 1.432788 * radius + 0.189269 * radius * radius + 0.001308 * radius * radius * radius
    )
    magnitude = radius - above / below
    same_head = row_index(WIDE, WIDE) // DH == feature // FEAT
    omega = jnp.where(same_head, jnp.where(prob > 0.5, magnitude, -magnitude), 0.0)
    project = jnp.dot(cosine_ref[...], omega, precision=HIGH, preferred_element_type=F32)
    upper_ref[0, 0], lower_ref[0, 0] = split(project)
    grown = jnp.exp(-0.5 / DH * jnp.sum(omega * omega, axis=0, keepdims=True))
    total = jnp.dot(
        jnp.broadcast_to(grown, (8, WIDE)),
        same_head.astype(F32),
        precision=HIGH,
        preferred_element_type=F32,
    )
    weight_ref[0, 0] = FEAT * grown / total[:1]


def feature_tables(seeds):
    return pl.pallas_call(
        tables_kernel,
        grid=(LAYERS, QUADS),
        in_specs=[
            pl.BlockSpec((1, WIDE, 1), lambda l, g: (l, g, 0)),
            whole((WIDE, WIDE)),
        ],
        out_specs=[
            pl.BlockSpec((1, 1, WIDE, WIDE), lambda l, g: (l, g, 0, 0)),
            pl.BlockSpec((1, 1, WIDE, WIDE), lambda l, g: (l, g, 0, 0)),
            pl.BlockSpec((1, 1, 1, WIDE), lambda l, g: (l, g, 0, 0)),
        ],
        out_shape=[
            jax.ShapeDtypeStruct((LAYERS, QUADS, WIDE, WIDE), BF16),
            jax.ShapeDtypeStruct((LAYERS, QUADS, WIDE, WIDE), BF16),
            jax.ShapeDtypeStruct((LAYERS, QUADS, 1, WIDE), F32),
        ],
        compiler_params=params(),
        name="feature_tables",
    )(seeds.reshape(LAYERS, HEADS * DH, 1), jnp.asarray(cosine_block()))


def turn(values, cosine, sine):
    lanes = values.shape[1]
    half = ROT // 2
    lane = lane_index(*values.shape) % DH
    swapped = jnp.where(
        lane < half, pltpu.roll(values, lanes - half, 1), pltpu.roll(values, half, 1)
    )
    return values * cosine + swapped * sine


def turn_back(values, cosine, sine):
    lanes = values.shape[1]
    half = ROT // 2
    lane = lane_index(*values.shape) % DH
    turned = values * sine
    swapped = jnp.where(
        lane < half, pltpu.roll(turned, lanes - half, 1), pltpu.roll(turned, half, 1)
    )
    return values * cosine + jnp.where(lane < ROT, swapped, 0.0)


def normalized(x_ref_rows, gain, offset):
    average = jnp.mean(x_ref_rows, -1, keepdims=True)
    centered = x_ref_rows - average
    variance = jnp.mean(centered * centered, -1, keepdims=True)
    return centered * lax.rsqrt(variance + EPSILON) * gain + offset


def start_layer(stream, x_ref, h_ref, gain_ref, offset_ref):
    length = h_ref.shape[0]
    step = min(128, length)

    @pl.loop(0, length // step)
    def _(index):
        rows = pl.ds(pl.multiple_of(index * step, step), step)
        values = stream[0][rows].astype(F32)
        if len(stream) > 1:
            values = values + (stream[1][rows] + stream[2][rows])
            x_ref[rows] = values
        h_ref[rows] = normalized(
            values, gain_ref[...].astype(F32), offset_ref[...].astype(F32)
        ).astype(BF16)


def gelu_parts(units):
    grown = jnp.exp(-0.5 * units * units)
    inverse = 1.0 / (1.0 + (0.3275911 * math.sqrt(0.5)) * jnp.abs(units))
    series = 0.5 * 1.061405429
    for factor in (-1.453152027, 1.421413741, -0.284496736, 0.254829592):
        series = series * inverse + 0.5 * factor
    tail = series * inverse * grown
    below = jnp.where(units >= 0.0, 1.0 - tail, tail)
    return below, grown * (1.0 / math.sqrt(2.0 * math.pi))


FF_BLOCK = 512


def mlp_forward_kernel(count, *refs):
    stream, refs = refs[:count], refs[count:]
    gain_ref, offset_ref, up_ref, bias_ref, down_ref, down_bias_ref = refs[:6]
    refs = refs[6:]
    x_ref = None
    if count > 1:
        x_ref, refs = refs[0], refs[1:]
    part_ref, h_ref, act_ref, slope_ref = refs
    step = pl.program_id(0)

    @pl.when(step == 0)
    def _():
        start_layer(stream, x_ref, h_ref, gain_ref, offset_ref)
        part_ref[...] = jnp.broadcast_to(down_bias_ref[...].astype(F32), part_ref.shape)

    for first in range(0, h_ref.shape[0], ROWS):
        rows = slice(first, first + ROWS)
        units = dot_nt(h_ref[rows], up_ref[0]) + bias_ref[0]
        below, density = gelu_parts(units)
        active = (units * below).astype(BF16)
        act_ref[0, rows] = active
        slope_ref[0, rows] = (below + units * density).astype(BF16)
        part_ref[rows] += dot_nn(active, down_ref[0, 0])


def plane_block(length, lanes):
    per_plane = 1024 // lanes
    return pl.BlockSpec((1, length, lanes), lambda j: (j // per_plane, 0, j % per_plane))


def mlp_forward(layer, stream, gain, offset, up, biases, down_weight, down_bias):
    length, width = stream[0].shape
    hidden = up.shape[1]
    blocks = hidden // FF_BLOCK
    state = jax.ShapeDtypeStruct((4, length, width), BF16)
    full = jax.ShapeDtypeStruct((length, width), F32)
    out_shape = [full, jax.ShapeDtypeStruct((length, width), BF16), state, state]
    out_specs = [whole((length, width)), whole((length, width))]
    out_specs += [plane_block(length, FF_BLOCK)] * 2
    if len(stream) > 1:
        out_shape, out_specs = [full] + out_shape, [whole((length, width))] + out_specs
    return pl.pallas_call(
        functools.partial(mlp_forward_kernel, len(stream)),
        grid=(blocks,),
        in_specs=[whole((length, width))] * len(stream)
        + [
            whole((1, width)),
            whole((1, width)),
            pl.BlockSpec((1, FF_BLOCK, width), lambda j: (layer, j, 0)),
            pl.BlockSpec((1, 1, FF_BLOCK), lambda j: (j, 0, 0)),
            pl.BlockSpec((1, 1, FF_BLOCK, width), lambda j: (0, layer, j, 0)),
            whole((1, width)),
        ],
        out_specs=out_specs,
        out_shape=out_shape,
        compiler_params=params(),
        name="mlp_forward",
    )(*stream, gain, offset, up, biases.reshape(blocks, 1, FF_BLOCK), down_weight, down_bias)


def mlp_backward_kernel(
    grad_ref, h_ref, act_ref, slope_ref, down_ref, up_ref,
    part_ref, weight_ref, near_ref, far_ref, bias_ref, grad_t, h_t,
):
    step = pl.program_id(0)

    @pl.when(step == 0)
    def _():
        grad_t[...] = grad_ref[...].T
        h_t[...] = h_ref[...].T
        part_ref[...] = jnp.zeros_like(part_ref)

    length = h_ref.shape[0]
    bias = jnp.zeros((1, FF_BLOCK), F32)
    pieces = []
    for first in range(0, length, ROWS):
        rows = slice(first, first + ROWS)
        grad_act = dot_nt(grad_ref[rows], down_ref[0, 0])
        grad_unit = (grad_act * slope_ref[0, rows].astype(F32)).astype(BF16)
        bias += jnp.sum(grad_unit.astype(F32), axis=0, keepdims=True)
        pieces.append(grad_unit)
        part_ref[rows] += dot_nn(grad_unit, up_ref[0])
    bias_ref[0] = bias
    units = jnp.concatenate(pieces, axis=0)
    half = near_ref.shape[2]
    for first in range(0, h_t.shape[0], ROWS):
        rows = slice(first, first + ROWS)
        for block in range(FF_BLOCK // WIDE):
            lanes = slice(block * WIDE, (block + 1) * WIDE)
            weight_ref[block, rows] = dot_nn(grad_t[rows], act_ref[0, :, lanes])
            up_grad = dot_nn(h_t[rows], units[:, lanes])
            near_ref[block, rows] = up_grad[:, :half]
            far_ref[block, rows] = up_grad[:, half:]


def mlp_backward(layer, grad, h, act, slope, down_weight, up):
    length, width = h.shape
    hidden = up.shape[1]
    blocks = hidden // FF_BLOCK
    per = FF_BLOCK // WIDE
    halves = jax.ShapeDtypeStruct((hidden // WIDE, width, WIDE // 2), F32)
    return pl.pallas_call(
        mlp_backward_kernel,
        grid=(blocks,),
        in_specs=[
            whole((length, width)),
            whole((length, width)),
            plane_block(length, FF_BLOCK),
            plane_block(length, FF_BLOCK),
            pl.BlockSpec((1, 1, FF_BLOCK, width), lambda j: (0, layer, j, 0)),
            pl.BlockSpec((1, FF_BLOCK, width), lambda j: (layer, j, 0)),
        ],
        out_specs=[
            whole((length, width)),
            pl.BlockSpec((per, width, WIDE), lambda j: (j, 0, 0)),
            pl.BlockSpec((per, width, WIDE // 2), lambda j: (j, 0, 0)),
            pl.BlockSpec((per, width, WIDE // 2), lambda j: (j, 0, 0)),
            pl.BlockSpec((1, 1, FF_BLOCK), lambda j: (j, 0, 0)),
        ],
        out_shape=[
            jax.ShapeDtypeStruct((length, width), F32),
            jax.ShapeDtypeStruct((hidden // WIDE, width, WIDE), F32),
            halves,
            halves,
            jax.ShapeDtypeStruct((blocks, 1, FF_BLOCK), F32),
        ],
        scratch_shapes=[pltpu.VMEM((width, length), BF16), pltpu.VMEM((width, length), BF16)],
        compiler_params=params(),
        name="mlp_backward",
    )(grad, h, act, slope, down_weight, up)


def head_sums(values, ones):
    upper, lower = split(values)
    return dot_nn(upper, ones) + dot_nn(lower, ones)


def same_head_ones():
    same = row_index(WIDE, WIDE) // DH == lane_index(WIDE, WIDE) // DH
    return jnp.where(same, 1.0, 0.0).astype(BF16)


def project_kernel(count, *refs):
    stream, refs = refs[:count], refs[count:]
    gain_ref, offset_ref, weight_ref, bias_ref = refs[:4]
    upper_ref, lower_ref, scale_ref, cosine_ref, sine_ref = refs[4:9]
    refs = refs[9:]
    x_ref = None
    if count > 1:
        x_ref, refs = refs[0], refs[1:]
    h_ref, state_ref, keys = refs
    step = pl.program_id(0)
    kind, group = step // QUADS, step % QUADS
    length = h_ref.shape[0]

    @pl.when(step == 0)
    def _():
        start_layer(stream, x_ref, h_ref, gain_ref, offset_ref)

    def features(values, rows):
        cosine = jnp.concatenate([cosine_ref[rows]] * (WIDE // PAIR), axis=1)
        sine = jnp.concatenate([sine_ref[rows]] * (WIDE // PAIR), axis=1)
        upper, lower = split(turn(values, cosine, sine))
        table_up, table_low = upper_ref[0, 0], lower_ref[0, 0]
        return dot_nn(upper, table_up) + (dot_nn(lower, table_up) + dot_nn(upper, table_low))

    @pl.when(kind == 0)
    def _():
        for first in range(0, length, ROWS):
            rows = slice(first, first + ROWS)
            values = dot_nt(h_ref[rows], weight_ref[0, 0]) + bias_ref[0]
            state_ref[0, rows] = jnp.exp(features(values, rows)).astype(BF16)

    @pl.when(kind == 1)
    def _():
        ones = same_head_ones()
        for first in range(0, length, ROWS):
            rows = slice(first, first + ROWS)
            values = dot_nt(h_ref[rows], weight_ref[0, 0]) + bias_ref[0]
            keys[group, rows] = values.astype(BF16)
            squares = head_sums(values * values, ones)
            logs = features(values, rows) - (0.5 / math.sqrt(DH)) * squares
            state_ref[0, rows] = (scale_ref[0, 0] * jnp.exp(logs)).astype(BF16)

    @pl.when(kind == 2)
    def _():
        state_ref[0] = keys[group]

    @pl.when(kind == 3)
    def _():
        for first in range(0, length, ROWS):
            rows = slice(first, first + ROWS)
            values = dot_nt(h_ref[rows], weight_ref[0, 0]) + bias_ref[0]
            state_ref[0, rows] = values.astype(BF16)


def project_forward(layer, stream, gain, offset, weight, biases, tables, rotary):
    length, width = stream[0].shape
    full = jax.ShapeDtypeStruct((length, width), F32)
    state = jax.ShapeDtypeStruct((4, length, width), BF16)
    out_shape = [jax.ShapeDtypeStruct((length, width), BF16), state]
    out_specs = [whole((length, width)), plane_block(length, WIDE)]
    if len(stream) > 1:
        out_shape, out_specs = [full] + out_shape, [whole((length, width))] + out_specs

    def source(j):
        return jnp.where(j < 2 * QUADS, j, jnp.maximum(j - QUADS, 2 * QUADS - 1))

    def table(j):
        return jnp.where(j < 2 * QUADS, j % QUADS, QUADS - 1)

    return pl.pallas_call(
        functools.partial(project_kernel, len(stream)),
        grid=(4 * QUADS,),
        in_specs=[whole((length, width))] * len(stream)
        + [
            whole((1, width)),
            whole((1, width)),
            pl.BlockSpec((1, 1, WIDE, width), lambda j: (0, layer, source(j), 0)),
            pl.BlockSpec((1, 1, WIDE), lambda j: (source(j), 0, 0)),
            pl.BlockSpec((1, 1, WIDE, WIDE), lambda j: (layer, table(j), 0, 0)),
            pl.BlockSpec((1, 1, WIDE, WIDE), lambda j: (layer, table(j), 0, 0)),
            pl.BlockSpec((1, 1, 1, WIDE), lambda j: (layer, table(j), 0, 0)),
            whole((length, PAIR)),
            whole((length, PAIR)),
        ],
        out_specs=out_specs,
        out_shape=out_shape,
        scratch_shapes=[pltpu.VMEM((QUADS, length, WIDE), BF16)],
        compiler_params=params(),
        name="project_forward",
    )(*stream, gain, offset, weight, biases.reshape(-1, 1, WIDE), *tables, *rotary)


def write_mask(starts_ref, mask_ref, flipped):
    length = mask_ref.shape[0]
    keys = lane_index(1, length)
    documents = sum((starts_ref[0, i] <= keys).astype(jnp.int32) for i in range(starts_ref.shape[1]))
    for first in range(0, length, ROWS):
        own = row_index(ROWS, 1) + first
        document = sum(
            (starts_ref[0, i] <= own).astype(jnp.int32) for i in range(starts_ref.shape[1])
        )
        order = (own <= keys) if flipped else (keys <= own)
        seen = (document == documents) & order
        mask_ref[first : first + ROWS] = jnp.where(seen, 1.0, 0.0).astype(BF16)


def attend_kernel(starts_ref, state_ref, out_ref, mask_ref):
    @pl.when(pl.program_id(0) == 0)
    def _():
        write_mask(starts_ref, mask_ref, False)

    length = mask_ref.shape[0]
    zero = jnp.zeros((), BF16)
    one = jnp.ones((), BF16)
    for first in range(0, length, ROWS):
        rows = slice(first, first + ROWS)
        finish = first + ROWS
        left = lane_index(finish, PAIR) < DH
        seen = mask_ref[rows, :finish] > zero
        sums = []
        for own in (left, ~left):
            keys = jnp.where(own, state_ref[1, :finish], zero)
            scores = dot_nt(state_ref[0, rows], keys).astype(BF16)
            scores = jnp.where(seen, scores, zero)
            sums.append(dot_nn(scores, jnp.where(own, state_ref[3, :finish], one)))
        left = lane_index(ROWS, PAIR) < DH
        numer = jnp.where(left, sums[0], sums[1])
        denom = jnp.where(left, pltpu.roll(sums[0], DH, 1), pltpu.roll(sums[1], DH, 1))
        inverse = 1.0 / denom
        out_ref[0, rows] = (numer * inverse).astype(BF16)
        out_ref[1, rows], out_ref[2, rows] = split(inverse)


def attend_forward(starts, state):
    _, length, width = state.shape
    block = pl.BlockSpec((4, length, PAIR), lambda p: (0, 0, p))
    return pl.pallas_call(
        attend_kernel,
        grid=(PAIRS,),
        in_specs=[pl.BlockSpec(memory_space=pltpu.SMEM), block],
        out_specs=block,
        out_shape=jax.ShapeDtypeStruct(state.shape, BF16),
        scratch_shapes=[pltpu.VMEM((length, length), BF16)],
        compiler_params=params(),
        name="attend_forward",
    )(starts, state)


def mix_kernel(mixed_ref, weight_ref, bias_ref, part_ref):
    part_ref[...] = dot_nn(mixed_ref[0], weight_ref[0, 0]) + bias_ref[0]


def mix_forward(layer, mixed, weight, biases):
    _, length, width = mixed.shape
    return pl.pallas_call(
        mix_kernel,
        grid=(QUADS,),
        in_specs=[
            pl.BlockSpec((1, length, width), lambda j: (0, 0, 0), pipeline_mode=pl.Buffered(1)),
            pl.BlockSpec((1, 1, width, WIDE), lambda j: (0, layer, 3, j)),
            pl.BlockSpec((1, 1, WIDE), lambda j: (3 * QUADS + j, 0, 0)),
        ],
        out_specs=pl.BlockSpec((length, WIDE), lambda j: (0, j)),
        out_shape=jax.ShapeDtypeStruct((length, width), F32),
        compiler_params=params(),
        name="mix_forward",
    )(mixed, weight, biases.reshape(-1, 1, WIDE))


def mix_backward_kernel(grad_ref, weight_ref, mixed_ref, out_ref):
    row, lane = row_index(WIDE, WIDE), lane_index(WIDE, WIDE)
    partner = (row // PAIR == lane // PAIR) & (row // DH != lane // DH)
    ones = jnp.where(partner, 1.0, 0.0).astype(BF16)
    length = grad_ref.shape[0]
    for first in range(0, length, ROWS):
        rows = slice(first, first + ROWS)
        grad = dot_nt(grad_ref[rows], weight_ref[0, 0]).astype(BF16).astype(F32)
        inverse = mixed_ref[1, rows].astype(F32) + mixed_ref[2, rows].astype(F32)
        scaled = grad * inverse
        upper, lower = split(-head_sums(scaled * mixed_ref[0, rows].astype(F32), ones))
        numer = scaled.astype(BF16)
        lane = lane_index(ROWS, WIDE)
        spare = jnp.where(
            lane % DH == 0, upper, jnp.where(lane % DH == 1, lower, jnp.zeros((), BF16))
        )
        left = lane % PAIR < DH
        out_ref[0, rows] = jnp.where(left, numer, spare)
        out_ref[1, rows] = jnp.where(left, spare, numer)


def mix_backward(layer, grad, weight, mixed):
    _, length, width = mixed.shape
    return pl.pallas_call(
        mix_backward_kernel,
        grid=(QUADS,),
        in_specs=[
            whole((length, width)),
            pl.BlockSpec((1, 1, WIDE, width), lambda j: (0, layer, 3 * QUADS + j, 0)),
            pl.BlockSpec((4, length, WIDE), lambda j: (0, 0, j)),
        ],
        out_specs=pl.BlockSpec((2, length, WIDE), lambda j: (0, 0, j)),
        out_shape=jax.ShapeDtypeStruct((2, length, width), BF16),
        compiler_params=params(),
        name="mix_backward",
    )(grad, weight, mixed)


def attend_backward_kernel(starts_ref, state_ref, numer_ref, out_ref, mask_ref, query_t):
    @pl.when(pl.program_id(0) == 0)
    def _():
        write_mask(starts_ref, mask_ref, True)

    length = mask_ref.shape[0]
    zero = jnp.zeros((), BF16)
    one = jnp.ones((), BF16)
    query_t[...] = jnp.zeros_like(query_t)
    for first in range(0, length, ROWS):
        rows = slice(first, first + ROWS)
        seen = mask_ref[rows, first:] > zero
        lane = lane_index(ROWS, PAIR)
        left = lane < DH
        spare = jnp.where(lane % DH < 2, one, zero)
        keys, values = state_ref[1, rows], state_ref[3, rows]
        queries = state_ref[0, first:]
        numer = jnp.where(lane_index(length - first, PAIR) < DH, numer_ref[0, first:], numer_ref[1, first:])
        grads = []
        for head, own in enumerate((left, ~left)):
            own_keys = jnp.where(own, keys, zero)
            scores = dot_nt(own_keys, queries).astype(BF16)
            scores = jnp.where(seen, scores, zero)
            grad_value = dot_nn(scores, numer)
            grad_scores = dot_nt(jnp.where(own, values, spare), numer_ref[head, first:]).astype(BF16)
            grad_scores = jnp.where(seen, grad_scores, zero)
            grad_key = dot_nn(grad_scores, queries)
            query_t[head, :, first:] += dot_nn(own_keys.T[head * DH : (head + 1) * DH], grad_scores)
            grads.append((grad_value, grad_key))
        out_ref[2, rows] = jnp.where(left, grads[0][0], grads[1][0]).astype(BF16)
        grad_key = jnp.where(left, grads[0][1], grads[1][1])
        out_ref[1, rows] = (grad_key * keys.astype(F32)).astype(BF16)
    for first in range(0, length, ROWS):
        rows = slice(first, first + ROWS)
        grad_query = jnp.concatenate([query_t[0, :, rows], query_t[1, :, rows]], axis=0).T
        out_ref[0, rows] = (grad_query * state_ref[0, rows].astype(F32)).astype(BF16)


def attend_backward(starts, state, numer):
    _, length, width = state.shape
    return pl.pallas_call(
        attend_backward_kernel,
        grid=(PAIRS,),
        in_specs=[
            pl.BlockSpec(memory_space=pltpu.SMEM),
            pl.BlockSpec((4, length, PAIR), lambda p: (0, 0, p)),
            pl.BlockSpec((2, length, PAIR), lambda p: (0, 0, p)),
        ],
        out_specs=pl.BlockSpec((3, length, PAIR), lambda p: (0, 0, p)),
        out_shape=jax.ShapeDtypeStruct((3, length, width), BF16),
        scratch_shapes=[
            pltpu.VMEM((length, length), BF16),
            pltpu.VMEM((2, DH, length), F32),
        ],
        compiler_params=params(),
        name="attend_backward",
    )(starts, state, numer)


def project_backward_kernel(
    grad_ref, h_ref, mixed_ref, feat_ref, keys_ref, table_ref, cosine_ref, sine_ref, weight_ref,
    part_ref, out_ref, bias_ref, grad_t, h_t, flow,
):
    step = pl.program_id(0)
    kind, length = step // QUADS, h_ref.shape[0]

    @pl.when(step == 0)
    def _():
        grad_t[...] = grad_ref[...].T
        h_t[...] = h_ref[...].T
        part_ref[...] = jnp.zeros_like(part_ref)

    def project_back(rows):
        cosine = jnp.concatenate([cosine_ref[rows]] * (WIDE // PAIR), axis=1)
        sine = jnp.concatenate([sine_ref[rows]] * (WIDE // PAIR), axis=1)
        return turn_back(dot_nt(feat_ref[0, rows], table_ref[0, 0]), cosine, sine)

    @pl.when(kind == 0)
    def _():
        flow[...] = mixed_ref[0]
        bias_ref[0] = jnp.sum(feat_ref[0, :1].astype(F32), axis=0, keepdims=True)

    @pl.when(kind == 1)
    def _():
        for first in range(0, length, ROWS):
            rows = slice(first, first + ROWS)
            flow[rows] = project_back(rows).astype(BF16)

    @pl.when(kind == 2)
    def _():
        ones = same_head_ones()
        for first in range(0, length, ROWS):
            rows = slice(first, first + ROWS)
            shrink = dot_nn(feat_ref[0, rows], ones) * (1.0 / math.sqrt(DH))
            flow[rows] = (project_back(rows) - keys_ref[0, rows].astype(F32) * shrink).astype(BF16)

    @pl.when(kind == 3)
    def _():
        flow[...] = feat_ref[0]

    @pl.when(kind > 0)
    def _():
        bias = jnp.zeros((1, WIDE), F32)
        for first in range(0, length, ROWS):
            rows = slice(first, first + ROWS)
            bias += jnp.sum(flow[rows].astype(F32), axis=0, keepdims=True)
            part_ref[rows] += dot_nn(flow[rows], weight_ref[0, 0])
            out_ref[0, rows] = dot_nn(h_t[rows], flow[...])
        bias_ref[0] = bias

    @pl.when(kind == 0)
    def _():
        for first in range(0, length, ROWS):
            rows = slice(first, first + ROWS)
            out_ref[0, rows] = dot_nn(grad_t[rows], flow[...])


def project_backward(layer, grad, h, mixed, feats, state, tables, rotary, weight):
    _, length, width = state.shape
    blocks = 4 * QUADS

    def at(j):
        return jnp.maximum(j - QUADS, 0)

    def target(j):
        return jnp.where(j < QUADS, 3 * QUADS + j, j - QUADS)

    return pl.pallas_call(
        project_backward_kernel,
        grid=(blocks,),
        in_specs=[
            whole((length, width)),
            whole((length, width)),
            pl.BlockSpec((1, length, WIDE), lambda j: (0, 0, jnp.minimum(j, QUADS - 1))),
            pl.BlockSpec((1, length, WIDE), lambda j: (at(j) // QUADS, 0, at(j) % QUADS)),
            pl.BlockSpec(
                (1, length, WIDE), lambda j: (2, 0, jnp.clip(j - 2 * QUADS, 0, QUADS - 1))
            ),
            pl.BlockSpec((1, 1, WIDE, WIDE), lambda j: (layer, at(j) % QUADS, 0, 0)),
            whole((length, PAIR)),
            whole((length, PAIR)),
            pl.BlockSpec((1, 1, WIDE, width), lambda j: (0, layer, at(j), 0)),
        ],
        out_specs=[
            whole((length, width)),
            pl.BlockSpec((1, width, WIDE), lambda j: (target(j), 0, 0)),
            pl.BlockSpec((1, 1, WIDE), lambda j: (target(j), 0, 0)),
        ],
        out_shape=[
            jax.ShapeDtypeStruct((length, width), F32),
            jax.ShapeDtypeStruct((blocks, width, WIDE), F32),
            jax.ShapeDtypeStruct((blocks, 1, WIDE), F32),
        ],
        scratch_shapes=[
            pltpu.VMEM((width, length), BF16),
            pltpu.VMEM((width, length), BF16),
            pltpu.VMEM((length, WIDE), BF16),
        ],
        compiler_params=params(),
        name="project_backward",
    )(grad, h, mixed, feats, state, tables[0], *rotary, weight)


def norm_backward_kernel(x_ref, own_ref, other_ref, grad_ref, gain_ref, out_ref, sums_ref):
    @pl.when(pl.program_id(0) == 0)
    def _():
        sums_ref[...] = jnp.zeros_like(sums_ref)

    values = x_ref[...].astype(F32)
    average = jnp.mean(values, -1, keepdims=True)
    centered = values - average
    variance = jnp.mean(centered * centered, -1, keepdims=True)
    inverse = lax.rsqrt(variance + EPSILON)
    unit = centered * inverse
    incoming = own_ref[...] + other_ref[...]
    grad_unit = incoming * gain_ref[...].astype(F32)
    first = jnp.mean(grad_unit, -1, keepdims=True)
    second = jnp.mean(grad_unit * unit, -1, keepdims=True)
    grad = grad_ref[...].astype(F32)
    out = grad + inverse * (grad_unit - first - unit * second)
    out_ref[...] = out.astype(out_ref.dtype)
    sums_ref[0:1] += jnp.sum(incoming * unit, axis=0, keepdims=True)
    sums_ref[1:2] += jnp.sum(incoming, axis=0, keepdims=True)
    sums_ref[2:3] += jnp.sum(grad, axis=0, keepdims=True)


def norm_backward(x, own, other, grad, gain, kind):
    length, width = own.shape
    block = pl.BlockSpec((ROWS, width), lambda i: (i, 0))
    return pl.pallas_call(
        norm_backward_kernel,
        grid=(length // ROWS,),
        in_specs=[block, block, block, block, whole((1, width))],
        out_specs=[block, whole((8, width))],
        out_shape=[
            jax.ShapeDtypeStruct((length, width), kind),
            jax.ShapeDtypeStruct((8, width), F32),
        ],
        compiler_params=params(),
        name="norm_backward",
    )(x, own, other, grad, gain)


def shards(
    tokens, cotangent, branch_weight, branch_bias, up_weight, down_bias,
    norm_gain, norm_bias, freq_seeds, doc_starts,
):
    is_attention = lax.axis_index("stream") == 0
    length, width = tokens.shape
    rotary = tuple(jnp.asarray(table) for table in rotary_rows(length))
    biases = branch_bias[0].astype(F32)
    tables = lax.cond(
        is_attention,
        lambda: tuple(feature_tables(freq_seeds)),
        lambda: (
            jnp.zeros((LAYERS, QUADS, WIDE, WIDE), BF16),
            jnp.zeros((LAYERS, QUADS, WIDE, WIDE), BF16),
            jnp.zeros((LAYERS, QUADS, 1, WIDE), F32),
        ),
    )
    swap = [(0, 1), (1, 0)]

    def attention(layer, stream):
        gain, offset = norm_gain[layer : layer + 1], norm_bias[layer : layer + 1]
        *x, h, state = project_forward(
            layer, stream, gain, offset, branch_weight, biases[layer], tables, rotary
        )
        mixed = attend_forward(doc_starts, state)
        part = mix_forward(layer, mixed, branch_weight, biases[layer])
        return tuple(x) + (part, h, state, mixed)

    def feed_forward(layer, stream):
        gain, offset = norm_gain[layer : layer + 1], norm_bias[layer : layer + 1]
        return tuple(
            mlp_forward(
                layer, stream, gain, offset, up_weight, biases[layer], branch_weight,
                down_bias[layer : layer + 1],
            )
        )

    stream = (tokens,)
    inputs, kept = [], []
    for layer in range(LAYERS):
        *x, part, h, state, mixed = lax.cond(
            is_attention,
            functools.partial(attention, layer, stream),
            functools.partial(feed_forward, layer, stream),
        )
        inputs.append(x[0] if x else tokens)
        kept.append((h, state, mixed))
        stream = (inputs[-1], part, lax.ppermute(part, "stream", swap))
    result = stream[0] + (stream[1] + stream[2])

    def attention_back(layer, grad):
        h, state, mixed = kept[layer]
        numer = mix_backward(layer, grad, branch_weight, mixed)
        feats = attend_backward(doc_starts, state, numer)
        part, weight, bias = project_backward(
            layer, grad, h, mixed, feats, state, tables, rotary, branch_weight
        )
        blank = jnp.zeros((weight.shape[0], width, WIDE // 2), F32)
        return part, weight, blank, blank, bias.reshape(-1, WIDE)

    def feed_forward_back(layer, grad):
        h, act, slope = kept[layer]
        part, weight, near, far, bias = mlp_backward(
            layer, grad, h, act, slope, branch_weight, up_weight
        )
        return part, weight, near, far, bias.reshape(-1, WIDE)

    grad = cotangent
    shares = [None] * LAYERS
    for layer in reversed(range(LAYERS)):
        part, weight, near, far, bias = lax.cond(
            is_attention,
            functools.partial(attention_back, layer, grad),
            functools.partial(feed_forward_back, layer, grad),
        )
        other = lax.ppermute(part, "stream", swap)
        kind = BF16 if layer else F32
        new_grad, sums = norm_backward(
            inputs[layer], part, other, grad, norm_gain[layer : layer + 1], kind
        )
        bias = jnp.where(
            is_attention & (jnp.arange(bias.shape[0])[:, None] >= 3 * QUADS),
            jnp.tile(sums[2].reshape(QUADS, WIDE), (bias.shape[0] // QUADS, 1)),
            bias,
        )
        scatter = functools.partial(
            lax.psum_scatter, axis_name="batch", scatter_dimension=0, tiled=True
        )
        if weight.shape[0] == lax.axis_size("batch"):
            near = lax.ppermute(near, "stream", [(1, 0)])
            up = jnp.where(is_attention, near, far)
            weight = rows_of(scatter(weight))
            up = rows_of(scatter(up))
        else:
            weight = scatter(rows_of(weight))
            up = rows_of(jnp.concatenate([near, far], axis=2))
            up = lax.psum_scatter(up, ("batch", "stream"), scatter_dimension=0, tiled=True)
        shares[layer] = (
            weight,
            scatter(bias.reshape(-1)),
            up,
            scatter(sums[2]),
            scatter(sums[0]),
            scatter(sums[1]),
        )
        grad = new_grad
    weight, bias, up, down, gain, offset = [list(group) for group in zip(*shares)]
    return (
        result,
        grad,
        jnp.stack(weight)[None],
        jnp.stack(bias)[None],
        jnp.stack(up),
        jnp.stack(down),
        jnp.stack(gain),
        jnp.stack(offset),
    )


def rows_of(blocks):
    return jnp.transpose(blocks, (0, 2, 1)).reshape(-1, blocks.shape[1])


def solution(mesh):
    placed = (
        P("batch", None),
        P("batch", None),
        P("stream", None, None, None),
        P("stream", None, None),
        P(),
        P(),
        P(),
        P(),
        P(),
        P("batch", None),
    )
    return jax.shard_map(
        shards,
        mesh=mesh,
        in_specs=placed,
        out_specs=(
            P("batch", None),
            P("batch", None),
            P("stream", None, "batch", None),
            P("stream", None, "batch"),
            P(None, ("batch", "stream"), None),
            P(None, "batch"),
            P(None, "batch"),
            P(None, "batch"),
        ),
        check_vma=False,
    )
```

```python
import functools
import math

import jax
import jax.numpy as jnp
import numpy as np
from jax import lax
from jax.experimental import pallas as pl
from jax.experimental.pallas import tpu as pltpu
from jax.sharding import PartitionSpec as P

HEADS = 16
DH = 64
ROT = 16
FEAT = 64
LAYERS = 2
EPSILON = 1e-05
HIGH = lax.Precision.HIGHEST
F32 = jnp.float32
BF16 = jnp.bfloat16
WIDE = 256
PAIR = 128
QUADS = HEADS * DH // WIDE
PAIRS = HEADS * DH // PAIR
ROWS = 256
VMEM_LIMIT = 56 * 1024 * 1024


def params():
    return pltpu.CompilerParams(vmem_limit_bytes=VMEM_LIMIT)


def whole(shape):
    zeros = (0,) * len(shape)
    return pl.BlockSpec(shape, lambda *_: zeros, pipeline_mode=pl.Buffered(1))


def dot_nn(left, right):
    return lax.dot_general(left, right, (((1,), (0,)), ((), ())), preferred_element_type=F32)


def dot_nt(left, right):
    return lax.dot_general(left, right, (((1,), (1,)), ((), ())), preferred_element_type=F32)


def split(values):
    upper = values.astype(BF16)
    return upper, (values - upper.astype(F32)).astype(BF16)


def lane_index(rows, lanes):
    return lax.broadcasted_iota(jnp.int32, (rows, lanes), 1)


def row_index(rows, lanes):
    return lax.broadcasted_iota(jnp.int32, (rows, lanes), 0)


def cosine_block():
    samples = np.arange(DH, dtype=np.float64)
    angles = math.pi * (samples[None, :] + 0.5) * samples[:, None] / DH
    table = np.cos(angles) * math.sqrt(2.0 / DH)
    table[0] *= math.sqrt(0.5)
    return np.kron(np.eye(WIDE // DH), table.T * DH ** (-0.25)).astype(np.float32)


def rotary_rows(length):
    position = np.arange(length, dtype=np.float32)
    inverse = (10000.0 ** (-np.arange(0, ROT, 2, dtype=np.float32) / ROT)).astype(np.float32)
    angles = position[:, None] * inverse[None, :]
    cosine, sine = np.cos(angles), np.sin(angles)
    rest = DH - ROT
    cosine_head = np.concatenate([cosine, cosine, np.ones((length, rest))], 1)
    sine_head = np.concatenate([-sine, sine, np.zeros((length, rest))], 1)
    repeat = PAIR // DH
    return (
        np.tile(cosine_head, (1, repeat)).astype(np.float32),
        np.tile(sine_head, (1, repeat)).astype(np.float32),
    )


def tables_kernel(seeds_ref, cosine_ref, upper_ref, lower_ref, weight_ref):
    feature = lane_index(WIDE, WIDE)
    lattice = (feature % FEAT) * seeds_ref[0] % FEAT
    prob = (lattice.astype(F32) + 0.5) / FEAT
    radius = jnp.sqrt(-2.0 * jnp.log(jnp.minimum(prob, 1.0 - prob)))
    above = 2.515517 + 0.802853 * radius + 0.010328 * radius * radius
    below = (
        1.0 + 1.432788 * radius + 0.189269 * radius * radius + 0.001308 * radius * radius * radius
    )
    magnitude = radius - above / below
    same_head = row_index(WIDE, WIDE) // DH == feature // FEAT
    omega = jnp.where(same_head, jnp.where(prob > 0.5, magnitude, -magnitude), 0.0)
    project = jnp.dot(cosine_ref[...], omega, precision=HIGH, preferred_element_type=F32)
    upper_ref[0, 0], lower_ref[0, 0] = split(project)
    grown = jnp.exp(-0.5 / DH * jnp.sum(omega * omega, axis=0, keepdims=True))
    total = jnp.dot(
        jnp.broadcast_to(grown, (8, WIDE)),
        same_head.astype(F32),
        precision=HIGH,
        preferred_element_type=F32,
    )
    weight_ref[0, 0] = FEAT * grown / total[:1]


def feature_tables(seeds):
    return pl.pallas_call(
        tables_kernel,
        grid=(LAYERS, QUADS),
        in_specs=[
            pl.BlockSpec((1, WIDE, 1), lambda l, g: (l, g, 0)),
            whole((WIDE, WIDE)),
        ],
        out_specs=[
            pl.BlockSpec((1, 1, WIDE, WIDE), lambda l, g: (l, g, 0, 0)),
            pl.BlockSpec((1, 1, WIDE, WIDE), lambda l, g: (l, g, 0, 0)),
            pl.BlockSpec((1, 1, 1, WIDE), lambda l, g: (l, g, 0, 0)),
        ],
        out_shape=[
            jax.ShapeDtypeStruct((LAYERS, QUADS, WIDE, WIDE), BF16),
            jax.ShapeDtypeStruct((LAYERS, QUADS, WIDE, WIDE), BF16),
            jax.ShapeDtypeStruct((LAYERS, QUADS, 1, WIDE), F32),
        ],
        compiler_params=params(),
        name="feature_tables",
    )(seeds.reshape(LAYERS, HEADS * DH, 1), jnp.asarray(cosine_block()))


def turn(values, cosine, sine):
    lanes = values.shape[1]
    half = ROT // 2
    lane = lane_index(*values.shape) % DH
    swapped = jnp.where(
        lane < half, pltpu.roll(values, lanes - half, 1), pltpu.roll(values, half, 1)
    )
    return values * cosine + swapped * sine


def turn_back(values, cosine, sine):
    lanes = values.shape[1]
    half = ROT // 2
    lane = lane_index(*values.shape) % DH
    turned = values * sine
    swapped = jnp.where(
        lane < half, pltpu.roll(turned, lanes - half, 1), pltpu.roll(turned, half, 1)
    )
    return values * cosine + jnp.where(lane < ROT, swapped, 0.0)


def normalized(x_ref_rows, gain, offset):
    average = jnp.mean(x_ref_rows, -1, keepdims=True)
    centered = x_ref_rows - average
    variance = jnp.mean(centered * centered, -1, keepdims=True)
    return centered * lax.rsqrt(variance + EPSILON) * gain + offset


def start_layer(stream, x_ref, h_ref, gain_ref, offset_ref):
    length = h_ref.shape[0]
    step = min(128, length)

    @pl.loop(0, length // step)
    def _(index):
        rows = pl.ds(pl.multiple_of(index * step, step), step)
        values = stream[0][rows].astype(F32)
        if len(stream) > 1:
            values = values + (stream[1][rows] + stream[2][rows])
            x_ref[rows] = values
        h_ref[rows] = normalized(
            values, gain_ref[...].astype(F32), offset_ref[...].astype(F32)
        ).astype(BF16)


def gelu_parts(units):
    grown = jnp.exp(-0.5 * units * units)
    inverse = 1.0 / (1.0 + (0.3275911 * math.sqrt(0.5)) * jnp.abs(units))
    series = 0.5 * 1.061405429
    for factor in (-1.453152027, 1.421413741, -0.284496736, 0.254829592):
        series = series * inverse + 0.5 * factor
    tail = series * inverse * grown
    below = jnp.where(units >= 0.0, 1.0 - tail, tail)
    return below, grown * (1.0 / math.sqrt(2.0 * math.pi))


FF_BLOCK = 512


def mlp_forward_kernel(count, *refs):
    stream, refs = refs[:count], refs[count:]
    gain_ref, offset_ref, up_ref, bias_ref, down_ref, down_bias_ref = refs[:6]
    refs = refs[6:]
    x_ref = None
    if count > 1:
        x_ref, refs = refs[0], refs[1:]
    part_ref, h_ref, act_ref, slope_ref = refs
    step = pl.program_id(0)

    @pl.when(step == 0)
    def _():
        start_layer(stream, x_ref, h_ref, gain_ref, offset_ref)
        part_ref[...] = jnp.broadcast_to(down_bias_ref[...].astype(F32), part_ref.shape)

    for first in range(0, h_ref.shape[0], ROWS):
        rows = slice(first, first + ROWS)
        units = dot_nt(h_ref[rows], up_ref[0]) + bias_ref[0]
        below, density = gelu_parts(units)
        active = (units * below).astype(BF16)
        act_ref[0, rows] = active
        slope_ref[0, rows] = (below + units * density).astype(BF16)
        part_ref[rows] += dot_nn(active, down_ref[0, 0])


def plane_block(length, lanes):
    per_plane = 1024 // lanes
    return pl.BlockSpec((1, length, lanes), lambda j: (j // per_plane, 0, j % per_plane))


def mlp_forward(layer, stream, gain, offset, up, biases, down_weight, down_bias):
    length, width = stream[0].shape
    hidden = up.shape[1]
    blocks = hidden // FF_BLOCK
    state = jax.ShapeDtypeStruct((4, length, width), BF16)
    full = jax.ShapeDtypeStruct((length, width), F32)
    out_shape = [full, jax.ShapeDtypeStruct((length, width), BF16), state, state]
    out_specs = [whole((length, width)), whole((length, width))]
    out_specs += [plane_block(length, FF_BLOCK)] * 2
    if len(stream) > 1:
        out_shape, out_specs = [full] + out_shape, [whole((length, width))] + out_specs
    return pl.pallas_call(
        functools.partial(mlp_forward_kernel, len(stream)),
        grid=(blocks,),
        in_specs=[whole((length, width))] * len(stream)
        + [
            whole((1, width)),
            whole((1, width)),
            pl.BlockSpec((1, FF_BLOCK, width), lambda j: (layer, j, 0)),
            pl.BlockSpec((1, 1, FF_BLOCK), lambda j: (j, 0, 0)),
            pl.BlockSpec((1, 1, FF_BLOCK, width), lambda j: (0, layer, j, 0)),
            whole((1, width)),
        ],
        out_specs=out_specs,
        out_shape=out_shape,
        compiler_params=params(),
        name="mlp_forward",
    )(*stream, gain, offset, up, biases.reshape(blocks, 1, FF_BLOCK), down_weight, down_bias)


def mlp_backward_kernel(
    grad_ref, h_ref, act_ref, slope_ref, down_ref, up_ref,
    part_ref, weight_ref, near_ref, far_ref, bias_ref, grad_t, h_t,
):
    step = pl.program_id(0)

    @pl.when(step == 0)
    def _():
        grad_t[...] = grad_ref[...].T
        h_t[...] = h_ref[...].T
        part_ref[...] = jnp.zeros_like(part_ref)

    length = h_ref.shape[0]
    bias = jnp.zeros((1, FF_BLOCK), F32)
    pieces = []
    for first in range(0, length, ROWS):
        rows = slice(first, first + ROWS)
        grad_act = dot_nt(grad_ref[rows], down_ref[0, 0])
        grad_unit = (grad_act * slope_ref[0, rows].astype(F32)).astype(BF16)
        bias += jnp.sum(grad_unit.astype(F32), axis=0, keepdims=True)
        pieces.append(grad_unit)
        part_ref[rows] += dot_nn(grad_unit, up_ref[0])
    bias_ref[0] = bias
    units = jnp.concatenate(pieces, axis=0)
    folded, half = near_ref.shape[1], near_ref.shape[2] // 2
    for first in range(0, h_t.shape[0], ROWS):
        rows = slice(first, first + ROWS)
        for block in range(FF_BLOCK // WIDE):
            lanes = slice(block * WIDE, (block + 1) * WIDE)
            weight_ref[block, rows] = dot_nn(grad_t[rows], act_ref[0, :, lanes])
            up_grad = dot_nn(h_t[rows], units[:, lanes])
            side = 0 if first < folded else half
            place = slice(first % folded, first % folded + ROWS)
            near_ref[block, place, side : side + half] = up_grad[:, :half]
            far_ref[block, place, side : side + half] = up_grad[:, half:]


def mlp_backward(layer, grad, h, act, slope, down_weight, up):
    length, width = h.shape
    hidden = up.shape[1]
    blocks = hidden // FF_BLOCK
    per = FF_BLOCK // WIDE
    halves = jax.ShapeDtypeStruct((hidden // WIDE, width // 2, WIDE), F32)
    return pl.pallas_call(
        mlp_backward_kernel,
        grid=(blocks,),
        in_specs=[
            whole((length, width)),
            whole((length, width)),
            plane_block(length, FF_BLOCK),
            plane_block(length, FF_BLOCK),
            pl.BlockSpec((1, 1, FF_BLOCK, width), lambda j: (0, layer, j, 0)),
            pl.BlockSpec((1, FF_BLOCK, width), lambda j: (layer, j, 0)),
        ],
        out_specs=[
            whole((length, width)),
            pl.BlockSpec((per, width, WIDE), lambda j: (j, 0, 0)),
            pl.BlockSpec((per, width // 2, WIDE), lambda j: (j, 0, 0)),
            pl.BlockSpec((per, width // 2, WIDE), lambda j: (j, 0, 0)),
            pl.BlockSpec((1, 1, FF_BLOCK), lambda j: (j, 0, 0)),
        ],
        out_shape=[
            jax.ShapeDtypeStruct((length, width), F32),
            jax.ShapeDtypeStruct((hidden // WIDE, width, WIDE), F32),
            halves,
            halves,
            jax.ShapeDtypeStruct((blocks, 1, FF_BLOCK), F32),
        ],
        scratch_shapes=[pltpu.VMEM((width, length), BF16), pltpu.VMEM((width, length), BF16)],
        compiler_params=params(),
        name="mlp_backward",
    )(grad, h, act, slope, down_weight, up)


def head_sums(values, ones):
    upper, lower = split(values)
    return dot_nn(upper, ones) + dot_nn(lower, ones)


def same_head_ones():
    same = row_index(WIDE, WIDE) // DH == lane_index(WIDE, WIDE) // DH
    return jnp.where(same, 1.0, 0.0).astype(BF16)


def project_kernel(count, *refs):
    stream, refs = refs[:count], refs[count:]
    gain_ref, offset_ref, weight_ref, bias_ref = refs[:4]
    upper_ref, lower_ref, scale_ref, cosine_ref, sine_ref = refs[4:9]
    refs = refs[9:]
    x_ref = None
    if count > 1:
        x_ref, refs = refs[0], refs[1:]
    h_ref, state_ref, keys = refs
    step = pl.program_id(0)
    kind, group = step // QUADS, step % QUADS
    length = h_ref.shape[0]

    @pl.when(step == 0)
    def _():
        start_layer(stream, x_ref, h_ref, gain_ref, offset_ref)

    def features(values, rows):
        cosine = jnp.concatenate([cosine_ref[rows]] * (WIDE // PAIR), axis=1)
        sine = jnp.concatenate([sine_ref[rows]] * (WIDE // PAIR), axis=1)
        upper, lower = split(turn(values, cosine, sine))
        table_up, table_low = upper_ref[0, 0], lower_ref[0, 0]
        return dot_nn(upper, table_up) + (dot_nn(lower, table_up) + dot_nn(upper, table_low))

    @pl.when(kind == 0)
    def _():
        for first in range(0, length, ROWS):
            rows = slice(first, first + ROWS)
            values = dot_nt(h_ref[rows], weight_ref[0, 0]) + bias_ref[0]
            state_ref[0, rows] = jnp.exp(features(values, rows)).astype(BF16)

    @pl.when(kind == 1)
    def _():
        ones = same_head_ones()
        for first in range(0, length, ROWS):
            rows = slice(first, first + ROWS)
            values = dot_nt(h_ref[rows], weight_ref[0, 0]) + bias_ref[0]
            keys[group, rows] = values.astype(BF16)
            squares = head_sums(values * values, ones)
            logs = features(values, rows) - (0.5 / math.sqrt(DH)) * squares
            state_ref[0, rows] = (scale_ref[0, 0] * jnp.exp(logs)).astype(BF16)

    @pl.when(kind == 2)
    def _():
        state_ref[0] = keys[group]

    @pl.when(kind == 3)
    def _():
        for first in range(0, length, ROWS):
            rows = slice(first, first + ROWS)
            values = dot_nt(h_ref[rows], weight_ref[0, 0]) + bias_ref[0]
            state_ref[0, rows] = values.astype(BF16)


def project_forward(layer, stream, gain, offset, weight, biases, tables, rotary):
    length, width = stream[0].shape
    full = jax.ShapeDtypeStruct((length, width), F32)
    state = jax.ShapeDtypeStruct((4, length, width), BF16)
    out_shape = [jax.ShapeDtypeStruct((length, width), BF16), state]
    out_specs = [whole((length, width)), plane_block(length, WIDE)]
    if len(stream) > 1:
        out_shape, out_specs = [full] + out_shape, [whole((length, width))] + out_specs

    def source(j):
        return jnp.where(j < 2 * QUADS, j, jnp.maximum(j - QUADS, 2 * QUADS - 1))

    def table(j):
        return jnp.where(j < 2 * QUADS, j % QUADS, QUADS - 1)

    return pl.pallas_call(
        functools.partial(project_kernel, len(stream)),
        grid=(4 * QUADS,),
        in_specs=[whole((length, width))] * len(stream)
        + [
            whole((1, width)),
            whole((1, width)),
            pl.BlockSpec((1, 1, WIDE, width), lambda j: (0, layer, source(j), 0)),
            pl.BlockSpec((1, 1, WIDE), lambda j: (source(j), 0, 0)),
            pl.BlockSpec((1, 1, WIDE, WIDE), lambda j: (layer, table(j), 0, 0)),
            pl.BlockSpec((1, 1, WIDE, WIDE), lambda j: (layer, table(j), 0, 0)),
            pl.BlockSpec((1, 1, 1, WIDE), lambda j: (layer, table(j), 0, 0)),
            whole((length, PAIR)),
            whole((length, PAIR)),
        ],
        out_specs=out_specs,
        out_shape=out_shape,
        scratch_shapes=[pltpu.VMEM((QUADS, length, WIDE), BF16)],
        compiler_params=params(),
        name="project_forward",
    )(*stream, gain, offset, weight, biases.reshape(-1, 1, WIDE), *tables, *rotary)


def write_mask(starts_ref, mask_ref, flipped):
    length = mask_ref.shape[0]
    keys = lane_index(1, length)
    documents = sum((starts_ref[0, i] <= keys).astype(jnp.int32) for i in range(starts_ref.shape[1]))
    for first in range(0, length, ROWS):
        own = row_index(ROWS, 1) + first
        document = sum(
            (starts_ref[0, i] <= own).astype(jnp.int32) for i in range(starts_ref.shape[1])
        )
        order = (own <= keys) if flipped else (keys <= own)
        seen = (document == documents) & order
        mask_ref[first : first + ROWS] = jnp.where(seen, 1.0, 0.0).astype(BF16)


def attend_kernel(starts_ref, state_ref, out_ref, mask_ref):
    @pl.when(pl.program_id(0) == 0)
    def _():
        write_mask(starts_ref, mask_ref, False)

    length = mask_ref.shape[0]
    zero = jnp.zeros((), BF16)
    one = jnp.ones((), BF16)
    for first in range(0, length, ROWS):
        rows = slice(first, first + ROWS)
        finish = first + ROWS
        left = lane_index(finish, PAIR) < DH
        seen = mask_ref[rows, :finish] > zero
        sums = []
        for own in (left, ~left):
            keys = jnp.where(own, state_ref[1, :finish], zero)
            scores = dot_nt(state_ref[0, rows], keys).astype(BF16)
            scores = jnp.where(seen, scores, zero)
            sums.append(dot_nn(scores, jnp.where(own, state_ref[3, :finish], one)))
        left = lane_index(ROWS, PAIR) < DH
        numer = jnp.where(left, sums[0], sums[1])
        denom = jnp.where(left, pltpu.roll(sums[0], DH, 1), pltpu.roll(sums[1], DH, 1))
        inverse = 1.0 / denom
        out_ref[0, rows] = (numer * inverse).astype(BF16)
        out_ref[1, rows], out_ref[2, rows] = split(inverse)


def attend_forward(starts, state):
    _, length, width = state.shape
    block = pl.BlockSpec((4, length, PAIR), lambda p: (0, 0, p))
    return pl.pallas_call(
        attend_kernel,
        grid=(PAIRS,),
        in_specs=[pl.BlockSpec(memory_space=pltpu.SMEM), block],
        out_specs=block,
        out_shape=jax.ShapeDtypeStruct(state.shape, BF16),
        scratch_shapes=[pltpu.VMEM((length, length), BF16)],
        compiler_params=params(),
        name="attend_forward",
    )(starts, state)


def mix_kernel(mixed_ref, weight_ref, bias_ref, part_ref):
    part_ref[...] = dot_nn(mixed_ref[0], weight_ref[0, 0]) + bias_ref[0]


def mix_forward(layer, mixed, weight, biases):
    _, length, width = mixed.shape
    return pl.pallas_call(
        mix_kernel,
        grid=(QUADS,),
        in_specs=[
            pl.BlockSpec((1, length, width), lambda j: (0, 0, 0), pipeline_mode=pl.Buffered(1)),
            pl.BlockSpec((1, 1, width, WIDE), lambda j: (0, layer, 3, j)),
            pl.BlockSpec((1, 1, WIDE), lambda j: (3 * QUADS + j, 0, 0)),
        ],
        out_specs=pl.BlockSpec((length, WIDE), lambda j: (0, j)),
        out_shape=jax.ShapeDtypeStruct((length, width), F32),
        compiler_params=params(),
        name="mix_forward",
    )(mixed, weight, biases.reshape(-1, 1, WIDE))


def mix_backward_kernel(grad_ref, weight_ref, mixed_ref, out_ref):
    row, lane = row_index(WIDE, WIDE), lane_index(WIDE, WIDE)
    partner = (row // PAIR == lane // PAIR) & (row // DH != lane // DH)
    ones = jnp.where(partner, 1.0, 0.0).astype(BF16)
    length = grad_ref.shape[0]
    for first in range(0, length, ROWS):
        rows = slice(first, first + ROWS)
        grad = dot_nt(grad_ref[rows], weight_ref[0, 0]).astype(BF16).astype(F32)
        inverse = mixed_ref[1, rows].astype(F32) + mixed_ref[2, rows].astype(F32)
        scaled = grad * inverse
        upper, lower = split(-head_sums(scaled * mixed_ref[0, rows].astype(F32), ones))
        numer = scaled.astype(BF16)
        lane = lane_index(ROWS, WIDE)
        spare = jnp.where(
            lane % DH == 0, upper, jnp.where(lane % DH == 1, lower, jnp.zeros((), BF16))
        )
        left = lane % PAIR < DH
        out_ref[0, rows] = jnp.where(left, numer, spare)
        out_ref[1, rows] = jnp.where(left, spare, numer)


def mix_backward(layer, grad, weight, mixed):
    _, length, width = mixed.shape
    return pl.pallas_call(
        mix_backward_kernel,
        grid=(QUADS,),
        in_specs=[
            whole((length, width)),
            pl.BlockSpec((1, 1, WIDE, width), lambda j: (0, layer, 3 * QUADS + j, 0)),
            pl.BlockSpec((4, length, WIDE), lambda j: (0, 0, j)),
        ],
        out_specs=pl.BlockSpec((2, length, WIDE), lambda j: (0, 0, j)),
        out_shape=jax.ShapeDtypeStruct((2, length, width), BF16),
        compiler_params=params(),
        name="mix_backward",
    )(grad, weight, mixed)


def attend_backward_kernel(starts_ref, state_ref, numer_ref, out_ref, mask_ref, query_t):
    @pl.when(pl.program_id(0) == 0)
    def _():
        write_mask(starts_ref, mask_ref, True)

    length = mask_ref.shape[0]
    zero = jnp.zeros((), BF16)
    one = jnp.ones((), BF16)
    query_t[...] = jnp.zeros_like(query_t)
    for first in range(0, length, ROWS):
        rows = slice(first, first + ROWS)
        seen = mask_ref[rows, first:] > zero
        lane = lane_index(ROWS, PAIR)
        left = lane < DH
        spare = jnp.where(lane % DH < 2, one, zero)
        keys, values = state_ref[1, rows], state_ref[3, rows]
        queries = state_ref[0, first:]
        numer = jnp.where(lane_index(length - first, PAIR) < DH, numer_ref[0, first:], numer_ref[1, first:])
        grads = []
        for head, own in enumerate((left, ~left)):
            own_keys = jnp.where(own, keys, zero)
            scores = dot_nt(own_keys, queries).astype(BF16)
            scores = jnp.where(seen, scores, zero)
            grad_value = dot_nn(scores, numer)
            grad_scores = dot_nt(jnp.where(own, values, spare), numer_ref[head, first:]).astype(BF16)
            grad_scores = jnp.where(seen, grad_scores, zero)
            grad_key = dot_nn(grad_scores, queries)
            query_t[head, :, first:] += dot_nn(own_keys.T[head * DH : (head + 1) * DH], grad_scores)
            grads.append((grad_value, grad_key))
        out_ref[2, rows] = jnp.where(left, grads[0][0], grads[1][0]).astype(BF16)
        grad_key = jnp.where(left, grads[0][1], grads[1][1])
        out_ref[1, rows] = (grad_key * keys.astype(F32)).astype(BF16)
    for first in range(0, length, ROWS):
        rows = slice(first, first + ROWS)
        grad_query = jnp.concatenate([query_t[0, :, rows], query_t[1, :, rows]], axis=0).T
        out_ref[0, rows] = (grad_query * state_ref[0, rows].astype(F32)).astype(BF16)


def attend_backward(starts, state, numer):
    _, length, width = state.shape
    return pl.pallas_call(
        attend_backward_kernel,
        grid=(PAIRS,),
        in_specs=[
            pl.BlockSpec(memory_space=pltpu.SMEM),
            pl.BlockSpec((4, length, PAIR), lambda p: (0, 0, p)),
            pl.BlockSpec((2, length, PAIR), lambda p: (0, 0, p)),
        ],
        out_specs=pl.BlockSpec((3, length, PAIR), lambda p: (0, 0, p)),
        out_shape=jax.ShapeDtypeStruct((3, length, width), BF16),
        scratch_shapes=[
            pltpu.VMEM((length, length), BF16),
            pltpu.VMEM((2, DH, length), F32),
        ],
        compiler_params=params(),
        name="attend_backward",
    )(starts, state, numer)


def project_backward_kernel(
    grad_ref, h_ref, mixed_ref, feat_ref, keys_ref, table_ref, cosine_ref, sine_ref, weight_ref,
    part_ref, out_ref, bias_ref, near_ref, far_ref, grad_t, h_t, flow,
):
    del near_ref, far_ref
    step = pl.program_id(0)
    kind, length = step // QUADS, h_ref.shape[0]

    @pl.when(step == 0)
    def _():
        grad_t[...] = grad_ref[...].T
        h_t[...] = h_ref[...].T
        part_ref[...] = jnp.zeros_like(part_ref)

    def project_back(rows):
        cosine = jnp.concatenate([cosine_ref[rows]] * (WIDE // PAIR), axis=1)
        sine = jnp.concatenate([sine_ref[rows]] * (WIDE // PAIR), axis=1)
        return turn_back(dot_nt(feat_ref[0, rows], table_ref[0, 0]), cosine, sine)

    @pl.when(kind == 0)
    def _():
        flow[...] = mixed_ref[0]
        bias_ref[0] = jnp.sum(feat_ref[0, :1].astype(F32), axis=0, keepdims=True)

    @pl.when(kind == 1)
    def _():
        for first in range(0, length, ROWS):
            rows = slice(first, first + ROWS)
            flow[rows] = project_back(rows).astype(BF16)

    @pl.when(kind == 2)
    def _():
        ones = same_head_ones()
        for first in range(0, length, ROWS):
            rows = slice(first, first + ROWS)
            shrink = dot_nn(feat_ref[0, rows], ones) * (1.0 / math.sqrt(DH))
            flow[rows] = (project_back(rows) - keys_ref[0, rows].astype(F32) * shrink).astype(BF16)

    @pl.when(kind == 3)
    def _():
        flow[...] = feat_ref[0]

    @pl.when(kind > 0)
    def _():
        bias = jnp.zeros((1, WIDE), F32)
        for first in range(0, length, ROWS):
            rows = slice(first, first + ROWS)
            bias += jnp.sum(flow[rows].astype(F32), axis=0, keepdims=True)
            part_ref[rows] += dot_nn(flow[rows], weight_ref[0, 0])
            out_ref[0, rows] = dot_nn(h_t[rows], flow[...])
        bias_ref[0] = bias

    @pl.when(kind == 0)
    def _():
        for first in range(0, length, ROWS):
            rows = slice(first, first + ROWS)
            out_ref[0, rows] = dot_nn(grad_t[rows], flow[...])


def project_backward(layer, grad, h, mixed, feats, state, tables, rotary, weight):
    _, length, width = state.shape
    blocks = 4 * QUADS

    def at(j):
        return jnp.maximum(j - QUADS, 0)

    def target(j):
        return jnp.where(j < QUADS, 3 * QUADS + j, j - QUADS)

    return pl.pallas_call(
        project_backward_kernel,
        grid=(blocks,),
        in_specs=[
            whole((length, width)),
            whole((length, width)),
            pl.BlockSpec((1, length, WIDE), lambda j: (0, 0, jnp.minimum(j, QUADS - 1))),
            pl.BlockSpec((1, length, WIDE), lambda j: (at(j) // QUADS, 0, at(j) % QUADS)),
            pl.BlockSpec(
                (1, length, WIDE), lambda j: (2, 0, jnp.clip(j - 2 * QUADS, 0, QUADS - 1))
            ),
            pl.BlockSpec((1, 1, WIDE, WIDE), lambda j: (layer, at(j) % QUADS, 0, 0)),
            whole((length, PAIR)),
            whole((length, PAIR)),
            pl.BlockSpec((1, 1, WIDE, width), lambda j: (0, layer, at(j), 0)),
        ],
        out_specs=[
            whole((length, width)),
            pl.BlockSpec((1, width, WIDE), lambda j: (target(j), 0, 0)),
            pl.BlockSpec((1, 1, WIDE), lambda j: (target(j), 0, 0)),
            pl.BlockSpec(memory_space=pl.ANY),
            pl.BlockSpec(memory_space=pl.ANY),
        ],
        out_shape=[
            jax.ShapeDtypeStruct((length, width), F32),
            jax.ShapeDtypeStruct((blocks, width, WIDE), F32),
            jax.ShapeDtypeStruct((blocks, 1, WIDE), F32),
            jax.ShapeDtypeStruct((blocks, width // 2, WIDE), F32),
            jax.ShapeDtypeStruct((blocks, width // 2, WIDE), F32),
        ],
        scratch_shapes=[
            pltpu.VMEM((width, length), BF16),
            pltpu.VMEM((width, length), BF16),
            pltpu.VMEM((length, WIDE), BF16),
        ],
        compiler_params=params(),
        name="project_backward",
    )(grad, h, mixed, feats, state, tables[0], *rotary, weight)


def norm_backward_kernel(x_ref, own_ref, other_ref, grad_ref, gain_ref, out_ref, sums_ref):
    @pl.when(pl.program_id(0) == 0)
    def _():
        sums_ref[...] = jnp.zeros_like(sums_ref)

    values = x_ref[...].astype(F32)
    average = jnp.mean(values, -1, keepdims=True)
    centered = values - average
    variance = jnp.mean(centered * centered, -1, keepdims=True)
    inverse = lax.rsqrt(variance + EPSILON)
    unit = centered * inverse
    incoming = own_ref[...] + other_ref[...]
    grad_unit = incoming * gain_ref[...].astype(F32)
    first = jnp.mean(grad_unit, -1, keepdims=True)
    second = jnp.mean(grad_unit * unit, -1, keepdims=True)
    grad = grad_ref[...].astype(F32)
    out = grad + inverse * (grad_unit - first - unit * second)
    out_ref[...] = out.astype(out_ref.dtype)
    sums_ref[0:1] += jnp.sum(incoming * unit, axis=0, keepdims=True)
    sums_ref[1:2] += jnp.sum(incoming, axis=0, keepdims=True)
    sums_ref[2:3] += jnp.sum(grad, axis=0, keepdims=True)


def norm_backward(x, own, other, grad, gain, kind):
    length, width = own.shape
    block = pl.BlockSpec((ROWS, width), lambda i: (i, 0))
    return pl.pallas_call(
        norm_backward_kernel,
        grid=(length // ROWS,),
        in_specs=[block, block, block, block, whole((1, width))],
        out_specs=[block, whole((8, width))],
        out_shape=[
            jax.ShapeDtypeStruct((length, width), kind),
            jax.ShapeDtypeStruct((8, width), F32),
        ],
        compiler_params=params(),
        name="norm_backward",
    )(x, own, other, grad, gain)


MESH = pl.DeviceIdType.MESH
UNIT = 8
SLOTS = 4
LAG = 1
ORDERS = ((0, 1, 2, 3), (1, 0, 2, 3), (0, 2, 3, 1), (1, 2, 3, 0), (0, 2, 3, 1), (1, 2, 3, 0))


def bit_of(index, bit):
    return (index // (1 << bit)) % 2


def flip(index, bit):
    return index + (1 << bit) * (1 - 2 * bit_of(index, bit))


def scatter_kernel(bits, rows, layers, *refs):
    sources, refs = refs[: 3 * layers], refs[3 * layers :]
    small_ref, weight_out, up_out, small_out = refs[:4]
    held, refs = refs[4:], None
    flows, stages = len(ORDERS), bits
    weight_sum, up_sum = held[:2]
    small_held = held[2 : 2 + stages]
    held = held[2 + stages :]
    held, sems = held[: flows * (stages + 1)], held[flows * (stages + 1) :]
    load_sem, send_sem, recv_sem, credit, small_send, small_recv = sems
    held = [held[f * (stages + 1) : (f + 1) * (stages + 1)] for f in range(flows)]
    me, core = lax.axis_index("batch"), lax.axis_index("stream")
    weight_units, up_units = rows[0] // UNIT, rows[1] // UNIT
    per_layer = weight_units + up_units
    total = per_layer * layers // flows

    barrier = pltpu.get_barrier_semaphore()
    for bit in range(bits):
        pl.semaphore_signal(
            barrier, inc=1, device_id={"batch": flip(me, bit)}, device_id_type=MESH
        )
    pl.semaphore_wait(barrier, bits)

    def view(order, stage, mine):
        left = sorted(set(range(bits)) - set(order[:stage]), reverse=True)
        pick = bit_of(me, order[stage])
        pick = pick if mine else 1 - pick
        return tuple(pick if bit == order[stage] else slice(None) for bit in left)

    def remote(flow, stage, slot, source):
        return pltpu.make_async_remote_copy(
            src_ref=source,
            dst_ref=held[flow][stage + 1].at[slot],
            send_sem=send_sem.at[flow, stage, slot],
            recv_sem=recv_sem.at[flow, stage, slot],
            device_id={"batch": flip(me, ORDERS[flow][stage])},
            device_id_type=MESH,
        )

    def sent_from(flow, stage, slot):
        if stage == 0:
            return held[flow][0].at[slot]
        return held[flow][stage].at[(slot,) + view(ORDERS[flow], stage, False)]

    def load(flow, slot, source):
        return pltpu.make_async_copy(source, held[flow][0].at[slot], load_sem.at[flow, slot])

    def return_credit(flow, stage, unit):
        @pl.when(unit + SLOTS < total)
        def _():
            pl.semaphore_signal(
                credit.at[flow, stage],
                inc=1,
                device_id={"batch": flip(me, ORDERS[flow][stage])},
                device_id_type=MESH,
            )

    def take_credit(flow, stage, unit):
        @pl.when(unit >= SLOTS)
        def _():
            pl.semaphore_wait(credit.at[flow, stage], 1)

    def places(place, act):
        for layer in range(layers):
            base = layer * per_layer
            middle = base + weight_units
            pl.when((place >= base) & (place < middle))(
                functools.partial(act, layer, False, (place - base) * UNIT)
            )
            pl.when((place >= middle) & (place < base + per_layer))(
                functools.partial(act, layer, True, (place - middle) * UNIT)
            )

    def begin(flow, unit):
        slot = lax.rem(unit, SLOTS)
        take_credit(flow, 0, unit)

        def start(source, row):
            at = (pl.ds(pl.multiple_of(row, UNIT), UNIT),)
            remote(flow, 0, slot, source.at[view(ORDERS[flow], 0, False) + at]).start()
            load(flow, slot, source.at[view(ORDERS[flow], 0, True) + at]).start()

        def act(layer, is_up, row):
            if not is_up:
                start(sources[3 * layer], row)
            else:
                for side in range(2):
                    pl.when(core == side)(
                        functools.partial(start, sources[3 * layer + 1 + side], row)
                    )

        places(unit * flows + flow, act)

    def advance(flow, stage, unit):
        slot = lax.rem(unit, SLOTS)
        order, buffer = ORDERS[flow], held[flow][stage]
        copy = remote(flow, stage - 1, slot, sent_from(flow, stage - 1, slot))
        copy.wait_recv()
        if stage == 1:
            kept = (slice(None),) * (bits - 1) + (pl.ds(0, UNIT),)
            kept = tuple(view(order, 0, True)) + kept[bits - 1 :]
            load(flow, slot, sources[0].at[kept]).wait()
            mine = held[flow][0][slot]
        else:
            mine = held[flow][stage - 1][(slot,) + view(order, stage - 1, True)]
        value = buffer[slot] + mine
        if stage < stages:
            buffer[slot] = value
            take_credit(flow, stage, unit)
            remote(flow, stage, slot, sent_from(flow, stage, slot)).start()
        else:

            def act(layer, is_up, row):
                target = up_sum if is_up else weight_sum
                target[layer, pl.ds(pl.multiple_of(row, UNIT), UNIT)] = value

            places(unit * flows + flow, act)
        copy.wait_send()
        if stage >= 2:
            return_credit(flow, stage - 2, unit)
        if stage == stages:
            return_credit(flow, stage - 1, unit)

    def small_copy(stage):
        source = small_ref if stage == 0 else small_held[stage - 1]
        return pltpu.make_async_remote_copy(
            src_ref=source.at[view(ORDERS[0], stage, False)],
            dst_ref=small_held[stage],
            send_sem=small_send.at[stage],
            recv_sem=small_recv.at[stage],
            device_id={"batch": flip(me, ORDERS[0][stage])},
            device_id_type=MESH,
        )

    def small_step(stage):
        if stage > 0:
            small_copy(stage - 1).wait()
            source = small_ref if stage == 1 else small_held[stage - 2]
            sums = small_held[stage - 1][...] + source[view(ORDERS[0], stage - 1, True)]
            if stage == stages:
                small_out[...] = sums
            else:
                small_held[stage - 1][...] = sums
        if stage < stages:
            small_copy(stage).start()

    def step(index, carry):
        for flow in range(flows):
            pl.when(index < total)(functools.partial(begin, flow, index))
        for flow in range(flows):
            for stage in range(1, stages + 1):
                unit = index - LAG * stage
                pl.when((unit >= 0) & (unit < total))(
                    functools.partial(advance, flow, stage, unit)
                )
        for stage in range(stages + 1):
            pl.when(index == stages + 2 * stage)(functools.partial(small_step, stage))
        return carry

    lax.fori_loop(0, total + LAG * stages, step, 0)
    half = WIDE // 2
    for layer in range(layers):
        weight_out[layers - 1 - layer] = weight_sum[layer].T
        folded = up_sum.shape[1]
        up_out[layers - 1 - layer, :, :folded] = up_sum[layer, :, :half].T
        up_out[layers - 1 - layer, :, folded:] = up_sum[layer, :, half:].T


def reduce_scatter(grads, small):
    layers = len(grads) // 3
    count, width = grads[0].shape[:2]
    folded = grads[1].shape[1]
    bits = count.bit_length() - 1
    small = jnp.pad(small, ((0, 0), (0, -small.shape[1] % 1024)))
    small = small.reshape((2,) * bits + (-1, 128))
    scratch = [pltpu.VMEM((layers, width, WIDE), F32), pltpu.VMEM((layers, folded, WIDE), F32)]
    scratch += [
        pltpu.VMEM((2,) * (bits - 1 - stage) + small.shape[-2:], F32) for stage in range(bits)
    ]
    for _ in ORDERS:
        for stage in range(bits + 1):
            lead = (SLOTS,) + (2,) * (bits - 1 - max(stage - 1, 0))
            scratch.append(pltpu.VMEM(lead + (UNIT, WIDE), F32))
    scratch += [
        pltpu.SemaphoreType.DMA((len(ORDERS), SLOTS)),
        pltpu.SemaphoreType.DMA((len(ORDERS), bits, SLOTS)),
        pltpu.SemaphoreType.DMA((len(ORDERS), bits, SLOTS)),
        pltpu.SemaphoreType.REGULAR((len(ORDERS), bits)),
        pltpu.SemaphoreType.DMA((bits,)),
        pltpu.SemaphoreType.DMA((bits,)),
    ]
    weight, up, small = pl.pallas_call(
        functools.partial(scatter_kernel, bits, (width, folded), layers),
        in_specs=[pl.BlockSpec(memory_space=pl.ANY)] * len(grads)
        + [pl.BlockSpec(memory_space=pltpu.VMEM)],
        out_specs=[pl.BlockSpec(memory_space=pltpu.VMEM)] * 3,
        out_shape=[
            jax.ShapeDtypeStruct((layers, WIDE, width), F32),
            jax.ShapeDtypeStruct((layers, WIDE // 2, width), F32),
            jax.ShapeDtypeStruct(small.shape[-2:], F32),
        ],
        scratch_shapes=scratch,
        compiler_params=pltpu.CompilerParams(
            collective_id=0, has_side_effects=True, vmem_limit_bytes=VMEM_LIMIT
        ),
        name="reduce_scatter",
    )(*[array.reshape((2,) * bits + array.shape[1:]) for array in grads], small)
    return weight, up, small.reshape(-1)


def shards(
    tokens, cotangent, branch_weight, branch_bias, up_weight, down_bias,
    norm_gain, norm_bias, freq_seeds, doc_starts,
):
    is_attention = lax.axis_index("stream") == 0
    length, width = tokens.shape
    rotary = tuple(jnp.asarray(table) for table in rotary_rows(length))
    biases = branch_bias[0].astype(F32)
    tables = lax.cond(
        is_attention,
        lambda: tuple(feature_tables(freq_seeds)),
        lambda: (
            jnp.zeros((LAYERS, QUADS, WIDE, WIDE), BF16),
            jnp.zeros((LAYERS, QUADS, WIDE, WIDE), BF16),
            jnp.zeros((LAYERS, QUADS, 1, WIDE), F32),
        ),
    )
    swap = [(0, 1), (1, 0)]

    def attention(layer, stream):
        gain, offset = norm_gain[layer : layer + 1], norm_bias[layer : layer + 1]
        *x, h, state = project_forward(
            layer, stream, gain, offset, branch_weight, biases[layer], tables, rotary
        )
        mixed = attend_forward(doc_starts, state)
        part = mix_forward(layer, mixed, branch_weight, biases[layer])
        return tuple(x) + (part, h, state, mixed)

    def feed_forward(layer, stream):
        gain, offset = norm_gain[layer : layer + 1], norm_bias[layer : layer + 1]
        return tuple(
            mlp_forward(
                layer, stream, gain, offset, up_weight, biases[layer], branch_weight,
                down_bias[layer : layer + 1],
            )
        )

    stream = (tokens,)
    inputs, kept = [], []
    for layer in range(LAYERS):
        *x, part, h, state, mixed = lax.cond(
            is_attention,
            functools.partial(attention, layer, stream),
            functools.partial(feed_forward, layer, stream),
        )
        inputs.append(x[0] if x else tokens)
        kept.append((h, state, mixed))
        stream = (inputs[-1], part, lax.ppermute(part, "stream", swap))
    result = stream[0] + (stream[1] + stream[2])

    def attention_back(layer, grad):
        h, state, mixed = kept[layer]
        numer = mix_backward(layer, grad, branch_weight, mixed)
        feats = attend_backward(doc_starts, state, numer)
        part, weight, bias, near, far = project_backward(
            layer, grad, h, mixed, feats, state, tables, rotary, branch_weight
        )
        return part, weight, near, far, bias.reshape(-1, WIDE)

    def feed_forward_back(layer, grad):
        h, act, slope = kept[layer]
        part, weight, near, far, bias = mlp_backward(
            layer, grad, h, act, slope, branch_weight, up_weight
        )
        return part, weight, near, far, bias.reshape(-1, WIDE)

    grad = cotangent
    count = lax.axis_size("batch")
    blocked = count == branch_weight.shape[2] // WIDE
    grads, vectors = [], []
    for layer in reversed(range(LAYERS)):
        part, weight, near, far, bias = lax.cond(
            is_attention,
            functools.partial(attention_back, layer, grad),
            functools.partial(feed_forward_back, layer, grad),
        )
        other = lax.ppermute(part, "stream", swap)
        if blocked:
            near = lax.ppermute(near, "stream", [(1, 0)])
        kind = BF16 if layer else F32
        new_grad, sums = norm_backward(
            inputs[layer], part, other, grad, norm_gain[layer : layer + 1], kind
        )
        bias = jnp.where(
            is_attention & (jnp.arange(bias.shape[0])[:, None] >= 3 * QUADS),
            jnp.tile(sums[2].reshape(QUADS, WIDE), (bias.shape[0] // QUADS, 1)),
            bias,
        )
        vectors = [bias.reshape(count, -1), sums[:3].reshape(3, count, -1)] + vectors
        grads += [weight, near, far]
        grad = new_grad
    small = jnp.concatenate(
        [part.reshape(count, -1) for part in vectors[0::2]]
        + [jnp.moveaxis(part, 0, 1).reshape(count, -1) for part in vectors[1::2]],
        axis=1,
    )
    if blocked:
        weight, up, small = reduce_scatter(grads, small)
    else:
        weight, up, small = scatter_rows(grads, small)
    each = branch_weight.shape[2] // count
    bias, sums = small[: LAYERS * each], small[LAYERS * each :]
    sums = sums[: LAYERS * 3 * (width // count)].reshape(LAYERS, 3, -1)
    return (
        result,
        grad,
        weight[None],
        bias.reshape(1, LAYERS, -1),
        up,
        sums[:, 2],
        sums[:, 0],
        sums[:, 1],
    )


def scatter_rows(grads, small):
    scatter = functools.partial(
        lax.psum_scatter, axis_name="batch", scatter_dimension=0, tiled=True
    )
    weights, ups = [], []
    for weight, near, far in zip(grads[0::3], grads[1::3], grads[2::3]):
        half = near.shape[2] // 2
        whole_up = [
            jnp.concatenate([side[..., :half], side[..., half:]], axis=1) for side in (near, far)
        ]
        whole_up = rows_of(jnp.concatenate(whole_up, axis=2))
        whole_up = jnp.where(lax.axis_index("stream") == 1, whole_up, 0.0)
        weights.append(scatter(rows_of(weight)))
        ups.append(
            lax.psum_scatter(whole_up, ("batch", "stream"), scatter_dimension=0, tiled=True)
        )
    return jnp.stack(weights[::-1]), jnp.stack(ups[::-1]), scatter(small)[0]


def rows_of(blocks):
    return jnp.transpose(blocks, (0, 2, 1)).reshape(-1, blocks.shape[1])


def solution(mesh):
    placed = (
        P("batch", None),
        P("batch", None),
        P("stream", None, None, None),
        P("stream", None, None),
        P(),
        P(),
        P(),
        P(),
        P(),
        P("batch", None),
    )
    return jax.shard_map(
        shards,
        mesh=mesh,
        in_specs=placed,
        out_specs=(
            P("batch", None),
            P("batch", None),
            P("stream", None, "batch", None),
            P("stream", None, "batch"),
            P(None, ("batch", "stream"), None),
            P(None, "batch"),
            P(None, "batch"),
            P(None, "batch"),
        ),
        check_vma=False,
    )
```

```python
import functools
import math
from typing import NamedTuple

import jax
import jax.numpy as jnp
import numpy as np
from jax import lax
from jax.experimental import pallas as pl
from jax.experimental.pallas import tpu as pltpu
from jax.sharding import PartitionSpec as P

HEADS = 16
DH = 64
ROT = 16
FEAT = 64
LAYERS = 2
EPSILON = 1e-05
HIGH = lax.Precision.HIGHEST
F32 = jnp.float32
BF16 = jnp.bfloat16
WIDE = 256
PAIR = 128
QUADS = HEADS * DH // WIDE
PAIRS = HEADS * DH // PAIR
ROWS = 256
VMEM_LIMIT = 56 * 1024 * 1024


def params():
    return pltpu.CompilerParams(vmem_limit_bytes=VMEM_LIMIT)


def whole(shape):
    zeros = (0,) * len(shape)
    return pl.BlockSpec(shape, lambda *_: zeros, pipeline_mode=pl.Buffered(1))


def dot_nn(left, right):
    return lax.dot_general(left, right, (((1,), (0,)), ((), ())), preferred_element_type=F32)


def dot_nt(left, right):
    return lax.dot_general(left, right, (((1,), (1,)), ((), ())), preferred_element_type=F32)


def split(values):
    upper = values.astype(BF16)
    return upper, (values - upper.astype(F32)).astype(BF16)


def lane_index(rows, lanes):
    return lax.broadcasted_iota(jnp.int32, (rows, lanes), 1)


def row_index(rows, lanes):
    return lax.broadcasted_iota(jnp.int32, (rows, lanes), 0)


def cosine_block():
    samples = np.arange(DH, dtype=np.float64)
    angles = math.pi * (samples[None, :] + 0.5) * samples[:, None] / DH
    table = np.cos(angles) * math.sqrt(2.0 / DH)
    table[0] *= math.sqrt(0.5)
    return np.kron(np.eye(WIDE // DH), table.T * DH ** (-0.25)).astype(np.float32)


def rotary_rows(length):
    position = np.arange(length, dtype=np.float32)
    inverse = (10000.0 ** (-np.arange(0, ROT, 2, dtype=np.float32) / ROT)).astype(np.float32)
    angles = position[:, None] * inverse[None, :]
    cosine, sine = np.cos(angles), np.sin(angles)
    rest = DH - ROT
    cosine_head = np.concatenate([cosine, cosine, np.ones((length, rest))], 1)
    sine_head = np.concatenate([-sine, sine, np.zeros((length, rest))], 1)
    repeat = PAIR // DH
    return (
        np.tile(cosine_head, (1, repeat)).astype(np.float32),
        np.tile(sine_head, (1, repeat)).astype(np.float32),
    )


def tables_kernel(seeds_ref, cosine_ref, upper_ref, lower_ref, weight_ref):
    feature = lane_index(WIDE, WIDE)
    lattice = (feature % FEAT) * seeds_ref[0] % FEAT
    prob = (lattice.astype(F32) + 0.5) / FEAT
    radius = jnp.sqrt(-2.0 * jnp.log(jnp.minimum(prob, 1.0 - prob)))
    above = 2.515517 + 0.802853 * radius + 0.010328 * radius * radius
    below = (
        1.0 + 1.432788 * radius + 0.189269 * radius * radius + 0.001308 * radius * radius * radius
    )
    magnitude = radius - above / below
    same_head = row_index(WIDE, WIDE) // DH == feature // FEAT
    omega = jnp.where(same_head, jnp.where(prob > 0.5, magnitude, -magnitude), 0.0)
    project = jnp.dot(cosine_ref[...], omega, precision=HIGH, preferred_element_type=F32)
    upper_ref[0, 0], lower_ref[0, 0] = split(project)
    grown = jnp.exp(-0.5 / DH * jnp.sum(omega * omega, axis=0, keepdims=True))
    total = jnp.dot(
        jnp.broadcast_to(grown, (8, WIDE)),
        same_head.astype(F32),
        precision=HIGH,
        preferred_element_type=F32,
    )
    weight_ref[0, 0] = FEAT * grown / total[:1]


def feature_tables(seeds):
    return pl.pallas_call(
        tables_kernel,
        grid=(LAYERS, QUADS),
        in_specs=[
            pl.BlockSpec((1, WIDE, 1), lambda l, g: (l, g, 0)),
            whole((WIDE, WIDE)),
        ],
        out_specs=[
            pl.BlockSpec((1, 1, WIDE, WIDE), lambda l, g: (l, g, 0, 0)),
            pl.BlockSpec((1, 1, WIDE, WIDE), lambda l, g: (l, g, 0, 0)),
            pl.BlockSpec((1, 1, 1, WIDE), lambda l, g: (l, g, 0, 0)),
        ],
        out_shape=[
            jax.ShapeDtypeStruct((LAYERS, QUADS, WIDE, WIDE), BF16),
            jax.ShapeDtypeStruct((LAYERS, QUADS, WIDE, WIDE), BF16),
            jax.ShapeDtypeStruct((LAYERS, QUADS, 1, WIDE), F32),
        ],
        compiler_params=params(),
        name="feature_tables",
    )(seeds.reshape(LAYERS, HEADS * DH, 1), jnp.asarray(cosine_block()))


def turn(values, cosine, sine):
    lanes = values.shape[1]
    half = ROT // 2
    lane = lane_index(*values.shape) % DH
    swapped = jnp.where(
        lane < half, pltpu.roll(values, lanes - half, 1), pltpu.roll(values, half, 1)
    )
    return values * cosine + swapped * sine


def turn_back(values, cosine, sine):
    lanes = values.shape[1]
    half = ROT // 2
    lane = lane_index(*values.shape) % DH
    turned = values * sine
    swapped = jnp.where(
        lane < half, pltpu.roll(turned, lanes - half, 1), pltpu.roll(turned, half, 1)
    )
    return values * cosine + jnp.where(lane < ROT, swapped, 0.0)


def normalized(x_ref_rows, gain, offset):
    average = jnp.mean(x_ref_rows, -1, keepdims=True)
    centered = x_ref_rows - average
    variance = jnp.mean(centered * centered, -1, keepdims=True)
    return centered * lax.rsqrt(variance + EPSILON) * gain + offset


def start_layer(stream, x_ref, h_ref, gain_ref, offset_ref):
    length = h_ref.shape[0]
    step = min(128, length)

    @pl.loop(0, length // step)
    def _(index):
        rows = pl.ds(pl.multiple_of(index * step, step), step)
        values = stream[0][rows].astype(F32)
        if len(stream) > 1:
            values = values + (stream[1][rows] + stream[2][rows])
            x_ref[rows] = values
        h_ref[rows] = normalized(
            values, gain_ref[...].astype(F32), offset_ref[...].astype(F32)
        ).astype(BF16)


def gelu_parts(units):
    grown = jnp.exp(-0.5 * units * units)
    inverse = 1.0 / (1.0 + (0.3275911 * math.sqrt(0.5)) * jnp.abs(units))
    series = 0.5 * 1.061405429
    for factor in (-1.453152027, 1.421413741, -0.284496736, 0.254829592):
        series = series * inverse + 0.5 * factor
    tail = series * inverse * grown
    below = jnp.where(units >= 0.0, 1.0 - tail, tail)
    return below, grown * (1.0 / math.sqrt(2.0 * math.pi))


FF_BLOCK = 512


def mlp_forward_kernel(count, *refs):
    stream, refs = refs[:count], refs[count:]
    gain_ref, offset_ref, up_ref, bias_ref, down_ref, down_bias_ref = refs[:6]
    refs = refs[6:]
    x_ref = None
    if count > 1:
        x_ref, refs = refs[0], refs[1:]
    part_ref, h_ref, act_ref, slope_ref = refs
    step = pl.program_id(0)

    @pl.when(step == 0)
    def _():
        start_layer(stream, x_ref, h_ref, gain_ref, offset_ref)
        part_ref[...] = jnp.broadcast_to(down_bias_ref[...].astype(F32), part_ref.shape)

    for first in range(0, h_ref.shape[0], ROWS):
        rows = slice(first, first + ROWS)
        units = dot_nt(h_ref[rows], up_ref[0]) + bias_ref[0]
        below, density = gelu_parts(units)
        active = (units * below).astype(BF16)
        act_ref[0, rows] = active
        slope_ref[0, rows] = (below + units * density).astype(BF16)
        part_ref[rows] += dot_nn(active, down_ref[0, 0])


def plane_block(length, lanes):
    per_plane = 1024 // lanes
    return pl.BlockSpec((1, length, lanes), lambda j: (j // per_plane, 0, j % per_plane))


def mlp_forward(layer, stream, gain, offset, up, biases, down_weight, down_bias):
    length, width = stream[0].shape
    hidden = up.shape[1]
    blocks = hidden // FF_BLOCK
    state = jax.ShapeDtypeStruct((4, length, width), BF16)
    full = jax.ShapeDtypeStruct((length, width), F32)
    out_shape = [full, jax.ShapeDtypeStruct((length, width), BF16), state, state]
    out_specs = [whole((length, width)), whole((length, width))]
    out_specs += [plane_block(length, FF_BLOCK)] * 2
    if len(stream) > 1:
        out_shape, out_specs = [full] + out_shape, [whole((length, width))] + out_specs
    return pl.pallas_call(
        functools.partial(mlp_forward_kernel, len(stream)),
        grid=(blocks,),
        in_specs=[whole((length, width))] * len(stream)
        + [
            whole((1, width)),
            whole((1, width)),
            pl.BlockSpec((1, FF_BLOCK, width), lambda j: (layer, j, 0)),
            pl.BlockSpec((1, 1, FF_BLOCK), lambda j: (j, 0, 0)),
            pl.BlockSpec((1, 1, FF_BLOCK, width), lambda j: (0, layer, j, 0)),
            whole((1, width)),
        ],
        out_specs=out_specs,
        out_shape=out_shape,
        compiler_params=params(),
        name="mlp_forward",
    )(*stream, gain, offset, up, biases.reshape(blocks, 1, FF_BLOCK), down_weight, down_bias)


def mlp_backward_kernel(
    grad_ref, h_ref, act_ref, slope_ref, down_ref, up_ref,
    part_ref, weight_ref, near_ref, far_ref, bias_ref, grad_t, h_t,
):
    step = pl.program_id(0)

    @pl.when(step == 0)
    def _():
        grad_t[...] = grad_ref[...].T
        h_t[...] = h_ref[...].T
        part_ref[...] = jnp.zeros_like(part_ref)

    length = h_ref.shape[0]
    bias = jnp.zeros((1, FF_BLOCK), F32)
    pieces = []
    for first in range(0, length, ROWS):
        rows = slice(first, first + ROWS)
        grad_act = dot_nt(grad_ref[rows], down_ref[0, 0])
        grad_unit = (grad_act * slope_ref[0, rows].astype(F32)).astype(BF16)
        bias += jnp.sum(grad_unit.astype(F32), axis=0, keepdims=True)
        pieces.append(grad_unit)
        part_ref[rows] += dot_nn(grad_unit, up_ref[0])
    bias_ref[0] = bias
    units = jnp.concatenate(pieces, axis=0)
    folded, half = near_ref.shape[1], near_ref.shape[2] // 2
    for first in range(0, h_t.shape[0], ROWS):
        rows = slice(first, first + ROWS)
        for block in range(FF_BLOCK // WIDE):
            lanes = slice(block * WIDE, (block + 1) * WIDE)
            weight_ref[block, rows] = dot_nn(grad_t[rows], act_ref[0, :, lanes])
            up_grad = dot_nn(h_t[rows], units[:, lanes])
            side = 0 if first < folded else half
            place = slice(first % folded, first % folded + ROWS)
            near_ref[block, place, side : side + half] = up_grad[:, :half]
            far_ref[block, place, side : side + half] = up_grad[:, half:]


def mlp_backward(layer, grad, h, act, slope, down_weight, up):
    length, width = h.shape
    hidden = up.shape[1]
    blocks = hidden // FF_BLOCK
    per = FF_BLOCK // WIDE
    halves = jax.ShapeDtypeStruct((hidden // WIDE, width // 2, WIDE), F32)
    return pl.pallas_call(
        mlp_backward_kernel,
        grid=(blocks,),
        in_specs=[
            whole((length, width)),
            whole((length, width)),
            plane_block(length, FF_BLOCK),
            plane_block(length, FF_BLOCK),
            pl.BlockSpec((1, 1, FF_BLOCK, width), lambda j: (0, layer, j, 0)),
            pl.BlockSpec((1, FF_BLOCK, width), lambda j: (layer, j, 0)),
        ],
        out_specs=[
            whole((length, width)),
            pl.BlockSpec((per, width, WIDE), lambda j: (j, 0, 0)),
            pl.BlockSpec((per, width // 2, WIDE), lambda j: (j, 0, 0)),
            pl.BlockSpec((per, width // 2, WIDE), lambda j: (j, 0, 0)),
            pl.BlockSpec((1, 1, FF_BLOCK), lambda j: (j, 0, 0)),
        ],
        out_shape=[
            jax.ShapeDtypeStruct((length, width), F32),
            jax.ShapeDtypeStruct((hidden // WIDE, width, WIDE), F32),
            halves,
            halves,
            jax.ShapeDtypeStruct((blocks, 1, FF_BLOCK), F32),
        ],
        scratch_shapes=[pltpu.VMEM((width, length), BF16), pltpu.VMEM((width, length), BF16)],
        compiler_params=params(),
        name="mlp_backward",
    )(grad, h, act, slope, down_weight, up)


def head_sums(values, ones):
    upper, lower = split(values)
    return dot_nn(upper, ones) + dot_nn(lower, ones)


def same_head_ones():
    same = row_index(WIDE, WIDE) // DH == lane_index(WIDE, WIDE) // DH
    return jnp.where(same, 1.0, 0.0).astype(BF16)


def project_kernel(count, *refs):
    stream, refs = refs[:count], refs[count:]
    gain_ref, offset_ref, weight_ref, bias_ref = refs[:4]
    upper_ref, lower_ref, scale_ref, cosine_ref, sine_ref = refs[4:9]
    refs = refs[9:]
    x_ref = None
    if count > 1:
        x_ref, refs = refs[0], refs[1:]
    h_ref, state_ref, keys = refs
    step = pl.program_id(0)
    kind, group = step // QUADS, step % QUADS
    length = h_ref.shape[0]

    @pl.when(step == 0)
    def _():
        start_layer(stream, x_ref, h_ref, gain_ref, offset_ref)

    def features(values, rows):
        cosine = jnp.concatenate([cosine_ref[rows]] * (WIDE // PAIR), axis=1)
        sine = jnp.concatenate([sine_ref[rows]] * (WIDE // PAIR), axis=1)
        upper, lower = split(turn(values, cosine, sine))
        table_up, table_low = upper_ref[0, 0], lower_ref[0, 0]
        return dot_nn(upper, table_up) + (dot_nn(lower, table_up) + dot_nn(upper, table_low))

    @pl.when(kind == 0)
    def _():
        for first in range(0, length, ROWS):
            rows = slice(first, first + ROWS)
            values = dot_nt(h_ref[rows], weight_ref[0, 0]) + bias_ref[0]
            state_ref[0, rows] = jnp.exp(features(values, rows)).astype(BF16)

    @pl.when(kind == 1)
    def _():
        ones = same_head_ones()
        for first in range(0, length, ROWS):
            rows = slice(first, first + ROWS)
            values = dot_nt(h_ref[rows], weight_ref[0, 0]) + bias_ref[0]
            keys[group, rows] = values.astype(BF16)
            squares = head_sums(values * values, ones)
            logs = features(values, rows) - (0.5 / math.sqrt(DH)) * squares
            state_ref[0, rows] = (scale_ref[0, 0] * jnp.exp(logs)).astype(BF16)

    @pl.when(kind == 2)
    def _():
        state_ref[0] = keys[group]

    @pl.when(kind == 3)
    def _():
        for first in range(0, length, ROWS):
            rows = slice(first, first + ROWS)
            values = dot_nt(h_ref[rows], weight_ref[0, 0]) + bias_ref[0]
            state_ref[0, rows] = values.astype(BF16)


def project_forward(layer, stream, gain, offset, weight, biases, tables, rotary):
    length, width = stream[0].shape
    full = jax.ShapeDtypeStruct((length, width), F32)
    state = jax.ShapeDtypeStruct((4, length, width), BF16)
    out_shape = [jax.ShapeDtypeStruct((length, width), BF16), state]
    out_specs = [whole((length, width)), plane_block(length, WIDE)]
    if len(stream) > 1:
        out_shape, out_specs = [full] + out_shape, [whole((length, width))] + out_specs

    def source(j):
        return jnp.where(j < 2 * QUADS, j, jnp.maximum(j - QUADS, 2 * QUADS - 1))

    def table(j):
        return jnp.where(j < 2 * QUADS, j % QUADS, QUADS - 1)

    return pl.pallas_call(
        functools.partial(project_kernel, len(stream)),
        grid=(4 * QUADS,),
        in_specs=[whole((length, width))] * len(stream)
        + [
            whole((1, width)),
            whole((1, width)),
            pl.BlockSpec((1, 1, WIDE, width), lambda j: (0, layer, source(j), 0)),
            pl.BlockSpec((1, 1, WIDE), lambda j: (source(j), 0, 0)),
            pl.BlockSpec((1, 1, WIDE, WIDE), lambda j: (layer, table(j), 0, 0)),
            pl.BlockSpec((1, 1, WIDE, WIDE), lambda j: (layer, table(j), 0, 0)),
            pl.BlockSpec((1, 1, 1, WIDE), lambda j: (layer, table(j), 0, 0)),
            whole((length, PAIR)),
            whole((length, PAIR)),
        ],
        out_specs=out_specs,
        out_shape=out_shape,
        scratch_shapes=[pltpu.VMEM((QUADS, length, WIDE), BF16)],
        compiler_params=params(),
        name="project_forward",
    )(*stream, gain, offset, weight, biases.reshape(-1, 1, WIDE), *tables, *rotary)


def write_mask(starts_ref, mask_ref, flipped):
    length = mask_ref.shape[0]
    keys = lane_index(1, length)
    documents = sum((starts_ref[0, i] <= keys).astype(jnp.int32) for i in range(starts_ref.shape[1]))
    for first in range(0, length, ROWS):
        own = row_index(ROWS, 1) + first
        document = sum(
            (starts_ref[0, i] <= own).astype(jnp.int32) for i in range(starts_ref.shape[1])
        )
        order = (own <= keys) if flipped else (keys <= own)
        seen = (document == documents) & order
        mask_ref[first : first + ROWS] = jnp.where(seen, 1.0, 0.0).astype(BF16)


def attend_kernel(starts_ref, state_ref, out_ref, mask_ref):
    @pl.when(pl.program_id(0) == 0)
    def _():
        write_mask(starts_ref, mask_ref, False)

    length = mask_ref.shape[0]
    zero = jnp.zeros((), BF16)
    one = jnp.ones((), BF16)
    for first in range(0, length, ROWS):
        rows = slice(first, first + ROWS)
        finish = first + ROWS
        left = lane_index(finish, PAIR) < DH
        seen = mask_ref[rows, :finish] > zero
        sums = []
        for own in (left, ~left):
            keys = jnp.where(own, state_ref[1, :finish], zero)
            scores = dot_nt(state_ref[0, rows], keys).astype(BF16)
            scores = jnp.where(seen, scores, zero)
            sums.append(dot_nn(scores, jnp.where(own, state_ref[3, :finish], one)))
        left = lane_index(ROWS, PAIR) < DH
        numer = jnp.where(left, sums[0], sums[1])
        denom = jnp.where(left, pltpu.roll(sums[0], DH, 1), pltpu.roll(sums[1], DH, 1))
        inverse = 1.0 / denom
        out_ref[0, rows] = (numer * inverse).astype(BF16)
        out_ref[1, rows], out_ref[2, rows] = split(inverse)


def attend_forward(starts, state):
    _, length, width = state.shape
    block = pl.BlockSpec((4, length, PAIR), lambda p: (0, 0, p))
    return pl.pallas_call(
        attend_kernel,
        grid=(PAIRS,),
        in_specs=[pl.BlockSpec(memory_space=pltpu.SMEM), block],
        out_specs=block,
        out_shape=jax.ShapeDtypeStruct(state.shape, BF16),
        scratch_shapes=[pltpu.VMEM((length, length), BF16)],
        compiler_params=params(),
        name="attend_forward",
    )(starts, state)


def mix_kernel(mixed_ref, weight_ref, bias_ref, part_ref):
    part_ref[...] = dot_nn(mixed_ref[0], weight_ref[0, 0]) + bias_ref[0]


def mix_forward(layer, mixed, weight, biases):
    _, length, width = mixed.shape
    return pl.pallas_call(
        mix_kernel,
        grid=(QUADS,),
        in_specs=[
            pl.BlockSpec((1, length, width), lambda j: (0, 0, 0), pipeline_mode=pl.Buffered(1)),
            pl.BlockSpec((1, 1, width, WIDE), lambda j: (0, layer, 3, j)),
            pl.BlockSpec((1, 1, WIDE), lambda j: (3 * QUADS + j, 0, 0)),
        ],
        out_specs=pl.BlockSpec((length, WIDE), lambda j: (0, j)),
        out_shape=jax.ShapeDtypeStruct((length, width), F32),
        compiler_params=params(),
        name="mix_forward",
    )(mixed, weight, biases.reshape(-1, 1, WIDE))


def mix_backward_kernel(grad_ref, weight_ref, mixed_ref, out_ref):
    row, lane = row_index(WIDE, WIDE), lane_index(WIDE, WIDE)
    partner = (row // PAIR == lane // PAIR) & (row // DH != lane // DH)
    ones = jnp.where(partner, 1.0, 0.0).astype(BF16)
    length = grad_ref.shape[0]
    for first in range(0, length, ROWS):
        rows = slice(first, first + ROWS)
        grad = dot_nt(grad_ref[rows], weight_ref[0, 0]).astype(BF16).astype(F32)
        inverse = mixed_ref[1, rows].astype(F32) + mixed_ref[2, rows].astype(F32)
        scaled = grad * inverse
        upper, lower = split(-head_sums(scaled * mixed_ref[0, rows].astype(F32), ones))
        numer = scaled.astype(BF16)
        lane = lane_index(ROWS, WIDE)
        spare = jnp.where(
            lane % DH == 0, upper, jnp.where(lane % DH == 1, lower, jnp.zeros((), BF16))
        )
        left = lane % PAIR < DH
        out_ref[0, rows] = jnp.where(left, numer, spare)
        out_ref[1, rows] = jnp.where(left, spare, numer)


def mix_backward(layer, grad, weight, mixed):
    _, length, width = mixed.shape
    return pl.pallas_call(
        mix_backward_kernel,
        grid=(QUADS,),
        in_specs=[
            whole((length, width)),
            pl.BlockSpec((1, 1, WIDE, width), lambda j: (0, layer, 3 * QUADS + j, 0)),
            pl.BlockSpec((4, length, WIDE), lambda j: (0, 0, j)),
        ],
        out_specs=pl.BlockSpec((2, length, WIDE), lambda j: (0, 0, j)),
        out_shape=jax.ShapeDtypeStruct((2, length, width), BF16),
        compiler_params=params(),
        name="mix_backward",
    )(grad, weight, mixed)


def attend_backward_kernel(starts_ref, state_ref, numer_ref, out_ref, mask_ref, query_t):
    @pl.when(pl.program_id(0) == 0)
    def _():
        write_mask(starts_ref, mask_ref, True)

    length = mask_ref.shape[0]
    zero = jnp.zeros((), BF16)
    one = jnp.ones((), BF16)
    query_t[...] = jnp.zeros_like(query_t)
    for first in range(0, length, ROWS):
        rows = slice(first, first + ROWS)
        seen = mask_ref[rows, first:] > zero
        lane = lane_index(ROWS, PAIR)
        left = lane < DH
        spare = jnp.where(lane % DH < 2, one, zero)
        keys, values = state_ref[1, rows], state_ref[3, rows]
        queries = state_ref[0, first:]
        numer = jnp.where(lane_index(length - first, PAIR) < DH, numer_ref[0, first:], numer_ref[1, first:])
        grads = []
        for head, own in enumerate((left, ~left)):
            own_keys = jnp.where(own, keys, zero)
            scores = dot_nt(own_keys, queries).astype(BF16)
            scores = jnp.where(seen, scores, zero)
            grad_value = dot_nn(scores, numer)
            grad_scores = dot_nt(jnp.where(own, values, spare), numer_ref[head, first:]).astype(BF16)
            grad_scores = jnp.where(seen, grad_scores, zero)
            grad_key = dot_nn(grad_scores, queries)
            query_t[head, :, first:] += dot_nn(own_keys.T[head * DH : (head + 1) * DH], grad_scores)
            grads.append((grad_value, grad_key))
        out_ref[2, rows] = jnp.where(left, grads[0][0], grads[1][0]).astype(BF16)
        grad_key = jnp.where(left, grads[0][1], grads[1][1])
        out_ref[1, rows] = (grad_key * keys.astype(F32)).astype(BF16)
    for first in range(0, length, ROWS):
        rows = slice(first, first + ROWS)
        grad_query = jnp.concatenate([query_t[0, :, rows], query_t[1, :, rows]], axis=0).T
        out_ref[0, rows] = (grad_query * state_ref[0, rows].astype(F32)).astype(BF16)


def attend_backward(starts, state, numer):
    _, length, width = state.shape
    return pl.pallas_call(
        attend_backward_kernel,
        grid=(PAIRS,),
        in_specs=[
            pl.BlockSpec(memory_space=pltpu.SMEM),
            pl.BlockSpec((4, length, PAIR), lambda p: (0, 0, p)),
            pl.BlockSpec((2, length, PAIR), lambda p: (0, 0, p)),
        ],
        out_specs=pl.BlockSpec((3, length, PAIR), lambda p: (0, 0, p)),
        out_shape=jax.ShapeDtypeStruct((3, length, width), BF16),
        scratch_shapes=[
            pltpu.VMEM((length, length), BF16),
            pltpu.VMEM((2, DH, length), F32),
        ],
        compiler_params=params(),
        name="attend_backward",
    )(starts, state, numer)


def project_backward_kernel(
    grad_ref, h_ref, mixed_ref, feat_ref, keys_ref, table_ref, cosine_ref, sine_ref, weight_ref,
    part_ref, out_ref, bias_ref, near_ref, far_ref, grad_t, h_t, flow,
):
    del near_ref, far_ref
    step = pl.program_id(0)
    kind, length = step // QUADS, h_ref.shape[0]

    @pl.when(step == 0)
    def _():
        grad_t[...] = grad_ref[...].T
        h_t[...] = h_ref[...].T
        part_ref[...] = jnp.zeros_like(part_ref)

    def project_back(rows):
        cosine = jnp.concatenate([cosine_ref[rows]] * (WIDE // PAIR), axis=1)
        sine = jnp.concatenate([sine_ref[rows]] * (WIDE // PAIR), axis=1)
        return turn_back(dot_nt(feat_ref[0, rows], table_ref[0, 0]), cosine, sine)

    @pl.when(kind == 0)
    def _():
        flow[...] = mixed_ref[0]
        bias_ref[0] = jnp.sum(feat_ref[0, :1].astype(F32), axis=0, keepdims=True)

    @pl.when(kind == 1)
    def _():
        for first in range(0, length, ROWS):
            rows = slice(first, first + ROWS)
            flow[rows] = project_back(rows).astype(BF16)

    @pl.when(kind == 2)
    def _():
        ones = same_head_ones()
        for first in range(0, length, ROWS):
            rows = slice(first, first + ROWS)
            shrink = dot_nn(feat_ref[0, rows], ones) * (1.0 / math.sqrt(DH))
            flow[rows] = (project_back(rows) - keys_ref[0, rows].astype(F32) * shrink).astype(BF16)

    @pl.when(kind == 3)
    def _():
        flow[...] = feat_ref[0]

    @pl.when(kind > 0)
    def _():
        bias = jnp.zeros((1, WIDE), F32)
        for first in range(0, length, ROWS):
            rows = slice(first, first + ROWS)
            bias += jnp.sum(flow[rows].astype(F32), axis=0, keepdims=True)
            part_ref[rows] += dot_nn(flow[rows], weight_ref[0, 0])
            out_ref[0, rows] = dot_nn(h_t[rows], flow[...])
        bias_ref[0] = bias

    @pl.when(kind == 0)
    def _():
        for first in range(0, length, ROWS):
            rows = slice(first, first + ROWS)
            out_ref[0, rows] = dot_nn(grad_t[rows], flow[...])


def project_backward(layer, grad, h, mixed, feats, state, tables, rotary, weight):
    _, length, width = state.shape
    blocks = 4 * QUADS

    def at(j):
        return jnp.maximum(j - QUADS, 0)

    def target(j):
        return jnp.where(j < QUADS, 3 * QUADS + j, j - QUADS)

    return pl.pallas_call(
        project_backward_kernel,
        grid=(blocks,),
        in_specs=[
            whole((length, width)),
            whole((length, width)),
            pl.BlockSpec((1, length, WIDE), lambda j: (0, 0, jnp.minimum(j, QUADS - 1))),
            pl.BlockSpec((1, length, WIDE), lambda j: (at(j) // QUADS, 0, at(j) % QUADS)),
            pl.BlockSpec(
                (1, length, WIDE), lambda j: (2, 0, jnp.clip(j - 2 * QUADS, 0, QUADS - 1))
            ),
            pl.BlockSpec((1, 1, WIDE, WIDE), lambda j: (layer, at(j) % QUADS, 0, 0)),
            whole((length, PAIR)),
            whole((length, PAIR)),
            pl.BlockSpec((1, 1, WIDE, width), lambda j: (0, layer, at(j), 0)),
        ],
        out_specs=[
            whole((length, width)),
            pl.BlockSpec((1, width, WIDE), lambda j: (target(j), 0, 0)),
            pl.BlockSpec((1, 1, WIDE), lambda j: (target(j), 0, 0)),
            pl.BlockSpec(memory_space=pl.ANY),
            pl.BlockSpec(memory_space=pl.ANY),
        ],
        out_shape=[
            jax.ShapeDtypeStruct((length, width), F32),
            jax.ShapeDtypeStruct((blocks, width, WIDE), F32),
            jax.ShapeDtypeStruct((blocks, 1, WIDE), F32),
            jax.ShapeDtypeStruct((blocks, width // 2, WIDE), F32),
            jax.ShapeDtypeStruct((blocks, width // 2, WIDE), F32),
        ],
        scratch_shapes=[
            pltpu.VMEM((width, length), BF16),
            pltpu.VMEM((width, length), BF16),
            pltpu.VMEM((length, WIDE), BF16),
        ],
        compiler_params=params(),
        name="project_backward",
    )(grad, h, mixed, feats, state, tables[0], *rotary, weight)


def norm_backward_kernel(x_ref, own_ref, other_ref, grad_ref, gain_ref, out_ref, sums_ref):
    @pl.when(pl.program_id(0) == 0)
    def _():
        sums_ref[...] = jnp.zeros_like(sums_ref)

    values = x_ref[...].astype(F32)
    average = jnp.mean(values, -1, keepdims=True)
    centered = values - average
    variance = jnp.mean(centered * centered, -1, keepdims=True)
    inverse = lax.rsqrt(variance + EPSILON)
    unit = centered * inverse
    incoming = own_ref[...] + other_ref[...]
    grad_unit = incoming * gain_ref[...].astype(F32)
    first = jnp.mean(grad_unit, -1, keepdims=True)
    second = jnp.mean(grad_unit * unit, -1, keepdims=True)
    grad = grad_ref[...].astype(F32)
    out = grad + inverse * (grad_unit - first - unit * second)
    out_ref[...] = out.astype(out_ref.dtype)
    sums_ref[0:1] += jnp.sum(incoming * unit, axis=0, keepdims=True)
    sums_ref[1:2] += jnp.sum(incoming, axis=0, keepdims=True)
    sums_ref[2:3] += jnp.sum(grad, axis=0, keepdims=True)


def norm_backward(x, own, other, grad, gain, kind):
    length, width = own.shape
    block = pl.BlockSpec((ROWS, width), lambda i: (i, 0))
    return pl.pallas_call(
        norm_backward_kernel,
        grid=(length // ROWS,),
        in_specs=[block, block, block, block, whole((1, width))],
        out_specs=[block, whole((8, width))],
        out_shape=[
            jax.ShapeDtypeStruct((length, width), kind),
            jax.ShapeDtypeStruct((8, width), F32),
        ],
        compiler_params=params(),
        name="norm_backward",
    )(x, own, other, grad, gain)


MESH = pl.DeviceIdType.MESH
UNIT = 8
SLOTS = 4
LAG = 1


class Flow(NamedTuple):
    order: tuple
    layer: int
    begun: int
    start: int
    segments: tuple


def first_rows(rows):
    cuts = (0, rows * 11 // 32, rows * 22 // 32, rows)
    return tuple(zip(cuts[:-1], cuts[1:]))


def begun_flows(rows, layer):
    orders = (((0, 1, 2, 3),) * 2, ((1, 0, 2, 3),) * 2, ((2, 0, 1, 3), (2, 1, 0, 3)))
    flows = []
    for way in range(3):
        for part in range(2):
            segments = []
            for is_up in range(2):
                first, finish = first_rows(rows[is_up])[way]
                half = (finish - first) // 2
                base = first_rows(rows[0])[way]
                base = base[1] - base[0] if is_up else 0
                segments.append(
                    (bool(is_up), first + part * half, half // UNIT, base + part * half)
                )
            flows.append(Flow(orders[way][part], layer, way, 0, tuple(segments)))
    return flows


def fresh_flows(rows, layer, start):
    orders = ((0, 1, 2, 3), (1, 0, 2, 3)) + ((0, 2, 3, 1), (1, 2, 3, 0)) * 2
    count = len(orders)
    flows, at = [], [0, 0]
    for index, order in enumerate(orders):
        segments = []
        for is_up in range(2):
            units = rows[is_up] // UNIT
            place = index if is_up == 0 else count - 1 - index
            share = units // count + (place < units % count)
            segments.append((bool(is_up), at[is_up] * UNIT, share, 0))
            at[is_up] += share
        flows.append(Flow(order, layer, -1, start, tuple(segments)))
    return flows


def units_of(flow):
    return sum(segment[2] for segment in flow.segments)


def bit_of(index, bit):
    return (index // (1 << bit)) % 2


def flip(index, bit):
    return index + (1 << bit) * (1 - 2 * bit_of(index, bit))


def scatter_kernel(bits, flows, layers, *refs):
    sources, refs = refs[: 3 * layers], refs[3 * layers :]
    halves, refs = refs[:3], refs[3:]
    small_ref, weight_out, up_out, small_out = refs[:4]
    stages = bits
    weight_sum, up_sum = refs[4:6]
    small_held = refs[6 : 6 + stages]
    held = refs[6 + stages :]
    held, sems = held[: len(flows) * (stages + 1)], held[len(flows) * (stages + 1) :]
    load_sem, send_sem, recv_sem, credit, small_send, small_recv = sems
    held = [held[f * (stages + 1) : (f + 1) * (stages + 1)] for f in range(len(flows))]
    me, core = lax.axis_index("batch"), lax.axis_index("stream")
    totals = [units_of(flow) for flow in flows]

    barrier = pltpu.get_barrier_semaphore()
    for bit in range(bits):
        pl.semaphore_signal(
            barrier, inc=1, device_id={"batch": flip(me, bit)}, device_id_type=MESH
        )
    pl.semaphore_wait(barrier, bits)

    def view(order, stage, mine):
        left = sorted(set(range(bits)) - set(order[:stage]), reverse=True)
        pick = bit_of(me, order[stage])
        pick = pick if mine else 1 - pick
        return tuple(pick if bit == order[stage] else slice(None) for bit in left)

    def remote(flow, stage, slot, source):
        return pltpu.make_async_remote_copy(
            src_ref=source,
            dst_ref=held[flow][stage + 1].at[slot],
            send_sem=send_sem.at[flow, stage, slot],
            recv_sem=recv_sem.at[flow, stage, slot],
            device_id={"batch": flip(me, flows[flow].order[stage])},
            device_id_type=MESH,
        )

    def sent_from(flow, stage, slot):
        if stage == 0:
            return held[flow][0].at[slot]
        return held[flow][stage].at[(slot,) + view(flows[flow].order, stage, False)]

    def load(flow, slot, source):
        return pltpu.make_async_copy(source, held[flow][0].at[slot], load_sem.at[flow, slot])

    def load_half(flow, slot, source):
        return pltpu.make_async_copy(
            source, held[flow][1].at[slot], recv_sem.at[flow, 0, slot]
        )

    def return_credit(flow, stage, unit):
        if stage == 0 and flows[flow].begun >= 0:
            return

        @pl.when(unit + SLOTS < totals[flow])
        def _():
            pl.semaphore_signal(
                credit.at[flow, stage],
                inc=1,
                device_id={"batch": flip(me, flows[flow].order[stage])},
                device_id_type=MESH,
            )

    def take_credit(flow, stage, unit):
        @pl.when(unit >= SLOTS)
        def _():
            pl.semaphore_wait(credit.at[flow, stage], 1)

    def places(flow, unit, act):
        base = 0
        for is_up, row, units, half_row in flows[flow].segments:
            offset = (unit - base) * UNIT
            pl.when((unit >= base) & (unit < base + units))(
                functools.partial(act, is_up, row + offset, half_row + offset)
            )
            base += units

    def begin(flow, unit):
        slot = lax.rem(unit, SLOTS)
        order, layer, begun = flows[flow][:3]
        if begun < 0:
            take_credit(flow, 0, unit)

        def start(source, row):
            at = (pl.ds(pl.multiple_of(row, UNIT), UNIT),)
            load(flow, slot, source.at[view(order, 0, True) + at]).start()
            if begun < 0:
                remote(flow, 0, slot, source.at[view(order, 0, False) + at]).start()

        def act(is_up, row, half_row):
            if begun >= 0:
                at = (slice(None),) * (bits - 1)
                at += (pl.ds(pl.multiple_of(half_row, UNIT), UNIT),)
                load_half(flow, slot, halves[begun].at[at]).start()
            if not is_up:
                start(sources[3 * layer], row)
            else:
                for side in range(2):
                    pl.when(core == side)(
                        functools.partial(start, sources[3 * layer + 1 + side], row)
                    )

        places(flow, unit, act)

    def advance(flow, stage, unit):
        slot = lax.rem(unit, SLOTS)
        order, layer, begun = flows[flow][:3]
        buffer = held[flow][stage]
        copy = remote(flow, stage - 1, slot, sent_from(flow, stage - 1, slot))
        if stage == 1 and begun >= 0:
            load_half(flow, slot, held[flow][0].at[slot]).wait()
        else:
            copy.wait_recv()
        if stage == 1:
            load(flow, slot, held[flow][1].at[slot]).wait()
            mine = held[flow][0][slot]
        else:
            mine = held[flow][stage - 1][(slot,) + view(order, stage - 1, True)]
        value = buffer[slot] + mine
        if stage < stages:
            buffer[slot] = value
            take_credit(flow, stage, unit)
            remote(flow, stage, slot, sent_from(flow, stage, slot)).start()
        else:

            def act(is_up, row, half_row):
                target = up_sum if is_up else weight_sum
                target[layer, pl.ds(pl.multiple_of(row, UNIT), UNIT)] = value

            places(flow, unit, act)
        if stage > 1 or begun < 0:
            copy.wait_send()
        if stage >= 2:
            return_credit(flow, stage - 2, unit)
        if stage == stages:
            return_credit(flow, stage - 1, unit)

    small_order = tuple(range(bits))

    def small_copy(stage):
        source = small_ref if stage == 0 else small_held[stage - 1]
        return pltpu.make_async_remote_copy(
            src_ref=source.at[view(small_order, stage, False)],
            dst_ref=small_held[stage],
            send_sem=small_send.at[stage],
            recv_sem=small_recv.at[stage],
            device_id={"batch": flip(me, small_order[stage])},
            device_id_type=MESH,
        )

    def small_step(stage):
        if stage > 0:
            small_copy(stage - 1).wait()
            source = small_ref if stage == 1 else small_held[stage - 2]
            sums = small_held[stage - 1][...] + source[view(small_order, stage - 1, True)]
            if stage == stages:
                small_out[...] = sums
            else:
                small_held[stage - 1][...] = sums
        if stage < stages:
            small_copy(stage).start()

    def step(index, carry):
        for place, flow in enumerate(flows):
            unit = index - flow.start
            pl.when((unit >= 0) & (unit < totals[place]))(
                functools.partial(begin, place, unit)
            )
        for place, flow in enumerate(flows):
            for stage in range(1, stages + 1):
                unit = index - flow.start - LAG * stage
                pl.when((unit >= 0) & (unit < totals[place]))(
                    functools.partial(advance, place, stage, unit)
                )
        for stage in range(stages + 1):
            pl.when(index == stages + 2 * stage)(functools.partial(small_step, stage))
        return carry

    last = max(flow.start + total for flow, total in zip(flows, totals))
    lax.fori_loop(0, last + LAG * stages, step, 0)
    half = WIDE // 2
    for layer in range(layers):
        weight_out[layers - 1 - layer] = weight_sum[layer].T
        folded = up_sum.shape[1]
        up_out[layers - 1 - layer, :, :folded] = up_sum[layer, :, :half].T
        up_out[layers - 1 - layer, :, folded:] = up_sum[layer, :, half:].T


def pack_halves(weight, near, far):
    count, width, lanes = weight.shape
    bits = count.bit_length() - 1
    rows = (width, near.shape[1])
    ranges = [first_rows(length) for length in rows]

    def kernel(weight_ref, near_ref, far_ref, *refs):
        outs, sems = refs[:3], refs[3]
        me, core = lax.axis_index("batch"), lax.axis_index("stream")

        def copies(source, is_up):
            for bit in range(3):
                first, finish = ranges[is_up][bit]
                base = ranges[0][bit][1] - ranges[0][bit][0] if is_up else 0
                at = [slice(None)] * bits + [pl.ds(first, finish - first)]
                at[bits - 1 - bit] = 1 - bit_of(me, bit)
                to = (slice(None),) * (bits - 1) + (pl.ds(base, finish - first),)
                yield pltpu.make_async_copy(
                    source.at[tuple(at)], outs[bit].at[to], sems.at[is_up, bit]
                )

        def start(source, is_up):
            for copy in copies(source, is_up):
                copy.start()

        start(weight_ref, 0)
        for side, source in enumerate((near_ref, far_ref)):
            pl.when(core == side)(functools.partial(start, source, 1))
        for copy in list(copies(weight_ref, 0)) + list(copies(near_ref, 1)):
            copy.wait()

    shapes = [
        (2,) * (bits - 1) + (sum(r[bit][1] - r[bit][0] for r in ranges), lanes) for bit in range(3)
    ]
    return pl.pallas_call(
        kernel,
        in_specs=[pl.BlockSpec(memory_space=pltpu.HBM)] * 3,
        out_specs=[pl.BlockSpec(memory_space=pltpu.HBM)] * 3,
        out_shape=[jax.ShapeDtypeStruct(shape, F32) for shape in shapes],
        scratch_shapes=[pltpu.SemaphoreType.DMA((2, 3))],
        name="pack_halves",
    )(*[array.reshape((2,) * bits + array.shape[1:]) for array in (weight, near, far)])


def send_halves(weight, near, far):
    count = weight.shape[0]
    received = []
    for bit, part in enumerate(pack_halves(weight, near, far)):
        pairs = [(source, flip(source, bit)) for source in range(count)]
        received.append(lax.ppermute(part, "batch", pairs))
    return received


def after(first, others):
    def kernel(*refs):
        del refs

    return pl.pallas_call(
        kernel,
        in_specs=[pl.BlockSpec(memory_space=pltpu.HBM)] * (1 + len(others)),
        out_specs=pl.BlockSpec(memory_space=pltpu.HBM),
        out_shape=jax.ShapeDtypeStruct(first.shape, first.dtype),
        input_output_aliases={0: 0},
        name="after",
    )(first, *others)


def reduce_scatter(grads, halves, small):
    layers = len(grads) // 3
    count, width = grads[0].shape[:2]
    folded = grads[1].shape[1]
    bits = count.bit_length() - 1
    small = jnp.pad(small, ((0, 0), (0, -small.shape[1] % 1024)))
    small = small.reshape((2,) * bits + (-1, 128))
    flows = begun_flows((width, folded), 0)
    for layer in range(1, layers):
        start = max(flow.start + units_of(flow) for flow in flows)
        flows = flows + fresh_flows((width, folded), layer, start)
    scratch = [pltpu.VMEM((layers, width, WIDE), F32), pltpu.VMEM((layers, folded, WIDE), F32)]
    scratch += [
        pltpu.VMEM((2,) * (bits - 1 - stage) + small.shape[-2:], F32) for stage in range(bits)
    ]
    for _ in flows:
        for stage in range(bits + 1):
            lead = (SLOTS,) + (2,) * (bits - 1 - max(stage - 1, 0))
            scratch.append(pltpu.VMEM(lead + (UNIT, WIDE), F32))
    scratch += [
        pltpu.SemaphoreType.DMA((len(flows), SLOTS)),
        pltpu.SemaphoreType.DMA((len(flows), bits, SLOTS)),
        pltpu.SemaphoreType.DMA((len(flows), bits, SLOTS)),
        pltpu.SemaphoreType.REGULAR((len(flows), bits)),
        pltpu.SemaphoreType.DMA((bits,)),
        pltpu.SemaphoreType.DMA((bits,)),
    ]
    weight, up, small = pl.pallas_call(
        functools.partial(scatter_kernel, bits, flows, layers),
        in_specs=[pl.BlockSpec(memory_space=pltpu.HBM)] * (len(grads) + len(halves))
        + [pl.BlockSpec(memory_space=pltpu.VMEM)],
        out_specs=[pl.BlockSpec(memory_space=pltpu.VMEM)] * 3,
        out_shape=[
            jax.ShapeDtypeStruct((layers, WIDE, width), F32),
            jax.ShapeDtypeStruct((layers, WIDE // 2, width), F32),
            jax.ShapeDtypeStruct(small.shape[-2:], F32),
        ],
        scratch_shapes=scratch,
        compiler_params=pltpu.CompilerParams(
            collective_id=0, has_side_effects=True, vmem_limit_bytes=VMEM_LIMIT
        ),
        name="reduce_scatter",
    )(*[array.reshape((2,) * bits + array.shape[1:]) for array in grads], *halves, small)
    return weight, up, small.reshape(-1)


def shards(
    tokens, cotangent, branch_weight, branch_bias, up_weight, down_bias,
    norm_gain, norm_bias, freq_seeds, doc_starts,
):
    is_attention = lax.axis_index("stream") == 0
    length, width = tokens.shape
    rotary = tuple(jnp.asarray(table) for table in rotary_rows(length))
    biases = branch_bias[0].astype(F32)
    tables = lax.cond(
        is_attention,
        lambda: tuple(feature_tables(freq_seeds)),
        lambda: (
            jnp.zeros((LAYERS, QUADS, WIDE, WIDE), BF16),
            jnp.zeros((LAYERS, QUADS, WIDE, WIDE), BF16),
            jnp.zeros((LAYERS, QUADS, 1, WIDE), F32),
        ),
    )
    swap = [(0, 1), (1, 0)]

    def attention(layer, stream):
        gain, offset = norm_gain[layer : layer + 1], norm_bias[layer : layer + 1]
        *x, h, state = project_forward(
            layer, stream, gain, offset, branch_weight, biases[layer], tables, rotary
        )
        mixed = attend_forward(doc_starts, state)
        part = mix_forward(layer, mixed, branch_weight, biases[layer])
        return tuple(x) + (part, h, state, mixed)

    def feed_forward(layer, stream):
        gain, offset = norm_gain[layer : layer + 1], norm_bias[layer : layer + 1]
        return tuple(
            mlp_forward(
                layer, stream, gain, offset, up_weight, biases[layer], branch_weight,
                down_bias[layer : layer + 1],
            )
        )

    stream = (tokens,)
    inputs, kept = [], []
    for layer in range(LAYERS):
        *x, part, h, state, mixed = lax.cond(
            is_attention,
            functools.partial(attention, layer, stream),
            functools.partial(feed_forward, layer, stream),
        )
        inputs.append(x[0] if x else tokens)
        kept.append((h, state, mixed))
        stream = (inputs[-1], part, lax.ppermute(part, "stream", swap))
    result = stream[0] + (stream[1] + stream[2])

    def attention_back(layer, grad):
        h, state, mixed = kept[layer]
        numer = mix_backward(layer, grad, branch_weight, mixed)
        feats = attend_backward(doc_starts, state, numer)
        part, weight, bias, near, far = project_backward(
            layer, grad, h, mixed, feats, state, tables, rotary, branch_weight
        )
        return part, weight, near, far, bias.reshape(-1, WIDE)

    def feed_forward_back(layer, grad):
        h, act, slope = kept[layer]
        part, weight, near, far, bias = mlp_backward(
            layer, grad, h, act, slope, branch_weight, up_weight
        )
        return part, weight, near, far, bias.reshape(-1, WIDE)

    grad = cotangent
    count = lax.axis_size("batch")
    blocked = count == branch_weight.shape[2] // WIDE
    grads, vectors = [], []
    for layer in reversed(range(LAYERS)):
        part, weight, near, far, bias = lax.cond(
            is_attention,
            functools.partial(attention_back, layer, grad),
            functools.partial(feed_forward_back, layer, grad),
        )
        if blocked and layer < LAYERS - 1:
            part = after(part, halves)
        other = lax.ppermute(part, "stream", swap)
        if blocked:
            near = lax.ppermute(near, "stream", [(1, 0)])
            if layer == LAYERS - 1:
                halves = send_halves(weight, near, far)
        kind = BF16 if layer else F32
        new_grad, sums = norm_backward(
            inputs[layer], part, other, grad, norm_gain[layer : layer + 1], kind
        )
        bias = jnp.where(
            is_attention & (jnp.arange(bias.shape[0])[:, None] >= 3 * QUADS),
            jnp.tile(sums[2].reshape(QUADS, WIDE), (bias.shape[0] // QUADS, 1)),
            bias,
        )
        vectors = [bias.reshape(count, -1), sums[:3].reshape(3, count, -1)] + vectors
        grads += [weight, near, far]
        grad = new_grad
    small = jnp.concatenate(
        [part.reshape(count, -1) for part in vectors[0::2]]
        + [jnp.moveaxis(part, 0, 1).reshape(count, -1) for part in vectors[1::2]],
        axis=1,
    )
    if blocked:
        weight, up, small = reduce_scatter(grads, halves, small)
    else:
        weight, up, small = scatter_rows(grads, small)
    each = branch_weight.shape[2] // count
    bias, sums = small[: LAYERS * each], small[LAYERS * each :]
    sums = sums[: LAYERS * 3 * (width // count)].reshape(LAYERS, 3, -1)
    return (
        result,
        grad,
        weight[None],
        bias.reshape(1, LAYERS, -1),
        up,
        sums[:, 2],
        sums[:, 0],
        sums[:, 1],
    )


def scatter_rows(grads, small):
    scatter = functools.partial(
        lax.psum_scatter, axis_name="batch", scatter_dimension=0, tiled=True
    )
    weights, ups = [], []
    for weight, near, far in zip(grads[0::3], grads[1::3], grads[2::3]):
        half = near.shape[2] // 2
        whole_up = [
            jnp.concatenate([side[..., :half], side[..., half:]], axis=1) for side in (near, far)
        ]
        whole_up = rows_of(jnp.concatenate(whole_up, axis=2))
        whole_up = jnp.where(lax.axis_index("stream") == 1, whole_up, 0.0)
        weights.append(scatter(rows_of(weight)))
        ups.append(
            lax.psum_scatter(whole_up, ("batch", "stream"), scatter_dimension=0, tiled=True)
        )
    return jnp.stack(weights[::-1]), jnp.stack(ups[::-1]), scatter(small)[0]


def rows_of(blocks):
    return jnp.transpose(blocks, (0, 2, 1)).reshape(-1, blocks.shape[1])


def solution(mesh):
    placed = (
        P("batch", None),
        P("batch", None),
        P("stream", None, None, None),
        P("stream", None, None),
        P(),
        P(),
        P(),
        P(),
        P(),
        P("batch", None),
    )
    return jax.shard_map(
        shards,
        mesh=mesh,
        in_specs=placed,
        out_specs=(
            P("batch", None),
            P("batch", None),
            P("stream", None, "batch", None),
            P("stream", None, "batch"),
            P(None, ("batch", "stream"), None),
            P(None, "batch"),
            P(None, "batch"),
            P(None, "batch"),
        ),
        check_vma=False,
    )
```

```python
import functools
import math
from typing import NamedTuple

import jax
import jax.numpy as jnp
import numpy as np
from jax import lax
from jax.experimental import pallas as pl
from jax.experimental.pallas import tpu as pltpu
from jax.sharding import PartitionSpec as P

HEADS = 16
DH = 64
ROT = 16
FEAT = 64
LAYERS = 2
EPSILON = 1e-05
HIGH = lax.Precision.HIGHEST
F32 = jnp.float32
BF16 = jnp.bfloat16
WIDE = 256
PAIR = 128
QUADS = HEADS * DH // WIDE
PAIRS = HEADS * DH // PAIR
ROWS = 256
VMEM_LIMIT = 56 * 1024 * 1024


def params():
    return pltpu.CompilerParams(vmem_limit_bytes=VMEM_LIMIT)


def whole(shape):
    zeros = (0,) * len(shape)
    return pl.BlockSpec(shape, lambda *_: zeros, pipeline_mode=pl.Buffered(1))


def dot_nn(left, right):
    return lax.dot_general(left, right, (((1,), (0,)), ((), ())), preferred_element_type=F32)


def dot_nt(left, right):
    return lax.dot_general(left, right, (((1,), (1,)), ((), ())), preferred_element_type=F32)


def split(values):
    upper = values.astype(BF16)
    return upper, (values - upper.astype(F32)).astype(BF16)


def lane_index(rows, lanes):
    return lax.broadcasted_iota(jnp.int32, (rows, lanes), 1)


def row_index(rows, lanes):
    return lax.broadcasted_iota(jnp.int32, (rows, lanes), 0)


def cosine_block():
    samples = np.arange(DH, dtype=np.float64)
    angles = math.pi * (samples[None, :] + 0.5) * samples[:, None] / DH
    table = np.cos(angles) * math.sqrt(2.0 / DH)
    table[0] *= math.sqrt(0.5)
    return np.kron(np.eye(WIDE // DH), table.T * DH ** (-0.25)).astype(np.float32)


def rotary_rows(length):
    position = np.arange(length, dtype=np.float32)
    inverse = (10000.0 ** (-np.arange(0, ROT, 2, dtype=np.float32) / ROT)).astype(np.float32)
    angles = position[:, None] * inverse[None, :]
    cosine, sine = np.cos(angles), np.sin(angles)
    rest = DH - ROT
    cosine_head = np.concatenate([cosine, cosine, np.ones((length, rest))], 1)
    sine_head = np.concatenate([-sine, sine, np.zeros((length, rest))], 1)
    repeat = PAIR // DH
    return (
        np.tile(cosine_head, (1, repeat)).astype(np.float32),
        np.tile(sine_head, (1, repeat)).astype(np.float32),
    )


def tables_kernel(seeds_ref, cosine_ref, upper_ref, lower_ref, weight_ref):
    feature = lane_index(WIDE, WIDE)
    lattice = (feature % FEAT) * seeds_ref[0] % FEAT
    prob = (lattice.astype(F32) + 0.5) / FEAT
    radius = jnp.sqrt(-2.0 * jnp.log(jnp.minimum(prob, 1.0 - prob)))
    above = 2.515517 + 0.802853 * radius + 0.010328 * radius * radius
    below = (
        1.0 + 1.432788 * radius + 0.189269 * radius * radius + 0.001308 * radius * radius * radius
    )
    magnitude = radius - above / below
    same_head = row_index(WIDE, WIDE) // DH == feature // FEAT
    omega = jnp.where(same_head, jnp.where(prob > 0.5, magnitude, -magnitude), 0.0)
    project = jnp.dot(cosine_ref[...], omega, precision=HIGH, preferred_element_type=F32)
    upper_ref[0, 0], lower_ref[0, 0] = split(project)
    grown = jnp.exp(-0.5 / DH * jnp.sum(omega * omega, axis=0, keepdims=True))
    total = jnp.dot(
        jnp.broadcast_to(grown, (8, WIDE)),
        same_head.astype(F32),
        precision=HIGH,
        preferred_element_type=F32,
    )
    weight_ref[0, 0] = FEAT * grown / total[:1]


def feature_tables(seeds):
    return pl.pallas_call(
        tables_kernel,
        grid=(LAYERS, QUADS),
        in_specs=[
            pl.BlockSpec((1, WIDE, 1), lambda l, g: (l, g, 0)),
            whole((WIDE, WIDE)),
        ],
        out_specs=[
            pl.BlockSpec((1, 1, WIDE, WIDE), lambda l, g: (l, g, 0, 0)),
            pl.BlockSpec((1, 1, WIDE, WIDE), lambda l, g: (l, g, 0, 0)),
            pl.BlockSpec((1, 1, 1, WIDE), lambda l, g: (l, g, 0, 0)),
        ],
        out_shape=[
            jax.ShapeDtypeStruct((LAYERS, QUADS, WIDE, WIDE), BF16),
            jax.ShapeDtypeStruct((LAYERS, QUADS, WIDE, WIDE), BF16),
            jax.ShapeDtypeStruct((LAYERS, QUADS, 1, WIDE), F32),
        ],
        compiler_params=params(),
        name="feature_tables",
    )(seeds.reshape(LAYERS, HEADS * DH, 1), jnp.asarray(cosine_block()))


def turn(values, cosine, sine):
    lanes = values.shape[1]
    half = ROT // 2
    lane = lane_index(*values.shape) % DH
    swapped = jnp.where(
        lane < half, pltpu.roll(values, lanes - half, 1), pltpu.roll(values, half, 1)
    )
    return values * cosine + swapped * sine


def turn_back(values, cosine, sine):
    lanes = values.shape[1]
    half = ROT // 2
    lane = lane_index(*values.shape) % DH
    turned = values * sine
    swapped = jnp.where(
        lane < half, pltpu.roll(turned, lanes - half, 1), pltpu.roll(turned, half, 1)
    )
    return values * cosine + jnp.where(lane < ROT, swapped, 0.0)


def normalized(x_ref_rows, gain, offset):
    average = jnp.mean(x_ref_rows, -1, keepdims=True)
    centered = x_ref_rows - average
    variance = jnp.mean(centered * centered, -1, keepdims=True)
    return centered * lax.rsqrt(variance + EPSILON) * gain + offset


def start_layer(stream, x_ref, h_ref, gain_ref, offset_ref):
    length = h_ref.shape[0]
    step = min(128, length)

    @pl.loop(0, length // step)
    def _(index):
        rows = pl.ds(pl.multiple_of(index * step, step), step)
        values = stream[0][rows].astype(F32)
        if len(stream) > 1:
            values = values + (stream[1][rows] + stream[2][rows])
            x_ref[rows] = values
        h_ref[rows] = normalized(
            values, gain_ref[...].astype(F32), offset_ref[...].astype(F32)
        ).astype(BF16)


def gelu_parts(units):
    below = 0.5 + 0.5 * lax.erf(units * math.sqrt(0.5))
    return below, jnp.exp(-0.5 * units * units) * (1.0 / math.sqrt(2.0 * math.pi))


FF_BLOCK = 1024
FF_ROWS = 512


def mlp_forward_kernel(count, *refs):
    stream, refs = refs[:count], refs[count:]
    gain_ref, offset_ref, up_ref, bias_ref, down_ref, down_bias_ref = refs[:6]
    refs = refs[6:]
    x_ref = None
    if count > 1:
        x_ref, refs = refs[0], refs[1:]
    part_ref, h_ref, act_ref, slope_ref = refs
    step = pl.program_id(0)

    @pl.when(step == 0)
    def _():
        start_layer(stream, x_ref, h_ref, gain_ref, offset_ref)
        part_ref[...] = jnp.broadcast_to(down_bias_ref[...].astype(F32), part_ref.shape)

    for first in range(0, h_ref.shape[0], FF_ROWS):
        rows = slice(first, first + FF_ROWS)
        units = dot_nt(h_ref[rows], up_ref[0]) + bias_ref[0]
        below, density = gelu_parts(units)
        active = (units * below).astype(BF16)
        act_ref[0, rows] = active
        slope_ref[0, rows] = (below + units * density).astype(BF16)
        part_ref[rows] += dot_nn(active, down_ref[0, 0])


def plane_block(length, lanes):
    per_plane = 1024 // lanes
    return pl.BlockSpec((1, length, lanes), lambda j: (j // per_plane, 0, j % per_plane))


def mlp_forward(layer, stream, gain, offset, up, biases, down_weight, down_bias):
    length, width = stream[0].shape
    hidden = up.shape[1]
    blocks = hidden // FF_BLOCK
    state = jax.ShapeDtypeStruct((4, length, width), BF16)
    full = jax.ShapeDtypeStruct((length, width), F32)
    out_shape = [full, jax.ShapeDtypeStruct((length, width), BF16), state, state]
    out_specs = [whole((length, width)), whole((length, width))]
    out_specs += [plane_block(length, FF_BLOCK)] * 2
    if len(stream) > 1:
        out_shape, out_specs = [full] + out_shape, [whole((length, width))] + out_specs
    return pl.pallas_call(
        functools.partial(mlp_forward_kernel, len(stream)),
        grid=(blocks,),
        in_specs=[whole((length, width))] * len(stream)
        + [
            whole((1, width)),
            whole((1, width)),
            pl.BlockSpec((1, FF_BLOCK, width), lambda j: (layer, j, 0)),
            pl.BlockSpec((1, 1, FF_BLOCK), lambda j: (j, 0, 0)),
            pl.BlockSpec((1, 1, FF_BLOCK, width), lambda j: (0, layer, j, 0)),
            whole((1, width)),
        ],
        out_specs=out_specs,
        out_shape=out_shape,
        compiler_params=params(),
        name="mlp_forward",
    )(*stream, gain, offset, up, biases.reshape(blocks, 1, FF_BLOCK), down_weight, down_bias)


def mlp_backward_kernel(
    grad_ref, h_ref, act_ref, slope_ref, down_ref, up_ref,
    part_ref, weight_ref, near_ref, far_ref, bias_ref, grad_t, h_t,
):
    step = pl.program_id(0)

    @pl.when(step == 0)
    def _():
        grad_t[...] = grad_ref[...].T
        h_t[...] = h_ref[...].T
        part_ref[...] = jnp.zeros_like(part_ref)

    length = h_ref.shape[0]
    bias = jnp.zeros((1, FF_BLOCK), F32)
    pieces = []
    for first in range(0, length, ROWS):
        rows = slice(first, first + ROWS)
        grad_act = dot_nt(grad_ref[rows], down_ref[0, 0])
        grad_unit = (grad_act * slope_ref[0, rows].astype(F32)).astype(BF16)
        bias += jnp.sum(grad_unit.astype(F32), axis=0, keepdims=True)
        pieces.append(grad_unit)
        part_ref[rows] += dot_nn(grad_unit, up_ref[0])
    bias_ref[0] = bias
    units = jnp.concatenate(pieces, axis=0)
    folded, half = near_ref.shape[1], near_ref.shape[2] // 2
    for first in range(0, h_t.shape[0], ROWS):
        rows = slice(first, first + ROWS)
        for block in range(FF_BLOCK // WIDE):
            lanes = slice(block * WIDE, (block + 1) * WIDE)
            weight_ref[block, rows] = dot_nn(grad_t[rows], act_ref[0, :, lanes])
            up_grad = dot_nn(h_t[rows], units[:, lanes])
            side = 0 if first < folded else half
            place = slice(first % folded, first % folded + ROWS)
            near_ref[block, place, side : side + half] = up_grad[:, :half]
            far_ref[block, place, side : side + half] = up_grad[:, half:]


def mlp_backward(layer, grad, h, act, slope, down_weight, up):
    length, width = h.shape
    hidden = up.shape[1]
    blocks = hidden // FF_BLOCK
    per = FF_BLOCK // WIDE
    halves = jax.ShapeDtypeStruct((hidden // WIDE, width // 2, WIDE), F32)
    return pl.pallas_call(
        mlp_backward_kernel,
        grid=(blocks,),
        in_specs=[
            whole((length, width)),
            whole((length, width)),
            plane_block(length, FF_BLOCK),
            plane_block(length, FF_BLOCK),
            pl.BlockSpec((1, 1, FF_BLOCK, width), lambda j: (0, layer, j, 0)),
            pl.BlockSpec((1, FF_BLOCK, width), lambda j: (layer, j, 0)),
        ],
        out_specs=[
            whole((length, width)),
            pl.BlockSpec((per, width, WIDE), lambda j: (j, 0, 0)),
            pl.BlockSpec((per, width // 2, WIDE), lambda j: (j, 0, 0)),
            pl.BlockSpec((per, width // 2, WIDE), lambda j: (j, 0, 0)),
            pl.BlockSpec((1, 1, FF_BLOCK), lambda j: (j, 0, 0)),
        ],
        out_shape=[
            jax.ShapeDtypeStruct((length, width), F32),
            jax.ShapeDtypeStruct((hidden // WIDE, width, WIDE), F32),
            halves,
            halves,
            jax.ShapeDtypeStruct((blocks, 1, FF_BLOCK), F32),
        ],
        scratch_shapes=[pltpu.VMEM((width, length), BF16), pltpu.VMEM((width, length), BF16)],
        compiler_params=params(),
        name="mlp_backward",
    )(grad, h, act, slope, down_weight, up)


def head_sums(values, ones):
    upper, lower = split(values)
    return dot_nn(upper, ones) + dot_nn(lower, ones)


def same_head_ones():
    same = row_index(WIDE, WIDE) // DH == lane_index(WIDE, WIDE) // DH
    return jnp.where(same, 1.0, 0.0).astype(BF16)


def write_mask(starts_ref, mask_ref, flipped):
    length = mask_ref.shape[0]
    keys = lane_index(1, length)
    documents = sum((starts_ref[0, i] <= keys).astype(jnp.int32) for i in range(starts_ref.shape[1]))
    for first in range(0, length, ROWS):
        own = row_index(ROWS, 1) + first
        document = sum(
            (starts_ref[0, i] <= own).astype(jnp.int32) for i in range(starts_ref.shape[1])
        )
        order = (own <= keys) if flipped else (keys <= own)
        seen = (document == documents) & order
        mask_ref[first : first + ROWS] = jnp.where(seen, 1.0, 0.0).astype(BF16)


def wide_rotary(cosine_ref, sine_ref, rows):
    return tuple(
        jnp.concatenate([ref[rows]] * (WIDE // PAIR), axis=1) for ref in (cosine_ref, sine_ref)
    )


def attention_forward_kernel(count, *refs):
    stream, refs = refs[:count], refs[count:]
    starts_ref, gain_ref, offset_ref, weight_ref, bias_ref, out_bias_ref = refs[:6]
    upper_ref, lower_ref, scale_ref, cosine_ref, sine_ref = refs[6:11]
    refs = refs[11:]
    x_ref = None
    if count > 1:
        x_ref, refs = refs[0], refs[1:]
    part_ref, h_ref, state_ref, mixed_ref, mask_ref = refs
    length = h_ref.shape[0]

    @pl.when(pl.program_id(0) == 0)
    def _():
        start_layer(stream, x_ref, h_ref, gain_ref, offset_ref)
        write_mask(starts_ref, mask_ref, False)
        part_ref[...] = jnp.broadcast_to(out_bias_ref[...], part_ref.shape)

    ones = same_head_ones()
    table_up, table_low = upper_ref[0, 0], lower_ref[0, 0]

    def features(values, rows):
        upper, lower = split(turn(values, *wide_rotary(cosine_ref, sine_ref, rows)))
        return dot_nn(upper, table_up) + (dot_nn(lower, table_up) + dot_nn(upper, table_low))

    for first in range(0, length, ROWS):
        rows = slice(first, first + ROWS)
        queries, keys, values = [
            dot_nt(h_ref[rows], weight_ref[0, 0, kind, 0]) + bias_ref[kind, 0] for kind in range(3)
        ]
        state_ref[0, rows] = jnp.exp(features(queries, rows)).astype(BF16)
        logs = features(keys, rows) - (0.5 / math.sqrt(DH)) * head_sums(keys * keys, ones)
        state_ref[1, rows] = (scale_ref[0, 0] * jnp.exp(logs)).astype(BF16)
        state_ref[2, rows] = keys.astype(BF16)
        state_ref[3, rows] = values.astype(BF16)

    zero = jnp.zeros((), BF16)
    one = jnp.ones((), BF16)
    for first in range(0, length, ROWS):
        rows = slice(first, first + ROWS)
        finish = first + ROWS
        left = lane_index(finish, PAIR) < DH
        seen = mask_ref[rows, :finish] > zero
        for pair in range(WIDE // PAIR):
            lanes = slice(pair * PAIR, (pair + 1) * PAIR)
            sums = []
            for own in (left, ~left):
                keys = jnp.where(own, state_ref[1, :finish, lanes], zero)
                scores = dot_nt(state_ref[0, rows, lanes], keys).astype(BF16)
                scores = jnp.where(seen, scores, zero)
                sums.append(dot_nn(scores, jnp.where(own, state_ref[3, :finish, lanes], one)))
            mine = lane_index(ROWS, PAIR) < DH
            numer = jnp.where(mine, sums[0], sums[1])
            denom = jnp.where(mine, pltpu.roll(sums[0], DH, 1), pltpu.roll(sums[1], DH, 1))
            inverse = 1.0 / denom
            mixed_ref[0, rows, lanes] = (numer * inverse).astype(BF16)
            mixed_ref[1, rows, lanes], mixed_ref[2, rows, lanes] = split(inverse)
        part_ref[rows] += dot_nn(mixed_ref[0, rows], weight_ref[0, 0, 3, 0])


def kinds_of(weight):
    return weight.reshape(weight.shape[:2] + (4, QUADS, WIDE, weight.shape[3]))


def attention_forward(layer, stream, starts, gain, offset, weight, biases, tables, rotary):
    length, width = stream[0].shape
    full = jax.ShapeDtypeStruct((length, width), F32)
    state = jax.ShapeDtypeStruct((4, length, width), BF16)
    out_shape = [full, jax.ShapeDtypeStruct((length, width), BF16), state, state]
    four = pl.BlockSpec((4, length, WIDE), lambda g: (0, 0, g))
    out_specs = [whole((length, width)), whole((length, width)), four, four]
    if len(stream) > 1:
        out_shape, out_specs = [full] + out_shape, [whole((length, width))] + out_specs
    return pl.pallas_call(
        functools.partial(attention_forward_kernel, len(stream)),
        grid=(QUADS,),
        in_specs=[whole((length, width))] * len(stream)
        + [
            pl.BlockSpec(memory_space=pltpu.SMEM),
            whole((1, width)),
            whole((1, width)),
            pl.BlockSpec((1, 1, 4, 1, WIDE, width), lambda g: (0, layer, 0, g, 0, 0)),
            pl.BlockSpec((4, 1, 1, WIDE), lambda g: (0, g, 0, 0)),
            whole((1, width)),
            pl.BlockSpec((1, 1, WIDE, WIDE), lambda g: (layer, g, 0, 0)),
            pl.BlockSpec((1, 1, WIDE, WIDE), lambda g: (layer, g, 0, 0)),
            pl.BlockSpec((1, 1, 1, WIDE), lambda g: (layer, g, 0, 0)),
            whole((length, PAIR)),
            whole((length, PAIR)),
        ],
        out_specs=out_specs,
        out_shape=out_shape,
        scratch_shapes=[pltpu.VMEM((length, length), BF16)],
        compiler_params=params(),
        name="attention_forward",
    )(
        *stream, starts, gain, offset, kinds_of(weight),
        biases.reshape(4, QUADS, 1, WIDE), biases[None, 3 * width :], *tables, *rotary,
    )


def attention_backward_kernel(
    starts_ref, grad_ref, h_ref, state_ref, mixed_ref, table_ref, cosine_ref, sine_ref, weight_ref,
    part_ref, out_ref, bias_ref, near_ref, far_ref,
    mask_ref, grad_t, h_t, numer_ref, feat_ref, flow, query_t,
):
    del near_ref, far_ref
    length = h_ref.shape[0]

    @pl.when(pl.program_id(0) == 0)
    def _():
        write_mask(starts_ref, mask_ref, True)
        grad_t[...] = grad_ref[...].T
        h_t[...] = h_ref[...].T
        part_ref[...] = jnp.zeros_like(part_ref)

    row, lane = row_index(WIDE, WIDE), lane_index(WIDE, WIDE)
    partner = (row // PAIR == lane // PAIR) & (row // DH != lane // DH)
    partner = jnp.where(partner, 1.0, 0.0).astype(BF16)
    zero = jnp.zeros((), BF16)
    one = jnp.ones((), BF16)
    for first in range(0, length, ROWS):
        rows = slice(first, first + ROWS)
        grad = dot_nt(grad_ref[rows], weight_ref[0, 0, 3, 0]).astype(BF16).astype(F32)
        inverse = mixed_ref[1, rows].astype(F32) + mixed_ref[2, rows].astype(F32)
        scaled = grad * inverse
        upper, lower = split(-head_sums(scaled * mixed_ref[0, rows].astype(F32), partner))
        numer = scaled.astype(BF16)
        lane = lane_index(ROWS, WIDE)
        spare = jnp.where(lane % DH == 0, upper, jnp.where(lane % DH == 1, lower, zero))
        left = lane % PAIR < DH
        numer_ref[0, rows] = jnp.where(left, numer, spare)
        numer_ref[1, rows] = jnp.where(left, spare, numer)

    for pair in range(WIDE // PAIR):
        lanes = slice(pair * PAIR, (pair + 1) * PAIR)
        query_t[...] = jnp.zeros_like(query_t)
        for first in range(0, length, ROWS):
            rows = slice(first, first + ROWS)
            seen = mask_ref[rows, first:] > zero
            lane = lane_index(ROWS, PAIR)
            left = lane < DH
            spare = jnp.where(lane % DH < 2, one, zero)
            keys, values = state_ref[1, rows, lanes], state_ref[3, rows, lanes]
            queries = state_ref[0, first:, lanes]
            numer = jnp.where(
                lane_index(length - first, PAIR) < DH,
                numer_ref[0, first:, lanes],
                numer_ref[1, first:, lanes],
            )
            grads = []
            for head, own in enumerate((left, ~left)):
                own_keys = jnp.where(own, keys, zero)
                scores = dot_nt(own_keys, queries).astype(BF16)
                scores = jnp.where(seen, scores, zero)
                grad_value = dot_nn(scores, numer)
                grad_scores = dot_nt(
                    jnp.where(own, values, spare), numer_ref[head, first:, lanes]
                ).astype(BF16)
                grad_scores = jnp.where(seen, grad_scores, zero)
                grad_key = dot_nn(grad_scores, queries)
                query_t[head, :, first:] += dot_nn(
                    own_keys.T[head * DH : (head + 1) * DH], grad_scores
                )
                grads.append((grad_value, grad_key))
            flow[2, rows, lanes] = jnp.where(left, grads[0][0], grads[1][0]).astype(BF16)
            grad_key = jnp.where(left, grads[0][1], grads[1][1])
            feat_ref[1, rows, lanes] = (grad_key * keys.astype(F32)).astype(BF16)
        for first in range(0, length, ROWS):
            rows = slice(first, first + ROWS)
            grad_query = jnp.concatenate([query_t[0, :, rows], query_t[1, :, rows]], axis=0).T
            feat_ref[0, rows, lanes] = (
                grad_query * state_ref[0, rows, lanes].astype(F32)
            ).astype(BF16)

    ones = same_head_ones()
    table = table_ref[0, 0]
    sums = [jnp.zeros((1, WIDE), F32)] * 3
    for first in range(0, length, ROWS):
        rows = slice(first, first + ROWS)
        cosine, sine = wide_rotary(cosine_ref, sine_ref, rows)
        flow[0, rows] = turn_back(dot_nt(feat_ref[0, rows], table), cosine, sine).astype(BF16)
        shrink = dot_nn(feat_ref[1, rows], ones) * (1.0 / math.sqrt(DH))
        turned = turn_back(dot_nt(feat_ref[1, rows], table), cosine, sine)
        flow[1, rows] = (turned - state_ref[2, rows].astype(F32) * shrink).astype(BF16)
        total = part_ref[rows]
        for kind in range(3):
            block = flow[kind, rows]
            sums[kind] = sums[kind] + jnp.sum(block.astype(F32), axis=0, keepdims=True)
            total = total + dot_nn(block, weight_ref[0, 0, kind, 0])
        part_ref[rows] = total
    for kind in range(3):
        bias_ref[kind, 0] = sums[kind]
    bias_ref[3, 0] = jnp.zeros((1, WIDE), F32)
    for first in range(0, h_t.shape[0], ROWS):
        rows = slice(first, first + ROWS)
        for kind in range(3):
            out_ref[kind, 0, rows] = dot_nn(h_t[rows], flow[kind])
        out_ref[3, 0, rows] = dot_nn(grad_t[rows], mixed_ref[0])


def attention_backward(layer, starts, grad, h, state, mixed, tables, rotary, weight):
    _, length, width = state.shape
    blocks = 4 * QUADS
    four = pl.BlockSpec((4, length, WIDE), lambda g: (0, 0, g))
    halves = jax.ShapeDtypeStruct((blocks, width // 2, WIDE), F32)
    part, out, bias, near, far = pl.pallas_call(
        attention_backward_kernel,
        grid=(QUADS,),
        in_specs=[
            pl.BlockSpec(memory_space=pltpu.SMEM),
            whole((length, width)),
            whole((length, width)),
            four,
            four,
            pl.BlockSpec((1, 1, WIDE, WIDE), lambda g: (layer, g, 0, 0)),
            whole((length, PAIR)),
            whole((length, PAIR)),
            pl.BlockSpec((1, 1, 4, 1, WIDE, width), lambda g: (0, layer, 0, g, 0, 0)),
        ],
        out_specs=[
            whole((length, width)),
            pl.BlockSpec((4, 1, width, WIDE), lambda g: (0, g, 0, 0)),
            pl.BlockSpec((4, 1, 1, WIDE), lambda g: (0, g, 0, 0)),
            pl.BlockSpec(memory_space=pl.ANY),
            pl.BlockSpec(memory_space=pl.ANY),
        ],
        out_shape=[
            jax.ShapeDtypeStruct((length, width), F32),
            jax.ShapeDtypeStruct((4, QUADS, width, WIDE), F32),
            jax.ShapeDtypeStruct((4, QUADS, 1, WIDE), F32),
            halves,
            halves,
        ],
        scratch_shapes=[
            pltpu.VMEM((length, length), BF16),
            pltpu.VMEM((width, length), BF16),
            pltpu.VMEM((width, length), BF16),
            pltpu.VMEM((2, length, WIDE), BF16),
            pltpu.VMEM((2, length, WIDE), BF16),
            pltpu.VMEM((3, length, WIDE), BF16),
            pltpu.VMEM((2, DH, length), F32),
        ],
        compiler_params=params(),
        name="attention_backward",
    )(starts, grad, h, state, mixed, tables[0], *rotary, kinds_of(weight))
    return part, out.reshape(blocks, width, WIDE), near, far, bias.reshape(blocks, WIDE)


def norm_backward_kernel(x_ref, own_ref, other_ref, grad_ref, gain_ref, out_ref, sums_ref):
    @pl.when(pl.program_id(0) == 0)
    def _():
        sums_ref[...] = jnp.zeros_like(sums_ref)

    values = x_ref[...].astype(F32)
    average = jnp.mean(values, -1, keepdims=True)
    centered = values - average
    variance = jnp.mean(centered * centered, -1, keepdims=True)
    inverse = lax.rsqrt(variance + EPSILON)
    unit = centered * inverse
    incoming = own_ref[...] + other_ref[...]
    grad_unit = incoming * gain_ref[...].astype(F32)
    first = jnp.mean(grad_unit, -1, keepdims=True)
    second = jnp.mean(grad_unit * unit, -1, keepdims=True)
    grad = grad_ref[...].astype(F32)
    out = grad + inverse * (grad_unit - first - unit * second)
    out_ref[...] = out.astype(out_ref.dtype)
    sums_ref[0:1] += jnp.sum(incoming * unit, axis=0, keepdims=True)
    sums_ref[1:2] += jnp.sum(incoming, axis=0, keepdims=True)
    sums_ref[2:3] += jnp.sum(grad, axis=0, keepdims=True)


def norm_backward(x, own, other, grad, gain, kind):
    length, width = own.shape
    block = pl.BlockSpec((ROWS, width), lambda i: (i, 0))
    return pl.pallas_call(
        norm_backward_kernel,
        grid=(length // ROWS,),
        in_specs=[block, block, block, block, whole((1, width))],
        out_specs=[block, whole((8, width))],
        out_shape=[
            jax.ShapeDtypeStruct((length, width), kind),
            jax.ShapeDtypeStruct((8, width), F32),
        ],
        compiler_params=params(),
        name="norm_backward",
    )(x, own, other, grad, gain)


MESH = pl.DeviceIdType.MESH
UNIT = 8
SLOTS = 4
LAG = 1


class Flow(NamedTuple):
    order: tuple
    layer: int
    begun: int
    start: int
    segments: tuple


def first_rows(rows):
    cuts = (0, rows * 11 // 32, rows * 22 // 32, rows)
    return tuple(zip(cuts[:-1], cuts[1:]))


def begun_flows(rows, layer):
    orders = (((0, 1, 2, 3),) * 2, ((1, 0, 2, 3),) * 2, ((2, 0, 1, 3), (2, 1, 0, 3)))
    flows = []
    for way in range(3):
        for part in range(2):
            segments = []
            for is_up in range(2):
                first, finish = first_rows(rows[is_up])[way]
                half = (finish - first) // 2
                base = first_rows(rows[0])[way]
                base = base[1] - base[0] if is_up else 0
                segments.append(
                    (bool(is_up), first + part * half, half // UNIT, base + part * half)
                )
            flows.append(Flow(orders[way][part], layer, way, 0, tuple(segments)))
    return flows


def fresh_flows(rows, layer, start):
    orders = ((0, 1, 2, 3), (1, 0, 2, 3)) + ((0, 2, 3, 1), (1, 2, 3, 0)) * 2
    count = len(orders)
    flows, at = [], [0, 0]
    for index, order in enumerate(orders):
        segments = []
        for is_up in range(2):
            units = rows[is_up] // UNIT
            place = index if is_up == 0 else count - 1 - index
            share = units // count + (place < units % count)
            segments.append((bool(is_up), at[is_up] * UNIT, share, 0))
            at[is_up] += share
        flows.append(Flow(order, layer, -1, start, tuple(segments)))
    return flows


def units_of(flow):
    return sum(segment[2] for segment in flow.segments)


def bit_of(index, bit):
    return (index // (1 << bit)) % 2


def flip(index, bit):
    return index + (1 << bit) * (1 - 2 * bit_of(index, bit))


def scatter_kernel(bits, flows, layers, *refs):
    sources, refs = refs[: 3 * layers], refs[3 * layers :]
    halves, refs = refs[:3], refs[3:]
    small_ref, weight_out, up_out, small_out = refs[:4]
    stages = bits
    weight_sum, up_sum = refs[4:6]
    small_held = refs[6 : 6 + stages]
    held = refs[6 + stages :]
    held, sems = held[: len(flows) * (stages + 1)], held[len(flows) * (stages + 1) :]
    load_sem, send_sem, recv_sem, credit, small_send, small_recv = sems
    held = [held[f * (stages + 1) : (f + 1) * (stages + 1)] for f in range(len(flows))]
    me, core = lax.axis_index("batch"), lax.axis_index("stream")
    totals = [units_of(flow) for flow in flows]

    barrier = pltpu.get_barrier_semaphore()
    for bit in range(bits):
        pl.semaphore_signal(
            barrier, inc=1, device_id={"batch": flip(me, bit)}, device_id_type=MESH
        )
    pl.semaphore_wait(barrier, bits)

    def view(order, stage, mine):
        left = sorted(set(range(bits)) - set(order[:stage]), reverse=True)
        pick = bit_of(me, order[stage])
        pick = pick if mine else 1 - pick
        return tuple(pick if bit == order[stage] else slice(None) for bit in left)

    def remote(flow, stage, slot, source):
        return pltpu.make_async_remote_copy(
            src_ref=source,
            dst_ref=held[flow][stage + 1].at[slot],
            send_sem=send_sem.at[flow, stage, slot],
            recv_sem=recv_sem.at[flow, stage, slot],
            device_id={"batch": flip(me, flows[flow].order[stage])},
            device_id_type=MESH,
        )

    def sent_from(flow, stage, slot):
        if stage == 0:
            return held[flow][0].at[slot]
        return held[flow][stage].at[(slot,) + view(flows[flow].order, stage, False)]

    def load(flow, slot, source):
        return pltpu.make_async_copy(source, held[flow][0].at[slot], load_sem.at[flow, slot])

    def load_half(flow, slot, source):
        return pltpu.make_async_copy(
            source, held[flow][1].at[slot], recv_sem.at[flow, 0, slot]
        )

    def return_credit(flow, stage, unit):
        if stage == 0 and flows[flow].begun >= 0:
            return

        @pl.when(unit + SLOTS < totals[flow])
        def _():
            pl.semaphore_signal(
                credit.at[flow, stage],
                inc=1,
                device_id={"batch": flip(me, flows[flow].order[stage])},
                device_id_type=MESH,
            )

    def take_credit(flow, stage, unit):
        @pl.when(unit >= SLOTS)
        def _():
            pl.semaphore_wait(credit.at[flow, stage], 1)

    def places(flow, unit, act):
        base = 0
        for is_up, row, units, half_row in flows[flow].segments:
            offset = (unit - base) * UNIT
            pl.when((unit >= base) & (unit < base + units))(
                functools.partial(act, is_up, row + offset, half_row + offset)
            )
            base += units

    def begin(flow, unit):
        slot = lax.rem(unit, SLOTS)
        order, layer, begun = flows[flow][:3]
        if begun < 0:
            take_credit(flow, 0, unit)

        def start(source, row):
            at = (pl.ds(pl.multiple_of(row, UNIT), UNIT),)
            load(flow, slot, source.at[view(order, 0, True) + at]).start()
            if begun < 0:
                remote(flow, 0, slot, source.at[view(order, 0, False) + at]).start()

        def act(is_up, row, half_row):
            if begun >= 0:
                at = (slice(None),) * (bits - 1)
                at += (pl.ds(pl.multiple_of(half_row, UNIT), UNIT),)
                load_half(flow, slot, halves[begun].at[at]).start()
            if not is_up:
                start(sources[3 * layer], row)
            else:
                for side in range(2):
                    pl.when(core == side)(
                        functools.partial(start, sources[3 * layer + 1 + side], row)
                    )

        places(flow, unit, act)

    def advance(flow, stage, unit):
        slot = lax.rem(unit, SLOTS)
        order, layer, begun = flows[flow][:3]
        buffer = held[flow][stage]
        copy = remote(flow, stage - 1, slot, sent_from(flow, stage - 1, slot))
        if stage == 1 and begun >= 0:
            load_half(flow, slot, held[flow][0].at[slot]).wait()
        else:
            copy.wait_recv()
        if stage == 1:
            load(flow, slot, held[flow][1].at[slot]).wait()
            mine = held[flow][0][slot]
        else:
            mine = held[flow][stage - 1][(slot,) + view(order, stage - 1, True)]
        value = buffer[slot] + mine
        if stage < stages:
            buffer[slot] = value
            take_credit(flow, stage, unit)
            remote(flow, stage, slot, sent_from(flow, stage, slot)).start()
        else:

            def act(is_up, row, half_row):
                target = up_sum if is_up else weight_sum
                target[layer, pl.ds(pl.multiple_of(row, UNIT), UNIT)] = value

            places(flow, unit, act)
        if stage > 1 or begun < 0:
            copy.wait_send()
        if stage >= 2:
            return_credit(flow, stage - 2, unit)
        if stage == stages:
            return_credit(flow, stage - 1, unit)

    small_order = tuple(range(bits))

    def small_copy(stage):
        source = small_ref if stage == 0 else small_held[stage - 1]
        return pltpu.make_async_remote_copy(
            src_ref=source.at[view(small_order, stage, False)],
            dst_ref=small_held[stage],
            send_sem=small_send.at[stage],
            recv_sem=small_recv.at[stage],
            device_id={"batch": flip(me, small_order[stage])},
            device_id_type=MESH,
        )

    def small_step(stage):
        if stage > 0:
            small_copy(stage - 1).wait()
            source = small_ref if stage == 1 else small_held[stage - 2]
            sums = small_held[stage - 1][...] + source[view(small_order, stage - 1, True)]
            if stage == stages:
                small_out[...] = sums
            else:
                small_held[stage - 1][...] = sums
        if stage < stages:
            small_copy(stage).start()

    def step(index, carry):
        for place, flow in enumerate(flows):
            unit = index - flow.start
            pl.when((unit >= 0) & (unit < totals[place]))(
                functools.partial(begin, place, unit)
            )
        for place, flow in enumerate(flows):
            for stage in range(1, stages + 1):
                unit = index - flow.start - LAG * stage
                pl.when((unit >= 0) & (unit < totals[place]))(
                    functools.partial(advance, place, stage, unit)
                )
        for stage in range(stages + 1):
            pl.when(index == stages + 2 * stage)(functools.partial(small_step, stage))
        return carry

    last = max(flow.start + total for flow, total in zip(flows, totals))
    lax.fori_loop(0, last + LAG * stages, step, 0)
    half = WIDE // 2
    for layer in range(layers):
        weight_out[layers - 1 - layer] = weight_sum[layer].T
        folded = up_sum.shape[1]
        up_out[layers - 1 - layer, :, :folded] = up_sum[layer, :, :half].T
        up_out[layers - 1 - layer, :, folded:] = up_sum[layer, :, half:].T


def pack_halves(weight, near, far):
    count, width, lanes = weight.shape
    bits = count.bit_length() - 1
    rows = (width, near.shape[1])
    ranges = [first_rows(length) for length in rows]

    def kernel(weight_ref, near_ref, far_ref, *refs):
        outs, held, loads, stores = refs[:3], refs[3:6], refs[6], refs[7]
        me, core = lax.axis_index("batch"), lax.axis_index("stream")

        def load(source, is_up, bit, part):
            first, finish = ranges[is_up][bit]
            base = ranges[0][bit][1] - ranges[0][bit][0] if is_up else 0
            others = [dim for dim in range(bits) if dim != bits - 1 - bit]
            at = [slice(None)] * bits + [pl.ds(first, finish - first)]
            at[bits - 1 - bit] = 1 - bit_of(me, bit)
            at[others[0]] = part
            to = (part,) + (slice(None),) * (bits - 2) + (pl.ds(base, finish - first),)
            return pltpu.make_async_copy(
                source.at[tuple(at)], held[bit].at[to], loads.at[is_up, bit, part]
            )

        def start(source, is_up):
            for part in range(2):
                for bit in range(3):
                    load(source, is_up, bit, part).start()

        start(weight_ref, 0)
        for side, source in enumerate((near_ref, far_ref)):
            pl.when(core == side)(functools.partial(start, source, 1))
        copies = []
        for part in range(2):
            for bit in range(3):
                load(weight_ref, 0, bit, part).wait()
                load(near_ref, 1, bit, part).wait()
                copy = pltpu.make_async_copy(
                    held[bit].at[part], outs[bit].at[part], stores.at[bit, part]
                )
                copy.start()
                copies.append(copy)
        for copy in copies:
            copy.wait()

    shapes = [
        (2,) * (bits - 1) + (sum(r[bit][1] - r[bit][0] for r in ranges), lanes) for bit in range(3)
    ]
    return pl.pallas_call(
        kernel,
        in_specs=[pl.BlockSpec(memory_space=pltpu.HBM)] * 3,
        out_specs=[pl.BlockSpec(memory_space=pltpu.HBM)] * 3,
        out_shape=[jax.ShapeDtypeStruct(shape, F32) for shape in shapes],
        scratch_shapes=[pltpu.VMEM(shape, F32) for shape in shapes]
        + [pltpu.SemaphoreType.DMA((2, 3, 2)), pltpu.SemaphoreType.DMA((3, 2))],
        compiler_params=params(),
        name="pack_halves",
    )(*[array.reshape((2,) * bits + array.shape[1:]) for array in (weight, near, far)])


def send_halves(weight, near, far):
    count = weight.shape[0]
    received = []
    for bit, part in enumerate(pack_halves(weight, near, far)):
        pairs = [(source, flip(source, bit)) for source in range(count)]
        received.append(lax.ppermute(part, "batch", pairs))
    return received


def after(first, others):
    def kernel(*refs):
        del refs

    return pl.pallas_call(
        kernel,
        in_specs=[pl.BlockSpec(memory_space=pltpu.HBM)] * (1 + len(others)),
        out_specs=pl.BlockSpec(memory_space=pltpu.HBM),
        out_shape=jax.ShapeDtypeStruct(first.shape, first.dtype),
        input_output_aliases={0: 0},
        name="after",
    )(first, *others)


def reduce_scatter(grads, halves, small):
    layers = len(grads) // 3
    count, width = grads[0].shape[:2]
    folded = grads[1].shape[1]
    bits = count.bit_length() - 1
    small = jnp.pad(small, ((0, 0), (0, -small.shape[1] % 1024)))
    small = small.reshape((2,) * bits + (-1, 128))
    flows = begun_flows((width, folded), 0)
    for layer in range(1, layers):
        start = max(flow.start + units_of(flow) for flow in flows)
        flows = flows + fresh_flows((width, folded), layer, start)
    scratch = [pltpu.VMEM((layers, width, WIDE), F32), pltpu.VMEM((layers, folded, WIDE), F32)]
    scratch += [
        pltpu.VMEM((2,) * (bits - 1 - stage) + small.shape[-2:], F32) for stage in range(bits)
    ]
    for _ in flows:
        for stage in range(bits + 1):
            lead = (SLOTS,) + (2,) * (bits - 1 - max(stage - 1, 0))
            scratch.append(pltpu.VMEM(lead + (UNIT, WIDE), F32))
    scratch += [
        pltpu.SemaphoreType.DMA((len(flows), SLOTS)),
        pltpu.SemaphoreType.DMA((len(flows), bits, SLOTS)),
        pltpu.SemaphoreType.DMA((len(flows), bits, SLOTS)),
        pltpu.SemaphoreType.REGULAR((len(flows), bits)),
        pltpu.SemaphoreType.DMA((bits,)),
        pltpu.SemaphoreType.DMA((bits,)),
    ]
    weight, up, small = pl.pallas_call(
        functools.partial(scatter_kernel, bits, flows, layers),
        in_specs=[pl.BlockSpec(memory_space=pltpu.HBM)] * (len(grads) + len(halves))
        + [pl.BlockSpec(memory_space=pltpu.VMEM)],
        out_specs=[pl.BlockSpec(memory_space=pltpu.VMEM)] * 3,
        out_shape=[
            jax.ShapeDtypeStruct((layers, WIDE, width), F32),
            jax.ShapeDtypeStruct((layers, WIDE // 2, width), F32),
            jax.ShapeDtypeStruct(small.shape[-2:], F32),
        ],
        scratch_shapes=scratch,
        compiler_params=pltpu.CompilerParams(
            collective_id=0, has_side_effects=True, vmem_limit_bytes=VMEM_LIMIT
        ),
        name="reduce_scatter",
    )(*[array.reshape((2,) * bits + array.shape[1:]) for array in grads], *halves, small)
    return weight, up, small.reshape(-1)


def shards(
    tokens, cotangent, branch_weight, branch_bias, up_weight, down_bias,
    norm_gain, norm_bias, freq_seeds, doc_starts,
):
    is_attention = lax.axis_index("stream") == 0
    length, width = tokens.shape
    rotary = tuple(jnp.asarray(table) for table in rotary_rows(length))
    biases = branch_bias[0].astype(F32)
    tables = lax.cond(
        is_attention,
        lambda: tuple(feature_tables(freq_seeds)),
        lambda: (
            jnp.zeros((LAYERS, QUADS, WIDE, WIDE), BF16),
            jnp.zeros((LAYERS, QUADS, WIDE, WIDE), BF16),
            jnp.zeros((LAYERS, QUADS, 1, WIDE), F32),
        ),
    )
    swap = [(0, 1), (1, 0)]

    def attention(layer, stream):
        gain, offset = norm_gain[layer : layer + 1], norm_bias[layer : layer + 1]
        return tuple(
            attention_forward(
                layer, stream, doc_starts, gain, offset, branch_weight, biases[layer], tables,
                rotary,
            )
        )

    def feed_forward(layer, stream):
        gain, offset = norm_gain[layer : layer + 1], norm_bias[layer : layer + 1]
        return tuple(
            mlp_forward(
                layer, stream, gain, offset, up_weight, biases[layer], branch_weight,
                down_bias[layer : layer + 1],
            )
        )

    stream = (tokens,)
    inputs, kept = [], []
    for layer in range(LAYERS):
        *x, part, h, state, mixed = lax.cond(
            is_attention,
            functools.partial(attention, layer, stream),
            functools.partial(feed_forward, layer, stream),
        )
        inputs.append(x[0] if x else tokens)
        kept.append((h, state, mixed))
        stream = (inputs[-1], part, lax.ppermute(part, "stream", swap))
    result = stream[0] + (stream[1] + stream[2])

    def attention_back(layer, grad):
        h, state, mixed = kept[layer]
        return attention_backward(
            layer, doc_starts, grad, h, state, mixed, tables, rotary, branch_weight
        )

    def feed_forward_back(layer, grad):
        h, act, slope = kept[layer]
        part, weight, near, far, bias = mlp_backward(
            layer, grad, h, act, slope, branch_weight, up_weight
        )
        return part, weight, near, far, bias.reshape(-1, WIDE)

    grad = cotangent
    count = lax.axis_size("batch")
    blocked = count == branch_weight.shape[2] // WIDE
    grads, vectors = [], []
    for layer in reversed(range(LAYERS)):
        part, weight, near, far, bias = lax.cond(
            is_attention,
            functools.partial(attention_back, layer, grad),
            functools.partial(feed_forward_back, layer, grad),
        )
        if blocked and layer < LAYERS - 1:
            part = after(part, halves)
        other = lax.ppermute(part, "stream", swap)
        if blocked:
            near = lax.ppermute(near, "stream", [(1, 0)])
            if layer == LAYERS - 1:
                halves = send_halves(weight, near, far)
        kind = BF16 if layer else F32
        new_grad, sums = norm_backward(
            inputs[layer], part, other, grad, norm_gain[layer : layer + 1], kind
        )
        bias = jnp.where(
            is_attention & (jnp.arange(bias.shape[0])[:, None] >= 3 * QUADS),
            jnp.tile(sums[2].reshape(QUADS, WIDE), (bias.shape[0] // QUADS, 1)),
            bias,
        )
        vectors = [bias.reshape(count, -1), sums[:3].reshape(3, count, -1)] + vectors
        grads += [weight, near, far]
        grad = new_grad
    small = jnp.concatenate(
        [part.reshape(count, -1) for part in vectors[0::2]]
        + [jnp.moveaxis(part, 0, 1).reshape(count, -1) for part in vectors[1::2]],
        axis=1,
    )
    if blocked:
        weight, up, small = reduce_scatter(grads, halves, small)
    else:
        weight, up, small = scatter_rows(grads, small)
    each = branch_weight.shape[2] // count
    bias, sums = small[: LAYERS * each], small[LAYERS * each :]
    sums = sums[: LAYERS * 3 * (width // count)].reshape(LAYERS, 3, -1)
    return (
        result,
        grad,
        weight[None],
        bias.reshape(1, LAYERS, -1),
        up,
        sums[:, 2],
        sums[:, 0],
        sums[:, 1],
    )


def scatter_rows(grads, small):
    scatter = functools.partial(
        lax.psum_scatter, axis_name="batch", scatter_dimension=0, tiled=True
    )
    weights, ups = [], []
    for weight, near, far in zip(grads[0::3], grads[1::3], grads[2::3]):
        half = near.shape[2] // 2
        whole_up = [
            jnp.concatenate([side[..., :half], side[..., half:]], axis=1) for side in (near, far)
        ]
        whole_up = rows_of(jnp.concatenate(whole_up, axis=2))
        whole_up = jnp.where(lax.axis_index("stream") == 1, whole_up, 0.0)
        weights.append(scatter(rows_of(weight)))
        ups.append(
            lax.psum_scatter(whole_up, ("batch", "stream"), scatter_dimension=0, tiled=True)
        )
    return jnp.stack(weights[::-1]), jnp.stack(ups[::-1]), scatter(small)[0]


def rows_of(blocks):
    return jnp.transpose(blocks, (0, 2, 1)).reshape(-1, blocks.shape[1])


def solution(mesh):
    placed = (
        P("batch", None),
        P("batch", None),
        P("stream", None, None, None),
        P("stream", None, None),
        P(),
        P(),
        P(),
        P(),
        P(),
        P("batch", None),
    )
    return jax.shard_map(
        shards,
        mesh=mesh,
        in_specs=placed,
        out_specs=(
            P("batch", None),
            P("batch", None),
            P("stream", None, "batch", None),
            P("stream", None, "batch"),
            P(None, ("batch", "stream"), None),
            P(None, "batch"),
            P(None, "batch"),
            P(None, "batch"),
        ),
        check_vma=False,
    )
```

```python
import functools
import math
from typing import NamedTuple

import jax
import jax.numpy as jnp
import numpy as np
from jax import lax
from jax.experimental import pallas as pl
from jax.experimental.pallas import tpu as pltpu
from jax.sharding import PartitionSpec as P

HEADS = 16
DH = 64
ROT = 16
FEAT = 64
LAYERS = 2
EPSILON = 1e-05
HIGH = lax.Precision.HIGHEST
F32 = jnp.float32
BF16 = jnp.bfloat16
WIDE = 256
PAIR = 128
QUADS = HEADS * DH // WIDE
PAIRS = HEADS * DH // PAIR
ROWS = 256
VMEM_LIMIT = 56 * 1024 * 1024


def params():
    return pltpu.CompilerParams(vmem_limit_bytes=VMEM_LIMIT)


def whole(shape):
    zeros = (0,) * len(shape)
    return pl.BlockSpec(shape, lambda *_: zeros, pipeline_mode=pl.Buffered(1))


def dot_nn(left, right):
    return lax.dot_general(left, right, (((1,), (0,)), ((), ())), preferred_element_type=F32)


def dot_nt(left, right):
    return lax.dot_general(left, right, (((1,), (1,)), ((), ())), preferred_element_type=F32)


def split(values):
    upper = values.astype(BF16)
    return upper, (values - upper.astype(F32)).astype(BF16)


def lane_index(rows, lanes):
    return lax.broadcasted_iota(jnp.int32, (rows, lanes), 1)


def row_index(rows, lanes):
    return lax.broadcasted_iota(jnp.int32, (rows, lanes), 0)


def cosine_block():
    samples = np.arange(DH, dtype=np.float64)
    angles = math.pi * (samples[None, :] + 0.5) * samples[:, None] / DH
    table = np.cos(angles) * math.sqrt(2.0 / DH)
    table[0] *= math.sqrt(0.5)
    return np.kron(np.eye(WIDE // DH), table.T * DH ** (-0.25)).astype(np.float32)


def rotary_rows(length):
    position = np.arange(length, dtype=np.float32)
    inverse = (10000.0 ** (-np.arange(0, ROT, 2, dtype=np.float32) / ROT)).astype(np.float32)
    angles = position[:, None] * inverse[None, :]
    cosine, sine = np.cos(angles), np.sin(angles)
    rest = DH - ROT
    cosine_head = np.concatenate([cosine, cosine, np.ones((length, rest))], 1)
    sine_head = np.concatenate([-sine, sine, np.zeros((length, rest))], 1)
    repeat = PAIR // DH
    return (
        np.tile(cosine_head, (1, repeat)).astype(np.float32),
        np.tile(sine_head, (1, repeat)).astype(np.float32),
    )


def tables_kernel(seeds_ref, cosine_ref, upper_ref, lower_ref, weight_ref):
    feature = lane_index(WIDE, WIDE)
    lattice = (feature % FEAT) * seeds_ref[0] % FEAT
    prob = (lattice.astype(F32) + 0.5) / FEAT
    radius = jnp.sqrt(-2.0 * jnp.log(jnp.minimum(prob, 1.0 - prob)))
    above = 2.515517 + 0.802853 * radius + 0.010328 * radius * radius
    below = (
        1.0 + 1.432788 * radius + 0.189269 * radius * radius + 0.001308 * radius * radius * radius
    )
    magnitude = radius - above / below
    same_head = row_index(WIDE, WIDE) // DH == feature // FEAT
    omega = jnp.where(same_head, jnp.where(prob > 0.5, magnitude, -magnitude), 0.0)
    project = jnp.dot(cosine_ref[...], omega, precision=HIGH, preferred_element_type=F32)
    upper_ref[0, 0], lower_ref[0, 0] = split(project)
    grown = jnp.exp(-0.5 / DH * jnp.sum(omega * omega, axis=0, keepdims=True))
    total = jnp.dot(
        jnp.broadcast_to(grown, (8, WIDE)),
        same_head.astype(F32),
        precision=HIGH,
        preferred_element_type=F32,
    )
    weight_ref[0, 0] = FEAT * grown / total[:1]


def feature_tables(seeds):
    return pl.pallas_call(
        tables_kernel,
        grid=(LAYERS, QUADS),
        in_specs=[
            pl.BlockSpec((1, WIDE, 1), lambda l, g: (l, g, 0)),
            whole((WIDE, WIDE)),
        ],
        out_specs=[
            pl.BlockSpec((1, 1, WIDE, WIDE), lambda l, g: (l, g, 0, 0)),
            pl.BlockSpec((1, 1, WIDE, WIDE), lambda l, g: (l, g, 0, 0)),
            pl.BlockSpec((1, 1, 1, WIDE), lambda l, g: (l, g, 0, 0)),
        ],
        out_shape=[
            jax.ShapeDtypeStruct((LAYERS, QUADS, WIDE, WIDE), BF16),
            jax.ShapeDtypeStruct((LAYERS, QUADS, WIDE, WIDE), BF16),
            jax.ShapeDtypeStruct((LAYERS, QUADS, 1, WIDE), F32),
        ],
        compiler_params=params(),
        name="feature_tables",
    )(seeds.reshape(LAYERS, HEADS * DH, 1), jnp.asarray(cosine_block()))


def turn(values, cosine, sine):
    lanes = values.shape[1]
    half = ROT // 2
    lane = lane_index(*values.shape) % DH
    swapped = jnp.where(
        lane < half, pltpu.roll(values, lanes - half, 1), pltpu.roll(values, half, 1)
    )
    return values * cosine + swapped * sine


def turn_back(values, cosine, sine):
    lanes = values.shape[1]
    half = ROT // 2
    lane = lane_index(*values.shape) % DH
    turned = values * sine
    swapped = jnp.where(
        lane < half, pltpu.roll(turned, lanes - half, 1), pltpu.roll(turned, half, 1)
    )
    return values * cosine + jnp.where(lane < ROT, swapped, 0.0)


def normalized(x_ref_rows, gain, offset):
    average = jnp.mean(x_ref_rows, -1, keepdims=True)
    centered = x_ref_rows - average
    variance = jnp.mean(centered * centered, -1, keepdims=True)
    return centered * lax.rsqrt(variance + EPSILON) * gain + offset


def start_layer(stream, x_ref, h_ref, gain_ref, offset_ref):
    length = h_ref.shape[0]
    step = min(128, length)

    @pl.loop(0, length // step)
    def _(index):
        rows = pl.ds(pl.multiple_of(index * step, step), step)
        values = stream[0][rows].astype(F32)
        if len(stream) > 1:
            values = values + (stream[1][rows] + stream[2][rows])
            x_ref[rows] = values
        h_ref[rows] = normalized(
            values, gain_ref[...].astype(F32), offset_ref[...].astype(F32)
        ).astype(BF16)


def gelu_parts(units):
    below = 0.5 + 0.5 * lax.erf(units * math.sqrt(0.5))
    return below, jnp.exp(-0.5 * units * units) * (1.0 / math.sqrt(2.0 * math.pi))


FF_BLOCK = 1024
FF_ROWS = 512


def mlp_forward_kernel(count, *refs):
    stream, refs = refs[:count], refs[count:]
    gain_ref, offset_ref, up_ref, bias_ref, down_ref, down_bias_ref = refs[:6]
    refs = refs[6:]
    x_ref = None
    if count > 1:
        x_ref, refs = refs[0], refs[1:]
    part_ref, h_ref, act_ref, slope_ref = refs
    step = pl.program_id(0)

    @pl.when(step == 0)
    def _():
        start_layer(stream, x_ref, h_ref, gain_ref, offset_ref)
        part_ref[...] = jnp.broadcast_to(down_bias_ref[...].astype(F32), part_ref.shape)

    for first in range(0, h_ref.shape[0], FF_ROWS):
        rows = slice(first, first + FF_ROWS)
        units = dot_nt(h_ref[rows], up_ref[0]) + bias_ref[0]
        below, density = gelu_parts(units)
        active = (units * below).astype(BF16)
        act_ref[0, rows] = active
        slope_ref[0, rows] = (below + units * density).astype(BF16)
        part_ref[rows] += dot_nn(active, down_ref[0, 0])


def plane_block(length, lanes):
    per_plane = 1024 // lanes
    return pl.BlockSpec((1, length, lanes), lambda j: (j // per_plane, 0, j % per_plane))


def mlp_forward(layer, stream, gain, offset, up, biases, down_weight, down_bias):
    length, width = stream[0].shape
    hidden = up.shape[1]
    blocks = hidden // FF_BLOCK
    state = jax.ShapeDtypeStruct((4, length, width), BF16)
    full = jax.ShapeDtypeStruct((length, width), F32)
    out_shape = [full, jax.ShapeDtypeStruct((length, width), BF16), state, state]
    out_specs = [whole((length, width)), whole((length, width))]
    out_specs += [plane_block(length, FF_BLOCK)] * 2
    if len(stream) > 1:
        out_shape, out_specs = [full] + out_shape, [whole((length, width))] + out_specs
    return pl.pallas_call(
        functools.partial(mlp_forward_kernel, len(stream)),
        grid=(blocks,),
        in_specs=[whole((length, width))] * len(stream)
        + [
            whole((1, width)),
            whole((1, width)),
            pl.BlockSpec((1, FF_BLOCK, width), lambda j: (layer, j, 0)),
            pl.BlockSpec((1, 1, FF_BLOCK), lambda j: (j, 0, 0)),
            pl.BlockSpec((1, 1, FF_BLOCK, width), lambda j: (0, layer, j, 0)),
            whole((1, width)),
        ],
        out_specs=out_specs,
        out_shape=out_shape,
        compiler_params=params(),
        name="mlp_forward",
    )(*stream, gain, offset, up, biases.reshape(blocks, 1, FF_BLOCK), down_weight, down_bias)


def mlp_backward_kernel(
    place_ref, grad_ref, h_ref, act_ref, slope_ref, down_ref, up_ref,
    part_ref, along_x, kept_x, along_y, kept_y, along_z, kept_z, bias_ref, grad_t, h_t, units,
):
    step = pl.program_id(0)

    @pl.when(step == 0)
    def _():
        grad_t[...] = grad_ref[...].T
        h_t[...] = h_ref[...].T
        part_ref[...] = jnp.zeros_like(part_ref)

    bias = jnp.zeros((1, FF_BLOCK), F32)
    for first in range(0, h_ref.shape[0], ROWS):
        rows = slice(first, first + ROWS)
        grad_act = dot_nt(grad_ref[rows], down_ref[0, 0])
        grad_unit = (grad_act * slope_ref[0, rows].astype(F32)).astype(BF16)
        bias += jnp.sum(grad_unit.astype(F32), axis=0, keepdims=True)
        units[rows] = grad_unit
        part_ref[rows] += dot_nn(grad_unit, up_ref[0])
    bias_ref[pl.ds(step, 1)] = bias

    def block(y, x):
        return pl.ds(pl.multiple_of((2 * y + x) * WIDE, WIDE), WIDE)

    near_x, near_y = place_ref[0], place_ref[1]
    split_rows = along_x.shape[2]
    for first in range(0, split_rows, ROWS):
        rows = slice(first, first + ROWS)
        other = slice(split_rows + first, split_rows + first + ROWS)
        for side in range(2):
            for target, x in ((along_x, 1 - near_x), (kept_x, near_x)):
                target[0, side, rows] = dot_nn(grad_t[rows], act_ref[0, :, block(side, x)])
            for target, y in ((along_y, 1 - near_y), (kept_y, near_y)):
                target[0, side, rows] = dot_nn(grad_t[other], act_ref[0, :, block(y, side)])

    def up_grads(target):
        for first in range(0, h_t.shape[0], ROWS):
            rows = slice(first, first + ROWS)
            for index in range(FF_BLOCK // WIDE):
                lanes = slice(index * WIDE, (index + 1) * WIDE)
                target[0, index, rows] = dot_nn(h_t[rows], units[:, lanes])

    stays = lax.rem(step, 2) == place_ref[2]
    pl.when(stays)(functools.partial(up_grads, kept_z))
    pl.when(jnp.logical_not(stays))(functools.partial(up_grads, along_z))


def halves_of(width):
    pair = (4, 2, width // 2, WIDE)
    single = (2, 4, width, WIDE)
    return [jax.ShapeDtypeStruct(shape, F32) for shape in (pair,) * 4 + (single,) * 2]


def mlp_backward(layer, place, grad, h, act, slope, down_weight, up):
    length, width = h.shape
    hidden = up.shape[1]
    blocks = hidden // FF_BLOCK
    pair = pl.BlockSpec((1, 2, width // 2, WIDE), lambda j, *_: (j, 0, 0, 0))
    single = pl.BlockSpec(
        (1, 4, width, WIDE), lambda j, *_: (j // 2, 0, 0, 0), pipeline_mode=pl.Buffered(1)
    )
    plane = pl.BlockSpec((1, length, FF_BLOCK), lambda j, *_: (j, 0, 0))
    return pl.pallas_call(
        mlp_backward_kernel,
        grid_spec=pltpu.PrefetchScalarGridSpec(
            num_scalar_prefetch=1,
            grid=(blocks,),
            in_specs=[
                whole((length, width)),
                whole((length, width)),
                plane,
                plane,
                pl.BlockSpec((1, 1, FF_BLOCK, width), lambda j, *_: (0, layer, j, 0)),
                pl.BlockSpec((1, FF_BLOCK, width), lambda j, *_: (layer, j, 0)),
            ],
            out_specs=[whole((length, width))] + [pair] * 4 + [single] * 2
            + [whole((blocks, FF_BLOCK))],
            scratch_shapes=[
                pltpu.VMEM((width, length), BF16),
                pltpu.VMEM((width, length), BF16),
                pltpu.VMEM((length, FF_BLOCK), BF16),
            ],
        ),
        out_shape=[jax.ShapeDtypeStruct((length, width), F32)] + halves_of(width)
        + [jax.ShapeDtypeStruct((blocks, FF_BLOCK), F32)],
        compiler_params=params(),
        name="mlp_backward",
    )(place, grad, h, act, slope, down_weight, up)


def head_sums(values, ones):
    upper, lower = split(values)
    return dot_nn(upper, ones) + dot_nn(lower, ones)


def same_head_ones():
    same = row_index(WIDE, WIDE) // DH == lane_index(WIDE, WIDE) // DH
    return jnp.where(same, 1.0, 0.0).astype(BF16)


def write_mask(starts_ref, mask_ref, flipped):
    length = mask_ref.shape[0]
    keys = lane_index(1, length)
    documents = sum((starts_ref[0, i] <= keys).astype(jnp.int32) for i in range(starts_ref.shape[1]))
    for first in range(0, length, ROWS):
        own = row_index(ROWS, 1) + first
        document = sum(
            (starts_ref[0, i] <= own).astype(jnp.int32) for i in range(starts_ref.shape[1])
        )
        order = (own <= keys) if flipped else (keys <= own)
        seen = (document == documents) & order
        mask_ref[first : first + ROWS] = jnp.where(seen, 1.0, 0.0).astype(BF16)


def wide_rotary(cosine_ref, sine_ref, rows):
    return tuple(
        jnp.concatenate([ref[rows]] * (WIDE // PAIR), axis=1) for ref in (cosine_ref, sine_ref)
    )


def attention_forward_kernel(count, *refs):
    stream, refs = refs[:count], refs[count:]
    starts_ref, gain_ref, offset_ref, weight_ref, bias_ref, out_bias_ref = refs[:6]
    upper_ref, lower_ref, scale_ref, cosine_ref, sine_ref = refs[6:11]
    refs = refs[11:]
    x_ref = None
    if count > 1:
        x_ref, refs = refs[0], refs[1:]
    part_ref, h_ref, state_ref, mixed_ref, mask_ref = refs
    length = h_ref.shape[0]

    @pl.when(pl.program_id(0) == 0)
    def _():
        start_layer(stream, x_ref, h_ref, gain_ref, offset_ref)
        write_mask(starts_ref, mask_ref, False)
        part_ref[...] = jnp.broadcast_to(out_bias_ref[...], part_ref.shape)

    ones = same_head_ones()
    table_up, table_low = upper_ref[0, 0], lower_ref[0, 0]

    def features(values, rows):
        upper, lower = split(turn(values, *wide_rotary(cosine_ref, sine_ref, rows)))
        return dot_nn(upper, table_up) + (dot_nn(lower, table_up) + dot_nn(upper, table_low))

    for first in range(0, length, ROWS):
        rows = slice(first, first + ROWS)
        queries, keys, values = [
            dot_nt(h_ref[rows], weight_ref[0, 0, kind, 0]) + bias_ref[kind, 0] for kind in range(3)
        ]
        state_ref[0, rows] = jnp.exp(features(queries, rows)).astype(BF16)
        logs = features(keys, rows) - (0.5 / math.sqrt(DH)) * head_sums(keys * keys, ones)
        state_ref[1, rows] = (scale_ref[0, 0] * jnp.exp(logs)).astype(BF16)
        state_ref[2, rows] = keys.astype(BF16)
        state_ref[3, rows] = values.astype(BF16)

    zero = jnp.zeros((), BF16)
    one = jnp.ones((), BF16)
    for first in range(0, length, ROWS):
        rows = slice(first, first + ROWS)
        finish = first + ROWS
        left = lane_index(finish, PAIR) < DH
        seen = mask_ref[rows, :finish] > zero
        for pair in range(WIDE // PAIR):
            lanes = slice(pair * PAIR, (pair + 1) * PAIR)
            sums = []
            for own in (left, ~left):
                keys = jnp.where(own, state_ref[1, :finish, lanes], zero)
                scores = dot_nt(state_ref[0, rows, lanes], keys).astype(BF16)
                scores = jnp.where(seen, scores, zero)
                sums.append(dot_nn(scores, jnp.where(own, state_ref[3, :finish, lanes], one)))
            mine = lane_index(ROWS, PAIR) < DH
            numer = jnp.where(mine, sums[0], sums[1])
            denom = jnp.where(mine, pltpu.roll(sums[0], DH, 1), pltpu.roll(sums[1], DH, 1))
            inverse = 1.0 / denom
            mixed_ref[0, rows, lanes] = (numer * inverse).astype(BF16)
            mixed_ref[1, rows, lanes], mixed_ref[2, rows, lanes] = split(inverse)
        part_ref[rows] += dot_nn(mixed_ref[0, rows], weight_ref[0, 0, 3, 0])


def kinds_of(weight):
    return weight.reshape(weight.shape[:2] + (4, QUADS, WIDE, weight.shape[3]))


def attention_forward(layer, stream, starts, gain, offset, weight, biases, tables, rotary):
    length, width = stream[0].shape
    full = jax.ShapeDtypeStruct((length, width), F32)
    state = jax.ShapeDtypeStruct((4, length, width), BF16)
    out_shape = [full, jax.ShapeDtypeStruct((length, width), BF16), state, state]
    four = pl.BlockSpec((4, length, WIDE), lambda g: (0, 0, g))
    out_specs = [whole((length, width)), whole((length, width)), four, four]
    if len(stream) > 1:
        out_shape, out_specs = [full] + out_shape, [whole((length, width))] + out_specs
    return pl.pallas_call(
        functools.partial(attention_forward_kernel, len(stream)),
        grid=(QUADS,),
        in_specs=[whole((length, width))] * len(stream)
        + [
            pl.BlockSpec(memory_space=pltpu.SMEM),
            whole((1, width)),
            whole((1, width)),
            pl.BlockSpec((1, 1, 4, 1, WIDE, width), lambda g: (0, layer, 0, g, 0, 0)),
            pl.BlockSpec((4, 1, 1, WIDE), lambda g: (0, g, 0, 0)),
            whole((1, width)),
            pl.BlockSpec((1, 1, WIDE, WIDE), lambda g: (layer, g, 0, 0)),
            pl.BlockSpec((1, 1, WIDE, WIDE), lambda g: (layer, g, 0, 0)),
            pl.BlockSpec((1, 1, 1, WIDE), lambda g: (layer, g, 0, 0)),
            whole((length, PAIR)),
            whole((length, PAIR)),
        ],
        out_specs=out_specs,
        out_shape=out_shape,
        scratch_shapes=[pltpu.VMEM((length, length), BF16)],
        compiler_params=params(),
        name="attention_forward",
    )(
        *stream, starts, gain, offset, kinds_of(weight),
        biases.reshape(4, QUADS, 1, WIDE), biases[None, 3 * width :], *tables, *rotary,
    )


def attention_backward_kernel(
    place_ref, starts_ref, grad_ref, h_ref, state_ref, mixed_ref, table_ref, cosine_ref, sine_ref,
    weight_ref, part_ref, along_x, kept_x, along_y, kept_y, along_z, kept_z, bias_ref,
    mask_ref, grad_t, h_t, numer_ref, feat_ref, flow, query_t,
):
    del along_z, kept_z
    group = pl.program_id(0)
    length = h_ref.shape[0]

    @pl.when(pl.program_id(0) == 0)
    def _():
        write_mask(starts_ref, mask_ref, True)
        grad_t[...] = grad_ref[...].T
        h_t[...] = h_ref[...].T
        part_ref[...] = jnp.zeros_like(part_ref)

    row, lane = row_index(WIDE, WIDE), lane_index(WIDE, WIDE)
    partner = (row // PAIR == lane // PAIR) & (row // DH != lane // DH)
    partner = jnp.where(partner, 1.0, 0.0).astype(BF16)
    zero = jnp.zeros((), BF16)
    one = jnp.ones((), BF16)
    for first in range(0, length, ROWS):
        rows = slice(first, first + ROWS)
        grad = dot_nt(grad_ref[rows], weight_ref[0, 0, 3, 0]).astype(BF16).astype(F32)
        inverse = mixed_ref[1, rows].astype(F32) + mixed_ref[2, rows].astype(F32)
        scaled = grad * inverse
        upper, lower = split(-head_sums(scaled * mixed_ref[0, rows].astype(F32), partner))
        numer = scaled.astype(BF16)
        lane = lane_index(ROWS, WIDE)
        spare = jnp.where(lane % DH == 0, upper, jnp.where(lane % DH == 1, lower, zero))
        left = lane % PAIR < DH
        numer_ref[0, rows] = jnp.where(left, numer, spare)
        numer_ref[1, rows] = jnp.where(left, spare, numer)

    for pair in range(WIDE // PAIR):
        lanes = slice(pair * PAIR, (pair + 1) * PAIR)
        query_t[...] = jnp.zeros_like(query_t)
        for first in range(0, length, ROWS):
            rows = slice(first, first + ROWS)
            seen = mask_ref[rows, first:] > zero
            lane = lane_index(ROWS, PAIR)
            left = lane < DH
            spare = jnp.where(lane % DH < 2, one, zero)
            keys, values = state_ref[1, rows, lanes], state_ref[3, rows, lanes]
            queries = state_ref[0, first:, lanes]
            numer = jnp.where(
                lane_index(length - first, PAIR) < DH,
                numer_ref[0, first:, lanes],
                numer_ref[1, first:, lanes],
            )
            grads = []
            for head, own in enumerate((left, ~left)):
                own_keys = jnp.where(own, keys, zero)
                scores = dot_nt(own_keys, queries).astype(BF16)
                scores = jnp.where(seen, scores, zero)
                grad_value = dot_nn(scores, numer)
                grad_scores = dot_nt(
                    jnp.where(own, values, spare), numer_ref[head, first:, lanes]
                ).astype(BF16)
                grad_scores = jnp.where(seen, grad_scores, zero)
                grad_key = dot_nn(grad_scores, queries)
                query_t[head, :, first:] += dot_nn(
                    own_keys.T[head * DH : (head + 1) * DH], grad_scores
                )
                grads.append((grad_value, grad_key))
            flow[2, rows, lanes] = jnp.where(left, grads[0][0], grads[1][0]).astype(BF16)
            grad_key = jnp.where(left, grads[0][1], grads[1][1])
            feat_ref[1, rows, lanes] = (grad_key * keys.astype(F32)).astype(BF16)
        for first in range(0, length, ROWS):
            rows = slice(first, first + ROWS)
            grad_query = jnp.concatenate([query_t[0, :, rows], query_t[1, :, rows]], axis=0).T
            feat_ref[0, rows, lanes] = (
                grad_query * state_ref[0, rows, lanes].astype(F32)
            ).astype(BF16)

    ones = same_head_ones()
    table = table_ref[0, 0]
    sums = [jnp.zeros((1, WIDE), F32)] * 3
    for first in range(0, length, ROWS):
        rows = slice(first, first + ROWS)
        cosine, sine = wide_rotary(cosine_ref, sine_ref, rows)
        flow[0, rows] = turn_back(dot_nt(feat_ref[0, rows], table), cosine, sine).astype(BF16)
        shrink = dot_nn(feat_ref[1, rows], ones) * (1.0 / math.sqrt(DH))
        turned = turn_back(dot_nt(feat_ref[1, rows], table), cosine, sine)
        flow[1, rows] = (turned - state_ref[2, rows].astype(F32) * shrink).astype(BF16)
        total = part_ref[rows]
        for kind in range(3):
            block = flow[kind, rows]
            sums[kind] = sums[kind] + jnp.sum(block.astype(F32), axis=0, keepdims=True)
            total = total + dot_nn(block, weight_ref[0, 0, kind, 0])
        part_ref[rows] = total
    for kind in range(3):
        bias_ref[kind : kind + 1] = sums[kind]
    lanes = pl.ds(pl.multiple_of(group * WIDE, WIDE), WIDE)
    bias_ref[3:4] = jnp.sum(grad_ref[:, lanes].astype(F32), axis=0, keepdims=True)
    split_rows = along_x.shape[2]

    def weights(target, base):
        for first in range(0, split_rows, ROWS):
            rows = slice(first, first + ROWS)
            held = slice(base + first, base + first + ROWS)
            for kind in range(3):
                target[kind, 0, rows] = dot_nn(h_t[held], flow[kind])
            target[3, 0, rows] = dot_nn(grad_t[held], mixed_ref[0])

    stays = lax.rem(group, 2) == place_ref[0]
    pl.when(stays)(functools.partial(weights, kept_x, 0))
    pl.when(jnp.logical_not(stays))(functools.partial(weights, along_x, 0))
    stays = group // 2 == place_ref[1]
    pl.when(stays)(functools.partial(weights, kept_y, split_rows))
    pl.when(jnp.logical_not(stays))(functools.partial(weights, along_y, split_rows))


def attention_backward(layer, place, starts, grad, h, state, mixed, tables, rotary, weight):
    _, length, width = state.shape
    four = pl.BlockSpec((4, length, WIDE), lambda g, *_: (0, 0, g))
    shape = (4, 1, width // 2, WIDE)
    first = pl.BlockSpec(shape, lambda g, *_: (0, g // 2, 0, 0))

    def second(side):
        def index(g, place_ref):
            y, chosen = g // 2, place_ref[1] if side else 1 - place_ref[1]
            at = jnp.where(y == chosen, g % 2, jnp.where(y < chosen, 0, 1))
            return 0, at, 0, 0

        return pl.BlockSpec(shape, index)

    return pl.pallas_call(
        attention_backward_kernel,
        grid_spec=pltpu.PrefetchScalarGridSpec(
            num_scalar_prefetch=1,
            grid=(QUADS,),
            in_specs=[
                pl.BlockSpec(memory_space=pltpu.SMEM),
                whole((length, width)),
                whole((length, width)),
                four,
                four,
                pl.BlockSpec((1, 1, WIDE, WIDE), lambda g, *_: (layer, g, 0, 0)),
                whole((length, PAIR)),
                whole((length, PAIR)),
                pl.BlockSpec((1, 1, 4, 1, WIDE, width), lambda g, *_: (0, layer, 0, g, 0, 0)),
            ],
            out_specs=[whole((length, width)), first, first, second(False), second(True)]
            + [pl.BlockSpec(memory_space=pl.ANY)] * 2
            + [pl.BlockSpec((4, WIDE), lambda g, *_: (0, g))],
            scratch_shapes=[
                pltpu.VMEM((length, length), BF16),
                pltpu.VMEM((width, length), BF16),
                pltpu.VMEM((width, length), BF16),
                pltpu.VMEM((2, length, WIDE), BF16),
                pltpu.VMEM((2, length, WIDE), BF16),
                pltpu.VMEM((3, length, WIDE), BF16),
                pltpu.VMEM((2, DH, length), F32),
            ],
        ),
        out_shape=[jax.ShapeDtypeStruct((length, width), F32)] + halves_of(width)
        + [jax.ShapeDtypeStruct((4, width), F32)],
        compiler_params=params(),
        name="attention_backward",
    )(place, starts, grad, h, state, mixed, tables[0], *rotary, kinds_of(weight))


def norm_gradient(values, incoming, grad, gain, sums_ref):
    average = jnp.mean(values, -1, keepdims=True)
    centered = values - average
    variance = jnp.mean(centered * centered, -1, keepdims=True)
    inverse = lax.rsqrt(variance + EPSILON)
    unit = centered * inverse
    grad_unit = incoming * gain
    first = jnp.mean(grad_unit, -1, keepdims=True)
    second = jnp.mean(grad_unit * unit, -1, keepdims=True)
    sums_ref[0:1] += jnp.sum(incoming * unit, axis=0, keepdims=True)
    sums_ref[1:2] += jnp.sum(incoming, axis=0, keepdims=True)
    sums_ref[2:3] += jnp.sum(grad, axis=0, keepdims=True)
    return grad + inverse * (grad_unit - first - unit * second)


def norm_backward_kernel(x_ref, own_ref, other_ref, grad_ref, gain_ref, out_ref, sums_ref):
    @pl.when(pl.program_id(0) == 0)
    def _():
        sums_ref[...] = jnp.zeros_like(sums_ref)

    out = norm_gradient(
        x_ref[...].astype(F32),
        own_ref[...] + other_ref[...],
        grad_ref[...].astype(F32),
        gain_ref[...].astype(F32),
        sums_ref,
    )
    out_ref[...] = out.astype(out_ref.dtype)


def norm_backward(x, own, other, grad, gain, kind):
    length, width = own.shape
    block = pl.BlockSpec((ROWS, width), lambda i: (i, 0))
    return pl.pallas_call(
        norm_backward_kernel,
        grid=(length // ROWS,),
        in_specs=[block, block, block, block, whole((1, width))],
        out_specs=[block, whole((8, width))],
        out_shape=[
            jax.ShapeDtypeStruct((length, width), kind),
            jax.ShapeDtypeStruct((8, width), F32),
        ],
        compiler_params=params(),
        name="norm_backward",
    )(x, own, other, grad, gain)


MESH = pl.DeviceIdType.MESH
UNIT = 8
SLOTS = 4
LAG = 1
JOB = 128


class Flow(NamedTuple):
    order: tuple
    family: int
    layer: int
    row: int
    units: int
    start: int


def flows_of(width, layer, start):
    rows = width // 4
    kinds = (
        ((0, 1, 2, 3), 0, 0),
        ((1, 0, 2, 3), 1, 0),
        ((2, 0, 1, 3), 2, 0),
        ((2, 1, 0, 3), 2, 1),
        ((0, 1, 2, 3), 0, 1),
        ((1, 0, 2, 3), 1, 1),
        ((2, 0, 1, 3), 2, 2),
        ((2, 1, 0, 3), 2, 3),
    )
    return [
        Flow(order, family, layer, part * rows, rows // UNIT, start)
        for order, family, part in kinds
    ]


def bit_of(index, bit):
    return (index // (1 << bit)) % 2


def flip(index, bit):
    return index + (1 << bit) * (1 - 2 * bit_of(index, bit))


def finish_kernel(
    bits, flows,
    kept_x1, kept_y1, kept_z1, came_x1, came_y1, came_z1,
    kept_x0, kept_y0, kept_z0, sent_x0, sent_y0, sent_z0,
    part_ref, tokens_ref, grad_ref, x_ref, own_ref, other_ref,
    bias0_ref, bias1_ref, sums1_ref, gain_ref,
    weight_out, up_out, small_out, result_out, grad_out,
    weight_sum, up_sum, up_turned, up_came, part, part_came, tokens, grad, x, own, other, sums,
    *scratch,
):
    stages = bits
    kept = ((kept_x1, kept_y1, kept_z1), (kept_x0, kept_y0, kept_z0))
    moved = ((came_x1, came_y1, came_z1), (sent_x0, sent_y0, sent_z0))
    held = scratch[: len(flows) * (stages + 1)]
    held = [held[f * (stages + 1) : (f + 1) * (stages + 1)] for f in range(len(flows))]
    small = scratch[len(flows) * (stages + 1) :][: stages + 1]
    small_came = scratch[len(flows) * (stages + 1) + stages + 1 :][:stages]
    load_sem, send_sem, recv_sem, credit, small_send, small_recv, job_sem, near_send, near_recv = (
        scratch[len(flows) * (stages + 1) + 2 * stages + 1 :]
    )
    me, core = lax.axis_index("batch"), lax.axis_index("stream")

    barrier = pltpu.get_barrier_semaphore()
    for bit in range(bits):
        pl.semaphore_signal(
            barrier, inc=1, device_id={"batch": flip(me, bit)}, device_id_type=MESH
        )
    pl.semaphore_signal(barrier, inc=1, device_id={"stream": 1 - core}, device_id_type=MESH)
    pl.semaphore_wait(barrier, bits + 1)

    exchange = pltpu.make_async_remote_copy(
        src_ref=part_ref,
        dst_ref=part_came,
        send_sem=near_send.at[2],
        recv_sem=near_recv.at[2],
        device_id={"stream": 1 - core},
        device_id_type=MESH,
    )
    loads = [
        pltpu.make_async_copy(source, target, job_sem.at[index])
        for index, (source, target) in enumerate(
            ((part_ref, part), (tokens_ref, tokens), (grad_ref, grad), (x_ref, x),
             (own_ref, own), (other_ref, other))
        )
    ]
    stores = [
        pltpu.make_async_copy(part, grad_out, job_sem.at[len(loads)]),
        pltpu.make_async_copy(x, result_out, job_sem.at[len(loads) + 1]),
    ]
    exchange.start()
    for copy in loads:
        copy.start()
    jobs = part.shape[0] // JOB
    norm_start, result_start = 3, 3 + jobs
    small_start = result_start + 1
    turn_start = max(flow.start + flow.units for flow in flows[: len(flows) // 2]) + stages + 1

    def norm_job(index):
        rows = pl.ds(pl.multiple_of((index - norm_start) * JOB, JOB), JOB)

        @pl.when(index == norm_start)
        def _():
            exchange.wait()
            for copy in loads[:3]:
                copy.wait()
            sums[...] = jnp.zeros_like(sums)

        part[rows] = norm_gradient(
            tokens[rows].astype(F32),
            part[rows] + part_came[rows],
            grad[rows].astype(F32),
            gain_ref[...].astype(F32),
            sums,
        )

    def result_job(index):
        rows = pl.ds(pl.multiple_of((index - result_start) * JOB, JOB), JOB)

        @pl.when(index == result_start)
        def _():
            stores[0].start()
            for copy in loads[3:]:
                copy.wait()

        x[rows] = x[rows] + (own[rows] + other[rows])

    def near_copy(layer):
        return pltpu.make_async_remote_copy(
            src_ref=up_turned.at[layer],
            dst_ref=up_came.at[layer],
            send_sem=near_send.at[layer],
            recv_sem=near_recv.at[layer],
            device_id={"stream": 0},
            device_id_type=MESH,
        )

    def turn_weights(layer):
        weight_out[len(moved) - 1 - layer] = weight_sum[layer].T

        @pl.when(core == 1)
        def _():
            up_turned[layer] = up_sum[layer, :, : WIDE // 2].T
            near_copy(layer).start()
            up_out[len(moved) - 1 - layer] = up_sum[layer, :, WIDE // 2 :].T

    def small_copy(stage):
        return pltpu.make_async_remote_copy(
            src_ref=small[stage],
            dst_ref=small_came[stage],
            send_sem=small_send.at[stage],
            recv_sem=small_recv.at[stage],
            device_id={"batch": flip(me, stage)},
            device_id_type=MESH,
        )

    def small_step(stage):
        if stage == 0:
            rows = bias0_ref.shape[0]
            small[0][0:rows] = bias0_ref[...]
            small[0][rows : 2 * rows] = bias1_ref[...]
            small[0][2 * rows : 2 * rows + 8] = sums1_ref[...]
            small[0][2 * rows + 8 : 2 * rows + 16] = sums[...]
        else:
            small_copy(stage - 1).wait()
            small[stage][...] = small[stage - 1][...] + small_came[stage - 1][...]
        if stage < stages:
            small_copy(stage).start()
        else:
            small_out[...] = small[stage][...]

    def view(order, stage, mine):
        left = sorted(set(range(bits)) - set(order[:stage]), reverse=True)
        pick = bit_of(me, order[stage])
        pick = pick if mine else 1 - pick
        return tuple(pick if bit == order[stage] else slice(None) for bit in left)

    def remote(place, stage, slot, source):
        return pltpu.make_async_remote_copy(
            src_ref=source,
            dst_ref=held[place][stage + 1].at[slot],
            send_sem=send_sem.at[place, stage, slot],
            recv_sem=recv_sem.at[place, stage, slot],
            device_id={"batch": flip(me, flows[place].order[stage])},
            device_id_type=MESH,
        )

    def sent_from(place, stage, slot):
        if stage == 0:
            return held[place][0].at[slot]
        return held[place][stage].at[(slot,) + view(flows[place].order, stage, False)]

    def load(place, slot, source):
        return pltpu.make_async_copy(source, held[place][0].at[slot], load_sem.at[place, slot])

    def load_came(place, slot, source):
        return pltpu.make_async_copy(
            source, held[place][1].at[slot], recv_sem.at[place, 0, slot]
        )

    def return_credit(place, stage, unit):
        if stage == 0 and flows[place].layer == 0:
            return

        @pl.when(unit + SLOTS < flows[place].units)
        def _():
            pl.semaphore_signal(
                credit.at[place, stage],
                inc=1,
                device_id={"batch": flip(me, flows[place].order[stage])},
                device_id_type=MESH,
            )

    def take_credit(place, stage, unit):
        @pl.when(unit >= SLOTS)
        def _():
            pl.semaphore_wait(credit.at[place, stage], 1)

    def begin(place, unit):
        slot = lax.rem(unit, SLOTS)
        _, family, layer, row, _, _ = flows[place]
        at = (slice(None),) * (bits - 1)
        at += (pl.ds(pl.multiple_of(row + unit * UNIT, UNIT), UNIT),)
        load(place, slot, kept[layer][family].at[at]).start()
        if layer == 0:
            load_came(place, slot, moved[layer][family].at[at]).start()
        else:
            take_credit(place, 0, unit)
            remote(place, 0, slot, moved[layer][family].at[at]).start()

    def advance(place, stage, unit):
        slot = lax.rem(unit, SLOTS)
        order, family, layer, row, _, _ = flows[place]
        buffer = held[place][stage]
        copy = remote(place, stage - 1, slot, sent_from(place, stage - 1, slot))
        if stage == 1 and layer == 0:
            load_came(place, slot, held[place][0].at[slot]).wait()
        else:
            copy.wait_recv()
        if stage == 1:
            load(place, slot, held[place][1].at[slot]).wait()
            mine = held[place][0][slot]
        else:
            mine = held[place][stage - 1][(slot,) + view(order, stage - 1, True)]
        value = buffer[slot] + mine
        if stage < stages:
            buffer[slot] = value
            take_credit(place, stage, unit)
            remote(place, stage, slot, sent_from(place, stage, slot)).start()
        else:
            target = up_sum if family == 2 else weight_sum
            base = row + (weight_sum.shape[1] // 2 if family == 1 else 0)
            target[layer, pl.ds(pl.multiple_of(base + unit * UNIT, UNIT), UNIT)] = value
        if stage > 1 or layer > 0:
            copy.wait_send()
        if stage >= 2:
            return_credit(place, stage - 2, unit)
        if stage == stages:
            return_credit(place, stage - 1, unit)

    def within(place, unit):
        inside = (unit >= 0) & (unit < flows[place].units)
        return inside & (core == 1) if flows[place].family == 2 else inside

    def step(index, carry):
        for place, flow in enumerate(flows):
            unit = index - flow.start
            pl.when(within(place, unit))(functools.partial(begin, place, unit))
        for place, flow in enumerate(flows):
            for stage in range(1, stages + 1):
                unit = index - flow.start - LAG * stage
                pl.when(within(place, unit))(functools.partial(advance, place, stage, unit))
        pl.when((index >= norm_start) & (index < norm_start + jobs))(
            functools.partial(norm_job, index)
        )
        pl.when((index >= result_start) & (index < result_start + jobs))(
            functools.partial(result_job, index)
        )
        for stage in range(stages + 1):
            pl.when(index == small_start + 2 * stage)(functools.partial(small_step, stage))
        pl.when(index == turn_start)(functools.partial(turn_weights, 0))
        return carry

    last = max(flow.start + flow.units for flow in flows)
    lax.fori_loop(0, last + LAG * stages, step, 0)
    stores[1].start()
    turn_weights(1)
    for layer in range(len(moved)):

        @pl.when(core == 0)
        def _():
            near_copy(layer).wait_recv()
            up_out[len(moved) - 1 - layer] = up_came[layer]

        @pl.when(core == 1)
        def _():
            near_copy(layer).wait_send()

    for copy in stores:
        copy.wait()


def finish(last, first, came, part, tokens, grad, x, own, other, biases, sums, gain):
    length, width = tokens.shape
    bits = 4
    split = (2,) * (bits - 1)
    flows = flows_of(width, 0, 0)
    flows += flows_of(width, 1, max(flow.start + flow.units for flow in flows))
    small = (2 * biases[0].shape[0] + 16, width)
    full = (length, width)
    scratch = [
        pltpu.VMEM((2, width, WIDE), F32),
        pltpu.VMEM((2, width, WIDE), F32),
        pltpu.VMEM((2, WIDE // 2, width), F32),
        pltpu.VMEM((2, WIDE // 2, width), F32),
        pltpu.VMEM(full, F32),
        pltpu.VMEM(full, F32),
        pltpu.VMEM(full, BF16),
        pltpu.VMEM(full, BF16),
        pltpu.VMEM(full, F32),
        pltpu.VMEM(full, F32),
        pltpu.VMEM(full, F32),
        pltpu.VMEM((8, width), F32),
    ]
    for _ in flows:
        for stage in range(bits + 1):
            lead = (SLOTS,) + (2,) * (bits - 1 - max(stage - 1, 0))
            scratch.append(pltpu.VMEM(lead + (UNIT, WIDE), F32))
    scratch += [pltpu.VMEM(small, F32)] * (2 * bits + 1)
    scratch += [
        pltpu.SemaphoreType.DMA((len(flows), SLOTS)),
        pltpu.SemaphoreType.DMA((len(flows), bits, SLOTS)),
        pltpu.SemaphoreType.DMA((len(flows), bits, SLOTS)),
        pltpu.SemaphoreType.REGULAR((len(flows), bits)),
        pltpu.SemaphoreType.DMA((bits,)),
        pltpu.SemaphoreType.DMA((bits,)),
        pltpu.SemaphoreType.DMA((8,)),
        pltpu.SemaphoreType.DMA((3,)),
        pltpu.SemaphoreType.DMA((3,)),
    ]
    large = [last[1], last[3], last[5], *came, first[1], first[3], first[5]]
    large += [first[0], first[2], first[4]]
    large = [array.reshape(split + array.shape[2:]) for array in large]
    return pl.pallas_call(
        functools.partial(finish_kernel, bits, flows),
        in_specs=[pl.BlockSpec(memory_space=pltpu.HBM)] * (len(large) + 6)
        + [pl.BlockSpec(memory_space=pltpu.VMEM)] * 4,
        out_specs=[pl.BlockSpec(memory_space=pltpu.VMEM)] * 3
        + [pl.BlockSpec(memory_space=pltpu.HBM)] * 2,
        out_shape=[
            jax.ShapeDtypeStruct((2, WIDE, width), F32),
            jax.ShapeDtypeStruct((2, WIDE // 2, width), F32),
            jax.ShapeDtypeStruct(small, F32),
            jax.ShapeDtypeStruct(full, F32),
            jax.ShapeDtypeStruct(full, F32),
        ],
        scratch_shapes=scratch,
        compiler_params=pltpu.CompilerParams(
            collective_id=0, has_side_effects=True, vmem_limit_bytes=VMEM_LIMIT
        ),
        name="finish",
    )(*large, part, tokens, grad, x, own, other, biases[0], biases[1], sums, gain)


def send_first(halves):
    count = lax.axis_size("batch")
    received = []
    for bit, part in enumerate(halves[0::2]):
        streams = (1,) if bit == 2 else (0, 1)
        pairs = [
            (2 * source + stream, 2 * flip(source, bit) + stream)
            for source in range(count)
            for stream in streams
        ]
        received.append(lax.ppermute(part, ("batch", "stream"), pairs))
    return received


def shards(
    tokens, cotangent, branch_weight, branch_bias, up_weight, down_bias,
    norm_gain, norm_bias, freq_seeds, doc_starts,
):
    is_attention = lax.axis_index("stream") == 0
    length, width = tokens.shape
    rotary = tuple(jnp.asarray(table) for table in rotary_rows(length))
    biases = branch_bias[0].astype(F32)
    tables = lax.cond(
        is_attention,
        lambda: tuple(feature_tables(freq_seeds)),
        lambda: (
            jnp.zeros((LAYERS, QUADS, WIDE, WIDE), BF16),
            jnp.zeros((LAYERS, QUADS, WIDE, WIDE), BF16),
            jnp.zeros((LAYERS, QUADS, 1, WIDE), F32),
        ),
    )
    swap = [(0, 1), (1, 0)]

    def attention(layer, stream):
        gain, offset = norm_gain[layer : layer + 1], norm_bias[layer : layer + 1]
        return tuple(
            attention_forward(
                layer, stream, doc_starts, gain, offset, branch_weight, biases[layer], tables,
                rotary,
            )
        )

    def feed_forward(layer, stream):
        gain, offset = norm_gain[layer : layer + 1], norm_bias[layer : layer + 1]
        return tuple(
            mlp_forward(
                layer, stream, gain, offset, up_weight, biases[layer], branch_weight,
                down_bias[layer : layer + 1],
            )
        )

    stream = (tokens,)
    inputs, kept = [], []
    for layer in range(LAYERS):
        *x, part, h, state, mixed = lax.cond(
            is_attention,
            functools.partial(attention, layer, stream),
            functools.partial(feed_forward, layer, stream),
        )
        inputs.append(x[0] if x else tokens)
        kept.append((h, state, mixed))
        stream = (inputs[-1], part, lax.ppermute(part, "stream", swap))
    result = stream[0] + (stream[1] + stream[2])

    count = lax.axis_size("batch")
    blocked = count == branch_weight.shape[2] // WIDE
    me = lax.axis_index("batch") if blocked else 0
    place = jnp.stack([jnp.asarray(bit_of(me, bit), jnp.int32) for bit in range(3)])

    def attention_back(layer, grad):
        h, state, mixed = kept[layer]
        return attention_backward(
            layer, place, doc_starts, grad, h, state, mixed, tables, rotary, branch_weight
        )

    def feed_forward_back(layer, grad):
        h, act, slope = kept[layer]
        return mlp_backward(layer, place, grad, h, act, slope, branch_weight, up_weight)

    def back(layer, grad):
        part, *halves, bias = lax.cond(
            is_attention,
            functools.partial(attention_back, layer, grad),
            functools.partial(feed_forward_back, layer, grad),
        )
        return part, halves, bias

    def norm_back(layer, part, grad, kind):
        other = lax.ppermute(part, "stream", swap)
        return norm_backward(
            inputs[layer], part, other, grad, norm_gain[layer : layer + 1], kind
        )

    part1, halves1, bias1 = back(1, cotangent)
    if blocked:
        came = send_first(halves1)
    grad0, sums1 = norm_back(1, part1, cotangent, BF16)
    part0, halves0, bias0 = back(0, grad0)
    if blocked:
        weight, up, small, result, input_grad = finish(
            halves1, halves0, came, part0, tokens, grad0, *stream, (bias0, bias1), sums1,
            norm_gain[:1],
        )
    else:
        result = stream[0] + (stream[1] + stream[2])
        input_grad, sums0 = norm_back(0, part0, grad0, F32)
        weight, up = scatter_rows((halves0, halves1))
        small = lax.psum(jnp.concatenate([bias0, bias1, sums1, sums0]), "batch")
    index, rows = lax.axis_index("batch"), bias0.shape[0]
    each, own = branch_weight.shape[2] // count, width // count
    biases = small[: 2 * rows].reshape(LAYERS, -1)
    sums = small[2 * rows :].reshape(LAYERS, 8, width)[::-1]
    sums = lax.dynamic_slice_in_dim(sums, index * own, own, axis=2)
    return (
        result,
        input_grad,
        weight[None],
        lax.dynamic_slice_in_dim(biases, index * each, each, axis=1)[None],
        up,
        sums[:, 2],
        sums[:, 0],
        sums[:, 1],
    )


def scatter_rows(layers):
    weights, ups = [], []
    for along_x, kept_x, along_y, kept_y, along_z, kept_z in layers:
        width = kept_z.shape[2]
        part_x = jnp.stack([kept_x, along_x], axis=2).reshape(-1, width // 2, WIDE)
        part_y = jnp.stack([kept_y, along_y], axis=1).reshape(-1, width // 2, WIDE)
        weight = rows_of(jnp.concatenate([part_x, part_y], axis=1))
        up = rows_of(jnp.stack([kept_z, along_z], axis=1).reshape(-1, width, WIDE))
        up = jnp.where(lax.axis_index("stream") == 1, up, 0.0)
        weights.append(lax.psum_scatter(weight, "batch", scatter_dimension=0, tiled=True))
        ups.append(lax.psum_scatter(up, ("batch", "stream"), scatter_dimension=0, tiled=True))
    return jnp.stack(weights), jnp.stack(ups)


def rows_of(blocks):
    return jnp.transpose(blocks, (0, 2, 1)).reshape(-1, blocks.shape[1])


def solution(mesh):
    placed = (
        P("batch", None),
        P("batch", None),
        P("stream", None, None, None),
        P("stream", None, None),
        P(),
        P(),
        P(),
        P(),
        P(),
        P("batch", None),
    )
    return jax.shard_map(
        shards,
        mesh=mesh,
        in_specs=placed,
        out_specs=(
            P("batch", None),
            P("batch", None),
            P("stream", None, "batch", None),
            P("stream", None, "batch"),
            P(None, ("batch", "stream"), None),
            P(None, "batch"),
            P(None, "batch"),
            P(None, "batch"),
        ),
        check_vma=False,
    )
```

```python
import functools
import math
from typing import NamedTuple

import jax
import jax.numpy as jnp
import numpy as np
from jax import lax
from jax.experimental import pallas as pl
from jax.experimental.pallas import tpu as pltpu
from jax.sharding import PartitionSpec as P

HEADS = 16
DH = 64
ROT = 16
FEAT = 64
LAYERS = 2
EPSILON = 1e-05
HIGH = lax.Precision.HIGHEST
F32 = jnp.float32
BF16 = jnp.bfloat16
WIDE = 256
PAIR = 128
QUADS = HEADS * DH // WIDE
PAIRS = HEADS * DH // PAIR
ROWS = 256
VMEM_LIMIT = 56 * 1024 * 1024


def params():
    return pltpu.CompilerParams(vmem_limit_bytes=VMEM_LIMIT)


def whole(shape):
    zeros = (0,) * len(shape)
    return pl.BlockSpec(shape, lambda *_: zeros, pipeline_mode=pl.Buffered(1))


def dot_nn(left, right):
    return lax.dot_general(left, right, (((1,), (0,)), ((), ())), preferred_element_type=F32)


def dot_tn(left, right):
    return lax.dot_general(left, right, (((0,), (0,)), ((), ())), preferred_element_type=F32)


def dot_nt(left, right):
    return lax.dot_general(left, right, (((1,), (1,)), ((), ())), preferred_element_type=F32)


def split(values):
    upper = values.astype(BF16)
    return upper, (values - upper.astype(F32)).astype(BF16)


def lane_index(rows, lanes):
    return lax.broadcasted_iota(jnp.int32, (rows, lanes), 1)


def row_index(rows, lanes):
    return lax.broadcasted_iota(jnp.int32, (rows, lanes), 0)


def cosine_block():
    samples = np.arange(DH, dtype=np.float64)
    angles = math.pi * (samples[None, :] + 0.5) * samples[:, None] / DH
    table = np.cos(angles) * math.sqrt(2.0 / DH)
    table[0] *= math.sqrt(0.5)
    return np.kron(np.eye(WIDE // DH), table.T * DH ** (-0.25)).astype(np.float32)


def rotary_rows(length):
    position = np.arange(length, dtype=np.float32)
    inverse = (10000.0 ** (-np.arange(0, ROT, 2, dtype=np.float32) / ROT)).astype(np.float32)
    angles = position[:, None] * inverse[None, :]
    cosine, sine = np.cos(angles), np.sin(angles)
    rest = DH - ROT
    cosine_head = np.concatenate([cosine, cosine, np.ones((length, rest))], 1)
    sine_head = np.concatenate([-sine, sine, np.zeros((length, rest))], 1)
    repeat = PAIR // DH
    return (
        np.tile(cosine_head, (1, repeat)).astype(np.float32),
        np.tile(sine_head, (1, repeat)).astype(np.float32),
    )


def tables_kernel(seeds_ref, cosine_ref, upper_ref, lower_ref, weight_ref):
    own = row_index(WIDE, DH) % DH == lane_index(WIDE, DH)
    feature = lane_index(WIDE, PAIR) % FEAT
    same_head = row_index(WIDE, WIDE) // DH == lane_index(WIDE, WIDE) // FEAT
    for group in range(QUADS):
        heads = [
            jnp.broadcast_to(seeds_ref[0, head : head + 1], (DH, DH))
            for head in range(group * QUADS, (group + 1) * QUADS)
        ]
        seeds = jnp.where(own, jnp.concatenate(heads, axis=0), 0)
        seeds = jnp.sum(seeds.astype(F32), axis=1, keepdims=True).astype(jnp.int32)
        lattice = (feature * seeds) & (FEAT - 1)
        prob = (lattice.astype(F32) + 0.5) * (1.0 / FEAT)
        radius = jnp.sqrt(-2.0 * jnp.log(jnp.minimum(prob, 1.0 - prob)))
        above = 2.515517 + 0.802853 * radius + 0.010328 * radius * radius
        below = (
            1.0
            + 1.432788 * radius
            + 0.189269 * radius * radius
            + 0.001308 * radius * radius * radius
        )
        magnitude = radius - above / below
        omega = jnp.where(prob > 0.5, magnitude, -magnitude)
        omega = jnp.where(same_head, jnp.concatenate([omega] * (WIDE // PAIR), axis=1), 0.0)
        project = jnp.dot(cosine_ref[...], omega, precision=HIGH, preferred_element_type=F32)
        upper_ref[0, group], lower_ref[0, group] = split(project)
        grown = jnp.exp(-0.5 / DH * jnp.sum(omega * omega, axis=0, keepdims=True))
        total = jnp.dot(
            jnp.broadcast_to(grown, (8, WIDE)),
            same_head.astype(F32),
            precision=HIGH,
            preferred_element_type=F32,
        )
        weight_ref[0, group] = FEAT * grown / total[:1]


def feature_tables(seeds):
    return pl.pallas_call(
        tables_kernel,
        grid=(LAYERS,),
        in_specs=[
            pl.BlockSpec((1, HEADS, DH), lambda l: (l, 0, 0)),
            whole((WIDE, WIDE)),
        ],
        out_specs=[
            pl.BlockSpec((1, QUADS, WIDE, WIDE), lambda l: (l, 0, 0, 0)),
            pl.BlockSpec((1, QUADS, WIDE, WIDE), lambda l: (l, 0, 0, 0)),
            pl.BlockSpec((1, QUADS, 1, WIDE), lambda l: (l, 0, 0, 0)),
        ],
        out_shape=[
            jax.ShapeDtypeStruct((LAYERS, QUADS, WIDE, WIDE), BF16),
            jax.ShapeDtypeStruct((LAYERS, QUADS, WIDE, WIDE), BF16),
            jax.ShapeDtypeStruct((LAYERS, QUADS, 1, WIDE), F32),
        ],
        compiler_params=params(),
        name="feature_tables",
    )(seeds, jnp.asarray(cosine_block()))


def turn(values, cosine, sine):
    lanes = values.shape[1]
    half = ROT // 2
    lane = lane_index(*values.shape) % DH
    swapped = jnp.where(
        lane < half, pltpu.roll(values, lanes - half, 1), pltpu.roll(values, half, 1)
    )
    return values * cosine + swapped * sine


def turn_back(values, cosine, sine):
    lanes = values.shape[1]
    half = ROT // 2
    lane = lane_index(*values.shape) % DH
    turned = values * sine
    swapped = jnp.where(
        lane < half, pltpu.roll(turned, lanes - half, 1), pltpu.roll(turned, half, 1)
    )
    return values * cosine + jnp.where(lane < ROT, swapped, 0.0)


def normalized(x_ref_rows, gain, offset):
    average = jnp.mean(x_ref_rows, -1, keepdims=True)
    centered = x_ref_rows - average
    variance = jnp.mean(centered * centered, -1, keepdims=True)
    return centered * lax.rsqrt(variance + EPSILON) * gain + offset


def start_layer(stream, x_ref, h_ref, gain_ref, offset_ref):
    length = h_ref.shape[0]
    step = min(128, length)

    @pl.loop(0, length // step)
    def _(index):
        rows = pl.ds(pl.multiple_of(index * step, step), step)
        values = stream[0][rows].astype(F32)
        if len(stream) > 1:
            values = values + (stream[1][rows] + stream[2][rows])
            x_ref[rows] = values
        h_ref[rows] = normalized(
            values, gain_ref[...].astype(F32), offset_ref[...].astype(F32)
        ).astype(BF16)


def gelu_parts(units):
    below = 0.5 + 0.5 * lax.erf(units * math.sqrt(0.5))
    return below, jnp.exp(-0.5 * units * units) * (1.0 / math.sqrt(2.0 * math.pi))


FF_BLOCK = 1024
FF_ROWS = 512


def mlp_forward_kernel(count, *refs):
    stream, refs = refs[:count], refs[count:]
    gain_ref, offset_ref, up_ref, bias_ref, down_ref, down_bias_ref = refs[:6]
    refs = refs[6:]
    x_ref = None
    if count > 1:
        x_ref, refs = refs[0], refs[1:]
    part_ref, h_ref, act_ref, slope_ref = refs
    step = pl.program_id(0)

    @pl.when(step == 0)
    def _():
        start_layer(stream, x_ref, h_ref, gain_ref, offset_ref)
        part_ref[...] = jnp.broadcast_to(down_bias_ref[...].astype(F32), part_ref.shape)

    for first in range(0, h_ref.shape[0], FF_ROWS):
        rows = slice(first, first + FF_ROWS)
        units = dot_nt(h_ref[rows], up_ref[0]) + bias_ref[0]
        below, density = gelu_parts(units)
        active = (units * below).astype(BF16)
        act_ref[0, rows] = active
        slope_ref[0, rows] = (below + units * density).astype(BF16)
        part_ref[rows] += dot_nn(active, down_ref[0, 0])


def plane_block(length, lanes):
    per_plane = 1024 // lanes
    return pl.BlockSpec((1, length, lanes), lambda j: (j // per_plane, 0, j % per_plane))


def mlp_forward(layer, stream, gain, offset, up, biases, down_weight, down_bias):
    length, width = stream[0].shape
    hidden = up.shape[1]
    blocks = hidden // FF_BLOCK
    state = jax.ShapeDtypeStruct((4, length, width), BF16)
    full = jax.ShapeDtypeStruct((length, width), F32)
    out_shape = [full, jax.ShapeDtypeStruct((length, width), BF16), state, state]
    out_specs = [whole((length, width)), whole((length, width))]
    out_specs += [plane_block(length, FF_BLOCK)] * 2
    if len(stream) > 1:
        out_shape, out_specs = [full] + out_shape, [whole((length, width))] + out_specs
    return pl.pallas_call(
        functools.partial(mlp_forward_kernel, len(stream)),
        grid=(blocks,),
        in_specs=[whole((length, width))] * len(stream)
        + [
            whole((1, width)),
            whole((1, width)),
            pl.BlockSpec((1, FF_BLOCK, width), lambda j: (layer, j, 0)),
            pl.BlockSpec((1, 1, FF_BLOCK), lambda j: (j, 0, 0)),
            pl.BlockSpec((1, 1, FF_BLOCK, width), lambda j: (0, layer, j, 0)),
            whole((1, width)),
        ],
        out_specs=out_specs,
        out_shape=out_shape,
        compiler_params=params(),
        name="mlp_forward",
    )(*stream, gain, offset, up, biases.reshape(blocks, 1, FF_BLOCK), down_weight, down_bias)


def add_stream(stream, result_ref):
    if stream:
        result_ref[...] = stream[0][...] + (stream[1][...] + stream[2][...])


def stream_specs(stream):
    specs = [
        pl.BlockSpec((part.shape[0] // 4, part.shape[1]), lambda j, *_: (j, 0)) for part in stream
    ]
    shapes = [jax.ShapeDtypeStruct(part.shape, F32) for part in stream[:1]]
    return specs, specs[:1], shapes


def mlp_backward_kernel(count, place_ref, *refs):
    stream, refs = refs[:count], refs[count:]
    grad_ref, h_ref, act_ref, slope_ref, down_ref, up_ref = refs[:6]
    result_ref, refs = (refs[6], refs[7:]) if count else (None, refs[6:])
    part_ref, along_x, kept_x, along_y, kept_y, along_z, kept_z, bias_ref = refs[:8]
    grad_t, h_t, units = refs[8:]
    del along_z, kept_z
    step = pl.program_id(0)
    add_stream(stream, result_ref)

    @pl.when(step == 0)
    def _():
        grad_t[...] = grad_ref[...].T
        h_t[...] = h_ref[...].T
        part_ref[...] = jnp.zeros_like(part_ref)

    bias = jnp.zeros((1, FF_BLOCK), F32)
    for first in range(0, h_ref.shape[0], ROWS):
        rows = slice(first, first + ROWS)
        grad_act = dot_nt(grad_ref[rows], down_ref[0, 0])
        grad_unit = (grad_act * slope_ref[0, rows].astype(F32)).astype(BF16)
        bias += jnp.sum(grad_unit.astype(F32), axis=0, keepdims=True)
        units[rows] = grad_unit
        part_ref[rows] += dot_nn(grad_unit, up_ref[0])
    bias_ref[pl.ds(step, 1)] = bias

    def block(y, x):
        return pl.ds(pl.multiple_of((2 * y + x) * WIDE, WIDE), WIDE)

    near_x, near_y = place_ref[0], place_ref[1]
    for first in range(0, h_t.shape[0], ROWS):
        rows = slice(first, first + ROWS)
        for side in range(2):
            for target, x in ((along_x, 1 - near_x), (kept_x, near_x)):
                target[0, side, rows] = dot_nn(grad_t[rows], act_ref[0, :, block(side, x)])
            for target, y in ((along_y, 1 - near_y), (kept_y, near_y)):
                target[0, side, rows] = dot_nn(h_t[rows], units[:, block(y, side)])


def halves_of(width):
    shapes = ((4, 2, width, WIDE),) * 4 + ((2, 4, width, WIDE),) * 2
    return [jax.ShapeDtypeStruct(shape, F32) for shape in shapes]


def mlp_backward(layer, place, grad, h, act, slope, down_weight, up, stream=()):
    length, width = h.shape
    hidden = up.shape[1]
    blocks = hidden // FF_BLOCK
    pair = pl.BlockSpec((1, 2, width, WIDE), lambda j, *_: (j, 0, 0, 0))
    plane = pl.BlockSpec((1, length, FF_BLOCK), lambda j, *_: (j, 0, 0))
    stream_in, stream_out, stream_shape = stream_specs(stream)
    return pl.pallas_call(
        functools.partial(mlp_backward_kernel, len(stream)),
        grid_spec=pltpu.PrefetchScalarGridSpec(
            num_scalar_prefetch=1,
            grid=(blocks,),
            in_specs=stream_in
            + [
                whole((length, width)),
                whole((length, width)),
                plane,
                plane,
                pl.BlockSpec((1, 1, FF_BLOCK, width), lambda j, *_: (0, layer, j, 0)),
                pl.BlockSpec((1, FF_BLOCK, width), lambda j, *_: (layer, j, 0)),
            ],
            out_specs=stream_out
            + [whole((length, width))]
            + [pair] * 4
            + [pl.BlockSpec(memory_space=pl.ANY)] * 2
            + [whole((blocks, FF_BLOCK))],
            scratch_shapes=[
                pltpu.VMEM((width, length), BF16),
                pltpu.VMEM((width, length), BF16),
                pltpu.VMEM((length, FF_BLOCK), BF16),
            ],
        ),
        out_shape=stream_shape
        + [jax.ShapeDtypeStruct((length, width), F32)]
        + halves_of(width)
        + [jax.ShapeDtypeStruct((blocks, FF_BLOCK), F32)],
        compiler_params=params(),
        name="mlp_backward",
    )(place, *stream, grad, h, act, slope, down_weight, up)


def head_sums(values, ones):
    upper, lower = split(values)
    return dot_nn(upper, ones) + dot_nn(lower, ones)


def same_head_ones():
    same = row_index(WIDE, WIDE) // DH == lane_index(WIDE, WIDE) // DH
    return jnp.where(same, 1.0, 0.0).astype(BF16)


def document_of(starts_ref, positions):
    return sum((starts_ref[0, i] <= positions).astype(jnp.int32) for i in range(starts_ref.shape[1]))


def write_mask(starts_ref, mask_ref, flipped):
    for first in range(0, mask_ref.shape[0], ROWS):
        lanes = lane_index(1, ROWS) + first
        own = row_index(ROWS, 1) + first
        order = (own <= lanes) if flipped else (lanes <= own)
        seen = (document_of(starts_ref, own) == document_of(starts_ref, lanes)) & order
        mask_ref[first : first + ROWS] = jnp.where(seen, 1.0, 0.0).astype(BF16)


def document_edges(starts_ref, length):
    edges = []
    for first in range(0, length, ROWS):
        rows = document_of(starts_ref, row_index(ROWS, 1) + first)
        here = document_of(starts_ref, first)
        later = document_of(starts_ref, first + ROWS)
        edges.append((rows == here, rows == later, here == later))
    return edges


def wide_rotary(cosine_ref, sine_ref, rows):
    return tuple(
        jnp.concatenate([ref[rows]] * (WIDE // PAIR), axis=1) for ref in (cosine_ref, sine_ref)
    )


def attention_forward_kernel(count, *refs):
    stream, refs = refs[:count], refs[count:]
    starts_ref, gain_ref, offset_ref, weight_ref, bias_ref, out_bias_ref = refs[:6]
    upper_ref, lower_ref, scale_ref, cosine_ref, sine_ref = refs[6:11]
    refs = refs[11:]
    x_ref = None
    if count > 1:
        x_ref, refs = refs[0], refs[1:]
    part_ref, h_ref, state_ref, mixed_ref, mask_ref = refs
    length = h_ref.shape[0]

    @pl.when(pl.program_id(0) == 0)
    def _():
        start_layer(stream, x_ref, h_ref, gain_ref, offset_ref)
        write_mask(starts_ref, mask_ref, False)
        part_ref[...] = jnp.broadcast_to(out_bias_ref[...], part_ref.shape)

    ones = same_head_ones()
    table_up, table_low = upper_ref[0, 0], lower_ref[0, 0]

    def features(values, rows):
        upper, lower = split(turn(values, *wide_rotary(cosine_ref, sine_ref, rows)))
        return dot_nn(upper, table_up) + (dot_nn(lower, table_up) + dot_nn(upper, table_low))

    for first in range(0, length, ROWS):
        rows = slice(first, first + ROWS)
        queries, keys, values = [
            dot_nt(h_ref[rows], weight_ref[0, 0, kind, 0]) + bias_ref[kind, 0] for kind in range(3)
        ]
        state_ref[0, rows] = jnp.exp(features(queries, rows)).astype(BF16)
        logs = features(keys, rows) - (0.5 / math.sqrt(DH)) * head_sums(keys * keys, ones)
        state_ref[1, rows] = (scale_ref[0, 0] * jnp.exp(logs)).astype(BF16)
        state_ref[2, rows] = keys.astype(BF16)
        state_ref[3, rows] = values.astype(BF16)

    zero = jnp.zeros((), BF16)
    one = jnp.ones((), BF16)
    left = lane_index(ROWS, PAIR) < DH
    row, lane = row_index(PAIR, 2 * PAIR), lane_index(PAIR, 2 * PAIR)
    same = row // DH == lane // PAIR
    edges = document_edges(starts_ref, length)
    for pair in range(WIDE // PAIR):
        lanes = slice(pair * PAIR, (pair + 1) * PAIR)
        before = None
        for block, (same_first, same_next, goes_on) in enumerate(edges):
            rows = slice(block * ROWS, (block + 1) * ROWS)
            seen = mask_ref[rows] > zero
            queries, keys = state_ref[0, rows, lanes], state_ref[1, rows, lanes]
            values = [jnp.where(own, state_ref[3, rows, lanes], one) for own in (left, ~left)]
            if block > 0:
                earlier = dot_nn(queries, before.astype(BF16))
                earlier = jnp.where(same_first, earlier, 0.0)
            sums = []
            for head, own in enumerate((left, ~left)):
                scores = dot_nt(queries, jnp.where(own, keys, zero)).astype(BF16)
                total = dot_nn(jnp.where(seen, scores, zero), values[head])
                if block > 0:
                    total = total + earlier[:, head * PAIR : (head + 1) * PAIR]
                sums.append(total)
            if block + 1 < len(edges):
                kept = jnp.where(same_next, keys, zero)
                added = jnp.where(same, dot_tn(kept, jnp.concatenate(values, axis=1)), 0.0)
                if block > 0:
                    added = added + jnp.where(goes_on, before, 0.0)
                before = added
            numer = jnp.where(left, sums[0], sums[1])
            denom = jnp.where(left, pltpu.roll(sums[0], DH, 1), pltpu.roll(sums[1], DH, 1))
            inverse = 1.0 / denom
            mixed_ref[0, rows, lanes] = (numer * inverse).astype(BF16)
            mixed_ref[1, rows, lanes], mixed_ref[2, rows, lanes] = split(inverse)
    for first in range(0, length, ROWS):
        rows = slice(first, first + ROWS)
        part_ref[rows] += dot_nn(mixed_ref[0, rows], weight_ref[0, 0, 3, 0])


def kinds_of(weight):
    return weight.reshape(weight.shape[:2] + (4, QUADS, WIDE, weight.shape[3]))


def attention_forward(layer, stream, starts, gain, offset, weight, biases, tables, rotary):
    length, width = stream[0].shape
    full = jax.ShapeDtypeStruct((length, width), F32)
    state = jax.ShapeDtypeStruct((4, length, width), BF16)
    out_shape = [full, jax.ShapeDtypeStruct((length, width), BF16), state, state]
    four = pl.BlockSpec((4, length, WIDE), lambda g: (0, 0, g))
    out_specs = [whole((length, width)), whole((length, width)), four, four]
    if len(stream) > 1:
        out_shape, out_specs = [full] + out_shape, [whole((length, width))] + out_specs
    return pl.pallas_call(
        functools.partial(attention_forward_kernel, len(stream)),
        grid=(QUADS,),
        in_specs=[whole((length, width))] * len(stream)
        + [
            pl.BlockSpec(memory_space=pltpu.SMEM),
            whole((1, width)),
            whole((1, width)),
            pl.BlockSpec((1, 1, 4, 1, WIDE, width), lambda g: (0, layer, 0, g, 0, 0)),
            pl.BlockSpec((4, 1, 1, WIDE), lambda g: (0, g, 0, 0)),
            whole((1, width)),
            pl.BlockSpec((1, 1, WIDE, WIDE), lambda g: (layer, g, 0, 0)),
            pl.BlockSpec((1, 1, WIDE, WIDE), lambda g: (layer, g, 0, 0)),
            pl.BlockSpec((1, 1, 1, WIDE), lambda g: (layer, g, 0, 0)),
            whole((length, PAIR)),
            whole((length, PAIR)),
        ],
        out_specs=out_specs,
        out_shape=out_shape,
        scratch_shapes=[pltpu.VMEM((length, ROWS), BF16)],
        compiler_params=params(),
        name="attention_forward",
    )(
        *stream, starts, gain, offset, kinds_of(weight),
        biases.reshape(4, QUADS, 1, WIDE), biases[None, 3 * width :], *tables, *rotary,
    )


def attention_backward_kernel(count, place_ref, *refs):
    stream, refs = refs[:count], refs[count:]
    starts_ref, grad_ref, h_ref, state_ref, mixed_ref, table_ref = refs[:6]
    cosine_ref, sine_ref, weight_ref = refs[6:9]
    result_ref, refs = (refs[9], refs[10:]) if count else (None, refs[9:])
    part_ref, along_x, kept_x, along_y, kept_y, along_z, kept_z, bias_ref = refs[:8]
    mask_ref, upright, numer_ref, feat_ref, flow = refs[8:]
    del along_x, kept_x, along_y, kept_y
    group = pl.program_id(0)
    length, width = h_ref.shape
    add_stream(stream, result_ref)

    @pl.when(pl.program_id(0) == 0)
    def _():
        write_mask(starts_ref, mask_ref, True)
        upright[0] = h_ref[...].T
        upright[1] = grad_ref[...].T
        part_ref[...] = jnp.zeros_like(part_ref)

    row, lane = row_index(WIDE, WIDE), lane_index(WIDE, WIDE)
    partner = (row // PAIR == lane // PAIR) & (row // DH != lane // DH)
    partner = jnp.where(partner, 1.0, 0.0).astype(BF16)
    zero = jnp.zeros((), BF16)
    one = jnp.ones((), BF16)
    for first in range(0, length, ROWS):
        rows = slice(first, first + ROWS)
        grad = dot_nt(grad_ref[rows], weight_ref[0, 0, 3, 0]).astype(BF16).astype(F32)
        inverse = mixed_ref[1, rows].astype(F32) + mixed_ref[2, rows].astype(F32)
        scaled = grad * inverse
        upper, lower = split(-head_sums(scaled * mixed_ref[0, rows].astype(F32), partner))
        numer = scaled.astype(BF16)
        lane = lane_index(ROWS, WIDE)
        spare = jnp.where(lane % DH == 0, upper, jnp.where(lane % DH == 1, lower, zero))
        left = lane % PAIR < DH
        numer_ref[0, rows] = jnp.where(left, numer, spare)
        numer_ref[1, rows] = jnp.where(left, spare, numer)

    left = lane_index(ROWS, PAIR) < DH
    spare = jnp.where(lane_index(ROWS, PAIR) % DH < 2, one, zero)
    row, lane = row_index(2 * PAIR, PAIR), lane_index(2 * PAIR, PAIR)
    same = row // PAIR == lane // DH
    row, lane = row_index(PAIR, PAIR), lane_index(PAIR, PAIR)
    same_head = row // DH == lane // DH
    edges = document_edges(starts_ref, length)
    blocks = range(len(edges))

    def both(upper_and_lower, sums):
        upper, lower = split(sums)
        return dot_nn(upper_and_lower, upper) + dot_nn(upper_and_lower, lower)

    for pair in range(WIDE // PAIR):
        lanes = slice(pair * PAIR, (pair + 1) * PAIR)

        def rows_of_block(block):
            rows = slice(block * ROWS, (block + 1) * ROWS)
            numers = [numer_ref[head, rows, lanes] for head in range(2)]
            values = state_ref[3, rows, lanes]
            values = [jnp.where(own, values, spare) for own in (left, ~left)]
            return rows, state_ref[0, rows, lanes], state_ref[1, rows, lanes], values, numers

        before, after = {}, {}
        for block in blocks[1:]:
            rows, queries, keys, values, numers = rows_of_block(block - 1)
            _, same_next, goes_on = edges[block - 1]
            kept = jnp.where(same_next, keys, zero)
            added = jnp.where(same, dot_tn(jnp.concatenate(values, axis=1), kept), 0.0)
            if block > 1:
                added = added + jnp.where(goes_on, before[block - 1], 0.0)
            before[block] = added
        for block in blocks[::-1][:-1]:
            rows, queries, keys, values, numers = rows_of_block(block)
            same_first, _, goes_on = edges[block]
            kept = jnp.where(same_first, queries, zero)
            keys_sum = jnp.where(same, dot_tn(jnp.concatenate(numers, axis=1), kept), 0.0)
            values_sum = dot_tn(kept, jnp.where(left, numers[0], numers[1]))
            values_sum = jnp.where(same_head, values_sum, 0.0)
            if block + 1 < len(edges):
                keys_sum = keys_sum + jnp.where(goes_on, after[block + 1][0], 0.0)
                values_sum = values_sum + jnp.where(goes_on, after[block + 1][1], 0.0)
            after[block] = (keys_sum, values_sum)
        for block in blocks:
            rows, queries, keys, values, numers = rows_of_block(block)
            same_first, same_next, _ = edges[block]
            seen = mask_ref[rows] > zero
            numer = jnp.where(left, numers[0], numers[1])
            grads = []
            grad_query = None
            for head, own in enumerate((left, ~left)):
                own_keys = jnp.where(own, keys, zero)
                scores = dot_nt(own_keys, queries).astype(BF16)
                grad_value = dot_nn(jnp.where(seen, scores, zero), numer)
                grad_scores = dot_nt(values[head], numers[head]).astype(BF16)
                grad_scores = jnp.where(seen, grad_scores, zero)
                grads.append((grad_value, dot_nn(grad_scores, queries)))
                from_head = dot_tn(grad_scores, own_keys)
                grad_query = from_head if head == 0 else grad_query + from_head
            grad_value = jnp.where(left, grads[0][0], grads[1][0])
            grad_key = jnp.where(left, grads[0][1], grads[1][1])
            if block + 1 < len(edges):
                keys_sum, values_sum = after[block + 1]
                late = both(jnp.concatenate(values, axis=1), keys_sum)
                grad_key = grad_key + jnp.where(same_next, late, 0.0)
                late = dot_nn(keys, values_sum.astype(BF16))
                grad_value = grad_value + jnp.where(same_next, late, 0.0)
            if block > 0:
                early = both(jnp.concatenate(numers, axis=1), before[block])
                grad_query = grad_query + jnp.where(same_first, early, 0.0)
            flow[2, rows, lanes] = grad_value.astype(BF16)
            feat_ref[1, rows, lanes] = (grad_key * keys.astype(F32)).astype(BF16)
            feat_ref[0, rows, lanes] = (grad_query * queries.astype(F32)).astype(BF16)

    ones = same_head_ones()
    table = table_ref[0, 0]
    sums = [jnp.zeros((1, WIDE), F32)] * 3
    for first in range(0, length, ROWS):
        rows = slice(first, first + ROWS)
        cosine, sine = wide_rotary(cosine_ref, sine_ref, rows)
        flow[0, rows] = turn_back(dot_nt(feat_ref[0, rows], table), cosine, sine).astype(BF16)
        shrink = dot_nn(feat_ref[1, rows], ones) * (1.0 / math.sqrt(DH))
        turned = turn_back(dot_nt(feat_ref[1, rows], table), cosine, sine)
        flow[1, rows] = (turned - state_ref[2, rows].astype(F32) * shrink).astype(BF16)
        total = part_ref[rows]
        for kind in range(3):
            block = flow[kind, rows]
            sums[kind] = sums[kind] + jnp.sum(block.astype(F32), axis=0, keepdims=True)
            total = total + dot_nn(block, weight_ref[0, 0, kind, 0])
        part_ref[rows] = total
    for kind in range(3):
        bias_ref[kind : kind + 1] = sums[kind]
    lanes = pl.ds(pl.multiple_of(group * WIDE, WIDE), WIDE)
    bias_ref[3:4] = jnp.sum(grad_ref[:, lanes].astype(F32), axis=0, keepdims=True)
    flow[3] = mixed_ref[0]
    for first in range(0, width, ROWS):
        rows = slice(first, first + ROWS)
        for far in range(2):
            for target, near in ((along_z, 1 - place_ref[2]), (kept_z, place_ref[2])):
                kind = 2 * far + near
                target[far, 0, rows] = dot_nn(upright[kind // 3, rows], flow[kind])


def attention_backward(
    layer, place, starts, grad, h, state, mixed, tables, rotary, weight, stream=()
):
    _, length, width = state.shape
    four = pl.BlockSpec((4, length, WIDE), lambda g, *_: (0, 0, g))
    halves = pl.BlockSpec((2, 1, width, WIDE), lambda g, *_: (0, g, 0, 0))
    stream_in, stream_out, stream_shape = stream_specs(stream)
    return pl.pallas_call(
        functools.partial(attention_backward_kernel, len(stream)),
        grid_spec=pltpu.PrefetchScalarGridSpec(
            num_scalar_prefetch=1,
            grid=(QUADS,),
            in_specs=stream_in
            + [
                pl.BlockSpec(memory_space=pltpu.SMEM),
                whole((length, width)),
                whole((length, width)),
                four,
                four,
                pl.BlockSpec((1, 1, WIDE, WIDE), lambda g, *_: (layer, g, 0, 0)),
                whole((length, PAIR)),
                whole((length, PAIR)),
                pl.BlockSpec((1, 1, 4, 1, WIDE, width), lambda g, *_: (0, layer, 0, g, 0, 0)),
            ],
            out_specs=stream_out
            + [whole((length, width))]
            + [pl.BlockSpec(memory_space=pl.ANY)] * 4
            + [halves, halves]
            + [pl.BlockSpec((4, WIDE), lambda g, *_: (0, g))],
            scratch_shapes=[
                pltpu.VMEM((length, ROWS), BF16),
                pltpu.VMEM((2, width, length), BF16),
                pltpu.VMEM((2, length, WIDE), BF16),
                pltpu.VMEM((2, length, WIDE), BF16),
                pltpu.VMEM((4, length, WIDE), BF16),
            ],
        ),
        out_shape=stream_shape
        + [jax.ShapeDtypeStruct((length, width), F32)]
        + halves_of(width)
        + [jax.ShapeDtypeStruct((4, width), F32)],
        compiler_params=params(),
        name="attention_backward",
    )(place, *stream, starts, grad, h, state, mixed, tables[0], *rotary, kinds_of(weight))


def norm_gradient(values, incoming, grad, gain, sums_ref):
    average = jnp.mean(values, -1, keepdims=True)
    centered = values - average
    variance = jnp.mean(centered * centered, -1, keepdims=True)
    inverse = lax.rsqrt(variance + EPSILON)
    unit = centered * inverse
    grad_unit = incoming * gain
    first = jnp.mean(grad_unit, -1, keepdims=True)
    second = jnp.mean(grad_unit * unit, -1, keepdims=True)
    sums_ref[0:1] += jnp.sum(incoming * unit, axis=0, keepdims=True)
    sums_ref[1:2] += jnp.sum(incoming, axis=0, keepdims=True)
    sums_ref[2:3] += jnp.sum(grad, axis=0, keepdims=True)
    return grad + inverse * (grad_unit - first - unit * second)


def norm_backward_kernel(x_ref, own_ref, other_ref, grad_ref, gain_ref, out_ref, sums_ref):
    @pl.when(pl.program_id(0) == 0)
    def _():
        sums_ref[...] = jnp.zeros_like(sums_ref)

    out = norm_gradient(
        x_ref[...].astype(F32),
        own_ref[...] + other_ref[...],
        grad_ref[...].astype(F32),
        gain_ref[...].astype(F32),
        sums_ref,
    )
    out_ref[...] = out.astype(out_ref.dtype)


def norm_backward(x, own, other, grad, gain, kind):
    length, width = own.shape
    block = pl.BlockSpec((ROWS, width), lambda i: (i, 0))
    return pl.pallas_call(
        norm_backward_kernel,
        grid=(length // ROWS,),
        in_specs=[block, block, block, block, whole((1, width))],
        out_specs=[block, whole((8, width))],
        out_shape=[
            jax.ShapeDtypeStruct((length, width), kind),
            jax.ShapeDtypeStruct((8, width), F32),
        ],
        compiler_params=params(),
        name="norm_backward",
    )(x, own, other, grad, gain)


MESH = pl.DeviceIdType.MESH
UNIT = 16
SLOTS = 4
LAG = 1
JOB = 128


class Flow(NamedTuple):
    order: tuple
    core: int
    family: int
    layer: int
    row: int
    units: int
    start: int
    place: int


def flows_of(width, layer, start):
    rows = width // 2
    kinds = (
        ((0, 1, 2, 3), 1, 0, 0, 0),
        ((1, 0, 2, 3), 1, 1, 0, 1),
        ((0, 1, 2, 3), 1, 0, 1, 2),
        ((1, 0, 2, 3), 1, 1, 1, 3),
        ((2, 0, 1, 3), 0, 2, 0, 0),
        ((2, 1, 0, 3), 0, 2, 1, 1),
    )
    return [
        Flow(order, core, family, layer, part * rows, rows // UNIT, start, 4 * layer + place)
        for order, core, family, part, place in kinds
    ]


def bit_of(index, bit):
    return (index // (1 << bit)) % 2


def flip(index, bit):
    return index + (1 << bit) * (1 - 2 * bit_of(index, bit))


def finish_kernel(
    bits, flows,
    kept_x1, kept_y1, kept_z1, came_x1, came_y1, came_z1,
    kept_x0, kept_y0, kept_z0, sent_x0, sent_y0, sent_z0,
    part_ref, tokens_ref, grad_ref,
    bias0_ref, bias1_ref, sums1_ref, gain_ref,
    weight_out, up_out, small_out, grad_out,
    weight_sum, up_sum, up_turned, up_came, part, part_came, tokens, grad, sums,
    *scratch,
):
    stages = bits
    kept = ((kept_x1, kept_y1, kept_z1), (kept_x0, kept_y0, kept_z0))
    moved = ((came_x1, came_y1, came_z1), (sent_x0, sent_y0, sent_z0))
    places = 1 + max(flow.place for flow in flows)
    held, scratch = scratch[: places * (stages + 1)], scratch[places * (stages + 1) :]
    held = [held[f * (stages + 1) : (f + 1) * (stages + 1)] for f in range(places)]
    small, small_came = scratch[: stages + 1], scratch[stages + 1 : 2 * stages + 1]
    load_sem, send_sem, recv_sem, credit, small_send, small_recv, job_sem, near_send, near_recv = (
        scratch[2 * stages + 1 :]
    )
    me, core = lax.axis_index("batch"), lax.axis_index("stream")

    barrier = pltpu.get_barrier_semaphore()
    for bit in range(bits):
        pl.semaphore_signal(
            barrier, inc=1, device_id={"batch": flip(me, bit)}, device_id_type=MESH
        )
    pl.semaphore_signal(barrier, inc=1, device_id={"stream": 1 - core}, device_id_type=MESH)
    pl.semaphore_wait(barrier, bits + 1)

    exchange = pltpu.make_async_remote_copy(
        src_ref=part_ref,
        dst_ref=part_came,
        send_sem=near_send.at[2],
        recv_sem=near_recv.at[2],
        device_id={"stream": 1 - core},
        device_id_type=MESH,
    )
    loads = [
        pltpu.make_async_copy(source, target, job_sem.at[index])
        for index, (source, target) in enumerate(
            ((part_ref, part), (tokens_ref, tokens), (grad_ref, grad))
        )
    ]
    store = pltpu.make_async_copy(part, grad_out, job_sem.at[len(loads)])
    exchange.start()
    for copy in loads:
        copy.start()
    jobs = part.shape[0] // JOB
    norm_start = 3
    small_start = norm_start + jobs
    turn_start = max(flow.start + flow.units for flow in flows if flow.layer == 0) + stages + 1

    def norm_job(index):
        rows = pl.ds(pl.multiple_of((index - norm_start) * JOB, JOB), JOB)

        @pl.when(index == norm_start)
        def _():
            exchange.wait()
            for copy in loads:
                copy.wait()
            sums[...] = jnp.zeros_like(sums)

        part[rows] = norm_gradient(
            tokens[rows].astype(F32),
            part[rows] + part_came[rows],
            grad[rows].astype(F32),
            gain_ref[...].astype(F32),
            sums,
        )

    def near_copy(layer):
        return pltpu.make_async_remote_copy(
            src_ref=up_turned.at[layer],
            dst_ref=up_came.at[layer],
            send_sem=near_send.at[layer],
            recv_sem=near_recv.at[layer],
            device_id={"stream": 0},
            device_id_type=MESH,
        )

    def turn_weights(layer):
        weight_out[len(moved) - 1 - layer] = weight_sum[layer].T

        @pl.when(core == 1)
        def _():
            up_turned[layer] = up_sum[layer, :, : WIDE // 2].T
            near_copy(layer).start()
            up_out[len(moved) - 1 - layer] = up_sum[layer, :, WIDE // 2 :].T

    def small_copy(stage):
        return pltpu.make_async_remote_copy(
            src_ref=small[stage],
            dst_ref=small_came[stage],
            send_sem=small_send.at[stage],
            recv_sem=small_recv.at[stage],
            device_id={"batch": flip(me, stage)},
            device_id_type=MESH,
        )

    def small_step(stage):
        if stage == 0:
            store.start()
            rows = bias0_ref.shape[0]
            small[0][0:rows] = bias0_ref[...]
            small[0][rows : 2 * rows] = bias1_ref[...]
            small[0][2 * rows : 2 * rows + 8] = sums1_ref[...]
            small[0][2 * rows + 8 : 2 * rows + 16] = sums[...]
        else:
            small_copy(stage - 1).wait()
            small[stage][...] = small[stage - 1][...] + small_came[stage - 1][...]
        if stage < stages:
            small_copy(stage).start()
        else:
            small_out[...] = small[stage][...]

    def view(order, stage, mine):
        left = sorted(set(range(bits)) - set(order[:stage]), reverse=True)
        pick = bit_of(me, order[stage])
        pick = pick if mine else 1 - pick
        return tuple(pick if bit == order[stage] else slice(None) for bit in left)

    def remote(flow, stage, slot, source):
        place = flow.place
        return pltpu.make_async_remote_copy(
            src_ref=source,
            dst_ref=held[place][stage + 1].at[slot],
            send_sem=send_sem.at[place, stage, slot],
            recv_sem=recv_sem.at[place, stage, slot],
            device_id={"batch": flip(me, flow.order[stage])},
            device_id_type=MESH,
        )

    def sent_from(flow, stage, slot):
        if stage == 0:
            return held[flow.place][0].at[slot]
        return held[flow.place][stage].at[(slot,) + view(flow.order, stage, False)]

    def load(flow, slot, source):
        place = flow.place
        return pltpu.make_async_copy(source, held[place][0].at[slot], load_sem.at[place, slot])

    def load_came(flow, slot, source):
        return pltpu.make_async_copy(
            source, held[flow.place][1].at[slot], recv_sem.at[flow.place, 0, slot]
        )

    def return_credit(flow, stage, unit):
        if stage == 0 and flow.layer == 0:
            return

        @pl.when(unit + SLOTS < flow.units)
        def _():
            pl.semaphore_signal(
                credit.at[flow.place, stage],
                inc=1,
                device_id={"batch": flip(me, flow.order[stage])},
                device_id_type=MESH,
            )

    def take_credit(flow, stage, unit):
        @pl.when(unit >= SLOTS)
        def _():
            pl.semaphore_wait(credit.at[flow.place, stage], 1)

    def begin(flow, unit):
        slot = lax.rem(unit, SLOTS)
        at = (slice(None),) * (bits - 1)
        at += (pl.ds(pl.multiple_of(flow.row + unit * UNIT, UNIT), UNIT),)
        load(flow, slot, kept[flow.layer][flow.family].at[at]).start()
        source = moved[flow.layer][flow.family].at[at]
        if flow.layer == 0:
            load_came(flow, slot, source).start()
        else:
            take_credit(flow, 0, unit)
            remote(flow, 0, slot, source).start()

    def advance(flow, stage, unit):
        slot = lax.rem(unit, SLOTS)
        buffers, begun = held[flow.place], flow.layer == 0
        copy = remote(flow, stage - 1, slot, sent_from(flow, stage - 1, slot))
        if stage == 1 and begun:
            load_came(flow, slot, buffers[0].at[slot]).wait()
        else:
            copy.wait_recv()
        if stage == 1:
            load(flow, slot, buffers[1].at[slot]).wait()
            mine = buffers[0][slot]
        else:
            mine = buffers[stage - 1][(slot,) + view(flow.order, stage - 1, True)]
        value = buffers[stage][slot] + mine
        if stage < stages:
            buffers[stage][slot] = value
            take_credit(flow, stage, unit)
            remote(flow, stage, slot, sent_from(flow, stage, slot)).start()
        else:
            target = up_sum if flow.family == 1 else weight_sum
            at = pl.ds(pl.multiple_of(flow.row + unit * UNIT, UNIT), UNIT)
            target[flow.layer, at] = value
        if stage > 1 or not begun:
            copy.wait_send()
        if stage >= 2:
            return_credit(flow, stage - 2, unit)
        if stage == stages:
            return_credit(flow, stage - 1, unit)

    def within(flow, unit):
        return (unit >= 0) & (unit < flow.units) & (core == flow.core)

    def step(index, carry):
        for flow in flows:
            unit = index - flow.start
            pl.when(within(flow, unit))(functools.partial(begin, flow, unit))
        for flow in flows:
            for stage in range(1, stages + 1):
                unit = index - flow.start - LAG * stage
                pl.when(within(flow, unit))(functools.partial(advance, flow, stage, unit))
        pl.when((index >= norm_start) & (index < norm_start + jobs))(
            functools.partial(norm_job, index)
        )
        for stage in range(stages + 1):
            pl.when(index == small_start + 2 * stage)(functools.partial(small_step, stage))
        pl.when(index == turn_start)(functools.partial(turn_weights, 0))
        return carry

    last = max(flow.start + flow.units for flow in flows)
    lax.fori_loop(0, last + LAG * stages, step, 0)
    turn_weights(1)
    for layer in range(len(moved)):

        @pl.when(core == 0)
        def _():
            near_copy(layer).wait_recv()
            up_out[len(moved) - 1 - layer] = up_came[layer]

        @pl.when(core == 1)
        def _():
            near_copy(layer).wait_send()

    store.wait()


def finish(last, first, came, part, tokens, grad, biases, sums, gain):
    length, width = tokens.shape
    bits = 4
    split = (2,) * (bits - 1)
    flows = flows_of(width, 0, 0)
    flows += flows_of(width, 1, max(flow.start + flow.units for flow in flows))
    small = (2 * biases[0].shape[0] + 16, width)
    full = (length, width)
    scratch = [
        pltpu.VMEM((2, width, WIDE), F32),
        pltpu.VMEM((2, width, WIDE), F32),
        pltpu.VMEM((2, WIDE // 2, width), F32),
        pltpu.VMEM((2, WIDE // 2, width), F32),
        pltpu.VMEM(full, F32),
        pltpu.VMEM(full, F32),
        pltpu.VMEM(full, BF16),
        pltpu.VMEM(full, BF16),
        pltpu.VMEM((8, width), F32),
    ]
    places = 1 + max(flow.place for flow in flows)
    for _ in range(places):
        for stage in range(bits + 1):
            lead = (SLOTS,) + (2,) * (bits - 1 - max(stage - 1, 0))
            scratch.append(pltpu.VMEM(lead + (UNIT, WIDE), F32))
    scratch += [pltpu.VMEM(small, F32)] * (2 * bits + 1)
    scratch += [
        pltpu.SemaphoreType.DMA((places, SLOTS)),
        pltpu.SemaphoreType.DMA((places, bits, SLOTS)),
        pltpu.SemaphoreType.DMA((places, bits, SLOTS)),
        pltpu.SemaphoreType.REGULAR((places, bits)),
        pltpu.SemaphoreType.DMA((bits,)),
        pltpu.SemaphoreType.DMA((bits,)),
        pltpu.SemaphoreType.DMA((4,)),
        pltpu.SemaphoreType.DMA((3,)),
        pltpu.SemaphoreType.DMA((3,)),
    ]
    large = [last[1], last[3], last[5], *came, first[1], first[3], first[5]]
    large += [first[0], first[2], first[4]]
    large = [array.reshape(split + array.shape[2:]) for array in large]
    return pl.pallas_call(
        functools.partial(finish_kernel, bits, flows),
        in_specs=[pl.BlockSpec(memory_space=pltpu.HBM)] * (len(large) + 3)
        + [pl.BlockSpec(memory_space=pltpu.VMEM)] * 4,
        out_specs=[pl.BlockSpec(memory_space=pltpu.VMEM)] * 3
        + [pl.BlockSpec(memory_space=pltpu.HBM)],
        out_shape=[
            jax.ShapeDtypeStruct((2, WIDE, width), F32),
            jax.ShapeDtypeStruct((2, WIDE // 2, width), F32),
            jax.ShapeDtypeStruct(small, F32),
            jax.ShapeDtypeStruct(full, F32),
        ],
        scratch_shapes=scratch,
        compiler_params=pltpu.CompilerParams(
            collective_id=0, has_side_effects=True, vmem_limit_bytes=VMEM_LIMIT
        ),
        name="finish",
    )(*large, part, tokens, grad, biases[0], biases[1], sums, gain)


def send_first(halves):
    count = lax.axis_size("batch")
    received = []
    for bit, part in enumerate(halves[0::2]):
        stream = 0 if bit == 2 else 1
        pairs = [
            (2 * source + stream, 2 * flip(source, bit) + stream) for source in range(count)
        ]
        received.append(lax.ppermute(part, ("batch", "stream"), pairs))
    return received


def shards(
    tokens, cotangent, branch_weight, branch_bias, up_weight, down_bias,
    norm_gain, norm_bias, freq_seeds, doc_starts,
):
    is_attention = lax.axis_index("stream") == 0
    length, width = tokens.shape
    rotary = tuple(jnp.asarray(table) for table in rotary_rows(length))
    biases = branch_bias[0].astype(F32)
    tables = lax.cond(
        is_attention,
        lambda: tuple(feature_tables(freq_seeds)),
        lambda: (
            jnp.zeros((LAYERS, QUADS, WIDE, WIDE), BF16),
            jnp.zeros((LAYERS, QUADS, WIDE, WIDE), BF16),
            jnp.zeros((LAYERS, QUADS, 1, WIDE), F32),
        ),
    )
    swap = [(0, 1), (1, 0)]

    def attention(layer, stream):
        gain, offset = norm_gain[layer : layer + 1], norm_bias[layer : layer + 1]
        return tuple(
            attention_forward(
                layer, stream, doc_starts, gain, offset, branch_weight, biases[layer], tables,
                rotary,
            )
        )

    def feed_forward(layer, stream):
        gain, offset = norm_gain[layer : layer + 1], norm_bias[layer : layer + 1]
        return tuple(
            mlp_forward(
                layer, stream, gain, offset, up_weight, biases[layer], branch_weight,
                down_bias[layer : layer + 1],
            )
        )

    stream = (tokens,)
    inputs, kept = [], []
    for layer in range(LAYERS):
        *x, part, h, state, mixed = lax.cond(
            is_attention,
            functools.partial(attention, layer, stream),
            functools.partial(feed_forward, layer, stream),
        )
        inputs.append(x[0] if x else tokens)
        kept.append((h, state, mixed))
        stream = (inputs[-1], part, lax.ppermute(part, "stream", swap))
    result = stream[0] + (stream[1] + stream[2])

    count = lax.axis_size("batch")
    blocked = count == branch_weight.shape[2] // WIDE
    me = lax.axis_index("batch") if blocked else 0
    place = jnp.stack([jnp.asarray(bit_of(me, bit), jnp.int32) for bit in range(3)])

    def attention_back(layer, grad, stream):
        h, state, mixed = kept[layer]
        return attention_backward(
            layer, place, doc_starts, grad, h, state, mixed, tables, rotary, branch_weight, stream
        )

    def feed_forward_back(layer, grad, stream):
        h, act, slope = kept[layer]
        return mlp_backward(
            layer, place, grad, h, act, slope, branch_weight, up_weight, stream
        )

    def back(layer, grad, stream=()):
        *result, part, a, b, c, d, e, f, bias = lax.cond(
            is_attention,
            functools.partial(attention_back, layer, grad, stream),
            functools.partial(feed_forward_back, layer, grad, stream),
        )
        return *result, part, (a, b, c, d, e, f), bias

    def norm_back(layer, part, grad, kind):
        other = lax.ppermute(part, "stream", swap)
        return norm_backward(
            inputs[layer], part, other, grad, norm_gain[layer : layer + 1], kind
        )

    part1, halves1, bias1 = back(1, cotangent)
    if blocked:
        came = send_first(halves1)
    grad0, sums1 = norm_back(1, part1, cotangent, BF16)
    result, part0, halves0, bias0 = back(0, grad0, stream)
    if blocked:
        weight, up, small, input_grad = finish(
            halves1, halves0, came, part0, tokens, grad0, (bias0, bias1), sums1, norm_gain[:1]
        )
    else:
        input_grad, sums0 = norm_back(0, part0, grad0, F32)
        weight, up = scatter_rows((halves0, halves1))
        small = lax.psum(jnp.concatenate([bias0, bias1, sums1, sums0]), "batch")
    index, rows = lax.axis_index("batch"), bias0.shape[0]
    each, own = branch_weight.shape[2] // count, width // count
    biases = small[: 2 * rows].reshape(LAYERS, -1)
    sums = small[2 * rows :].reshape(LAYERS, 8, width)[::-1]
    sums = lax.dynamic_slice_in_dim(sums, index * own, own, axis=2)
    return (
        result,
        input_grad,
        weight[None],
        lax.dynamic_slice_in_dim(biases, index * each, each, axis=1)[None],
        up,
        sums[:, 2],
        sums[:, 0],
        sums[:, 1],
    )


def scatter_rows(layers):
    weights, ups = [], []
    for along_x, kept_x, along_y, kept_y, along_z, kept_z in layers:
        blocks = (-1,) + kept_x.shape[2:]
        weight = jnp.where(
            lax.axis_index("stream") == 1,
            jnp.stack([kept_x, along_x], axis=2).reshape(blocks),
            jnp.stack([kept_z, along_z], axis=1).reshape(blocks),
        )
        weight = rows_of(weight)
        up = rows_of(jnp.stack([kept_y, along_y], axis=1).reshape(blocks))
        up = jnp.where(lax.axis_index("stream") == 1, up, 0.0)
        weights.append(lax.psum_scatter(weight, "batch", scatter_dimension=0, tiled=True))
        ups.append(lax.psum_scatter(up, ("batch", "stream"), scatter_dimension=0, tiled=True))
    return jnp.stack(weights), jnp.stack(ups)


def rows_of(blocks):
    return jnp.transpose(blocks, (0, 2, 1)).reshape(-1, blocks.shape[1])


def solution(mesh):
    placed = (
        P("batch", None),
        P("batch", None),
        P("stream", None, None, None),
        P("stream", None, None),
        P(),
        P(),
        P(),
        P(),
        P(),
        P("batch", None),
    )
    return jax.shard_map(
        shards,
        mesh=mesh,
        in_specs=placed,
        out_specs=(
            P("batch", None),
            P("batch", None),
            P("stream", None, "batch", None),
            P("stream", None, "batch"),
            P(None, ("batch", "stream"), None),
            P(None, "batch"),
            P(None, "batch"),
            P(None, "batch"),
        ),
        check_vma=False,
    )
```

```python
import functools
import math
from typing import NamedTuple

import jax
import jax.numpy as jnp
import numpy as np
from jax import lax
from jax.experimental import pallas as pl
from jax.experimental.pallas import tpu as pltpu
from jax.sharding import PartitionSpec as P

HEADS = 16
DH = 64
ROT = 16
FEAT = 64
LAYERS = 2
EPSILON = 1e-05
HIGH = lax.Precision.HIGHEST
F32 = jnp.float32
BF16 = jnp.bfloat16
WIDE = 256
PAIR = 128
QUADS = HEADS * DH // WIDE
PAIRS = HEADS * DH // PAIR
ROWS = 256
VMEM_LIMIT = 56 * 1024 * 1024


def params():
    return pltpu.CompilerParams(vmem_limit_bytes=VMEM_LIMIT)


def whole(shape):
    zeros = (0,) * len(shape)
    return pl.BlockSpec(shape, lambda *_: zeros, pipeline_mode=pl.Buffered(1))


def dot_nn(left, right):
    return lax.dot_general(left, right, (((1,), (0,)), ((), ())), preferred_element_type=F32)


def dot_tn(left, right):
    return lax.dot_general(left, right, (((0,), (0,)), ((), ())), preferred_element_type=F32)


def dot_nt(left, right):
    return lax.dot_general(left, right, (((1,), (1,)), ((), ())), preferred_element_type=F32)


def split(values):
    upper = values.astype(BF16)
    return upper, (values - upper.astype(F32)).astype(BF16)


def lane_index(rows, lanes):
    return lax.broadcasted_iota(jnp.int32, (rows, lanes), 1)


def row_index(rows, lanes):
    return lax.broadcasted_iota(jnp.int32, (rows, lanes), 0)


def cosine_block():
    samples = np.arange(DH, dtype=np.float64)
    angles = math.pi * (samples[None, :] + 0.5) * samples[:, None] / DH
    table = np.cos(angles) * math.sqrt(2.0 / DH)
    table[0] *= math.sqrt(0.5)
    return np.kron(np.eye(WIDE // DH), table.T * DH ** (-0.25)).astype(np.float32)


def rotary_rows(length):
    position = np.arange(length, dtype=np.float32)
    inverse = (10000.0 ** (-np.arange(0, ROT, 2, dtype=np.float32) / ROT)).astype(np.float32)
    angles = position[:, None] * inverse[None, :]
    cosine, sine = np.cos(angles), np.sin(angles)
    rest = DH - ROT
    cosine_head = np.concatenate([cosine, cosine, np.ones((length, rest))], 1)
    sine_head = np.concatenate([-sine, sine, np.zeros((length, rest))], 1)
    repeat = PAIR // DH
    return (
        np.tile(cosine_head, (1, repeat)).astype(np.float32),
        np.tile(sine_head, (1, repeat)).astype(np.float32),
    )


def tables_kernel(seeds_ref, cosine_ref, upper_ref, lower_ref, weight_ref):
    own = row_index(WIDE, DH) % DH == lane_index(WIDE, DH)
    feature = lane_index(WIDE, PAIR) % FEAT
    same_head = row_index(WIDE, WIDE) // DH == lane_index(WIDE, WIDE) // FEAT
    for group in range(QUADS):
        heads = [
            jnp.broadcast_to(seeds_ref[0, head : head + 1], (DH, DH))
            for head in range(group * QUADS, (group + 1) * QUADS)
        ]
        seeds = jnp.where(own, jnp.concatenate(heads, axis=0), 0)
        seeds = jnp.sum(seeds.astype(F32), axis=1, keepdims=True).astype(jnp.int32)
        lattice = (feature * seeds) & (FEAT - 1)
        prob = (lattice.astype(F32) + 0.5) * (1.0 / FEAT)
        radius = jnp.sqrt(-2.0 * jnp.log(jnp.minimum(prob, 1.0 - prob)))
        above = 2.515517 + 0.802853 * radius + 0.010328 * radius * radius
        below = (
            1.0
            + 1.432788 * radius
            + 0.189269 * radius * radius
            + 0.001308 * radius * radius * radius
        )
        magnitude = radius - above / below
        omega = jnp.where(prob > 0.5, magnitude, -magnitude)
        omega = jnp.where(same_head, jnp.concatenate([omega] * (WIDE // PAIR), axis=1), 0.0)
        project = jnp.dot(cosine_ref[...], omega, precision=HIGH, preferred_element_type=F32)
        upper_ref[0, group], lower_ref[0, group] = split(project)
        grown = jnp.exp(-0.5 / DH * jnp.sum(omega * omega, axis=0, keepdims=True))
        total = jnp.dot(
            jnp.broadcast_to(grown, (8, WIDE)),
            same_head.astype(F32),
            precision=HIGH,
            preferred_element_type=F32,
        )
        weight_ref[0, group] = FEAT * grown / total[:1]


def feature_tables(seeds):
    return pl.pallas_call(
        tables_kernel,
        grid=(LAYERS,),
        in_specs=[
            pl.BlockSpec((1, HEADS, DH), lambda l: (l, 0, 0)),
            whole((WIDE, WIDE)),
        ],
        out_specs=[
            pl.BlockSpec((1, QUADS, WIDE, WIDE), lambda l: (l, 0, 0, 0)),
            pl.BlockSpec((1, QUADS, WIDE, WIDE), lambda l: (l, 0, 0, 0)),
            pl.BlockSpec((1, QUADS, 1, WIDE), lambda l: (l, 0, 0, 0)),
        ],
        out_shape=[
            jax.ShapeDtypeStruct((LAYERS, QUADS, WIDE, WIDE), BF16),
            jax.ShapeDtypeStruct((LAYERS, QUADS, WIDE, WIDE), BF16),
            jax.ShapeDtypeStruct((LAYERS, QUADS, 1, WIDE), F32),
        ],
        compiler_params=params(),
        name="feature_tables",
    )(seeds, jnp.asarray(cosine_block()))


def turn(values, cosine, sine):
    lanes = values.shape[1]
    half = ROT // 2
    lane = lane_index(*values.shape) % DH
    swapped = jnp.where(
        lane < half, pltpu.roll(values, lanes - half, 1), pltpu.roll(values, half, 1)
    )
    return values * cosine + swapped * sine


def turn_back(values, cosine, sine):
    lanes = values.shape[1]
    half = ROT // 2
    lane = lane_index(*values.shape) % DH
    turned = values * sine
    swapped = jnp.where(
        lane < half, pltpu.roll(turned, lanes - half, 1), pltpu.roll(turned, half, 1)
    )
    return values * cosine + jnp.where(lane < ROT, swapped, 0.0)


def normalized(x_ref_rows, gain, offset):
    average = jnp.mean(x_ref_rows, -1, keepdims=True)
    centered = x_ref_rows - average
    variance = jnp.mean(centered * centered, -1, keepdims=True)
    return centered * lax.rsqrt(variance + EPSILON) * gain + offset


def start_layer(stream, x_ref, h_ref, gain_ref, offset_ref):
    length = h_ref.shape[0]
    step = min(128, length)

    @pl.loop(0, length // step)
    def _(index):
        rows = pl.ds(pl.multiple_of(index * step, step), step)
        values = stream[0][rows].astype(F32)
        if len(stream) > 1:
            values = values + (stream[1][rows] + stream[2][rows])
            x_ref[rows] = values
        h_ref[rows] = normalized(
            values, gain_ref[...].astype(F32), offset_ref[...].astype(F32)
        ).astype(BF16)


def gelu_parts(units):
    below = 0.5 + 0.5 * lax.erf(units * math.sqrt(0.5))
    return below, jnp.exp(-0.5 * units * units) * (1.0 / math.sqrt(2.0 * math.pi))


FF_BLOCK = 1024
FF_ROWS = 512


def mlp_forward_kernel(layer, count, *refs):
    stream, refs = refs[:count], refs[count:]
    gain_ref, offset_ref, up_ref, bias_ref, down_ref, down_bias_ref = refs[:6]
    gain_ref, offset_ref, down_bias_ref = [
        ref.at[layer : layer + 1] for ref in (gain_ref, offset_ref, down_bias_ref)
    ]
    refs = refs[6:]
    x_ref = None
    if count > 1:
        x_ref, refs = refs[0], refs[1:]
    part_ref, h_ref, act_ref, slope_ref = refs
    step = pl.program_id(0)

    @pl.when(step == 0)
    def _():
        start_layer(stream, x_ref, h_ref, gain_ref, offset_ref)
        part_ref[...] = jnp.broadcast_to(down_bias_ref[...].astype(F32), part_ref.shape)

    for first in range(0, h_ref.shape[0], FF_ROWS):
        rows = slice(first, first + FF_ROWS)
        units = dot_nt(h_ref[rows], up_ref[0]) + bias_ref[0]
        below, density = gelu_parts(units)
        active = (units * below).astype(BF16)
        act_ref[0, rows] = active
        slope_ref[0, rows] = (below + units * density).astype(BF16)
        part_ref[rows] += dot_nn(active, down_ref[0, 0])


def plane_block(length, lanes):
    per_plane = 1024 // lanes
    return pl.BlockSpec((1, length, lanes), lambda j: (j // per_plane, 0, j % per_plane))


def mlp_forward(layer, stream, gain, offset, up, biases, down_weight, down_bias):
    length, width = stream[0].shape
    hidden = up.shape[1]
    blocks = hidden // FF_BLOCK
    state = jax.ShapeDtypeStruct((4, length, width), BF16)
    full = jax.ShapeDtypeStruct((length, width), F32)
    out_shape = [full, jax.ShapeDtypeStruct((length, width), BF16), state, state]
    out_specs = [whole((length, width)), whole((length, width))]
    out_specs += [plane_block(length, FF_BLOCK)] * 2
    if len(stream) > 1:
        out_shape, out_specs = [full] + out_shape, [whole((length, width))] + out_specs
    return pl.pallas_call(
        functools.partial(mlp_forward_kernel, layer, len(stream)),
        grid=(blocks,),
        in_specs=[whole((length, width))] * len(stream)
        + [
            whole((LAYERS, width)),
            whole((LAYERS, width)),
            pl.BlockSpec((1, FF_BLOCK, width), lambda j: (layer, j, 0)),
            pl.BlockSpec((1, 1, FF_BLOCK), lambda j: (layer * blocks + j, 0, 0)),
            pl.BlockSpec((1, 1, FF_BLOCK, width), lambda j: (0, layer, j, 0)),
            whole((LAYERS, width)),
        ],
        out_specs=out_specs,
        out_shape=out_shape,
        compiler_params=params(),
        name="mlp_forward",
    )(*stream, gain, offset, up, biases, down_weight, down_bias)


def add_stream(stream, result_ref):
    if stream:
        result_ref[...] = stream[0][...] + (stream[1][...] + stream[2][...])


def stream_specs(stream):
    specs = [
        pl.BlockSpec((part.shape[0] // 4, part.shape[1]), lambda j, *_: (j, 0)) for part in stream
    ]
    shapes = [jax.ShapeDtypeStruct(part.shape, F32) for part in stream[:1]]
    return specs, specs[:1], shapes


def mlp_backward_kernel(count, place_ref, *refs):
    stream, refs = refs[:count], refs[count:]
    grad_ref, h_ref, act_ref, slope_ref, down_ref, up_ref = refs[:6]
    result_ref, refs = (refs[6], refs[7:]) if count else (None, refs[6:])
    part_ref, along_x, kept_x, along_y, kept_y, bias_ref = refs[:6]
    grad_t, h_t, units = refs[6:]
    step = pl.program_id(0)
    add_stream(stream, result_ref)

    @pl.when(step == 0)
    def _():
        grad_t[...] = grad_ref[...].T
        h_t[...] = h_ref[...].T
        part_ref[...] = jnp.zeros_like(part_ref)

    bias = jnp.zeros((1, FF_BLOCK), F32)
    for first in range(0, h_ref.shape[0], ROWS):
        rows = slice(first, first + ROWS)
        grad_act = dot_nt(grad_ref[rows], down_ref[0, 0])
        grad_unit = (grad_act * slope_ref[0, rows].astype(F32)).astype(BF16)
        bias += jnp.sum(grad_unit.astype(F32), axis=0, keepdims=True)
        units[rows] = grad_unit
        part_ref[rows] += dot_nn(grad_unit, up_ref[0])
    bias_ref[pl.ds(step, 1)] = bias

    def block(y, x):
        return pl.ds(pl.multiple_of((2 * y + x) * WIDE, WIDE), WIDE)

    near_x, near_y = place_ref[0], place_ref[1]
    for first in range(0, h_t.shape[0], ROWS):
        rows = slice(first, first + ROWS)
        for side in range(2):
            for target, x in ((along_x, 1 - near_x), (kept_x, near_x)):
                target[0, side, rows] = dot_nn(grad_t[rows], act_ref[0, :, block(side, x)])
            for target, y in ((along_y, 1 - near_y), (kept_y, near_y)):
                target[0, side, rows] = dot_nn(h_t[rows], units[:, block(y, side)])


def halves_of(width, weight):
    shapes = (weight,) * 2 + ((4, 2, width, WIDE),) * 2
    return [jax.ShapeDtypeStruct(shape, F32) for shape in shapes]


def flat_halves(part, sent, kept, sent_up, kept_up, bias):
    halves = [half.reshape((-1,) + half.shape[2:]) for half in (sent, kept, sent_up, kept_up)]
    return (part, *halves, bias)


def mlp_backward(layer, place, grad, h, act, slope, down_weight, up, stream=()):
    length, width = h.shape
    hidden = up.shape[1]
    blocks = hidden // FF_BLOCK
    pair = pl.BlockSpec((1, 2, width, WIDE), lambda j, *_: (j, 0, 0, 0))
    plane = pl.BlockSpec((1, length, FF_BLOCK), lambda j, *_: (j, 0, 0))
    stream_in, stream_out, stream_shape = stream_specs(stream)
    return pl.pallas_call(
        functools.partial(mlp_backward_kernel, len(stream)),
        grid_spec=pltpu.PrefetchScalarGridSpec(
            num_scalar_prefetch=1,
            grid=(blocks,),
            in_specs=stream_in
            + [
                whole((length, width)),
                whole((length, width)),
                plane,
                plane,
                pl.BlockSpec((1, 1, FF_BLOCK, width), lambda j, *_: (0, layer, j, 0)),
                pl.BlockSpec((1, FF_BLOCK, width), lambda j, *_: (layer, j, 0)),
            ],
            out_specs=stream_out
            + [whole((length, width))]
            + [pair] * 4
            + [whole((blocks, FF_BLOCK))],
            scratch_shapes=[
                pltpu.VMEM((width, length), BF16),
                pltpu.VMEM((width, length), BF16),
                pltpu.VMEM((length, FF_BLOCK), BF16),
            ],
        ),
        out_shape=stream_shape
        + [jax.ShapeDtypeStruct((length, width), F32)]
        + halves_of(width, (4, 2, width, WIDE))
        + [jax.ShapeDtypeStruct((blocks, FF_BLOCK), F32)],
        compiler_params=params(),
        name="mlp_backward",
    )(place, *stream, grad, h, act, slope, down_weight, up)


def head_sums(values, ones):
    upper, lower = split(values)
    return dot_nn(upper, ones) + dot_nn(lower, ones)


def same_head_ones():
    same = row_index(WIDE, WIDE) // DH == lane_index(WIDE, WIDE) // DH
    return jnp.where(same, 1.0, 0.0).astype(BF16)


def document_of(starts_ref, positions):
    return sum((starts_ref[0, i] <= positions).astype(jnp.int32) for i in range(starts_ref.shape[1]))


def write_mask(starts_ref, mask_ref, flipped):
    for first in range(0, mask_ref.shape[0], ROWS):
        lanes = lane_index(1, ROWS) + first
        own = row_index(ROWS, 1) + first
        order = (own <= lanes) if flipped else (lanes <= own)
        seen = (document_of(starts_ref, own) == document_of(starts_ref, lanes)) & order
        mask_ref[first : first + ROWS] = jnp.where(seen, 1.0, 0.0).astype(BF16)


def document_edges(starts_ref, length):
    edges = []
    for first in range(0, length, ROWS):
        rows = document_of(starts_ref, row_index(ROWS, 1) + first)
        here = document_of(starts_ref, first)
        later = document_of(starts_ref, first + ROWS)
        edges.append((rows == here, rows == later, here == later))
    return edges


def wide_rotary(cosine_ref, sine_ref, rows):
    return tuple(
        jnp.concatenate([ref[rows]] * (WIDE // PAIR), axis=1) for ref in (cosine_ref, sine_ref)
    )


def attention_forward_kernel(layer, count, *refs):
    stream, refs = refs[:count], refs[count:]
    starts_ref, gain_ref, offset_ref, weight_ref, bias_ref = refs[:5]
    gain_ref, offset_ref = [ref.at[layer : layer + 1] for ref in (gain_ref, offset_ref)]
    kind_rows = bias_ref.shape[0] // LAYERS
    upper_ref, lower_ref, scale_ref, cosine_ref, sine_ref = refs[5:10]
    refs = refs[10:]
    x_ref = None
    if count > 1:
        x_ref, refs = refs[0], refs[1:]
    part_ref, h_ref, state_ref, mixed_ref, mask_ref = refs
    length = h_ref.shape[0]

    @pl.when(pl.program_id(0) == 0)
    def _():
        start_layer(stream, x_ref, h_ref, gain_ref, offset_ref)
        write_mask(starts_ref, mask_ref, False)
        last = layer * kind_rows + 3
        part_ref[...] = jnp.broadcast_to(bias_ref[last], part_ref.shape)

    ones = same_head_ones()
    table_up, table_low = upper_ref[0, 0], lower_ref[0, 0]
    lanes_of_step = pl.ds(pl.multiple_of(pl.program_id(0) * WIDE, WIDE), WIDE)

    def features(values, rows):
        upper, lower = split(turn(values, *wide_rotary(cosine_ref, sine_ref, rows)))
        return dot_nn(upper, table_up) + (dot_nn(lower, table_up) + dot_nn(upper, table_low))

    for first in range(0, length, ROWS):
        rows = slice(first, first + ROWS)
        queries, keys, values = [
            dot_nt(h_ref[rows], weight_ref[0, 0, kind, 0])
            + bias_ref[layer * kind_rows + kind, :, lanes_of_step]
            for kind in range(3)
        ]
        state_ref[0, rows] = jnp.exp(features(queries, rows)).astype(BF16)
        logs = features(keys, rows) - (0.5 / math.sqrt(DH)) * head_sums(keys * keys, ones)
        state_ref[1, rows] = (scale_ref[0, 0] * jnp.exp(logs)).astype(BF16)
        state_ref[2, rows] = keys.astype(BF16)
        state_ref[3, rows] = values.astype(BF16)

    zero = jnp.zeros((), BF16)
    one = jnp.ones((), BF16)
    left = lane_index(ROWS, PAIR) < DH
    row, lane = row_index(PAIR, 2 * PAIR), lane_index(PAIR, 2 * PAIR)
    same = row // DH == lane // PAIR
    edges = document_edges(starts_ref, length)
    for pair in range(WIDE // PAIR):
        lanes = slice(pair * PAIR, (pair + 1) * PAIR)
        before = None
        for block, (same_first, same_next, goes_on) in enumerate(edges):
            rows = slice(block * ROWS, (block + 1) * ROWS)
            seen = mask_ref[rows] > zero
            queries, keys = state_ref[0, rows, lanes], state_ref[1, rows, lanes]
            values = [jnp.where(own, state_ref[3, rows, lanes], one) for own in (left, ~left)]
            if block > 0:
                earlier = dot_nn(queries, before.astype(BF16))
                earlier = jnp.where(same_first, earlier, 0.0)
            sums = []
            for head, own in enumerate((left, ~left)):
                scores = dot_nt(queries, jnp.where(own, keys, zero)).astype(BF16)
                total = dot_nn(jnp.where(seen, scores, zero), values[head])
                if block > 0:
                    total = total + earlier[:, head * PAIR : (head + 1) * PAIR]
                sums.append(total)
            if block + 1 < len(edges):
                kept = jnp.where(same_next, keys, zero)
                added = jnp.where(same, dot_tn(kept, jnp.concatenate(values, axis=1)), 0.0)
                if block > 0:
                    added = added + jnp.where(goes_on, before, 0.0)
                before = added
            numer = jnp.where(left, sums[0], sums[1])
            denom = jnp.where(left, pltpu.roll(sums[0], DH, 1), pltpu.roll(sums[1], DH, 1))
            inverse = 1.0 / denom
            mixed_ref[0, rows, lanes] = (numer * inverse).astype(BF16)
            mixed_ref[1, rows, lanes], mixed_ref[2, rows, lanes] = split(inverse)
    for first in range(0, length, ROWS):
        rows = slice(first, first + ROWS)
        part_ref[rows] += dot_nn(mixed_ref[0, rows], weight_ref[0, 0, 3, 0])


def kinds_of(weight):
    return weight.reshape(weight.shape[:2] + (4, QUADS, WIDE, weight.shape[3]))


def attention_forward(layer, stream, starts, gain, offset, weight, biases, tables, rotary):
    length, width = stream[0].shape
    full = jax.ShapeDtypeStruct((length, width), F32)
    state = jax.ShapeDtypeStruct((4, length, width), BF16)
    out_shape = [full, jax.ShapeDtypeStruct((length, width), BF16), state, state]
    four = pl.BlockSpec((4, length, WIDE), lambda g: (0, 0, g))
    out_specs = [whole((length, width)), whole((length, width)), four, four]
    if len(stream) > 1:
        out_shape, out_specs = [full] + out_shape, [whole((length, width))] + out_specs
    return pl.pallas_call(
        functools.partial(attention_forward_kernel, layer, len(stream)),
        grid=(QUADS,),
        in_specs=[whole((length, width))] * len(stream)
        + [
            pl.BlockSpec(memory_space=pltpu.SMEM),
            whole((LAYERS, width)),
            whole((LAYERS, width)),
            pl.BlockSpec((1, 1, 4, 1, WIDE, width), lambda g: (0, layer, 0, g, 0, 0)),
            whole((LAYERS * 4, 1, width)),
            pl.BlockSpec((1, 1, WIDE, WIDE), lambda g: (layer, g, 0, 0)),
            pl.BlockSpec((1, 1, WIDE, WIDE), lambda g: (layer, g, 0, 0)),
            pl.BlockSpec((1, 1, 1, WIDE), lambda g: (layer, g, 0, 0)),
            whole((length, PAIR)),
            whole((length, PAIR)),
        ],
        out_specs=out_specs,
        out_shape=out_shape,
        scratch_shapes=[pltpu.VMEM((length, ROWS), BF16)],
        compiler_params=params(),
        name="attention_forward",
    )(
        *stream, starts, gain, offset, kinds_of(weight),
        biases, *tables, *rotary,
    )


def attention_backward_kernel(count, place_ref, *refs):
    stream, refs = refs[:count], refs[count:]
    starts_ref, grad_ref, h_ref, state_ref, mixed_ref, table_ref = refs[:6]
    cosine_ref, sine_ref, weight_ref = refs[6:9]
    result_ref, refs = (refs[9], refs[10:]) if count else (None, refs[9:])
    part_ref, along_z, kept_z, _, _, bias_ref = refs[:6]
    mask_ref, upright, numer_ref, feat_ref, flow = refs[6:]
    group = pl.program_id(0)
    length, width = h_ref.shape
    add_stream(stream, result_ref)

    @pl.when(pl.program_id(0) == 0)
    def _():
        write_mask(starts_ref, mask_ref, True)
        upright[0] = h_ref[...].T
        upright[1] = grad_ref[...].T
        part_ref[...] = jnp.zeros_like(part_ref)

    row, lane = row_index(WIDE, WIDE), lane_index(WIDE, WIDE)
    partner = (row // PAIR == lane // PAIR) & (row // DH != lane // DH)
    partner = jnp.where(partner, 1.0, 0.0).astype(BF16)
    zero = jnp.zeros((), BF16)
    one = jnp.ones((), BF16)
    for first in range(0, length, ROWS):
        rows = slice(first, first + ROWS)
        grad = dot_nt(grad_ref[rows], weight_ref[0, 0, 3, 0]).astype(BF16).astype(F32)
        inverse = mixed_ref[1, rows].astype(F32) + mixed_ref[2, rows].astype(F32)
        scaled = grad * inverse
        upper, lower = split(-head_sums(scaled * mixed_ref[0, rows].astype(F32), partner))
        numer = scaled.astype(BF16)
        lane = lane_index(ROWS, WIDE)
        spare = jnp.where(lane % DH == 0, upper, jnp.where(lane % DH == 1, lower, zero))
        left = lane % PAIR < DH
        numer_ref[0, rows] = jnp.where(left, numer, spare)
        numer_ref[1, rows] = jnp.where(left, spare, numer)

    left = lane_index(ROWS, PAIR) < DH
    spare = jnp.where(lane_index(ROWS, PAIR) % DH < 2, one, zero)
    row, lane = row_index(2 * PAIR, PAIR), lane_index(2 * PAIR, PAIR)
    same = row // PAIR == lane // DH
    row, lane = row_index(PAIR, PAIR), lane_index(PAIR, PAIR)
    same_head = row // DH == lane // DH
    edges = document_edges(starts_ref, length)
    blocks = range(len(edges))

    def both(upper_and_lower, sums):
        upper, lower = split(sums)
        return dot_nn(upper_and_lower, upper) + dot_nn(upper_and_lower, lower)

    for pair in range(WIDE // PAIR):
        lanes = slice(pair * PAIR, (pair + 1) * PAIR)

        def rows_of_block(block):
            rows = slice(block * ROWS, (block + 1) * ROWS)
            numers = [numer_ref[head, rows, lanes] for head in range(2)]
            values = state_ref[3, rows, lanes]
            values = [jnp.where(own, values, spare) for own in (left, ~left)]
            return rows, state_ref[0, rows, lanes], state_ref[1, rows, lanes], values, numers

        before, after = {}, {}
        for block in blocks[1:]:
            rows, queries, keys, values, numers = rows_of_block(block - 1)
            _, same_next, goes_on = edges[block - 1]
            kept = jnp.where(same_next, keys, zero)
            added = jnp.where(same, dot_tn(jnp.concatenate(values, axis=1), kept), 0.0)
            if block > 1:
                added = added + jnp.where(goes_on, before[block - 1], 0.0)
            before[block] = added
        for block in blocks[::-1][:-1]:
            rows, queries, keys, values, numers = rows_of_block(block)
            same_first, _, goes_on = edges[block]
            kept = jnp.where(same_first, queries, zero)
            keys_sum = jnp.where(same, dot_tn(jnp.concatenate(numers, axis=1), kept), 0.0)
            values_sum = dot_tn(kept, jnp.where(left, numers[0], numers[1]))
            values_sum = jnp.where(same_head, values_sum, 0.0)
            if block + 1 < len(edges):
                keys_sum = keys_sum + jnp.where(goes_on, after[block + 1][0], 0.0)
                values_sum = values_sum + jnp.where(goes_on, after[block + 1][1], 0.0)
            after[block] = (keys_sum, values_sum)
        for block in blocks:
            rows, queries, keys, values, numers = rows_of_block(block)
            same_first, same_next, _ = edges[block]
            seen = mask_ref[rows] > zero
            numer = jnp.where(left, numers[0], numers[1])
            grads = []
            grad_query = None
            for head, own in enumerate((left, ~left)):
                own_keys = jnp.where(own, keys, zero)
                scores = dot_nt(own_keys, queries).astype(BF16)
                grad_value = dot_nn(jnp.where(seen, scores, zero), numer)
                grad_scores = dot_nt(values[head], numers[head]).astype(BF16)
                grad_scores = jnp.where(seen, grad_scores, zero)
                grads.append((grad_value, dot_nn(grad_scores, queries)))
                from_head = dot_tn(grad_scores, own_keys)
                grad_query = from_head if head == 0 else grad_query + from_head
            grad_value = jnp.where(left, grads[0][0], grads[1][0])
            grad_key = jnp.where(left, grads[0][1], grads[1][1])
            if block + 1 < len(edges):
                keys_sum, values_sum = after[block + 1]
                late = both(jnp.concatenate(values, axis=1), keys_sum)
                grad_key = grad_key + jnp.where(same_next, late, 0.0)
                late = dot_nn(keys, values_sum.astype(BF16))
                grad_value = grad_value + jnp.where(same_next, late, 0.0)
            if block > 0:
                early = both(jnp.concatenate(numers, axis=1), before[block])
                grad_query = grad_query + jnp.where(same_first, early, 0.0)
            flow[2, rows, lanes] = grad_value.astype(BF16)
            feat_ref[1, rows, lanes] = (grad_key * keys.astype(F32)).astype(BF16)
            feat_ref[0, rows, lanes] = (grad_query * queries.astype(F32)).astype(BF16)

    ones = same_head_ones()
    table = table_ref[0, 0]
    sums = [jnp.zeros((1, WIDE), F32)] * 3
    for first in range(0, length, ROWS):
        rows = slice(first, first + ROWS)
        cosine, sine = wide_rotary(cosine_ref, sine_ref, rows)
        flow[0, rows] = turn_back(dot_nt(feat_ref[0, rows], table), cosine, sine).astype(BF16)
        shrink = dot_nn(feat_ref[1, rows], ones) * (1.0 / math.sqrt(DH))
        turned = turn_back(dot_nt(feat_ref[1, rows], table), cosine, sine)
        flow[1, rows] = (turned - state_ref[2, rows].astype(F32) * shrink).astype(BF16)
        total = part_ref[rows]
        for kind in range(3):
            block = flow[kind, rows]
            sums[kind] = sums[kind] + jnp.sum(block.astype(F32), axis=0, keepdims=True)
            total = total + dot_nn(block, weight_ref[0, 0, kind, 0])
        part_ref[rows] = total
    for kind in range(3):
        bias_ref[kind : kind + 1] = sums[kind]
    lanes = pl.ds(pl.multiple_of(group * WIDE, WIDE), WIDE)
    bias_ref[3:4] = jnp.sum(grad_ref[:, lanes].astype(F32), axis=0, keepdims=True)
    flow[3] = mixed_ref[0]
    for first in range(0, width, ROWS):
        rows = slice(first, first + ROWS)
        for far in range(2):
            for target, near in ((along_z, 1 - place_ref[2]), (kept_z, place_ref[2])):
                kind = 2 * far + near
                target[far, 0, rows] = dot_nn(upright[kind // 3, rows], flow[kind])


def attention_backward(
    layer, place, starts, grad, h, state, mixed, tables, rotary, weight, stream=()
):
    _, length, width = state.shape
    four = pl.BlockSpec((4, length, WIDE), lambda g, *_: (0, 0, g))
    halves = pl.BlockSpec((2, 1, width, WIDE), lambda g, *_: (0, g, 0, 0))
    stream_in, stream_out, stream_shape = stream_specs(stream)
    return pl.pallas_call(
        functools.partial(attention_backward_kernel, len(stream)),
        grid_spec=pltpu.PrefetchScalarGridSpec(
            num_scalar_prefetch=1,
            grid=(QUADS,),
            in_specs=stream_in
            + [
                pl.BlockSpec(memory_space=pltpu.SMEM),
                whole((length, width)),
                whole((length, width)),
                four,
                four,
                pl.BlockSpec((1, 1, WIDE, WIDE), lambda g, *_: (layer, g, 0, 0)),
                whole((length, PAIR)),
                whole((length, PAIR)),
                pl.BlockSpec((1, 1, 4, 1, WIDE, width), lambda g, *_: (0, layer, 0, g, 0, 0)),
            ],
            out_specs=stream_out
            + [whole((length, width))]
            + [halves, halves]
            + [pl.BlockSpec(memory_space=pl.ANY)] * 2
            + [pl.BlockSpec((4, WIDE), lambda g, *_: (0, g))],
            scratch_shapes=[
                pltpu.VMEM((length, ROWS), BF16),
                pltpu.VMEM((2, width, length), BF16),
                pltpu.VMEM((2, length, WIDE), BF16),
                pltpu.VMEM((2, length, WIDE), BF16),
                pltpu.VMEM((4, length, WIDE), BF16),
            ],
        ),
        out_shape=stream_shape
        + [jax.ShapeDtypeStruct((length, width), F32)]
        + halves_of(width, (2, 4, width, WIDE))
        + [jax.ShapeDtypeStruct((4, width), F32)],
        compiler_params=params(),
        name="attention_backward",
    )(place, *stream, starts, grad, h, state, mixed, tables[0], *rotary, kinds_of(weight))


def norm_gradient(values, incoming, grad, gain, sums_ref):
    average = jnp.mean(values, -1, keepdims=True)
    centered = values - average
    variance = jnp.mean(centered * centered, -1, keepdims=True)
    inverse = lax.rsqrt(variance + EPSILON)
    unit = centered * inverse
    grad_unit = incoming * gain
    first = jnp.mean(grad_unit, -1, keepdims=True)
    second = jnp.mean(grad_unit * unit, -1, keepdims=True)
    sums_ref[0:1] += jnp.sum(incoming * unit, axis=0, keepdims=True)
    sums_ref[1:2] += jnp.sum(incoming, axis=0, keepdims=True)
    sums_ref[2:3] += jnp.sum(grad, axis=0, keepdims=True)
    return grad + inverse * (grad_unit - first - unit * second)


def norm_backward_kernel(layer, x_ref, own_ref, other_ref, grad_ref, gain_ref, out_ref, sums_ref):
    @pl.when(pl.program_id(0) == 0)
    def _():
        sums_ref[...] = jnp.zeros_like(sums_ref)

    out = norm_gradient(
        x_ref[...].astype(F32),
        own_ref[...] + other_ref[...],
        grad_ref[...].astype(F32),
        gain_ref[layer : layer + 1].astype(F32),
        sums_ref,
    )
    out_ref[...] = out.astype(out_ref.dtype)


def norm_backward(layer, x, own, other, grad, gain, kind):
    length, width = own.shape
    block = pl.BlockSpec((ROWS, width), lambda i: (i, 0))
    return pl.pallas_call(
        functools.partial(norm_backward_kernel, layer),
        grid=(length // ROWS,),
        in_specs=[block, block, block, block, whole((LAYERS, width))],
        out_specs=[block, whole((8, width))],
        out_shape=[
            jax.ShapeDtypeStruct((length, width), kind),
            jax.ShapeDtypeStruct((8, width), F32),
        ],
        compiler_params=params(),
        name="norm_backward",
    )(x, own, other, grad, gain)


MESH = pl.DeviceIdType.MESH
UNIT = 16
SLOTS = 6
LAG = 2


class Flow(NamedTuple):
    order: tuple
    core: int
    is_up: int
    layer: int
    row: int
    units: int
    start: int
    place: int


def flows_of(width, layer, start):
    rows = width // 2
    kinds = (
        ((0, 1, 2, 3), 1, 0, 0, 0),
        ((1, 0, 2, 3), 1, 1, 0, 1),
        ((0, 1, 2, 3), 1, 0, 1, 2),
        ((1, 0, 2, 3), 1, 1, 1, 3),
        ((2, 0, 1, 3), 0, 0, 0, 0),
        ((2, 1, 0, 3), 0, 0, 1, 1),
    )
    return [
        Flow(order, core, is_up, layer, part * rows, rows // UNIT, start, 4 * layer + place)
        for order, core, is_up, part, place in kinds
    ]


def bit_of(index, bit):
    return (index // (1 << bit)) % 2


def flip(index, bit):
    return index + (1 << bit) * (1 - 2 * bit_of(index, bit))


def finish_kernel(
    bits, flows,
    kept_weight1, kept_up1, came_weight1, came_up1,
    kept_weight0, kept_up0, sent_weight0, sent_up0,
    bias0_ref, bias1_ref, sums1_ref, sums0_ref,
    weight_out, up_out, small_out,
    weight_sum, up_sum, up_turned, up_came,
    *scratch,
):
    stages = bits
    kept = ((kept_weight1, kept_up1), (kept_weight0, kept_up0))
    moved = ((came_weight1, came_up1), (sent_weight0, sent_up0))
    small_parts = (bias0_ref, bias1_ref, sums1_ref, sums0_ref)
    places = 1 + max(flow.place for flow in flows)
    held, scratch = scratch[: places * (stages + 1)], scratch[places * (stages + 1) :]
    held = [held[f * (stages + 1) : (f + 1) * (stages + 1)] for f in range(places)]
    small, small_came = scratch[: stages + 1], scratch[stages + 1 : 2 * stages + 1]
    load_sem, send_sem, recv_sem, credit, small_send, small_recv, near_send, near_recv = (
        scratch[2 * stages + 1 :]
    )
    me, core = lax.axis_index("batch"), lax.axis_index("stream")

    barrier = pltpu.get_barrier_semaphore()
    for bit in range(bits):
        pl.semaphore_signal(
            barrier, inc=1, device_id={"batch": flip(me, bit)}, device_id_type=MESH
        )
    pl.semaphore_signal(barrier, inc=1, device_id={"stream": 1 - core}, device_id_type=MESH)
    pl.semaphore_wait(barrier, bits + 1)

    small_start = 2
    turn_start = max(flow.start + flow.units for flow in flows if flow.layer == 1)
    turn_start += LAG * stages + 1

    def near_copy(layer):
        return pltpu.make_async_remote_copy(
            src_ref=up_turned.at[layer],
            dst_ref=up_came.at[layer],
            send_sem=near_send.at[layer],
            recv_sem=near_recv.at[layer],
            device_id={"stream": 0},
            device_id_type=MESH,
        )

    def turn_weights(layer):
        weight_out[len(moved) - 1 - layer] = weight_sum[layer].T

        @pl.when(core == 1)
        def _():
            up_turned[layer] = up_sum[layer, :, : WIDE // 2].T
            near_copy(layer).start()
            up_out[len(moved) - 1 - layer] = up_sum[layer, :, WIDE // 2 :].T

    def small_copy(stage):
        return pltpu.make_async_remote_copy(
            src_ref=small[stage],
            dst_ref=small_came[stage],
            send_sem=small_send.at[stage],
            recv_sem=small_recv.at[stage],
            device_id={"batch": flip(me, stage)},
            device_id_type=MESH,
        )

    def small_step(stage):
        if stage == 0:
            row = 0
            for part in small_parts:
                small[0][row : row + part.shape[0]] = part[...]
                row += part.shape[0]
        else:
            small_copy(stage - 1).wait()
            small[stage][...] = small[stage - 1][...] + small_came[stage - 1][...]
        if stage < stages:
            small_copy(stage).start()
        else:
            small_out[...] = small[stage][...]

    def view(order, stage, mine):
        left = sorted(set(range(bits)) - set(order[:stage]), reverse=True)
        pick = bit_of(me, order[stage])
        pick = pick if mine else 1 - pick
        return tuple(pick if bit == order[stage] else slice(None) for bit in left)

    def remote(flow, stage, slot, source):
        place = flow.place
        return pltpu.make_async_remote_copy(
            src_ref=source,
            dst_ref=held[place][stage + 1].at[slot],
            send_sem=send_sem.at[place, stage, slot],
            recv_sem=recv_sem.at[place, stage, slot],
            device_id={"batch": flip(me, flow.order[stage])},
            device_id_type=MESH,
        )

    def sent_from(flow, stage, slot):
        if stage == 0:
            return held[flow.place][0].at[slot]
        return held[flow.place][stage].at[(slot,) + view(flow.order, stage, False)]

    def load(flow, slot, source):
        place = flow.place
        return pltpu.make_async_copy(source, held[place][0].at[slot], load_sem.at[place, slot])

    def load_came(flow, slot, source):
        return pltpu.make_async_copy(
            source, held[flow.place][1].at[slot], recv_sem.at[flow.place, 0, slot]
        )

    def return_credit(flow, stage, unit):
        if stage == 0 and flow.layer == 0:
            return

        @pl.when(unit + SLOTS < flow.units)
        def _():
            pl.semaphore_signal(
                credit.at[flow.place, stage],
                inc=1,
                device_id={"batch": flip(me, flow.order[stage])},
                device_id_type=MESH,
            )

    def take_credit(flow, stage, unit):
        @pl.when(unit >= SLOTS)
        def _():
            pl.semaphore_wait(credit.at[flow.place, stage], 1)

    def begin(flow, unit):
        slot = lax.rem(unit, SLOTS)
        at = (slice(None),) * (bits - 1)
        at += (pl.ds(pl.multiple_of(flow.row + unit * UNIT, UNIT), UNIT),)
        load(flow, slot, kept[flow.layer][flow.is_up].at[at]).start()
        source = moved[flow.layer][flow.is_up].at[at]
        if flow.layer == 0:
            load_came(flow, slot, source).start()
        else:
            take_credit(flow, 0, unit)
            remote(flow, 0, slot, source).start()

    def advance(flow, stage, unit):
        slot = lax.rem(unit, SLOTS)
        buffers, begun = held[flow.place], flow.layer == 0
        copy = remote(flow, stage - 1, slot, sent_from(flow, stage - 1, slot))
        if stage == 1 and begun:
            load_came(flow, slot, buffers[0].at[slot]).wait()
        else:
            copy.wait_recv()
        if stage == 1:
            load(flow, slot, buffers[1].at[slot]).wait()
            mine = buffers[0][slot]
        else:
            mine = buffers[stage - 1][(slot,) + view(flow.order, stage - 1, True)]
        value = buffers[stage][slot] + mine
        if stage < stages:
            buffers[stage][slot] = value
            take_credit(flow, stage, unit)
            remote(flow, stage, slot, sent_from(flow, stage, slot)).start()
        else:
            target = up_sum if flow.is_up else weight_sum
            at = pl.ds(pl.multiple_of(flow.row + unit * UNIT, UNIT), UNIT)
            target[flow.layer, at] = value
        if stage > 1 or not begun:
            copy.wait_send()
        if stage >= 2:
            return_credit(flow, stage - 2, unit)
        if stage == stages:
            return_credit(flow, stage - 1, unit)

    def within(flow, unit):
        return (unit >= 0) & (unit < flow.units) & (core == flow.core)

    def step(index, carry):
        for flow in flows:
            unit = index - flow.start
            pl.when(within(flow, unit))(functools.partial(begin, flow, unit))
        for flow in flows:
            for stage in range(1, stages + 1):
                unit = index - flow.start - LAG * stage
                pl.when(within(flow, unit))(functools.partial(advance, flow, stage, unit))
        for stage in range(stages + 1):
            pl.when(index == small_start + 2 * stage)(functools.partial(small_step, stage))
        pl.when(index == turn_start)(functools.partial(turn_weights, 1))
        return carry

    last = max(flow.start + flow.units for flow in flows)
    lax.fori_loop(0, last + LAG * stages, step, 0)
    turn_weights(0)
    for layer in range(len(moved)):

        @pl.when(core == 0)
        def _():
            near_copy(layer).wait_recv()
            up_out[len(moved) - 1 - layer] = up_came[layer]

        @pl.when(core == 1)
        def _():
            near_copy(layer).wait_send()


def finish(last, first, came, smalls):
    width = last[0].shape[1]
    bits = 4
    split = (2,) * (bits - 1)
    flows = flows_of(width, 1, 0)
    flows += flows_of(width, 0, max(flow.start + flow.units for flow in flows))
    small = (sum(part.shape[0] for part in smalls), width)
    scratch = [
        pltpu.VMEM((2, width, WIDE), F32),
        pltpu.VMEM((2, width, WIDE), F32),
        pltpu.VMEM((2, WIDE // 2, width), F32),
        pltpu.VMEM((2, WIDE // 2, width), F32),
    ]
    places = 1 + max(flow.place for flow in flows)
    for _ in range(places):
        for stage in range(bits + 1):
            lead = (SLOTS,) + (2,) * (bits - 1 - max(stage - 1, 0))
            scratch.append(pltpu.VMEM(lead + (UNIT, WIDE), F32))
    scratch += [pltpu.VMEM(small, F32)] * (2 * bits + 1)
    scratch += [
        pltpu.SemaphoreType.DMA((places, SLOTS)),
        pltpu.SemaphoreType.DMA((places, bits, SLOTS)),
        pltpu.SemaphoreType.DMA((places, bits, SLOTS)),
        pltpu.SemaphoreType.REGULAR((places, bits)),
        pltpu.SemaphoreType.DMA((bits,)),
        pltpu.SemaphoreType.DMA((bits,)),
        pltpu.SemaphoreType.DMA((2,)),
        pltpu.SemaphoreType.DMA((2,)),
    ]
    large = [last[1], last[3], *came, first[1], first[3], first[0], first[2]]
    large = [array.reshape(split + array.shape[1:]) for array in large]
    return pl.pallas_call(
        functools.partial(finish_kernel, bits, flows),
        in_specs=[pl.BlockSpec(memory_space=pltpu.HBM)] * len(large)
        + [pl.BlockSpec(memory_space=pltpu.VMEM)] * len(smalls),
        out_specs=[pl.BlockSpec(memory_space=pltpu.VMEM)] * 3,
        out_shape=[
            jax.ShapeDtypeStruct((2, WIDE, width), F32),
            jax.ShapeDtypeStruct((2, WIDE // 2, width), F32),
            jax.ShapeDtypeStruct(small, F32),
        ],
        scratch_shapes=scratch,
        compiler_params=pltpu.CompilerParams(
            collective_id=0, has_side_effects=True, vmem_limit_bytes=VMEM_LIMIT
        ),
        name="finish",
    )(*large, *smalls)


def send_first(halves):
    count = lax.axis_size("batch")

    def pairs(stream, bit):
        return [(2 * source + stream, 2 * flip(source, bit) + stream) for source in range(count)]

    axes = ("batch", "stream")
    return [
        lax.ppermute(halves[0], axes, pairs(0, 2) + pairs(1, 0)),
        lax.ppermute(halves[2], axes, pairs(1, 1)),
    ]


def shards(
    tokens, cotangent, branch_weight, branch_bias, up_weight, down_bias,
    norm_gain, norm_bias, freq_seeds, doc_starts,
):
    is_attention = lax.axis_index("stream") == 0
    length, width = tokens.shape
    rotary = tuple(jnp.asarray(table) for table in rotary_rows(length))
    biases = branch_bias[0].astype(F32).reshape(-1, 1, width)
    tables = lax.cond(
        is_attention,
        lambda: tuple(feature_tables(freq_seeds)),
        lambda: (
            jnp.zeros((LAYERS, QUADS, WIDE, WIDE), BF16),
            jnp.zeros((LAYERS, QUADS, WIDE, WIDE), BF16),
            jnp.zeros((LAYERS, QUADS, 1, WIDE), F32),
        ),
    )
    swap = [(0, 1), (1, 0)]

    def attention(layer, stream):
        return tuple(
            attention_forward(
                layer, stream, doc_starts, norm_gain, norm_bias, branch_weight, biases, tables,
                rotary,
            )
        )

    def feed_forward(layer, stream):
        return tuple(
            mlp_forward(
                layer, stream, norm_gain, norm_bias, up_weight, biases, branch_weight, down_bias
            )
        )

    stream = (tokens,)
    inputs, kept = [], []
    for layer in range(LAYERS):
        *x, part, h, state, mixed = lax.cond(
            is_attention,
            functools.partial(attention, layer, stream),
            functools.partial(feed_forward, layer, stream),
        )
        inputs.append(x[0] if x else tokens)
        kept.append((h, state, mixed))
        stream = (inputs[-1], part, lax.ppermute(part, "stream", swap))
    result = stream[0] + (stream[1] + stream[2])

    count = lax.axis_size("batch")
    blocked = count == branch_weight.shape[2] // WIDE
    me = lax.axis_index("batch") if blocked else 0
    place = jnp.stack([jnp.asarray(bit_of(me, bit), jnp.int32) for bit in range(3)])

    def attention_back(layer, grad, stream):
        h, state, mixed = kept[layer]
        *result, part, a, b, c, d, bias = attention_backward(
            layer, place, doc_starts, grad, h, state, mixed, tables, rotary, branch_weight, stream
        )
        return *result, *flat_halves(part, a, b, c, d, bias)

    def feed_forward_back(layer, grad, stream):
        h, act, slope = kept[layer]
        *result, part, a, b, c, d, bias = mlp_backward(
            layer, place, grad, h, act, slope, branch_weight, up_weight, stream
        )
        return *result, *flat_halves(part, a, b, c, d, bias)

    def back(layer, grad, stream=()):
        *result, part, a, b, c, d, bias = lax.cond(
            is_attention,
            functools.partial(attention_back, layer, grad, stream),
            functools.partial(feed_forward_back, layer, grad, stream),
        )
        return *result, part, (a, b, c, d), bias

    def norm_back(layer, part, grad, kind):
        other = lax.ppermute(part, "stream", swap)
        return norm_backward(layer, inputs[layer], part, other, grad, norm_gain, kind)

    part1, halves1, bias1 = back(1, cotangent)
    if blocked:
        came = send_first(halves1)
    grad0, sums1 = norm_back(1, part1, cotangent, BF16)
    result, part0, halves0, bias0 = back(0, grad0, stream)
    input_grad, sums0 = norm_back(0, part0, grad0, F32)
    if blocked:
        weight, up, small = finish(halves1, halves0, came, (bias0, bias1, sums1, sums0))
    else:
        weight, up = scatter_rows((halves0, halves1))
        small = lax.psum(jnp.concatenate([bias0, bias1, sums1, sums0]), "batch")
    index, rows = lax.axis_index("batch"), bias0.shape[0]
    each, own = branch_weight.shape[2] // count, width // count
    biases = small[: 2 * rows].reshape(LAYERS, -1)
    sums = small[2 * rows :].reshape(LAYERS, 8, width)[::-1]
    sums = lax.dynamic_slice_in_dim(sums, index * own, own, axis=2)
    return (
        result,
        input_grad,
        weight[None],
        lax.dynamic_slice_in_dim(biases, index * each, each, axis=1)[None],
        up,
        sums[:, 2],
        sums[:, 0],
        sums[:, 1],
    )


def scatter_rows(layers):
    weights, ups = [], []
    for sent, kept, sent_up, kept_up in layers:
        blocks = (-1,) + kept.shape[1:]
        wide, far = (4, 2) + kept.shape[1:], (2, 4) + kept.shape[1:]
        weight = jnp.where(
            lax.axis_index("stream") == 1,
            jnp.stack([kept.reshape(wide), sent.reshape(wide)], axis=2).reshape(blocks),
            jnp.stack([kept.reshape(far), sent.reshape(far)], axis=1).reshape(blocks),
        )
        weight = rows_of(weight)
        up = jnp.stack([kept_up.reshape(wide), sent_up.reshape(wide)], axis=1)
        up = rows_of(up.reshape(blocks))
        up = jnp.where(lax.axis_index("stream") == 1, up, 0.0)
        weights.append(lax.psum_scatter(weight, "batch", scatter_dimension=0, tiled=True))
        ups.append(lax.psum_scatter(up, ("batch", "stream"), scatter_dimension=0, tiled=True))
    return jnp.stack(weights), jnp.stack(ups)


def rows_of(blocks):
    return jnp.transpose(blocks, (0, 2, 1)).reshape(-1, blocks.shape[1])


def solution(mesh):
    placed = (
        P("batch", None),
        P("batch", None),
        P("stream", None, None, None),
        P("stream", None, None),
        P(),
        P(),
        P(),
        P(),
        P(),
        P("batch", None),
    )
    return jax.shard_map(
        shards,
        mesh=mesh,
        in_specs=placed,
        out_specs=(
            P("batch", None),
            P("batch", None),
            P("stream", None, "batch", None),
            P("stream", None, "batch"),
            P(None, ("batch", "stream"), None),
            P(None, "batch"),
            P(None, "batch"),
            P(None, "batch"),
        ),
        check_vma=False,
    )
```

```python
import functools
import math
from typing import NamedTuple

import jax
import jax.numpy as jnp
import numpy as np
from jax import lax
from jax.experimental import pallas as pl
from jax.experimental.pallas import tpu as pltpu
from jax.sharding import PartitionSpec as P

HEADS = 16
DH = 64
ROT = 16
FEAT = 64
LAYERS = 2
EPSILON = 1e-05
HIGH = lax.Precision.HIGHEST
F32 = jnp.float32
BF16 = jnp.bfloat16
WIDE = 256
PAIR = 128
QUADS = HEADS * DH // WIDE
PAIRS = HEADS * DH // PAIR
ROWS = 256
VMEM_LIMIT = 56 * 1024 * 1024


def params():
    return pltpu.CompilerParams(vmem_limit_bytes=VMEM_LIMIT)


def whole(shape):
    zeros = (0,) * len(shape)
    return pl.BlockSpec(shape, lambda *_: zeros, pipeline_mode=pl.Buffered(1))


def dot_nn(left, right):
    return lax.dot_general(left, right, (((1,), (0,)), ((), ())), preferred_element_type=F32)


def dot_tn(left, right):
    return lax.dot_general(left, right, (((0,), (0,)), ((), ())), preferred_element_type=F32)


def dot_nt(left, right):
    return lax.dot_general(left, right, (((1,), (1,)), ((), ())), preferred_element_type=F32)


def split(values):
    upper = values.astype(BF16)
    return upper, (values - upper.astype(F32)).astype(BF16)


def lane_index(rows, lanes):
    return lax.broadcasted_iota(jnp.int32, (rows, lanes), 1)


def row_index(rows, lanes):
    return lax.broadcasted_iota(jnp.int32, (rows, lanes), 0)


def cosine_block():
    samples = np.arange(DH, dtype=np.float64)
    angles = math.pi * (samples[None, :] + 0.5) * samples[:, None] / DH
    table = np.cos(angles) * math.sqrt(2.0 / DH)
    table[0] *= math.sqrt(0.5)
    return np.kron(np.eye(WIDE // DH), table.T * DH ** (-0.25)).astype(np.float32)


def rotary_rows(length):
    position = np.arange(length, dtype=np.float32)
    inverse = (10000.0 ** (-np.arange(0, ROT, 2, dtype=np.float32) / ROT)).astype(np.float32)
    angles = position[:, None] * inverse[None, :]
    cosine, sine = np.cos(angles), np.sin(angles)
    rest = DH - ROT
    cosine_head = np.concatenate([cosine, cosine, np.ones((length, rest))], 1)
    sine_head = np.concatenate([-sine, sine, np.zeros((length, rest))], 1)
    repeat = PAIR // DH
    return (
        np.tile(cosine_head, (1, repeat)).astype(np.float32),
        np.tile(sine_head, (1, repeat)).astype(np.float32),
    )


def tables_kernel(seeds_ref, cosine_ref, upper_ref, lower_ref, weight_ref):
    own = row_index(WIDE, DH) % DH == lane_index(WIDE, DH)
    feature = lane_index(WIDE, PAIR) % FEAT
    same_head = row_index(WIDE, WIDE) // DH == lane_index(WIDE, WIDE) // FEAT
    for group in range(QUADS):
        heads = [
            jnp.broadcast_to(seeds_ref[0, head : head + 1], (DH, DH))
            for head in range(group * QUADS, (group + 1) * QUADS)
        ]
        seeds = jnp.where(own, jnp.concatenate(heads, axis=0), 0)
        seeds = jnp.sum(seeds.astype(F32), axis=1, keepdims=True).astype(jnp.int32)
        lattice = (feature * seeds) & (FEAT - 1)
        prob = (lattice.astype(F32) + 0.5) * (1.0 / FEAT)
        radius = jnp.sqrt(-2.0 * jnp.log(jnp.minimum(prob, 1.0 - prob)))
        above = 2.515517 + 0.802853 * radius + 0.010328 * radius * radius
        below = (
            1.0
            + 1.432788 * radius
            + 0.189269 * radius * radius
            + 0.001308 * radius * radius * radius
        )
        magnitude = radius - above / below
        omega = jnp.where(prob > 0.5, magnitude, -magnitude)
        omega = jnp.where(same_head, jnp.concatenate([omega] * (WIDE // PAIR), axis=1), 0.0)
        project = jnp.dot(cosine_ref[...], omega, precision=HIGH, preferred_element_type=F32)
        upper_ref[0, group], lower_ref[0, group] = split(project)
        grown = jnp.exp(-0.5 / DH * jnp.sum(omega * omega, axis=0, keepdims=True))
        total = jnp.dot(
            jnp.broadcast_to(grown, (8, WIDE)),
            same_head.astype(F32),
            precision=HIGH,
            preferred_element_type=F32,
        )
        weight_ref[0, group] = FEAT * grown / total[:1]


def feature_tables(seeds):
    return pl.pallas_call(
        tables_kernel,
        grid=(LAYERS,),
        in_specs=[
            pl.BlockSpec((1, HEADS, DH), lambda l: (l, 0, 0)),
            whole((WIDE, WIDE)),
        ],
        out_specs=[
            pl.BlockSpec((1, QUADS, WIDE, WIDE), lambda l: (l, 0, 0, 0)),
            pl.BlockSpec((1, QUADS, WIDE, WIDE), lambda l: (l, 0, 0, 0)),
            pl.BlockSpec((1, QUADS, 1, WIDE), lambda l: (l, 0, 0, 0)),
        ],
        out_shape=[
            jax.ShapeDtypeStruct((LAYERS, QUADS, WIDE, WIDE), BF16),
            jax.ShapeDtypeStruct((LAYERS, QUADS, WIDE, WIDE), BF16),
            jax.ShapeDtypeStruct((LAYERS, QUADS, 1, WIDE), F32),
        ],
        compiler_params=params(),
        name="feature_tables",
    )(seeds, jnp.asarray(cosine_block()))


def turn(values, cosine, sine):
    lanes = values.shape[1]
    half = ROT // 2
    lane = lane_index(*values.shape) % DH
    swapped = jnp.where(
        lane < half, pltpu.roll(values, lanes - half, 1), pltpu.roll(values, half, 1)
    )
    return values * cosine + swapped * sine


def turn_back(values, cosine, sine):
    lanes = values.shape[1]
    half = ROT // 2
    lane = lane_index(*values.shape) % DH
    turned = values * sine
    swapped = jnp.where(
        lane < half, pltpu.roll(turned, lanes - half, 1), pltpu.roll(turned, half, 1)
    )
    return values * cosine + jnp.where(lane < ROT, swapped, 0.0)


def normalized(x_ref_rows, gain, offset):
    average = jnp.mean(x_ref_rows, -1, keepdims=True)
    centered = x_ref_rows - average
    variance = jnp.mean(centered * centered, -1, keepdims=True)
    return centered * lax.rsqrt(variance + EPSILON) * gain + offset


def start_layer(stream, x_ref, h_ref, gain_ref, offset_ref):
    length = h_ref.shape[0]
    step = min(128, length)

    @pl.loop(0, length // step)
    def _(index):
        rows = pl.ds(pl.multiple_of(index * step, step), step)
        values = stream[0][rows].astype(F32)
        if len(stream) > 1:
            values = values + (stream[1][rows] + stream[2][rows])
            x_ref[rows] = values
        h_ref[rows] = normalized(
            values, gain_ref[...].astype(F32), offset_ref[...].astype(F32)
        ).astype(BF16)


JOB = 128


def start_last_layer(stream, x_hbm, buffers, loads, stores, h_ref, gain_ref, offset_ref):
    gain, offset = gain_ref[...].astype(F32), offset_ref[...].astype(F32)
    jobs = h_ref.shape[0] // JOB

    def rows_at(index):
        return pl.ds(pl.multiple_of(index * JOB, JOB), JOB)

    def load(part, index):
        rows = rows_at(index)
        return pltpu.make_async_copy(
            stream[part].at[rows], buffers[part].at[rows], loads.at[part, index]
        )

    def store(index):
        rows = rows_at(index)
        return pltpu.make_async_copy(buffers[1].at[rows], x_hbm.at[rows], stores.at[index])

    @pl.loop(0, jobs)
    def _(index):
        for part in range(len(stream)):
            load(part, index).start()

    @pl.loop(0, jobs)
    def _(index):
        rows = rows_at(index)
        for part in range(len(stream)):
            load(part, index).wait()
        values = buffers[0][rows].astype(F32) + (buffers[1][rows] + buffers[2][rows])
        buffers[1][rows] = values
        store(index).start()
        h_ref[rows] = normalized(values, gain, offset).astype(BF16)

    @pl.loop(0, jobs)
    def _(index):
        store(index).wait()


def chunk_semaphores(length):
    return [
        pltpu.SemaphoreType.DMA((3, length // JOB)),
        pltpu.SemaphoreType.DMA((length // JOB,)),
    ]


def gelu_parts(units):
    below = 0.5 + 0.5 * lax.erf(units * math.sqrt(0.5))
    return below, jnp.exp(-0.5 * units * units) * (1.0 / math.sqrt(2.0 * math.pi))


FF_BLOCK = 1024
FF_ROWS = 512


def mlp_forward_kernel(layer, count, *refs):
    stream, refs = refs[:count], refs[count:]
    gain_ref, offset_ref, up_ref, bias_ref, down_ref, down_bias_ref = refs[:6]
    gain_ref, offset_ref, down_bias_ref = [
        ref.at[layer : layer + 1] for ref in (gain_ref, offset_ref, down_bias_ref)
    ]
    refs = refs[6:]
    x_ref = None
    if count > 1:
        x_ref, refs = refs[0], refs[1:]
    part_ref, h_ref, act_ref, slope_ref = refs
    step = pl.program_id(0)

    @pl.when(step == 0)
    def _():
        start_layer(stream, x_ref, h_ref, gain_ref, offset_ref)
        part_ref[...] = jnp.broadcast_to(down_bias_ref[...].astype(F32), part_ref.shape)

    for first in range(0, h_ref.shape[0], FF_ROWS):
        rows = slice(first, first + FF_ROWS)
        units = dot_nt(h_ref[rows], up_ref[0]) + bias_ref[0]
        below, density = gelu_parts(units)
        active = (units * below).astype(BF16)
        act_ref[0, rows] = active
        slope_ref[0, rows] = (below + units * density).astype(BF16)
        part_ref[rows] += dot_nn(active, down_ref[0, 0])


def plane_block(length, lanes):
    per_plane = 1024 // lanes
    return pl.BlockSpec((1, length, lanes), lambda j: (j // per_plane, 0, j % per_plane))


def mlp_forward(layer, stream, gain, offset, up, biases, down_weight, down_bias):
    length, width = stream[0].shape
    hidden = up.shape[1]
    blocks = hidden // FF_BLOCK
    state = jax.ShapeDtypeStruct((4, length, width), BF16)
    full = jax.ShapeDtypeStruct((length, width), F32)
    out_shape = [full, jax.ShapeDtypeStruct((length, width), BF16), state, state]
    out_specs = [whole((length, width)), whole((length, width))]
    out_specs += [plane_block(length, FF_BLOCK)] * 2
    if len(stream) > 1:
        out_shape, out_specs = [full] + out_shape, [whole((length, width))] + out_specs
    return pl.pallas_call(
        functools.partial(mlp_forward_kernel, layer, len(stream)),
        grid=(blocks,),
        in_specs=[whole((length, width))] * len(stream)
        + [
            whole((LAYERS, width)),
            whole((LAYERS, width)),
            pl.BlockSpec((1, FF_BLOCK, width), lambda j: (layer, j, 0)),
            pl.BlockSpec((1, 1, FF_BLOCK), lambda j: (layer * blocks + j, 0, 0)),
            pl.BlockSpec((1, 1, FF_BLOCK, width), lambda j: (0, layer, j, 0)),
            whole((LAYERS, width)),
        ],
        out_specs=out_specs,
        out_shape=out_shape,
        compiler_params=params(),
        name="mlp_forward",
    )(*stream, gain, offset, up, biases, down_weight, down_bias)


def add_stream(stream, result_ref):
    if stream:
        result_ref[...] = stream[0][...] + (stream[1][...] + stream[2][...])


def stream_specs(stream):
    specs = [
        pl.BlockSpec((part.shape[0] // 4, part.shape[1]), lambda j, *_: (j, 0)) for part in stream
    ]
    shapes = [jax.ShapeDtypeStruct(part.shape, F32) for part in stream[:1]]
    return specs, specs[:1], shapes


def mlp_backward_kernel(count, place_ref, *refs):
    stream, refs = refs[:count], refs[count:]
    grad_ref, h_ref, act_ref, slope_ref, down_ref, up_ref = refs[:6]
    result_ref, refs = (refs[6], refs[7:]) if count else (None, refs[6:])
    part_ref, along_x, kept_x, along_y, kept_y, bias_ref = refs[:6]
    grad_t, h_t, units = refs[6:]
    step = pl.program_id(0)
    add_stream(stream, result_ref)

    @pl.when(step == 0)
    def _():
        grad_t[...] = grad_ref[...].T
        h_t[...] = h_ref[...].T
        part_ref[...] = jnp.zeros_like(part_ref)

    bias = jnp.zeros((1, FF_BLOCK), F32)
    for first in range(0, h_ref.shape[0], ROWS):
        rows = slice(first, first + ROWS)
        grad_act = dot_nt(grad_ref[rows], down_ref[0, 0])
        grad_unit = (grad_act * slope_ref[0, rows].astype(F32)).astype(BF16)
        bias += jnp.sum(grad_unit.astype(F32), axis=0, keepdims=True)
        units[rows] = grad_unit
        part_ref[rows] += dot_nn(grad_unit, up_ref[0])
    bias_ref[pl.ds(step, 1)] = bias

    mlp_weights(
        place_ref, grad_t, h_t, act_ref.at[0], units, along_x, kept_x, along_y, kept_y
    )


def mlp_weights(place_ref, grad_t, h_t, act, units, along_x, kept_x, along_y, kept_y):
    def block(y, x):
        return pl.ds(pl.multiple_of((2 * y + x) * WIDE, WIDE), WIDE)

    near_x, near_y = place_ref[0], place_ref[1]
    for first in range(0, h_t.shape[0], ROWS):
        rows = slice(first, first + ROWS)
        for side in range(2):
            for target, x in ((along_x, 1 - near_x), (kept_x, near_x)):
                target[0, side, rows] = dot_nn(grad_t[rows], act[:, block(side, x)])
            for target, y in ((along_y, 1 - near_y), (kept_y, near_y)):
                target[0, side, rows] = dot_nn(h_t[rows], units[:, block(y, side)])


def mlp_last_kernel(layer, place_ref, *refs):
    stream, refs = refs[:3], refs[3:]
    gain_ref, offset_ref, up_ref, bias_ref, down_ref, down_bias_ref, grad_ref = refs[:7]
    gain_ref, offset_ref, down_bias_ref = [
        ref.at[layer : layer + 1] for ref in (gain_ref, offset_ref, down_bias_ref)
    ]
    x_hbm, part_ref, grad_part, along_x, kept_x, along_y, kept_y, bias_out = refs[7:15]
    h_ref, grad_t, h_t, act, units, loads, stores = refs[15:]
    step = pl.program_id(0)

    @pl.when(step == 0)
    def _():
        buffers = (act, part_ref, grad_part)
        start_last_layer(stream, x_hbm, buffers, loads, stores, h_ref, gain_ref, offset_ref)
        part_ref[...] = jnp.broadcast_to(down_bias_ref[...].astype(F32), part_ref.shape)
        grad_part[...] = jnp.zeros_like(grad_part)
        grad_t[...] = grad_ref[...].T
        h_t[...] = h_ref[...].T

    bias = jnp.zeros((1, FF_BLOCK), F32)
    for first in range(0, h_ref.shape[0], ROWS):
        rows = slice(first, first + ROWS)
        hidden = dot_nt(h_ref[rows], up_ref[0]) + bias_ref[0]
        below, density = gelu_parts(hidden)
        active = (hidden * below).astype(BF16)
        act[rows] = active
        part_ref[rows] += dot_nn(active, down_ref[0, 0])
        grad_act = dot_nt(grad_ref[rows], down_ref[0, 0])
        grad_unit = (grad_act * (below + hidden * density)).astype(BF16)
        bias += jnp.sum(grad_unit.astype(F32), axis=0, keepdims=True)
        units[rows] = grad_unit
        grad_part[rows] += dot_nn(grad_unit, up_ref[0])
    bias_out[pl.ds(step, 1)] = bias
    mlp_weights(place_ref, grad_t, h_t, act, units, along_x, kept_x, along_y, kept_y)


def mlp_last(layer, place, stream, gain, offset, up, biases, down_weight, down_bias, grad):
    length, width = stream[0].shape
    blocks = up.shape[1] // FF_BLOCK
    full = jax.ShapeDtypeStruct((length, width), F32)
    pair = pl.BlockSpec((1, 2, width, WIDE), lambda j, *_: (j, 0, 0, 0))
    return pl.pallas_call(
        functools.partial(mlp_last_kernel, layer),
        grid_spec=pltpu.PrefetchScalarGridSpec(
            num_scalar_prefetch=1,
            grid=(blocks,),
            in_specs=[pl.BlockSpec(memory_space=pltpu.HBM)] * 3
            + [
                whole((LAYERS, width)),
                whole((LAYERS, width)),
                pl.BlockSpec((1, FF_BLOCK, width), lambda j, *_: (layer, j, 0)),
                pl.BlockSpec((1, 1, FF_BLOCK), lambda j, *_: (layer * blocks + j, 0, 0)),
                pl.BlockSpec((1, 1, FF_BLOCK, width), lambda j, *_: (0, layer, j, 0)),
                whole((LAYERS, width)),
                whole((length, width)),
            ],
            out_specs=[pl.BlockSpec(memory_space=pltpu.HBM)]
            + [whole((length, width))] * 2
            + [pair] * 4
            + [whole((blocks, FF_BLOCK))],
            scratch_shapes=[
                pltpu.VMEM((length, width), BF16),
                pltpu.VMEM((width, length), BF16),
                pltpu.VMEM((width, length), BF16),
                pltpu.VMEM((length, FF_BLOCK), BF16),
                pltpu.VMEM((length, FF_BLOCK), BF16),
            ]
            + chunk_semaphores(length),
        ),
        out_shape=[full, full, full]
        + halves_of(width, (4, 2, width, WIDE))
        + [jax.ShapeDtypeStruct((blocks, FF_BLOCK), F32)],
        compiler_params=params(),
        name="mlp_last",
    )(place, *stream, gain, offset, up, biases, down_weight, down_bias, grad)


def halves_of(width, weight):
    shapes = (weight,) * 2 + ((4, 2, width, WIDE),) * 2
    return [jax.ShapeDtypeStruct(shape, F32) for shape in shapes]


def flat_halves(part, sent, kept, sent_up, kept_up, bias):
    halves = [half.reshape((-1,) + half.shape[2:]) for half in (sent, kept, sent_up, kept_up)]
    return (part, *halves, bias)


def mlp_backward(layer, place, grad, h, act, slope, down_weight, up, stream=()):
    length, width = h.shape
    hidden = up.shape[1]
    blocks = hidden // FF_BLOCK
    pair = pl.BlockSpec((1, 2, width, WIDE), lambda j, *_: (j, 0, 0, 0))
    plane = pl.BlockSpec((1, length, FF_BLOCK), lambda j, *_: (j, 0, 0))
    stream_in, stream_out, stream_shape = stream_specs(stream)
    return pl.pallas_call(
        functools.partial(mlp_backward_kernel, len(stream)),
        grid_spec=pltpu.PrefetchScalarGridSpec(
            num_scalar_prefetch=1,
            grid=(blocks,),
            in_specs=stream_in
            + [
                whole((length, width)),
                whole((length, width)),
                plane,
                plane,
                pl.BlockSpec((1, 1, FF_BLOCK, width), lambda j, *_: (0, layer, j, 0)),
                pl.BlockSpec((1, FF_BLOCK, width), lambda j, *_: (layer, j, 0)),
            ],
            out_specs=stream_out
            + [whole((length, width))]
            + [pair] * 4
            + [whole((blocks, FF_BLOCK))],
            scratch_shapes=[
                pltpu.VMEM((width, length), BF16),
                pltpu.VMEM((width, length), BF16),
                pltpu.VMEM((length, FF_BLOCK), BF16),
            ],
        ),
        out_shape=stream_shape
        + [jax.ShapeDtypeStruct((length, width), F32)]
        + halves_of(width, (4, 2, width, WIDE))
        + [jax.ShapeDtypeStruct((blocks, FF_BLOCK), F32)],
        compiler_params=params(),
        name="mlp_backward",
    )(place, *stream, grad, h, act, slope, down_weight, up)


def head_sums(values, ones):
    upper, lower = split(values)
    return dot_nn(upper, ones) + dot_nn(lower, ones)


def same_head_ones():
    same = row_index(WIDE, WIDE) // DH == lane_index(WIDE, WIDE) // DH
    return jnp.where(same, 1.0, 0.0).astype(BF16)


def document_of(starts_ref, positions):
    return sum((starts_ref[0, i] <= positions).astype(jnp.int32) for i in range(starts_ref.shape[1]))


def write_mask(starts_ref, mask_ref, flipped):
    for first in range(0, mask_ref.shape[0], ROWS):
        lanes = lane_index(1, ROWS) + first
        own = row_index(ROWS, 1) + first
        order = (own <= lanes) if flipped else (lanes <= own)
        seen = (document_of(starts_ref, own) == document_of(starts_ref, lanes)) & order
        mask_ref[first : first + ROWS] = jnp.where(seen, 1.0, 0.0).astype(BF16)


def document_edges(starts_ref, length):
    edges = []
    for first in range(0, length, ROWS):
        rows = document_of(starts_ref, row_index(ROWS, 1) + first)
        here = document_of(starts_ref, first)
        later = document_of(starts_ref, first + ROWS)
        edges.append((rows == here, rows == later, here == later))
    return edges


def wide_rotary(cosine_ref, sine_ref, rows):
    return tuple(
        jnp.concatenate([ref[rows]] * (WIDE // PAIR), axis=1) for ref in (cosine_ref, sine_ref)
    )


def attend_heads(
    first_bias, starts_ref, weight_ref, bias_ref, upper_ref, lower_ref, scale_ref, cosine_ref,
    sine_ref, part_ref, h_ref, state_ref, mixed_ref, mask_ref,
):
    length = h_ref.shape[0]
    ones = same_head_ones()
    table_up, table_low = upper_ref[0, 0], lower_ref[0, 0]
    lanes_of_step = pl.ds(pl.multiple_of(pl.program_id(0) * WIDE, WIDE), WIDE)

    def features(values, rows):
        upper, lower = split(turn(values, *wide_rotary(cosine_ref, sine_ref, rows)))
        return dot_nn(upper, table_up) + (dot_nn(lower, table_up) + dot_nn(upper, table_low))

    for first in range(0, length, ROWS):
        rows = slice(first, first + ROWS)
        queries, keys, values = [
            dot_nt(h_ref[rows], weight_ref[0, 0, kind, 0])
            + bias_ref[first_bias + kind, :, lanes_of_step]
            for kind in range(3)
        ]
        state_ref[0, rows] = jnp.exp(features(queries, rows)).astype(BF16)
        logs = features(keys, rows) - (0.5 / math.sqrt(DH)) * head_sums(keys * keys, ones)
        state_ref[1, rows] = (scale_ref[0, 0] * jnp.exp(logs)).astype(BF16)
        state_ref[2, rows] = keys.astype(BF16)
        state_ref[3, rows] = values.astype(BF16)

    zero = jnp.zeros((), BF16)
    one = jnp.ones((), BF16)
    left = lane_index(ROWS, PAIR) < DH
    row, lane = row_index(PAIR, 2 * PAIR), lane_index(PAIR, 2 * PAIR)
    same = row // DH == lane // PAIR
    edges = document_edges(starts_ref, length)
    for pair in range(WIDE // PAIR):
        lanes = slice(pair * PAIR, (pair + 1) * PAIR)
        before = None
        for block, (same_first, same_next, goes_on) in enumerate(edges):
            rows = slice(block * ROWS, (block + 1) * ROWS)
            seen = mask_ref[rows] > zero
            queries, keys = state_ref[0, rows, lanes], state_ref[1, rows, lanes]
            values = [jnp.where(own, state_ref[3, rows, lanes], one) for own in (left, ~left)]
            if block > 0:
                earlier = dot_nn(queries, before.astype(BF16))
                earlier = jnp.where(same_first, earlier, 0.0)
            sums = []
            for head, own in enumerate((left, ~left)):
                scores = dot_nt(queries, jnp.where(own, keys, zero)).astype(BF16)
                total = dot_nn(jnp.where(seen, scores, zero), values[head])
                if block > 0:
                    total = total + earlier[:, head * PAIR : (head + 1) * PAIR]
                sums.append(total)
            if block + 1 < len(edges):
                kept = jnp.where(same_next, keys, zero)
                added = jnp.where(same, dot_tn(kept, jnp.concatenate(values, axis=1)), 0.0)
                if block > 0:
                    added = added + jnp.where(goes_on, before, 0.0)
                before = added
            numer = jnp.where(left, sums[0], sums[1])
            denom = jnp.where(left, pltpu.roll(sums[0], DH, 1), pltpu.roll(sums[1], DH, 1))
            inverse = 1.0 / denom
            mixed_ref[0, rows, lanes] = (numer * inverse).astype(BF16)
            mixed_ref[1, rows, lanes], mixed_ref[2, rows, lanes] = split(inverse)
    for first in range(0, length, ROWS):
        rows = slice(first, first + ROWS)
        part_ref[rows] += dot_nn(mixed_ref[0, rows], weight_ref[0, 0, 3, 0])


def attention_forward_kernel(layer, count, *refs):
    stream, refs = refs[:count], refs[count:]
    starts_ref, gain_ref, offset_ref, weight_ref, bias_ref = refs[:5]
    gain_ref, offset_ref = [ref.at[layer : layer + 1] for ref in (gain_ref, offset_ref)]
    first_bias = layer * (bias_ref.shape[0] // LAYERS)
    upper_ref, lower_ref, scale_ref, cosine_ref, sine_ref = refs[5:10]
    refs = refs[10:]
    x_ref = None
    if count > 1:
        x_ref, refs = refs[0], refs[1:]
    part_ref, h_ref, state_ref, mixed_ref, mask_ref = refs

    @pl.when(pl.program_id(0) == 0)
    def _():
        start_layer(stream, x_ref, h_ref, gain_ref, offset_ref)
        write_mask(starts_ref, mask_ref, False)
        part_ref[...] = jnp.broadcast_to(bias_ref[first_bias + 3], part_ref.shape)

    attend_heads(
        first_bias, starts_ref, weight_ref, bias_ref, upper_ref, lower_ref, scale_ref, cosine_ref,
        sine_ref, part_ref, h_ref, state_ref, mixed_ref, mask_ref,
    )


def kinds_of(weight):
    return weight.reshape(weight.shape[:2] + (4, QUADS, WIDE, weight.shape[3]))


def attention_forward(layer, stream, starts, gain, offset, weight, biases, tables, rotary):
    length, width = stream[0].shape
    full = jax.ShapeDtypeStruct((length, width), F32)
    state = jax.ShapeDtypeStruct((4, length, width), BF16)
    out_shape = [full, jax.ShapeDtypeStruct((length, width), BF16), state, state]
    four = pl.BlockSpec((4, length, WIDE), lambda g: (0, 0, g))
    out_specs = [whole((length, width)), whole((length, width)), four, four]
    if len(stream) > 1:
        out_shape, out_specs = [full] + out_shape, [whole((length, width))] + out_specs
    return pl.pallas_call(
        functools.partial(attention_forward_kernel, layer, len(stream)),
        grid=(QUADS,),
        in_specs=[whole((length, width))] * len(stream)
        + [
            pl.BlockSpec(memory_space=pltpu.SMEM),
            whole((LAYERS, width)),
            whole((LAYERS, width)),
            pl.BlockSpec((1, 1, 4, 1, WIDE, width), lambda g: (0, layer, 0, g, 0, 0)),
            whole((LAYERS * 4, 1, width)),
            pl.BlockSpec((1, 1, WIDE, WIDE), lambda g: (layer, g, 0, 0)),
            pl.BlockSpec((1, 1, WIDE, WIDE), lambda g: (layer, g, 0, 0)),
            pl.BlockSpec((1, 1, 1, WIDE), lambda g: (layer, g, 0, 0)),
            whole((length, PAIR)),
            whole((length, PAIR)),
        ],
        out_specs=out_specs,
        out_shape=out_shape,
        scratch_shapes=[pltpu.VMEM((length, ROWS), BF16)],
        compiler_params=params(),
        name="attention_forward",
    )(
        *stream, starts, gain, offset, kinds_of(weight),
        biases, *tables, *rotary,
    )


def attend_heads_back(
    place_ref, starts_ref, grad_ref, state_ref, mixed_ref, table_ref, cosine_ref, sine_ref,
    weight_ref, part_ref, along_z, kept_z, bias_ref, mask_ref, upright, numer_ref, feat_ref, flow,
):
    group = pl.program_id(0)
    length, width = grad_ref.shape
    row, lane = row_index(WIDE, WIDE), lane_index(WIDE, WIDE)
    partner = (row // PAIR == lane // PAIR) & (row // DH != lane // DH)
    partner = jnp.where(partner, 1.0, 0.0).astype(BF16)
    zero = jnp.zeros((), BF16)
    one = jnp.ones((), BF16)
    for first in range(0, length, ROWS):
        rows = slice(first, first + ROWS)
        grad = dot_nt(grad_ref[rows], weight_ref[0, 0, 3, 0]).astype(BF16).astype(F32)
        inverse = mixed_ref[1, rows].astype(F32) + mixed_ref[2, rows].astype(F32)
        scaled = grad * inverse
        upper, lower = split(-head_sums(scaled * mixed_ref[0, rows].astype(F32), partner))
        numer = scaled.astype(BF16)
        lane = lane_index(ROWS, WIDE)
        spare = jnp.where(lane % DH == 0, upper, jnp.where(lane % DH == 1, lower, zero))
        left = lane % PAIR < DH
        numer_ref[0, rows] = jnp.where(left, numer, spare)
        numer_ref[1, rows] = jnp.where(left, spare, numer)

    left = lane_index(ROWS, PAIR) < DH
    spare = jnp.where(lane_index(ROWS, PAIR) % DH < 2, one, zero)
    row, lane = row_index(2 * PAIR, PAIR), lane_index(2 * PAIR, PAIR)
    same = row // PAIR == lane // DH
    row, lane = row_index(PAIR, PAIR), lane_index(PAIR, PAIR)
    same_head = row // DH == lane // DH
    edges = document_edges(starts_ref, length)
    blocks = range(len(edges))

    def both(upper_and_lower, sums):
        upper, lower = split(sums)
        return dot_nn(upper_and_lower, upper) + dot_nn(upper_and_lower, lower)

    for pair in range(WIDE // PAIR):
        lanes = slice(pair * PAIR, (pair + 1) * PAIR)

        def rows_of_block(block):
            rows = slice(block * ROWS, (block + 1) * ROWS)
            numers = [numer_ref[head, rows, lanes] for head in range(2)]
            values = state_ref[3, rows, lanes]
            values = [jnp.where(own, values, spare) for own in (left, ~left)]
            return rows, state_ref[0, rows, lanes], state_ref[1, rows, lanes], values, numers

        before, after = {}, {}
        for block in blocks[1:]:
            rows, queries, keys, values, numers = rows_of_block(block - 1)
            _, same_next, goes_on = edges[block - 1]
            kept = jnp.where(same_next, keys, zero)
            added = jnp.where(same, dot_tn(jnp.concatenate(values, axis=1), kept), 0.0)
            if block > 1:
                added = added + jnp.where(goes_on, before[block - 1], 0.0)
            before[block] = added
        for block in blocks[::-1][:-1]:
            rows, queries, keys, values, numers = rows_of_block(block)
            same_first, _, goes_on = edges[block]
            kept = jnp.where(same_first, queries, zero)
            keys_sum = jnp.where(same, dot_tn(jnp.concatenate(numers, axis=1), kept), 0.0)
            values_sum = dot_tn(kept, jnp.where(left, numers[0], numers[1]))
            values_sum = jnp.where(same_head, values_sum, 0.0)
            if block + 1 < len(edges):
                keys_sum = keys_sum + jnp.where(goes_on, after[block + 1][0], 0.0)
                values_sum = values_sum + jnp.where(goes_on, after[block + 1][1], 0.0)
            after[block] = (keys_sum, values_sum)
        for block in blocks:
            rows, queries, keys, values, numers = rows_of_block(block)
            same_first, same_next, _ = edges[block]
            seen = mask_ref[rows] > zero
            numer = jnp.where(left, numers[0], numers[1])
            grads = []
            grad_query = None
            for head, own in enumerate((left, ~left)):
                own_keys = jnp.where(own, keys, zero)
                scores = dot_nt(own_keys, queries).astype(BF16)
                grad_value = dot_nn(jnp.where(seen, scores, zero), numer)
                grad_scores = dot_nt(values[head], numers[head]).astype(BF16)
                grad_scores = jnp.where(seen, grad_scores, zero)
                grads.append((grad_value, dot_nn(grad_scores, queries)))
                from_head = dot_tn(grad_scores, own_keys)
                grad_query = from_head if head == 0 else grad_query + from_head
            grad_value = jnp.where(left, grads[0][0], grads[1][0])
            grad_key = jnp.where(left, grads[0][1], grads[1][1])
            if block + 1 < len(edges):
                keys_sum, values_sum = after[block + 1]
                late = both(jnp.concatenate(values, axis=1), keys_sum)
                grad_key = grad_key + jnp.where(same_next, late, 0.0)
                late = dot_nn(keys, values_sum.astype(BF16))
                grad_value = grad_value + jnp.where(same_next, late, 0.0)
            if block > 0:
                early = both(jnp.concatenate(numers, axis=1), before[block])
                grad_query = grad_query + jnp.where(same_first, early, 0.0)
            flow[2, rows, lanes] = grad_value.astype(BF16)
            feat_ref[1, rows, lanes] = (grad_key * keys.astype(F32)).astype(BF16)
            feat_ref[0, rows, lanes] = (grad_query * queries.astype(F32)).astype(BF16)

    ones = same_head_ones()
    table = table_ref[0, 0]
    sums = [jnp.zeros((1, WIDE), F32)] * 3
    for first in range(0, length, ROWS):
        rows = slice(first, first + ROWS)
        cosine, sine = wide_rotary(cosine_ref, sine_ref, rows)
        flow[0, rows] = turn_back(dot_nt(feat_ref[0, rows], table), cosine, sine).astype(BF16)
        shrink = dot_nn(feat_ref[1, rows], ones) * (1.0 / math.sqrt(DH))
        turned = turn_back(dot_nt(feat_ref[1, rows], table), cosine, sine)
        flow[1, rows] = (turned - state_ref[2, rows].astype(F32) * shrink).astype(BF16)
        total = part_ref[rows]
        for kind in range(3):
            block = flow[kind, rows]
            sums[kind] = sums[kind] + jnp.sum(block.astype(F32), axis=0, keepdims=True)
            total = total + dot_nn(block, weight_ref[0, 0, kind, 0])
        part_ref[rows] = total
    for kind in range(3):
        bias_ref[kind : kind + 1] = sums[kind]
    lanes = pl.ds(pl.multiple_of(group * WIDE, WIDE), WIDE)
    bias_ref[3:4] = jnp.sum(grad_ref[:, lanes].astype(F32), axis=0, keepdims=True)
    flow[3] = mixed_ref[0]
    for first in range(0, width, ROWS):
        rows = slice(first, first + ROWS)
        for far in range(2):
            for target, near in ((along_z, 1 - place_ref[2]), (kept_z, place_ref[2])):
                kind = 2 * far + near
                target[far, 0, rows] = dot_nn(upright[kind // 3, rows], flow[kind])


def attention_backward_kernel(count, place_ref, *refs):
    stream, refs = refs[:count], refs[count:]
    starts_ref, grad_ref, h_ref, state_ref, mixed_ref, table_ref = refs[:6]
    cosine_ref, sine_ref, weight_ref = refs[6:9]
    result_ref, refs = (refs[9], refs[10:]) if count else (None, refs[9:])
    part_ref, along_z, kept_z, _, _, bias_ref = refs[:6]
    mask_ref, upright, numer_ref, feat_ref, flow = refs[6:]
    add_stream(stream, result_ref)

    @pl.when(pl.program_id(0) == 0)
    def _():
        write_mask(starts_ref, mask_ref, True)
        upright[0] = h_ref[...].T
        upright[1] = grad_ref[...].T
        part_ref[...] = jnp.zeros_like(part_ref)

    attend_heads_back(
        place_ref, starts_ref, grad_ref, state_ref, mixed_ref, table_ref, cosine_ref, sine_ref,
        weight_ref, part_ref, along_z, kept_z, bias_ref, mask_ref, upright, numer_ref, feat_ref,
        flow,
    )


def attention_backward(
    layer, place, starts, grad, h, state, mixed, tables, rotary, weight, stream=()
):
    _, length, width = state.shape
    four = pl.BlockSpec((4, length, WIDE), lambda g, *_: (0, 0, g))
    halves = pl.BlockSpec((2, 1, width, WIDE), lambda g, *_: (0, g, 0, 0))
    stream_in, stream_out, stream_shape = stream_specs(stream)
    return pl.pallas_call(
        functools.partial(attention_backward_kernel, len(stream)),
        grid_spec=pltpu.PrefetchScalarGridSpec(
            num_scalar_prefetch=1,
            grid=(QUADS,),
            in_specs=stream_in
            + [
                pl.BlockSpec(memory_space=pltpu.SMEM),
                whole((length, width)),
                whole((length, width)),
                four,
                four,
                pl.BlockSpec((1, 1, WIDE, WIDE), lambda g, *_: (layer, g, 0, 0)),
                whole((length, PAIR)),
                whole((length, PAIR)),
                pl.BlockSpec((1, 1, 4, 1, WIDE, width), lambda g, *_: (0, layer, 0, g, 0, 0)),
            ],
            out_specs=stream_out
            + [whole((length, width))]
            + [halves, halves]
            + [pl.BlockSpec(memory_space=pl.ANY)] * 2
            + [pl.BlockSpec((4, WIDE), lambda g, *_: (0, g))],
            scratch_shapes=[
                pltpu.VMEM((length, ROWS), BF16),
                pltpu.VMEM((2, width, length), BF16),
                pltpu.VMEM((2, length, WIDE), BF16),
                pltpu.VMEM((2, length, WIDE), BF16),
                pltpu.VMEM((4, length, WIDE), BF16),
            ],
        ),
        out_shape=stream_shape
        + [jax.ShapeDtypeStruct((length, width), F32)]
        + halves_of(width, (2, 4, width, WIDE))
        + [jax.ShapeDtypeStruct((4, width), F32)],
        compiler_params=params(),
        name="attention_backward",
    )(place, *stream, starts, grad, h, state, mixed, tables[0], *rotary, kinds_of(weight))


def attention_last_kernel(layer, place_ref, *refs):
    stream, refs = refs[:3], refs[3:]
    starts_ref, gain_ref, offset_ref, weight_ref, bias_ref = refs[:5]
    gain_ref, offset_ref = [ref.at[layer : layer + 1] for ref in (gain_ref, offset_ref)]
    first_bias = layer * (bias_ref.shape[0] // LAYERS)
    upper_ref, lower_ref, scale_ref, cosine_ref, sine_ref, grad_ref = refs[5:11]
    x_hbm, part_ref, grad_part, along_z, kept_z, _, _, bias_out = refs[11:19]
    h_ref, state_ref, mixed_ref, mask_ref, mask_back = refs[19:24]
    upright, numer_ref, feat_ref, flow, loads, stores = refs[24:]

    @pl.when(pl.program_id(0) == 0)
    def _():
        buffers = (upright.at[0], part_ref, grad_part)
        start_last_layer(stream, x_hbm, buffers, loads, stores, h_ref, gain_ref, offset_ref)
        write_mask(starts_ref, mask_ref, False)
        write_mask(starts_ref, mask_back, True)
        part_ref[...] = jnp.broadcast_to(bias_ref[first_bias + 3], part_ref.shape)
        grad_part[...] = jnp.zeros_like(grad_part)
        upright[0] = h_ref[...].T
        upright[1] = grad_ref[...].T

    attend_heads(
        first_bias, starts_ref, weight_ref, bias_ref, upper_ref, lower_ref, scale_ref, cosine_ref,
        sine_ref, part_ref, h_ref, state_ref, mixed_ref, mask_ref,
    )
    attend_heads_back(
        place_ref, starts_ref, grad_ref, state_ref, mixed_ref, upper_ref, cosine_ref, sine_ref,
        weight_ref, grad_part, along_z, kept_z, bias_out, mask_back, upright, numer_ref, feat_ref,
        flow,
    )


def attention_last(
    layer, place, stream, starts, gain, offset, weight, biases, tables, rotary, grad
):
    length, width = stream[0].shape
    full = jax.ShapeDtypeStruct((length, width), F32)
    halves = pl.BlockSpec((2, 1, width, WIDE), lambda g, *_: (0, g, 0, 0))
    return pl.pallas_call(
        functools.partial(attention_last_kernel, layer),
        grid_spec=pltpu.PrefetchScalarGridSpec(
            num_scalar_prefetch=1,
            grid=(QUADS,),
            in_specs=[pl.BlockSpec(memory_space=pltpu.HBM)] * 3
            + [
                pl.BlockSpec(memory_space=pltpu.SMEM),
                whole((LAYERS, width)),
                whole((LAYERS, width)),
                pl.BlockSpec((1, 1, 4, 1, WIDE, width), lambda g, *_: (0, layer, 0, g, 0, 0)),
                whole((LAYERS * 4, 1, width)),
                pl.BlockSpec((1, 1, WIDE, WIDE), lambda g, *_: (layer, g, 0, 0)),
                pl.BlockSpec((1, 1, WIDE, WIDE), lambda g, *_: (layer, g, 0, 0)),
                pl.BlockSpec((1, 1, 1, WIDE), lambda g, *_: (layer, g, 0, 0)),
                whole((length, PAIR)),
                whole((length, PAIR)),
                whole((length, width)),
            ],
            out_specs=[pl.BlockSpec(memory_space=pltpu.HBM)]
            + [whole((length, width))] * 2
            + [halves, halves]
            + [pl.BlockSpec(memory_space=pl.ANY)] * 2
            + [pl.BlockSpec((4, WIDE), lambda g, *_: (0, g))],
            scratch_shapes=[
                pltpu.VMEM((length, width), BF16),
                pltpu.VMEM((4, length, WIDE), BF16),
                pltpu.VMEM((3, length, WIDE), BF16),
                pltpu.VMEM((length, ROWS), BF16),
                pltpu.VMEM((length, ROWS), BF16),
                pltpu.VMEM((2, width, length), BF16),
                pltpu.VMEM((2, length, WIDE), BF16),
                pltpu.VMEM((2, length, WIDE), BF16),
                pltpu.VMEM((4, length, WIDE), BF16),
            ]
            + chunk_semaphores(length),
        ),
        out_shape=[full, full, full]
        + halves_of(width, (2, 4, width, WIDE))
        + [jax.ShapeDtypeStruct((4, width), F32)],
        compiler_params=params(),
        name="attention_last",
    )(
        place, *stream, starts, gain, offset, kinds_of(weight), biases, *tables, *rotary, grad
    )


def norm_gradient(values, incoming, grad, gain, sums_ref):
    average = jnp.mean(values, -1, keepdims=True)
    centered = values - average
    variance = jnp.mean(centered * centered, -1, keepdims=True)
    inverse = lax.rsqrt(variance + EPSILON)
    unit = centered * inverse
    grad_unit = incoming * gain
    first = jnp.mean(grad_unit, -1, keepdims=True)
    second = jnp.mean(grad_unit * unit, -1, keepdims=True)
    sums_ref[0:1] += jnp.sum(incoming * unit, axis=0, keepdims=True)
    sums_ref[1:2] += jnp.sum(incoming, axis=0, keepdims=True)
    sums_ref[2:3] += jnp.sum(grad, axis=0, keepdims=True)
    return grad + inverse * (grad_unit - first - unit * second)


def norm_backward_kernel(layer, x_ref, own_ref, other_ref, grad_ref, gain_ref, out_ref, sums_ref):
    @pl.when(pl.program_id(0) == 0)
    def _():
        sums_ref[...] = jnp.zeros_like(sums_ref)

    out = norm_gradient(
        x_ref[...].astype(F32),
        own_ref[...] + other_ref[...],
        grad_ref[...].astype(F32),
        gain_ref[layer : layer + 1].astype(F32),
        sums_ref,
    )
    out_ref[...] = out.astype(out_ref.dtype)


def norm_backward(layer, x, own, other, grad, gain, kind):
    length, width = own.shape
    block = pl.BlockSpec((ROWS, width), lambda i: (i, 0))
    return pl.pallas_call(
        functools.partial(norm_backward_kernel, layer),
        grid=(length // ROWS,),
        in_specs=[block, block, block, block, whole((LAYERS, width))],
        out_specs=[block, whole((8, width))],
        out_shape=[
            jax.ShapeDtypeStruct((length, width), kind),
            jax.ShapeDtypeStruct((8, width), F32),
        ],
        compiler_params=params(),
        name="norm_backward",
    )(x, own, other, grad, gain)


MESH = pl.DeviceIdType.MESH
UNIT = 16
SLOTS = 6
LAG = 2


class Flow(NamedTuple):
    order: tuple
    core: int
    is_up: int
    layer: int
    row: int
    units: int
    start: int
    place: int


def flows_of(width, layer, start):
    rows = width // 2
    kinds = (
        ((0, 1, 2, 3), 1, 0, 0, 0),
        ((1, 0, 2, 3), 1, 1, 0, 1),
        ((0, 1, 2, 3), 1, 0, 1, 2),
        ((1, 0, 2, 3), 1, 1, 1, 3),
        ((2, 0, 1, 3), 0, 0, 0, 0),
        ((2, 1, 0, 3), 0, 0, 1, 1),
    )
    return [
        Flow(order, core, is_up, layer, part * rows, rows // UNIT, start, 4 * layer + place)
        for order, core, is_up, part, place in kinds
    ]


def bit_of(index, bit):
    return (index // (1 << bit)) % 2


def flip(index, bit):
    return index + (1 << bit) * (1 - 2 * bit_of(index, bit))


def finish_kernel(
    bits, flows,
    kept_weight1, kept_up1, came_weight1, came_up1,
    kept_weight0, kept_up0, sent_weight0, sent_up0,
    bias0_ref, bias1_ref, sums1_ref, sums0_ref,
    weight_out, up_out, small_out,
    weight_sum, up_sum, up_turned, up_came,
    *scratch,
):
    stages = bits
    kept = ((kept_weight1, kept_up1), (kept_weight0, kept_up0))
    moved = ((came_weight1, came_up1), (sent_weight0, sent_up0))
    small_parts = (bias0_ref, bias1_ref, sums1_ref, sums0_ref)
    places = 1 + max(flow.place for flow in flows)
    held, scratch = scratch[: places * (stages + 1)], scratch[places * (stages + 1) :]
    held = [held[f * (stages + 1) : (f + 1) * (stages + 1)] for f in range(places)]
    small, small_came = scratch[: stages + 1], scratch[stages + 1 : 2 * stages + 1]
    load_sem, send_sem, recv_sem, credit, small_send, small_recv, near_send, near_recv = (
        scratch[2 * stages + 1 :]
    )
    me, core = lax.axis_index("batch"), lax.axis_index("stream")

    barrier = pltpu.get_barrier_semaphore()
    for bit in range(bits):
        pl.semaphore_signal(
            barrier, inc=1, device_id={"batch": flip(me, bit)}, device_id_type=MESH
        )
    pl.semaphore_signal(barrier, inc=1, device_id={"stream": 1 - core}, device_id_type=MESH)
    pl.semaphore_wait(barrier, bits + 1)

    small_start = 2
    turn_start = max(flow.start + flow.units for flow in flows if flow.layer == 1)
    turn_start += LAG * stages + 1

    def near_copy(layer):
        return pltpu.make_async_remote_copy(
            src_ref=up_turned.at[layer],
            dst_ref=up_came.at[layer],
            send_sem=near_send.at[layer],
            recv_sem=near_recv.at[layer],
            device_id={"stream": 0},
            device_id_type=MESH,
        )

    def turn_weights(layer):
        weight_out[len(moved) - 1 - layer] = weight_sum[layer].T

        @pl.when(core == 1)
        def _():
            up_turned[layer] = up_sum[layer, :, : WIDE // 2].T
            near_copy(layer).start()
            up_out[len(moved) - 1 - layer] = up_sum[layer, :, WIDE // 2 :].T

    def small_copy(stage):
        return pltpu.make_async_remote_copy(
            src_ref=small[stage],
            dst_ref=small_came[stage],
            send_sem=small_send.at[stage],
            recv_sem=small_recv.at[stage],
            device_id={"batch": flip(me, stage)},
            device_id_type=MESH,
        )

    def small_step(stage):
        if stage == 0:
            row = 0
            for part in small_parts:
                small[0][row : row + part.shape[0]] = part[...]
                row += part.shape[0]
        else:
            small_copy(stage - 1).wait()
            small[stage][...] = small[stage - 1][...] + small_came[stage - 1][...]
        if stage < stages:
            small_copy(stage).start()
        else:
            small_out[...] = small[stage][...]

    def view(order, stage, mine):
        left = sorted(set(range(bits)) - set(order[:stage]), reverse=True)
        pick = bit_of(me, order[stage])
        pick = pick if mine else 1 - pick
        return tuple(pick if bit == order[stage] else slice(None) for bit in left)

    def remote(flow, stage, slot, source):
        place = flow.place
        return pltpu.make_async_remote_copy(
            src_ref=source,
            dst_ref=held[place][stage + 1].at[slot],
            send_sem=send_sem.at[place, stage, slot],
            recv_sem=recv_sem.at[place, stage, slot],
            device_id={"batch": flip(me, flow.order[stage])},
            device_id_type=MESH,
        )

    def sent_from(flow, stage, slot):
        if stage == 0:
            return held[flow.place][0].at[slot]
        return held[flow.place][stage].at[(slot,) + view(flow.order, stage, False)]

    def load(flow, slot, source):
        place = flow.place
        return pltpu.make_async_copy(source, held[place][0].at[slot], load_sem.at[place, slot])

    def load_came(flow, slot, source):
        return pltpu.make_async_copy(
            source, held[flow.place][1].at[slot], recv_sem.at[flow.place, 0, slot]
        )

    def return_credit(flow, stage, unit):
        if stage == 0 and flow.layer == 0:
            return

        @pl.when(unit + SLOTS < flow.units)
        def _():
            pl.semaphore_signal(
                credit.at[flow.place, stage],
                inc=1,
                device_id={"batch": flip(me, flow.order[stage])},
                device_id_type=MESH,
            )

    def take_credit(flow, stage, unit):
        @pl.when(unit >= SLOTS)
        def _():
            pl.semaphore_wait(credit.at[flow.place, stage], 1)

    def begin(flow, unit):
        slot = lax.rem(unit, SLOTS)
        at = (slice(None),) * (bits - 1)
        at += (pl.ds(pl.multiple_of(flow.row + unit * UNIT, UNIT), UNIT),)
        load(flow, slot, kept[flow.layer][flow.is_up].at[at]).start()
        source = moved[flow.layer][flow.is_up].at[at]
        if flow.layer == 0:
            load_came(flow, slot, source).start()
        else:
            take_credit(flow, 0, unit)
            remote(flow, 0, slot, source).start()

    def advance(flow, stage, unit):
        slot = lax.rem(unit, SLOTS)
        buffers, begun = held[flow.place], flow.layer == 0
        copy = remote(flow, stage - 1, slot, sent_from(flow, stage - 1, slot))
        if stage == 1 and begun:
            load_came(flow, slot, buffers[0].at[slot]).wait()
        else:
            copy.wait_recv()
        if stage == 1:
            load(flow, slot, buffers[1].at[slot]).wait()
            mine = buffers[0][slot]
        else:
            mine = buffers[stage - 1][(slot,) + view(flow.order, stage - 1, True)]
        value = buffers[stage][slot] + mine
        if stage < stages:
            buffers[stage][slot] = value
            take_credit(flow, stage, unit)
            remote(flow, stage, slot, sent_from(flow, stage, slot)).start()
        else:
            target = up_sum if flow.is_up else weight_sum
            at = pl.ds(pl.multiple_of(flow.row + unit * UNIT, UNIT), UNIT)
            target[flow.layer, at] = value
        if stage > 1 or not begun:
            copy.wait_send()
        if stage >= 2:
            return_credit(flow, stage - 2, unit)
        if stage == stages:
            return_credit(flow, stage - 1, unit)

    def within(flow, unit):
        return (unit >= 0) & (unit < flow.units) & (core == flow.core)

    def step(index, carry):
        for flow in flows:
            unit = index - flow.start
            pl.when(within(flow, unit))(functools.partial(begin, flow, unit))
        for flow in flows:
            for stage in range(1, stages + 1):
                unit = index - flow.start - LAG * stage
                pl.when(within(flow, unit))(functools.partial(advance, flow, stage, unit))
        for stage in range(stages + 1):
            pl.when(index == small_start + 2 * stage)(functools.partial(small_step, stage))
        pl.when(index == turn_start)(functools.partial(turn_weights, 1))
        return carry

    last = max(flow.start + flow.units for flow in flows)
    lax.fori_loop(0, last + LAG * stages, step, 0)
    turn_weights(0)
    for layer in range(len(moved)):

        @pl.when(core == 0)
        def _():
            near_copy(layer).wait_recv()
            up_out[len(moved) - 1 - layer] = up_came[layer]

        @pl.when(core == 1)
        def _():
            near_copy(layer).wait_send()


def finish(last, first, came, smalls):
    width = last[0].shape[1]
    bits = 4
    split = (2,) * (bits - 1)
    flows = flows_of(width, 1, 0)
    flows += flows_of(width, 0, max(flow.start + flow.units for flow in flows))
    small = (sum(part.shape[0] for part in smalls), width)
    scratch = [
        pltpu.VMEM((2, width, WIDE), F32),
        pltpu.VMEM((2, width, WIDE), F32),
        pltpu.VMEM((2, WIDE // 2, width), F32),
        pltpu.VMEM((2, WIDE // 2, width), F32),
    ]
    places = 1 + max(flow.place for flow in flows)
    for _ in range(places):
        for stage in range(bits + 1):
            lead = (SLOTS,) + (2,) * (bits - 1 - max(stage - 1, 0))
            scratch.append(pltpu.VMEM(lead + (UNIT, WIDE), F32))
    scratch += [pltpu.VMEM(small, F32)] * (2 * bits + 1)
    scratch += [
        pltpu.SemaphoreType.DMA((places, SLOTS)),
        pltpu.SemaphoreType.DMA((places, bits, SLOTS)),
        pltpu.SemaphoreType.DMA((places, bits, SLOTS)),
        pltpu.SemaphoreType.REGULAR((places, bits)),
        pltpu.SemaphoreType.DMA((bits,)),
        pltpu.SemaphoreType.DMA((bits,)),
        pltpu.SemaphoreType.DMA((2,)),
        pltpu.SemaphoreType.DMA((2,)),
    ]
    large = [last[1], last[3], *came, first[1], first[3], first[0], first[2]]
    large = [array.reshape(split + array.shape[1:]) for array in large]
    return pl.pallas_call(
        functools.partial(finish_kernel, bits, flows),
        in_specs=[pl.BlockSpec(memory_space=pltpu.HBM)] * len(large)
        + [pl.BlockSpec(memory_space=pltpu.VMEM)] * len(smalls),
        out_specs=[pl.BlockSpec(memory_space=pltpu.VMEM)] * 3,
        out_shape=[
            jax.ShapeDtypeStruct((2, WIDE, width), F32),
            jax.ShapeDtypeStruct((2, WIDE // 2, width), F32),
            jax.ShapeDtypeStruct(small, F32),
        ],
        scratch_shapes=scratch,
        compiler_params=pltpu.CompilerParams(
            collective_id=0, has_side_effects=True, vmem_limit_bytes=VMEM_LIMIT
        ),
        name="finish",
    )(*large, *smalls)


def send_first(halves):
    count = lax.axis_size("batch")

    def pairs(stream, bit):
        return [(2 * source + stream, 2 * flip(source, bit) + stream) for source in range(count)]

    axes = ("batch", "stream")
    return [
        lax.ppermute(halves[0], axes, pairs(0, 2) + pairs(1, 0)),
        lax.ppermute(halves[2], axes, pairs(1, 1)),
    ]


def shards(
    tokens, cotangent, branch_weight, branch_bias, up_weight, down_bias,
    norm_gain, norm_bias, freq_seeds, doc_starts,
):
    is_attention = lax.axis_index("stream") == 0
    length, width = tokens.shape
    rotary = tuple(jnp.asarray(table) for table in rotary_rows(length))
    biases = branch_bias[0].astype(F32).reshape(-1, 1, width)
    tables = lax.cond(
        is_attention,
        lambda: tuple(feature_tables(freq_seeds)),
        lambda: (
            jnp.zeros((LAYERS, QUADS, WIDE, WIDE), BF16),
            jnp.zeros((LAYERS, QUADS, WIDE, WIDE), BF16),
            jnp.zeros((LAYERS, QUADS, 1, WIDE), F32),
        ),
    )
    swap = [(0, 1), (1, 0)]

    def attention(layer, stream):
        return tuple(
            attention_forward(
                layer, stream, doc_starts, norm_gain, norm_bias, branch_weight, biases, tables,
                rotary,
            )
        )

    def feed_forward(layer, stream):
        return tuple(
            mlp_forward(
                layer, stream, norm_gain, norm_bias, up_weight, biases, branch_weight, down_bias
            )
        )

    count = lax.axis_size("batch")
    blocked = count == branch_weight.shape[2] // WIDE
    me = lax.axis_index("batch") if blocked else 0
    place = jnp.stack([jnp.asarray(bit_of(me, bit), jnp.int32) for bit in range(3)])

    part, *kept = lax.cond(
        is_attention,
        functools.partial(attention, 0, (tokens,)),
        functools.partial(feed_forward, 0, (tokens,)),
    )
    stream = (tokens, part, lax.ppermute(part, "stream", swap))

    def attention_ends():
        x, part, *back = attention_last(
            1, place, stream, doc_starts, norm_gain, norm_bias, branch_weight, biases, tables,
            rotary, cotangent,
        )
        return x, part, *flat_halves(*back)

    def feed_forward_ends():
        x, part, *back = mlp_last(
            1, place, stream, norm_gain, norm_bias, up_weight, biases, branch_weight, down_bias,
            cotangent,
        )
        return x, part, *flat_halves(*back)

    x1, part, part1, *halves1, bias1 = lax.cond(is_attention, attention_ends, feed_forward_ends)
    stream = (x1, part, lax.ppermute(part, "stream", swap))

    def attention_back(layer, grad, stream):
        h, state, mixed = kept
        *result, part, a, b, c, d, bias = attention_backward(
            layer, place, doc_starts, grad, h, state, mixed, tables, rotary, branch_weight, stream
        )
        return *result, *flat_halves(part, a, b, c, d, bias)

    def feed_forward_back(layer, grad, stream):
        h, act, slope = kept
        *result, part, a, b, c, d, bias = mlp_backward(
            layer, place, grad, h, act, slope, branch_weight, up_weight, stream
        )
        return *result, *flat_halves(part, a, b, c, d, bias)

    def back(layer, grad, stream=()):
        *result, part, a, b, c, d, bias = lax.cond(
            is_attention,
            functools.partial(attention_back, layer, grad, stream),
            functools.partial(feed_forward_back, layer, grad, stream),
        )
        return *result, part, (a, b, c, d), bias

    def norm_back(layer, x, part, grad, kind):
        other = lax.ppermute(part, "stream", swap)
        return norm_backward(layer, x, part, other, grad, norm_gain, kind)

    if blocked:
        came = send_first(halves1)
    grad0, sums1 = norm_back(1, x1, part1, cotangent, BF16)
    result, part0, halves0, bias0 = back(0, grad0, stream)
    input_grad, sums0 = norm_back(0, tokens, part0, grad0, F32)
    if blocked:
        weight, up, small = finish(halves1, halves0, came, (bias0, bias1, sums1, sums0))
    else:
        weight, up = scatter_rows((halves0, halves1))
        small = lax.psum(jnp.concatenate([bias0, bias1, sums1, sums0]), "batch")
    index, rows = lax.axis_index("batch"), bias0.shape[0]
    each, own = branch_weight.shape[2] // count, width // count
    biases = small[: 2 * rows].reshape(LAYERS, -1)
    sums = small[2 * rows :].reshape(LAYERS, 8, width)[::-1]
    sums = lax.dynamic_slice_in_dim(sums, index * own, own, axis=2)
    return (
        result,
        input_grad,
        weight[None],
        lax.dynamic_slice_in_dim(biases, index * each, each, axis=1)[None],
        up,
        sums[:, 2],
        sums[:, 0],
        sums[:, 1],
    )


def scatter_rows(layers):
    weights, ups = [], []
    for sent, kept, sent_up, kept_up in layers:
        blocks = (-1,) + kept.shape[1:]
        wide, far = (4, 2) + kept.shape[1:], (2, 4) + kept.shape[1:]
        weight = jnp.where(
            lax.axis_index("stream") == 1,
            jnp.stack([kept.reshape(wide), sent.reshape(wide)], axis=2).reshape(blocks),
            jnp.stack([kept.reshape(far), sent.reshape(far)], axis=1).reshape(blocks),
        )
        weight = rows_of(weight)
        up = jnp.stack([kept_up.reshape(wide), sent_up.reshape(wide)], axis=1)
        up = rows_of(up.reshape(blocks))
        up = jnp.where(lax.axis_index("stream") == 1, up, 0.0)
        weights.append(lax.psum_scatter(weight, "batch", scatter_dimension=0, tiled=True))
        ups.append(lax.psum_scatter(up, ("batch", "stream"), scatter_dimension=0, tiled=True))
    return jnp.stack(weights), jnp.stack(ups)


def rows_of(blocks):
    return jnp.transpose(blocks, (0, 2, 1)).reshape(-1, blocks.shape[1])


def solution(mesh):
    placed = (
        P("batch", None),
        P("batch", None),
        P("stream", None, None, None),
        P("stream", None, None),
        P(),
        P(),
        P(),
        P(),
        P(),
        P("batch", None),
    )
    return jax.shard_map(
        shards,
        mesh=mesh,
        in_specs=placed,
        out_specs=(
            P("batch", None),
            P("batch", None),
            P("stream", None, "batch", None),
            P("stream", None, "batch"),
            P(None, ("batch", "stream"), None),
            P(None, "batch"),
            P(None, "batch"),
            P(None, "batch"),
        ),
        check_vma=False,
    )
```

```python
import functools
import math
from typing import NamedTuple

import jax
import jax.numpy as jnp
import numpy as np
from jax import lax
from jax.experimental import pallas as pl
from jax.experimental.pallas import tpu as pltpu
from jax.sharding import PartitionSpec as P

HEADS = 16
DH = 64
ROT = 16
FEAT = 64
LAYERS = 2
EPSILON = 1e-05
HIGH = lax.Precision.HIGHEST
F32 = jnp.float32
BF16 = jnp.bfloat16
WIDE = 256
PAIR = 128
QUADS = HEADS * DH // WIDE
PAIRS = HEADS * DH // PAIR
ROWS = 256
VMEM_LIMIT = 56 * 1024 * 1024


def params():
    return pltpu.CompilerParams(vmem_limit_bytes=VMEM_LIMIT)


def whole(shape):
    zeros = (0,) * len(shape)
    return pl.BlockSpec(shape, lambda *_: zeros, pipeline_mode=pl.Buffered(1))


def dot_nn(left, right):
    return lax.dot_general(left, right, (((1,), (0,)), ((), ())), preferred_element_type=F32)


def dot_tn(left, right):
    return lax.dot_general(left, right, (((0,), (0,)), ((), ())), preferred_element_type=F32)


def dot_nt(left, right):
    return lax.dot_general(left, right, (((1,), (1,)), ((), ())), preferred_element_type=F32)


def split(values):
    upper = values.astype(BF16)
    return upper, (values - upper.astype(F32)).astype(BF16)


def lane_index(rows, lanes):
    return lax.broadcasted_iota(jnp.int32, (rows, lanes), 1)


def row_index(rows, lanes):
    return lax.broadcasted_iota(jnp.int32, (rows, lanes), 0)


def cosine_block():
    samples = np.arange(DH, dtype=np.float64)
    angles = math.pi * (samples[None, :] + 0.5) * samples[:, None] / DH
    table = np.cos(angles) * math.sqrt(2.0 / DH)
    table[0] *= math.sqrt(0.5)
    return (table.T * DH ** (-0.25)).astype(np.float32)


def rotary_rows(length):
    position = np.arange(length, dtype=np.float32)
    inverse = (10000.0 ** (-np.arange(0, ROT, 2, dtype=np.float32) / ROT)).astype(np.float32)
    angles = position[:, None] * inverse[None, :]
    cosine, sine = np.cos(angles), np.sin(angles)
    rest = DH - ROT
    cosine_head = np.concatenate([cosine, cosine, np.ones((length, rest))], 1)
    sine_head = np.concatenate([-sine, sine, np.zeros((length, rest))], 1)
    repeat = PAIR // DH
    return (
        np.tile(cosine_head, (1, repeat)).astype(np.float32),
        np.tile(sine_head, (1, repeat)).astype(np.float32),
    )


def tables_kernel(seeds_ref, cosine_ref, upper_ref, lower_ref, weight_ref):
    feature = lane_index(DH, WIDE) % FEAT
    same_head = row_index(WIDE, WIDE) // DH == lane_index(WIDE, WIDE) // FEAT
    ones = jnp.where(same_head, 1.0, 0.0).astype(BF16)
    pick = (row_index(QUADS, WIDE) == lane_index(QUADS, WIDE) // FEAT).astype(BF16)
    cosine = cosine_ref[...]
    for group in range(QUADS):
        seeds = seeds_ref[0, group * QUADS : (group + 1) * QUADS].astype(F32).astype(BF16)
        seeds = dot_tn(seeds, pick).astype(jnp.int32)
        lattice = (feature * seeds) & (FEAT - 1)
        prob = (lattice.astype(F32) + 0.5) * (1.0 / FEAT)
        radius = jnp.sqrt(-2.0 * jnp.log(jnp.minimum(prob, 1.0 - prob)))
        above = 2.515517 + 0.802853 * radius + 0.010328 * radius * radius
        below = (
            1.0
            + 1.432788 * radius
            + 0.189269 * radius * radius
            + 0.001308 * radius * radius * radius
        )
        magnitude = radius - above / below
        omega = jnp.where(prob > 0.5, magnitude, -magnitude)
        project = jnp.dot(cosine, omega, precision=HIGH, preferred_element_type=F32)
        project = jnp.concatenate([project] * QUADS, axis=0)
        upper_ref[0, group], lower_ref[0, group] = split(jnp.where(same_head, project, 0.0))
        grown = jnp.exp(-0.5 / DH * jnp.sum(omega * omega, axis=0, keepdims=True))
        upper, rest = split(jnp.broadcast_to(grown, (8, WIDE)))
        total = dot_nn(upper, ones) + dot_nn(rest, ones)
        weight_ref[0, group] = FEAT * grown / total[:1]


def feature_tables(seeds):
    return pl.pallas_call(
        tables_kernel,
        grid=(LAYERS,),
        in_specs=[
            pl.BlockSpec((1, HEADS, DH), lambda l: (l, 0, 0)),
            whole((DH, DH)),
        ],
        out_specs=[
            pl.BlockSpec((1, QUADS, WIDE, WIDE), lambda l: (l, 0, 0, 0)),
            pl.BlockSpec((1, QUADS, WIDE, WIDE), lambda l: (l, 0, 0, 0)),
            pl.BlockSpec((1, QUADS, 1, WIDE), lambda l: (l, 0, 0, 0)),
        ],
        out_shape=[
            jax.ShapeDtypeStruct((LAYERS, QUADS, WIDE, WIDE), BF16),
            jax.ShapeDtypeStruct((LAYERS, QUADS, WIDE, WIDE), BF16),
            jax.ShapeDtypeStruct((LAYERS, QUADS, 1, WIDE), F32),
        ],
        compiler_params=params(),
        name="feature_tables",
    )(seeds, jnp.asarray(cosine_block()))


def turn(values, cosine, sine):
    lanes = values.shape[1]
    half = ROT // 2
    lane = lane_index(*values.shape) % DH
    swapped = jnp.where(
        lane < half, pltpu.roll(values, lanes - half, 1), pltpu.roll(values, half, 1)
    )
    return values * cosine + swapped * sine


def turn_back(values, cosine, sine):
    lanes = values.shape[1]
    half = ROT // 2
    lane = lane_index(*values.shape) % DH
    turned = values * sine
    swapped = jnp.where(
        lane < half, pltpu.roll(turned, lanes - half, 1), pltpu.roll(turned, half, 1)
    )
    return values * cosine + jnp.where(lane < ROT, swapped, 0.0)


def normalized(x_ref_rows, gain, offset):
    average = jnp.mean(x_ref_rows, -1, keepdims=True)
    centered = x_ref_rows - average
    variance = jnp.mean(centered * centered, -1, keepdims=True)
    return centered * lax.rsqrt(variance + EPSILON) * gain + offset


def start_layer(stream, x_ref, h_ref, gain_ref, offset_ref):
    length = h_ref.shape[0]
    step = min(128, length)

    @pl.loop(0, length // step)
    def _(index):
        rows = pl.ds(pl.multiple_of(index * step, step), step)
        values = stream[0][rows].astype(F32)
        if len(stream) > 1:
            values = values + (stream[1][rows] + stream[2][rows])
            x_ref[rows] = values
        h_ref[rows] = normalized(
            values, gain_ref[...].astype(F32), offset_ref[...].astype(F32)
        ).astype(BF16)


JOB = 128


def start_last_layer(stream, x_hbm, buffers, loads, stores, h_ref, gain_ref, offset_ref):
    gain, offset = gain_ref[...].astype(F32), offset_ref[...].astype(F32)
    jobs = h_ref.shape[0] // JOB

    def rows_at(index):
        return pl.ds(pl.multiple_of(index * JOB, JOB), JOB)

    def load(part, index):
        rows = rows_at(index)
        return pltpu.make_async_copy(
            stream[part].at[rows], buffers[part].at[rows], loads.at[part, index]
        )

    def store(index):
        rows = rows_at(index)
        return pltpu.make_async_copy(buffers[1].at[rows], x_hbm.at[rows], stores.at[index])

    @pl.loop(0, jobs)
    def _(index):
        for part in range(len(stream)):
            load(part, index).start()

    @pl.loop(0, jobs)
    def _(index):
        rows = rows_at(index)
        for part in range(len(stream)):
            load(part, index).wait()
        values = buffers[0][rows].astype(F32) + (buffers[1][rows] + buffers[2][rows])
        buffers[1][rows] = values
        store(index).start()
        h_ref[rows] = normalized(values, gain, offset).astype(BF16)

    @pl.loop(0, jobs)
    def _(index):
        store(index).wait()


def chunk_semaphores(length):
    return [
        pltpu.SemaphoreType.DMA((3, length // JOB)),
        pltpu.SemaphoreType.DMA((length // JOB,)),
    ]


def gelu_parts(units):
    below = 0.5 + 0.5 * lax.erf(units * math.sqrt(0.5))
    return below, jnp.exp(-0.5 * units * units) * (1.0 / math.sqrt(2.0 * math.pi))


FF_BLOCK = 1024
FF_ROWS = 512


def mlp_forward_kernel(layer, count, *refs):
    stream, refs = refs[:count], refs[count:]
    gain_ref, offset_ref, up_ref, bias_ref, down_ref, down_bias_ref = refs[:6]
    gain_ref, offset_ref, down_bias_ref = [
        ref.at[layer : layer + 1] for ref in (gain_ref, offset_ref, down_bias_ref)
    ]
    refs = refs[6:]
    x_ref = None
    if count > 1:
        x_ref, refs = refs[0], refs[1:]
    part_ref, h_ref, act_ref, slope_ref = refs
    step = pl.program_id(0)

    @pl.when(step == 0)
    def _():
        start_layer(stream, x_ref, h_ref, gain_ref, offset_ref)
        part_ref[...] = jnp.broadcast_to(down_bias_ref[...].astype(F32), part_ref.shape)

    for first in range(0, h_ref.shape[0], FF_ROWS):
        rows = slice(first, first + FF_ROWS)
        units = dot_nt(h_ref[rows], up_ref[0]) + bias_ref[0]
        below, density = gelu_parts(units)
        active = (units * below).astype(BF16)
        act_ref[0, rows] = active
        slope_ref[0, rows] = (below + units * density).astype(BF16)
        part_ref[rows] += dot_nn(active, down_ref[0, 0])


def plane_block(length, lanes):
    per_plane = 1024 // lanes
    return pl.BlockSpec((1, length, lanes), lambda j: (j // per_plane, 0, j % per_plane))


def mlp_forward(layer, stream, gain, offset, up, biases, down_weight, down_bias):
    length, width = stream[0].shape
    hidden = up.shape[1]
    blocks = hidden // FF_BLOCK
    state = jax.ShapeDtypeStruct((4, length, width), BF16)
    full = jax.ShapeDtypeStruct((length, width), F32)
    out_shape = [full, jax.ShapeDtypeStruct((length, width), BF16), state, state]
    out_specs = [whole((length, width)), whole((length, width))]
    out_specs += [plane_block(length, FF_BLOCK)] * 2
    if len(stream) > 1:
        out_shape, out_specs = [full] + out_shape, [whole((length, width))] + out_specs
    return pl.pallas_call(
        functools.partial(mlp_forward_kernel, layer, len(stream)),
        grid=(blocks,),
        in_specs=[whole((length, width))] * len(stream)
        + [
            whole((LAYERS, width)),
            whole((LAYERS, width)),
            pl.BlockSpec((1, FF_BLOCK, width), lambda j: (layer, j, 0)),
            pl.BlockSpec((1, 1, FF_BLOCK), lambda j: (layer * blocks + j, 0, 0)),
            pl.BlockSpec((1, 1, FF_BLOCK, width), lambda j: (0, layer, j, 0)),
            whole((LAYERS, width)),
        ],
        out_specs=out_specs,
        out_shape=out_shape,
        compiler_params=params(),
        name="mlp_forward",
    )(*stream, gain, offset, up, biases, down_weight, down_bias)


def add_stream(stream, result_ref):
    if stream:
        result_ref[...] = stream[0][...] + (stream[1][...] + stream[2][...])


def stream_specs(stream):
    specs = [
        pl.BlockSpec((part.shape[0] // 4, part.shape[1]), lambda j, *_: (j, 0)) for part in stream
    ]
    shapes = [jax.ShapeDtypeStruct(part.shape, F32) for part in stream[:1]]
    return specs, specs[:1], shapes


def mlp_backward_kernel(count, place_ref, *refs):
    stream, refs = refs[:count], refs[count:]
    grad_ref, h_ref, act_ref, slope_ref, down_ref, up_ref = refs[:6]
    result_ref, refs = (refs[6], refs[7:]) if count else (None, refs[6:])
    part_ref, along_x, kept_x, along_y, kept_y, bias_ref = refs[:6]
    grad_t, h_t, units = refs[6:]
    step = pl.program_id(0)
    add_stream(stream, result_ref)

    @pl.when(step == 0)
    def _():
        grad_t[...] = grad_ref[...].T
        h_t[...] = h_ref[...].T
        part_ref[...] = jnp.zeros_like(part_ref)

    bias = jnp.zeros((1, FF_BLOCK), F32)
    for first in range(0, h_ref.shape[0], ROWS):
        rows = slice(first, first + ROWS)
        grad_act = dot_nt(grad_ref[rows], down_ref[0, 0])
        grad_unit = (grad_act * slope_ref[0, rows].astype(F32)).astype(BF16)
        bias += jnp.sum(grad_unit.astype(F32), axis=0, keepdims=True)
        units[rows] = grad_unit
        part_ref[rows] += dot_nn(grad_unit, up_ref[0])
    bias_ref[pl.ds(step, 1)] = bias

    mlp_weights(
        place_ref, grad_t, h_t, act_ref.at[0], units, along_x, kept_x, along_y, kept_y
    )


def mlp_weights(place_ref, grad_t, h_t, act, units, along_x, kept_x, along_y, kept_y):
    def block(y, x):
        return pl.ds(pl.multiple_of((2 * y + x) * WIDE, WIDE), WIDE)

    near_x, near_y = place_ref[0], place_ref[1]

    @pl.loop(0, h_t.shape[0] // ROWS)
    def _(index):
        rows = pl.ds(pl.multiple_of(index * ROWS, ROWS), ROWS)
        for side in range(2):
            for target, x in ((along_x, 1 - near_x), (kept_x, near_x)):
                target[0, side, rows] = dot_nn(grad_t[rows], act[:, block(side, x)])
            for target, y in ((along_y, 1 - near_y), (kept_y, near_y)):
                target[0, side, rows] = dot_nn(h_t[rows], units[:, block(y, side)])


def mlp_last_kernel(layer, place_ref, *refs):
    stream, refs = refs[:3], refs[3:]
    gain_ref, offset_ref, up_ref, bias_ref, down_ref, down_bias_ref, grad_ref = refs[:7]
    gain_ref, offset_ref, down_bias_ref = [
        ref.at[layer : layer + 1] for ref in (gain_ref, offset_ref, down_bias_ref)
    ]
    x_hbm, part_ref, grad_part, along_x, kept_x, along_y, kept_y, bias_out = refs[7:15]
    h_ref, grad_t, h_t, act, units, loads, stores = refs[15:]
    step = pl.program_id(0)

    @pl.when(step == 0)
    def _():
        buffers = (act, part_ref, grad_part)
        start_last_layer(stream, x_hbm, buffers, loads, stores, h_ref, gain_ref, offset_ref)
        part_ref[...] = jnp.broadcast_to(down_bias_ref[...].astype(F32), part_ref.shape)
        grad_part[...] = jnp.zeros_like(grad_part)
        grad_t[...] = grad_ref[...].T
        h_t[...] = h_ref[...].T

    here = pl.ds(step, 1)
    bias_out[here] = jnp.zeros((1, FF_BLOCK), F32)

    @pl.loop(0, h_ref.shape[0] // ROWS)
    def _(index):
        rows = pl.ds(pl.multiple_of(index * ROWS, ROWS), ROWS)
        hidden = dot_nt(h_ref[rows], up_ref[0]) + bias_ref[0]
        below, density = gelu_parts(hidden)
        active = (hidden * below).astype(BF16)
        act[rows] = active
        part_ref[rows] += dot_nn(active, down_ref[0, 0])
        grad_act = dot_nt(grad_ref[rows], down_ref[0, 0])
        grad_unit = (grad_act * (below + hidden * density)).astype(BF16)
        bias_out[here] += jnp.sum(grad_unit.astype(F32), axis=0, keepdims=True)
        units[rows] = grad_unit
        grad_part[rows] += dot_nn(grad_unit, up_ref[0])
    mlp_weights(place_ref, grad_t, h_t, act, units, along_x, kept_x, along_y, kept_y)


def mlp_last(layer, place, stream, gain, offset, up, biases, down_weight, down_bias, grad):
    length, width = stream[0].shape
    blocks = up.shape[1] // FF_BLOCK
    full = jax.ShapeDtypeStruct((length, width), F32)
    pair = pl.BlockSpec((1, 2, width, WIDE), lambda j, *_: (j, 0, 0, 0))
    return pl.pallas_call(
        functools.partial(mlp_last_kernel, layer),
        grid_spec=pltpu.PrefetchScalarGridSpec(
            num_scalar_prefetch=1,
            grid=(blocks,),
            in_specs=[pl.BlockSpec(memory_space=pltpu.HBM)] * 3
            + [
                whole((LAYERS, width)),
                whole((LAYERS, width)),
                pl.BlockSpec((1, FF_BLOCK, width), lambda j, *_: (layer, j, 0)),
                pl.BlockSpec((1, 1, FF_BLOCK), lambda j, *_: (layer * blocks + j, 0, 0)),
                pl.BlockSpec((1, 1, FF_BLOCK, width), lambda j, *_: (0, layer, j, 0)),
                whole((LAYERS, width)),
                whole((length, width)),
            ],
            out_specs=[pl.BlockSpec(memory_space=pltpu.HBM)]
            + [whole((length, width))] * 2
            + [pair] * 4
            + [whole((blocks, FF_BLOCK))],
            scratch_shapes=[
                pltpu.VMEM((length, width), BF16),
                pltpu.VMEM((width, length), BF16),
                pltpu.VMEM((width, length), BF16),
                pltpu.VMEM((length, FF_BLOCK), BF16),
                pltpu.VMEM((length, FF_BLOCK), BF16),
            ]
            + chunk_semaphores(length),
        ),
        out_shape=[full, full, full]
        + halves_of(width, (4, 2, width, WIDE))
        + [jax.ShapeDtypeStruct((blocks, FF_BLOCK), F32)],
        compiler_params=params(),
        name="mlp_last",
    )(place, *stream, gain, offset, up, biases, down_weight, down_bias, grad)


def halves_of(width, weight):
    shapes = (weight,) * 2 + ((4, 2, width, WIDE),) * 2
    return [jax.ShapeDtypeStruct(shape, F32) for shape in shapes]


def flat_halves(part, sent, kept, sent_up, kept_up, bias):
    halves = [half.reshape((-1,) + half.shape[2:]) for half in (sent, kept, sent_up, kept_up)]
    return (part, *halves, bias)


def mlp_backward(layer, place, grad, h, act, slope, down_weight, up, stream=()):
    length, width = h.shape
    hidden = up.shape[1]
    blocks = hidden // FF_BLOCK
    pair = pl.BlockSpec((1, 2, width, WIDE), lambda j, *_: (j, 0, 0, 0))
    plane = pl.BlockSpec((1, length, FF_BLOCK), lambda j, *_: (j, 0, 0))
    stream_in, stream_out, stream_shape = stream_specs(stream)
    return pl.pallas_call(
        functools.partial(mlp_backward_kernel, len(stream)),
        grid_spec=pltpu.PrefetchScalarGridSpec(
            num_scalar_prefetch=1,
            grid=(blocks,),
            in_specs=stream_in
            + [
                whole((length, width)),
                whole((length, width)),
                plane,
                plane,
                pl.BlockSpec((1, 1, FF_BLOCK, width), lambda j, *_: (0, layer, j, 0)),
                pl.BlockSpec((1, FF_BLOCK, width), lambda j, *_: (layer, j, 0)),
            ],
            out_specs=stream_out
            + [whole((length, width))]
            + [pair] * 4
            + [whole((blocks, FF_BLOCK))],
            scratch_shapes=[
                pltpu.VMEM((width, length), BF16),
                pltpu.VMEM((width, length), BF16),
                pltpu.VMEM((length, FF_BLOCK), BF16),
            ],
        ),
        out_shape=stream_shape
        + [jax.ShapeDtypeStruct((length, width), F32)]
        + halves_of(width, (4, 2, width, WIDE))
        + [jax.ShapeDtypeStruct((blocks, FF_BLOCK), F32)],
        compiler_params=params(),
        name="mlp_backward",
    )(place, *stream, grad, h, act, slope, down_weight, up)


def head_sums(values, ones):
    upper, lower = split(values)
    return dot_nn(upper, ones) + dot_nn(lower, ones)


def same_head_ones():
    same = row_index(WIDE, WIDE) // DH == lane_index(WIDE, WIDE) // DH
    return jnp.where(same, 1.0, 0.0).astype(BF16)


def document_of(starts_ref, positions):
    return sum((starts_ref[0, i] <= positions).astype(jnp.int32) for i in range(starts_ref.shape[1]))


def write_mask(starts_ref, mask_ref, flipped):
    for first in range(0, mask_ref.shape[0], ROWS):
        lanes = lane_index(1, ROWS) + first
        own = row_index(ROWS, 1) + first
        order = (own <= lanes) if flipped else (lanes <= own)
        seen = (document_of(starts_ref, own) == document_of(starts_ref, lanes)) & order
        mask_ref[first : first + ROWS] = jnp.where(seen, 1.0, 0.0).astype(BF16)


def document_edges(starts_ref, length):
    edges = []
    for first in range(0, length, ROWS):
        rows = document_of(starts_ref, row_index(ROWS, 1) + first)
        here = document_of(starts_ref, first)
        later = document_of(starts_ref, first + ROWS)
        edges.append((rows == here, rows == later, here == later))
    return edges


def wide_rotary(cosine_ref, sine_ref, rows):
    return tuple(
        jnp.concatenate([ref[rows]] * (WIDE // PAIR), axis=1) for ref in (cosine_ref, sine_ref)
    )


def attend_heads(
    first_bias, starts_ref, weight_ref, bias_ref, upper_ref, lower_ref, scale_ref, cosine_ref,
    sine_ref, part_ref, h_ref, state_ref, mixed_ref, mask_ref,
):
    length = h_ref.shape[0]
    ones = same_head_ones()
    table_up, table_low = upper_ref[0, 0], lower_ref[0, 0]
    lanes_of_step = pl.ds(pl.multiple_of(pl.program_id(0) * WIDE, WIDE), WIDE)

    def features(values, rows):
        upper, lower = split(turn(values, *wide_rotary(cosine_ref, sine_ref, rows)))
        return dot_nn(upper, table_up) + (dot_nn(lower, table_up) + dot_nn(upper, table_low))

    for first in range(0, length, ROWS):
        rows = slice(first, first + ROWS)
        queries, keys, values = [
            dot_nt(h_ref[rows], weight_ref[0, 0, kind, 0])
            + bias_ref[first_bias + kind, :, lanes_of_step]
            for kind in range(3)
        ]
        state_ref[0, rows] = jnp.exp(features(queries, rows)).astype(BF16)
        logs = features(keys, rows) - (0.5 / math.sqrt(DH)) * head_sums(keys * keys, ones)
        state_ref[1, rows] = (scale_ref[0, 0] * jnp.exp(logs)).astype(BF16)
        state_ref[2, rows] = keys.astype(BF16)
        state_ref[3, rows] = values.astype(BF16)

    zero = jnp.zeros((), BF16)
    one = jnp.ones((), BF16)
    left = lane_index(ROWS, PAIR) < DH
    row, lane = row_index(PAIR, 2 * PAIR), lane_index(PAIR, 2 * PAIR)
    same = row // DH == lane // PAIR
    edges = document_edges(starts_ref, length)
    for pair in range(WIDE // PAIR):
        lanes = slice(pair * PAIR, (pair + 1) * PAIR)
        before = None
        for block, (same_first, same_next, goes_on) in enumerate(edges):
            rows = slice(block * ROWS, (block + 1) * ROWS)
            seen = mask_ref[rows] > zero
            queries, keys = state_ref[0, rows, lanes], state_ref[1, rows, lanes]
            values = [jnp.where(own, state_ref[3, rows, lanes], one) for own in (left, ~left)]
            if block > 0:
                earlier = dot_nn(queries, before.astype(BF16))
                earlier = jnp.where(same_first, earlier, 0.0)
            sums = []
            for head, own in enumerate((left, ~left)):
                scores = dot_nt(queries, jnp.where(own, keys, zero)).astype(BF16)
                total = dot_nn(jnp.where(seen, scores, zero), values[head])
                if block > 0:
                    total = total + earlier[:, head * PAIR : (head + 1) * PAIR]
                sums.append(total)
            if block + 1 < len(edges):
                kept = jnp.where(same_next, keys, zero)
                added = jnp.where(same, dot_tn(kept, jnp.concatenate(values, axis=1)), 0.0)
                if block > 0:
                    added = added + jnp.where(goes_on, before, 0.0)
                before = added
            numer = jnp.where(left, sums[0], sums[1])
            denom = jnp.where(left, pltpu.roll(sums[0], DH, 1), pltpu.roll(sums[1], DH, 1))
            inverse = 1.0 / denom
            mixed_ref[0, rows, lanes] = (numer * inverse).astype(BF16)
            mixed_ref[1, rows, lanes], mixed_ref[2, rows, lanes] = split(inverse)
    for first in range(0, length, ROWS):
        rows = slice(first, first + ROWS)
        part_ref[rows] += dot_nn(mixed_ref[0, rows], weight_ref[0, 0, 3, 0])


def attention_forward_kernel(layer, count, *refs):
    stream, refs = refs[:count], refs[count:]
    starts_ref, gain_ref, offset_ref, weight_ref, bias_ref = refs[:5]
    gain_ref, offset_ref = [ref.at[layer : layer + 1] for ref in (gain_ref, offset_ref)]
    first_bias = layer * (bias_ref.shape[0] // LAYERS)
    upper_ref, lower_ref, scale_ref, cosine_ref, sine_ref = refs[5:10]
    refs = refs[10:]
    x_ref = None
    if count > 1:
        x_ref, refs = refs[0], refs[1:]
    part_ref, h_ref, state_ref, mixed_ref, mask_ref = refs

    @pl.when(pl.program_id(0) == 0)
    def _():
        start_layer(stream, x_ref, h_ref, gain_ref, offset_ref)
        write_mask(starts_ref, mask_ref, False)
        part_ref[...] = jnp.broadcast_to(bias_ref[first_bias + 3], part_ref.shape)

    attend_heads(
        first_bias, starts_ref, weight_ref, bias_ref, upper_ref, lower_ref, scale_ref, cosine_ref,
        sine_ref, part_ref, h_ref, state_ref, mixed_ref, mask_ref,
    )


def kinds_of(weight):
    return weight.reshape(weight.shape[:2] + (4, QUADS, WIDE, weight.shape[3]))


def attention_forward(layer, stream, starts, gain, offset, weight, biases, tables, rotary):
    length, width = stream[0].shape
    full = jax.ShapeDtypeStruct((length, width), F32)
    state = jax.ShapeDtypeStruct((4, length, width), BF16)
    out_shape = [full, jax.ShapeDtypeStruct((length, width), BF16), state, state]
    four = pl.BlockSpec((4, length, WIDE), lambda g: (0, 0, g))
    out_specs = [whole((length, width)), whole((length, width)), four, four]
    if len(stream) > 1:
        out_shape, out_specs = [full] + out_shape, [whole((length, width))] + out_specs
    return pl.pallas_call(
        functools.partial(attention_forward_kernel, layer, len(stream)),
        grid=(QUADS,),
        in_specs=[whole((length, width))] * len(stream)
        + [
            pl.BlockSpec(memory_space=pltpu.SMEM),
            whole((LAYERS, width)),
            whole((LAYERS, width)),
            pl.BlockSpec((1, 1, 4, 1, WIDE, width), lambda g: (0, layer, 0, g, 0, 0)),
            whole((LAYERS * 4, 1, width)),
            pl.BlockSpec((1, 1, WIDE, WIDE), lambda g: (layer, g, 0, 0)),
            pl.BlockSpec((1, 1, WIDE, WIDE), lambda g: (layer, g, 0, 0)),
            pl.BlockSpec((1, 1, 1, WIDE), lambda g: (layer, g, 0, 0)),
            whole((length, PAIR)),
            whole((length, PAIR)),
        ],
        out_specs=out_specs,
        out_shape=out_shape,
        scratch_shapes=[pltpu.VMEM((length, ROWS), BF16)],
        compiler_params=params(),
        name="attention_forward",
    )(
        *stream, starts, gain, offset, kinds_of(weight),
        biases, *tables, *rotary,
    )


def attend_heads_back(
    place_ref, starts_ref, grad_ref, state_ref, mixed_ref, table_ref, cosine_ref, sine_ref,
    weight_ref, part_ref, along_z, kept_z, bias_ref, mask_ref, upright, numer_ref, feat_ref, flow,
):
    group = pl.program_id(0)
    length, width = grad_ref.shape
    row, lane = row_index(WIDE, WIDE), lane_index(WIDE, WIDE)
    partner = (row // PAIR == lane // PAIR) & (row // DH != lane // DH)
    partner = jnp.where(partner, 1.0, 0.0).astype(BF16)
    zero = jnp.zeros((), BF16)
    one = jnp.ones((), BF16)
    for first in range(0, length, ROWS):
        rows = slice(first, first + ROWS)
        grad = dot_nt(grad_ref[rows], weight_ref[0, 0, 3, 0]).astype(BF16).astype(F32)
        inverse = mixed_ref[1, rows].astype(F32) + mixed_ref[2, rows].astype(F32)
        scaled = grad * inverse
        upper, lower = split(-head_sums(scaled * mixed_ref[0, rows].astype(F32), partner))
        numer = scaled.astype(BF16)
        lane = lane_index(ROWS, WIDE)
        spare = jnp.where(lane % DH == 0, upper, jnp.where(lane % DH == 1, lower, zero))
        left = lane % PAIR < DH
        numer_ref[0, rows] = jnp.where(left, numer, spare)
        numer_ref[1, rows] = jnp.where(left, spare, numer)

    left = lane_index(ROWS, PAIR) < DH
    spare = jnp.where(lane_index(ROWS, PAIR) % DH < 2, one, zero)
    row, lane = row_index(2 * PAIR, PAIR), lane_index(2 * PAIR, PAIR)
    same = row // PAIR == lane // DH
    row, lane = row_index(PAIR, PAIR), lane_index(PAIR, PAIR)
    same_head = row // DH == lane // DH
    edges = document_edges(starts_ref, length)
    blocks = range(len(edges))

    def both(upper_and_lower, sums):
        upper, lower = split(sums)
        return dot_nn(upper_and_lower, upper) + dot_nn(upper_and_lower, lower)

    for pair in range(WIDE // PAIR):
        lanes = slice(pair * PAIR, (pair + 1) * PAIR)

        def rows_of_block(block):
            rows = slice(block * ROWS, (block + 1) * ROWS)
            numers = [numer_ref[head, rows, lanes] for head in range(2)]
            values = state_ref[3, rows, lanes]
            values = [jnp.where(own, values, spare) for own in (left, ~left)]
            return rows, state_ref[0, rows, lanes], state_ref[1, rows, lanes], values, numers

        before, after = {}, {}
        for block in blocks[1:]:
            rows, queries, keys, values, numers = rows_of_block(block - 1)
            _, same_next, goes_on = edges[block - 1]
            kept = jnp.where(same_next, keys, zero)
            added = jnp.where(same, dot_tn(jnp.concatenate(values, axis=1), kept), 0.0)
            if block > 1:
                added = added + jnp.where(goes_on, before[block - 1], 0.0)
            before[block] = added
        for block in blocks[::-1][:-1]:
            rows, queries, keys, values, numers = rows_of_block(block)
            same_first, _, goes_on = edges[block]
            kept = jnp.where(same_first, queries, zero)
            keys_sum = jnp.where(same, dot_tn(jnp.concatenate(numers, axis=1), kept), 0.0)
            values_sum = dot_tn(kept, jnp.where(left, numers[0], numers[1]))
            values_sum = jnp.where(same_head, values_sum, 0.0)
            if block + 1 < len(edges):
                keys_sum = keys_sum + jnp.where(goes_on, after[block + 1][0], 0.0)
                values_sum = values_sum + jnp.where(goes_on, after[block + 1][1], 0.0)
            after[block] = (keys_sum, values_sum)
        for block in blocks:
            rows, queries, keys, values, numers = rows_of_block(block)
            same_first, same_next, _ = edges[block]
            seen = mask_ref[rows] > zero
            numer = jnp.where(left, numers[0], numers[1])
            grads = []
            grad_query = None
            for head, own in enumerate((left, ~left)):
                own_keys = jnp.where(own, keys, zero)
                scores = dot_nt(own_keys, queries).astype(BF16)
                grad_value = dot_nn(jnp.where(seen, scores, zero), numer)
                grad_scores = dot_nt(values[head], numers[head]).astype(BF16)
                grad_scores = jnp.where(seen, grad_scores, zero)
                grads.append((grad_value, dot_nn(grad_scores, queries)))
                from_head = dot_tn(grad_scores, own_keys)
                grad_query = from_head if head == 0 else grad_query + from_head
            grad_value = jnp.where(left, grads[0][0], grads[1][0])
            grad_key = jnp.where(left, grads[0][1], grads[1][1])
            if block + 1 < len(edges):
                keys_sum, values_sum = after[block + 1]
                late = both(jnp.concatenate(values, axis=1), keys_sum)
                grad_key = grad_key + jnp.where(same_next, late, 0.0)
                late = dot_nn(keys, values_sum.astype(BF16))
                grad_value = grad_value + jnp.where(same_next, late, 0.0)
            if block > 0:
                early = both(jnp.concatenate(numers, axis=1), before[block])
                grad_query = grad_query + jnp.where(same_first, early, 0.0)
            flow[2, rows, lanes] = grad_value.astype(BF16)
            feat_ref[1, rows, lanes] = (grad_key * keys.astype(F32)).astype(BF16)
            feat_ref[0, rows, lanes] = (grad_query * queries.astype(F32)).astype(BF16)

    ones = same_head_ones()
    table = table_ref[0, 0]
    sums = [jnp.zeros((1, WIDE), F32)] * 3
    for first in range(0, length, ROWS):
        rows = slice(first, first + ROWS)
        cosine, sine = wide_rotary(cosine_ref, sine_ref, rows)
        flow[0, rows] = turn_back(dot_nt(feat_ref[0, rows], table), cosine, sine).astype(BF16)
        shrink = dot_nn(feat_ref[1, rows], ones) * (1.0 / math.sqrt(DH))
        turned = turn_back(dot_nt(feat_ref[1, rows], table), cosine, sine)
        flow[1, rows] = (turned - state_ref[2, rows].astype(F32) * shrink).astype(BF16)
        total = part_ref[rows]
        for kind in range(3):
            block = flow[kind, rows]
            sums[kind] = sums[kind] + jnp.sum(block.astype(F32), axis=0, keepdims=True)
            total = total + dot_nn(block, weight_ref[0, 0, kind, 0])
        part_ref[rows] = total
    for kind in range(3):
        bias_ref[kind : kind + 1] = sums[kind]
    lanes = pl.ds(pl.multiple_of(group * WIDE, WIDE), WIDE)
    bias_ref[3:4] = jnp.sum(grad_ref[:, lanes].astype(F32), axis=0, keepdims=True)
    flow[3] = mixed_ref[0]
    for first in range(0, width, ROWS):
        rows = slice(first, first + ROWS)
        for far in range(2):
            for target, near in ((along_z, 1 - place_ref[2]), (kept_z, place_ref[2])):
                kind = 2 * far + near
                target[far, 0, rows] = dot_nn(upright[kind // 3, rows], flow[kind])


def attention_backward_kernel(count, place_ref, *refs):
    stream, refs = refs[:count], refs[count:]
    starts_ref, grad_ref, h_ref, state_ref, mixed_ref, table_ref = refs[:6]
    cosine_ref, sine_ref, weight_ref = refs[6:9]
    result_ref, refs = (refs[9], refs[10:]) if count else (None, refs[9:])
    part_ref, along_z, kept_z, _, _, bias_ref = refs[:6]
    mask_ref, upright, numer_ref, feat_ref, flow = refs[6:]
    add_stream(stream, result_ref)

    @pl.when(pl.program_id(0) == 0)
    def _():
        write_mask(starts_ref, mask_ref, True)
        upright[0] = h_ref[...].T
        upright[1] = grad_ref[...].T
        part_ref[...] = jnp.zeros_like(part_ref)

    attend_heads_back(
        place_ref, starts_ref, grad_ref, state_ref, mixed_ref, table_ref, cosine_ref, sine_ref,
        weight_ref, part_ref, along_z, kept_z, bias_ref, mask_ref, upright, numer_ref, feat_ref,
        flow,
    )


def attention_backward(
    layer, place, starts, grad, h, state, mixed, tables, rotary, weight, stream=()
):
    _, length, width = state.shape
    four = pl.BlockSpec((4, length, WIDE), lambda g, *_: (0, 0, g))
    halves = pl.BlockSpec((2, 1, width, WIDE), lambda g, *_: (0, g, 0, 0))
    stream_in, stream_out, stream_shape = stream_specs(stream)
    return pl.pallas_call(
        functools.partial(attention_backward_kernel, len(stream)),
        grid_spec=pltpu.PrefetchScalarGridSpec(
            num_scalar_prefetch=1,
            grid=(QUADS,),
            in_specs=stream_in
            + [
                pl.BlockSpec(memory_space=pltpu.SMEM),
                whole((length, width)),
                whole((length, width)),
                four,
                four,
                pl.BlockSpec((1, 1, WIDE, WIDE), lambda g, *_: (layer, g, 0, 0)),
                whole((length, PAIR)),
                whole((length, PAIR)),
                pl.BlockSpec((1, 1, 4, 1, WIDE, width), lambda g, *_: (0, layer, 0, g, 0, 0)),
            ],
            out_specs=stream_out
            + [whole((length, width))]
            + [halves, halves]
            + [pl.BlockSpec(memory_space=pl.ANY)] * 2
            + [pl.BlockSpec((4, WIDE), lambda g, *_: (0, g))],
            scratch_shapes=[
                pltpu.VMEM((length, ROWS), BF16),
                pltpu.VMEM((2, width, length), BF16),
                pltpu.VMEM((2, length, WIDE), BF16),
                pltpu.VMEM((2, length, WIDE), BF16),
                pltpu.VMEM((4, length, WIDE), BF16),
            ],
        ),
        out_shape=stream_shape
        + [jax.ShapeDtypeStruct((length, width), F32)]
        + halves_of(width, (2, 4, width, WIDE))
        + [jax.ShapeDtypeStruct((4, width), F32)],
        compiler_params=params(),
        name="attention_backward",
    )(place, *stream, starts, grad, h, state, mixed, tables[0], *rotary, kinds_of(weight))


def attention_last_kernel(layer, place_ref, *refs):
    stream, refs = refs[:3], refs[3:]
    starts_ref, gain_ref, offset_ref, weight_ref, bias_ref = refs[:5]
    gain_ref, offset_ref = [ref.at[layer : layer + 1] for ref in (gain_ref, offset_ref)]
    first_bias = layer * (bias_ref.shape[0] // LAYERS)
    upper_ref, lower_ref, scale_ref, cosine_ref, sine_ref, grad_ref = refs[5:11]
    x_hbm, part_ref, grad_part, along_z, kept_z, _, _, bias_out = refs[11:19]
    h_ref, state_ref, mixed_ref, mask_ref, mask_back = refs[19:24]
    upright, numer_ref, feat_ref, flow, loads, stores = refs[24:]

    @pl.when(pl.program_id(0) == 0)
    def _():
        buffers = (upright.at[0], part_ref, grad_part)
        start_last_layer(stream, x_hbm, buffers, loads, stores, h_ref, gain_ref, offset_ref)
        write_mask(starts_ref, mask_ref, False)
        write_mask(starts_ref, mask_back, True)
        part_ref[...] = jnp.broadcast_to(bias_ref[first_bias + 3], part_ref.shape)
        grad_part[...] = jnp.zeros_like(grad_part)
        upright[0] = h_ref[...].T
        upright[1] = grad_ref[...].T

    attend_heads(
        first_bias, starts_ref, weight_ref, bias_ref, upper_ref, lower_ref, scale_ref, cosine_ref,
        sine_ref, part_ref, h_ref, state_ref, mixed_ref, mask_ref,
    )
    attend_heads_back(
        place_ref, starts_ref, grad_ref, state_ref, mixed_ref, upper_ref, cosine_ref, sine_ref,
        weight_ref, grad_part, along_z, kept_z, bias_out, mask_back, upright, numer_ref, feat_ref,
        flow,
    )


def attention_last(
    layer, place, stream, starts, gain, offset, weight, biases, tables, rotary, grad
):
    length, width = stream[0].shape
    full = jax.ShapeDtypeStruct((length, width), F32)
    halves = pl.BlockSpec((2, 1, width, WIDE), lambda g, *_: (0, g, 0, 0))
    return pl.pallas_call(
        functools.partial(attention_last_kernel, layer),
        grid_spec=pltpu.PrefetchScalarGridSpec(
            num_scalar_prefetch=1,
            grid=(QUADS,),
            in_specs=[pl.BlockSpec(memory_space=pltpu.HBM)] * 3
            + [
                pl.BlockSpec(memory_space=pltpu.SMEM),
                whole((LAYERS, width)),
                whole((LAYERS, width)),
                pl.BlockSpec((1, 1, 4, 1, WIDE, width), lambda g, *_: (0, layer, 0, g, 0, 0)),
                whole((LAYERS * 4, 1, width)),
                pl.BlockSpec((1, 1, WIDE, WIDE), lambda g, *_: (layer, g, 0, 0)),
                pl.BlockSpec((1, 1, WIDE, WIDE), lambda g, *_: (layer, g, 0, 0)),
                pl.BlockSpec((1, 1, 1, WIDE), lambda g, *_: (layer, g, 0, 0)),
                whole((length, PAIR)),
                whole((length, PAIR)),
                whole((length, width)),
            ],
            out_specs=[pl.BlockSpec(memory_space=pltpu.HBM)]
            + [whole((length, width))] * 2
            + [halves, halves]
            + [pl.BlockSpec(memory_space=pl.ANY)] * 2
            + [pl.BlockSpec((4, WIDE), lambda g, *_: (0, g))],
            scratch_shapes=[
                pltpu.VMEM((length, width), BF16),
                pltpu.VMEM((4, length, WIDE), BF16),
                pltpu.VMEM((3, length, WIDE), BF16),
                pltpu.VMEM((length, ROWS), BF16),
                pltpu.VMEM((length, ROWS), BF16),
                pltpu.VMEM((2, width, length), BF16),
                pltpu.VMEM((2, length, WIDE), BF16),
                pltpu.VMEM((2, length, WIDE), BF16),
                pltpu.VMEM((4, length, WIDE), BF16),
            ]
            + chunk_semaphores(length),
        ),
        out_shape=[full, full, full]
        + halves_of(width, (2, 4, width, WIDE))
        + [jax.ShapeDtypeStruct((4, width), F32)],
        compiler_params=params(),
        name="attention_last",
    )(
        place, *stream, starts, gain, offset, kinds_of(weight), biases, *tables, *rotary, grad
    )


def norm_gradient(values, incoming, grad, gain, sums_ref):
    average = jnp.mean(values, -1, keepdims=True)
    centered = values - average
    variance = jnp.mean(centered * centered, -1, keepdims=True)
    inverse = lax.rsqrt(variance + EPSILON)
    unit = centered * inverse
    grad_unit = incoming * gain
    first = jnp.mean(grad_unit, -1, keepdims=True)
    second = jnp.mean(grad_unit * unit, -1, keepdims=True)
    sums_ref[0:1] += jnp.sum(incoming * unit, axis=0, keepdims=True)
    sums_ref[1:2] += jnp.sum(incoming, axis=0, keepdims=True)
    sums_ref[2:3] += jnp.sum(grad, axis=0, keepdims=True)
    return grad + inverse * (grad_unit - first - unit * second)


def norm_backward_kernel(layer, x_ref, own_ref, other_ref, grad_ref, gain_ref, out_ref, sums_ref):
    @pl.when(pl.program_id(0) == 0)
    def _():
        sums_ref[...] = jnp.zeros_like(sums_ref)

    out = norm_gradient(
        x_ref[...].astype(F32),
        own_ref[...] + other_ref[...],
        grad_ref[...].astype(F32),
        gain_ref[layer : layer + 1].astype(F32),
        sums_ref,
    )
    out_ref[...] = out.astype(out_ref.dtype)


def norm_backward(layer, x, own, other, grad, gain, kind):
    length, width = own.shape
    block = pl.BlockSpec((ROWS, width), lambda i: (i, 0))
    return pl.pallas_call(
        functools.partial(norm_backward_kernel, layer),
        grid=(length // ROWS,),
        in_specs=[block, block, block, block, whole((LAYERS, width))],
        out_specs=[block, whole((8, width))],
        out_shape=[
            jax.ShapeDtypeStruct((length, width), kind),
            jax.ShapeDtypeStruct((8, width), F32),
        ],
        compiler_params=params(),
        name="norm_backward",
    )(x, own, other, grad, gain)


MESH = pl.DeviceIdType.MESH
UNIT = 16
SLOTS = 6
LAG = 2


class Flow(NamedTuple):
    order: tuple
    core: int
    is_up: int
    layer: int
    row: int
    units: int
    start: int
    place: int


def flows_of(width, layer, start):
    rows = width // 2
    kinds = (
        ((0, 1, 2, 3), 1, 0, 0, 0),
        ((1, 0, 2, 3), 1, 1, 0, 1),
        ((0, 1, 2, 3), 1, 0, 1, 2),
        ((1, 0, 2, 3), 1, 1, 1, 3),
        ((2, 0, 1, 3), 0, 0, 0, 0),
        ((2, 1, 0, 3), 0, 0, 1, 1),
    )
    return [
        Flow(order, core, is_up, layer, part * rows, rows // UNIT, start, 4 * layer + place)
        for order, core, is_up, part, place in kinds
    ]


def bit_of(index, bit):
    return (index // (1 << bit)) % 2


def flip(index, bit):
    return index + (1 << bit) * (1 - 2 * bit_of(index, bit))


def finish_kernel(
    bits, flows,
    kept_weight1, kept_up1, came_weight1, came_up1,
    kept_weight0, kept_up0, sent_weight0, sent_up0,
    bias0_ref, bias1_ref, sums1_ref, sums0_ref,
    weight_sum, up_out, small_out,
    up_sum, up_near, up_came,
    *scratch,
):
    stages = bits
    kept = ((kept_weight1, kept_up1), (kept_weight0, kept_up0))
    moved = ((came_weight1, came_up1), (sent_weight0, sent_up0))
    small_parts = (bias0_ref, bias1_ref, sums1_ref, sums0_ref)
    places = 1 + max(flow.place for flow in flows)
    held, scratch = scratch[: places * (stages + 1)], scratch[places * (stages + 1) :]
    held = [held[f * (stages + 1) : (f + 1) * (stages + 1)] for f in range(places)]
    small, small_came = scratch[: stages + 1], scratch[stages + 1 : 2 * stages + 1]
    load_sem, send_sem, recv_sem, credit, small_send, small_recv, near_send, near_recv = (
        scratch[2 * stages + 1 :]
    )
    me, core = lax.axis_index("batch"), lax.axis_index("stream")

    barrier = pltpu.get_barrier_semaphore()
    for bit in range(bits):
        pl.semaphore_signal(
            barrier, inc=1, device_id={"batch": flip(me, bit)}, device_id_type=MESH
        )
    pl.semaphore_signal(barrier, inc=1, device_id={"stream": 1 - core}, device_id_type=MESH)
    pl.semaphore_wait(barrier, bits + 1)

    small_start = 2
    turn_start = max(flow.start + flow.units for flow in flows if flow.layer == 1)
    turn_start += LAG * stages + 1

    def near_copy(layer):
        return pltpu.make_async_remote_copy(
            src_ref=up_near.at[layer],
            dst_ref=up_came.at[layer],
            send_sem=near_send.at[layer],
            recv_sem=near_recv.at[layer],
            device_id={"stream": 0},
            device_id_type=MESH,
        )

    def part_up(layer):
        @pl.when(core == 1)
        def _():
            up_near[layer] = up_sum[layer, :, : WIDE // 2]
            near_copy(layer).start()
            up_out[layer] = up_sum[layer, :, WIDE // 2 :]

    def small_copy(stage):
        return pltpu.make_async_remote_copy(
            src_ref=small[stage],
            dst_ref=small_came[stage],
            send_sem=small_send.at[stage],
            recv_sem=small_recv.at[stage],
            device_id={"batch": flip(me, stage)},
            device_id_type=MESH,
        )

    def small_step(stage):
        if stage == 0:
            row = 0
            for part in small_parts:
                small[0][row : row + part.shape[0]] = part[...]
                row += part.shape[0]
        else:
            small_copy(stage - 1).wait()
            small[stage][...] = small[stage - 1][...] + small_came[stage - 1][...]
        if stage < stages:
            small_copy(stage).start()
        else:
            small_out[...] = small[stage][...]

    def view(order, stage, mine):
        left = sorted(set(range(bits)) - set(order[:stage]), reverse=True)
        pick = bit_of(me, order[stage])
        pick = pick if mine else 1 - pick
        return tuple(pick if bit == order[stage] else slice(None) for bit in left)

    def remote(flow, stage, slot, source):
        place = flow.place
        return pltpu.make_async_remote_copy(
            src_ref=source,
            dst_ref=held[place][stage + 1].at[slot],
            send_sem=send_sem.at[place, stage, slot],
            recv_sem=recv_sem.at[place, stage, slot],
            device_id={"batch": flip(me, flow.order[stage])},
            device_id_type=MESH,
        )

    def sent_from(flow, stage, slot):
        if stage == 0:
            return held[flow.place][0].at[slot]
        return held[flow.place][stage].at[(slot,) + view(flow.order, stage, False)]

    def load(flow, slot, source):
        place = flow.place
        return pltpu.make_async_copy(source, held[place][0].at[slot], load_sem.at[place, slot])

    def load_came(flow, slot, source):
        return pltpu.make_async_copy(
            source, held[flow.place][1].at[slot], recv_sem.at[flow.place, 0, slot]
        )

    def return_credit(flow, stage, unit):
        if stage == 0 and flow.layer == 0:
            return

        @pl.when(unit + SLOTS < flow.units)
        def _():
            pl.semaphore_signal(
                credit.at[flow.place, stage],
                inc=1,
                device_id={"batch": flip(me, flow.order[stage])},
                device_id_type=MESH,
            )

    def take_credit(flow, stage, unit):
        @pl.when(unit >= SLOTS)
        def _():
            pl.semaphore_wait(credit.at[flow.place, stage], 1)

    def begin(flow, unit):
        slot = lax.rem(unit, SLOTS)
        at = (slice(None),) * (bits - 1)
        at += (pl.ds(pl.multiple_of(flow.row + unit * UNIT, UNIT), UNIT),)
        load(flow, slot, kept[flow.layer][flow.is_up].at[at]).start()
        source = moved[flow.layer][flow.is_up].at[at]
        if flow.layer == 0:
            load_came(flow, slot, source).start()
        else:
            take_credit(flow, 0, unit)
            remote(flow, 0, slot, source).start()

    def advance(flow, stage, unit):
        slot = lax.rem(unit, SLOTS)
        buffers, begun = held[flow.place], flow.layer == 0
        copy = remote(flow, stage - 1, slot, sent_from(flow, stage - 1, slot))
        if stage == 1 and begun:
            load_came(flow, slot, buffers[0].at[slot]).wait()
        else:
            copy.wait_recv()
        if stage == 1:
            load(flow, slot, buffers[1].at[slot]).wait()
            mine = buffers[0][slot]
        else:
            mine = buffers[stage - 1][(slot,) + view(flow.order, stage - 1, True)]
        value = buffers[stage][slot] + mine
        if stage < stages:
            buffers[stage][slot] = value
            take_credit(flow, stage, unit)
            remote(flow, stage, slot, sent_from(flow, stage, slot)).start()
        else:
            target = up_sum if flow.is_up else weight_sum
            at = pl.ds(pl.multiple_of(flow.row + unit * UNIT, UNIT), UNIT)
            target[flow.layer, at] = value
        if stage > 1 or not begun:
            copy.wait_send()
        if stage >= 2:
            return_credit(flow, stage - 2, unit)
        if stage == stages:
            return_credit(flow, stage - 1, unit)

    def within(flow, unit):
        return (unit >= 0) & (unit < flow.units) & (core == flow.core)

    def step(index, carry):
        for flow in flows:
            unit = index - flow.start
            pl.when(within(flow, unit))(functools.partial(begin, flow, unit))
        for flow in flows:
            for stage in range(1, stages + 1):
                unit = index - flow.start - LAG * stage
                pl.when(within(flow, unit))(functools.partial(advance, flow, stage, unit))
        for stage in range(stages + 1):
            pl.when(index == small_start + 2 * stage)(functools.partial(small_step, stage))
        pl.when(index == turn_start)(functools.partial(part_up, 1))
        return carry

    last = max(flow.start + flow.units for flow in flows)
    lax.fori_loop(0, last + LAG * stages, step, 0)
    part_up(0)
    for layer in range(len(moved)):

        @pl.when(core == 0)
        def _():
            near_copy(layer).wait_recv()
            up_out[layer] = up_came[layer]

        @pl.when(core == 1)
        def _():
            near_copy(layer).wait_send()


def finish(last, first, came, smalls):
    width = last[0].shape[1]
    bits = 4
    split = (2,) * (bits - 1)
    flows = flows_of(width, 1, 0)
    flows += flows_of(width, 0, max(flow.start + flow.units for flow in flows))
    small = (sum(part.shape[0] for part in smalls), width)
    scratch = [
        pltpu.VMEM((2, width, WIDE), F32),
        pltpu.VMEM((2, width, WIDE // 2), F32),
        pltpu.VMEM((2, width, WIDE // 2), F32),
    ]
    places = 1 + max(flow.place for flow in flows)
    for _ in range(places):
        for stage in range(bits + 1):
            lead = (SLOTS,) + (2,) * (bits - 1 - max(stage - 1, 0))
            scratch.append(pltpu.VMEM(lead + (UNIT, WIDE), F32))
    scratch += [pltpu.VMEM(small, F32)] * (2 * bits + 1)
    scratch += [
        pltpu.SemaphoreType.DMA((places, SLOTS)),
        pltpu.SemaphoreType.DMA((places, bits, SLOTS)),
        pltpu.SemaphoreType.DMA((places, bits, SLOTS)),
        pltpu.SemaphoreType.REGULAR((places, bits)),
        pltpu.SemaphoreType.DMA((bits,)),
        pltpu.SemaphoreType.DMA((bits,)),
        pltpu.SemaphoreType.DMA((2,)),
        pltpu.SemaphoreType.DMA((2,)),
    ]
    large = [last[1], last[3], *came, first[1], first[3], first[0], first[2]]
    large = [array.reshape(split + array.shape[1:]) for array in large]
    return pl.pallas_call(
        functools.partial(finish_kernel, bits, flows),
        in_specs=[pl.BlockSpec(memory_space=pltpu.HBM)] * len(large)
        + [pl.BlockSpec(memory_space=pltpu.VMEM)] * len(smalls),
        out_specs=[pl.BlockSpec(memory_space=pltpu.VMEM)] * 3,
        out_shape=[
            jax.ShapeDtypeStruct((2, width, WIDE), F32),
            jax.ShapeDtypeStruct((2, width, WIDE // 2), F32),
            jax.ShapeDtypeStruct(small, F32),
        ],
        scratch_shapes=scratch,
        compiler_params=pltpu.CompilerParams(
            collective_id=0, has_side_effects=True, vmem_limit_bytes=VMEM_LIMIT
        ),
        name="finish",
    )(*large, *smalls)


def hand_out_kernel(
    rows, own, index_ref, weight_ref, up_ref, small_ref,
    weight_out, up_out, bias_out, down_out, gain_out, offset_out,
):
    index = index_ref[0]
    layers = weight_ref.shape[0]
    for layer in range(layers):
        weight_out[layer] = weight_ref[layers - 1 - layer].T
        up_out[layer] = up_ref[layers - 1 - layer].T
        per_row = small_ref.shape[1] // WIDE
        lanes = pl.ds(pl.multiple_of(lax.rem(index, per_row) * WIDE, WIDE), WIDE)
        row = pl.ds(layer * rows + index // per_row, 1)
        bias_out[layer : layer + 1] = small_ref[row, lanes]
        first = 2 * rows + 8 * (layers - 1 - layer)
        width = small_ref.shape[1]
        sums = pltpu.roll(small_ref[first : first + 8], lax.rem(width - index * own, width), 1)
        gain_out[layer : layer + 1] = sums[0:1, :own]
        offset_out[layer : layer + 1] = sums[1:2, :own]
        down_out[layer : layer + 1] = sums[2:3, :own]


def hand_out(weight, up, small, rows, own):
    layers, width, _ = weight.shape
    vector = jax.ShapeDtypeStruct((layers, own), F32)
    return pl.pallas_call(
        functools.partial(hand_out_kernel, rows, own),
        in_specs=[pl.BlockSpec(memory_space=pltpu.SMEM)]
        + [pl.BlockSpec(memory_space=pltpu.VMEM)] * 3,
        out_specs=[pl.BlockSpec(memory_space=pltpu.VMEM)] * 6,
        out_shape=[
            jax.ShapeDtypeStruct((layers, WIDE, width), F32),
            jax.ShapeDtypeStruct((layers, WIDE // 2, width), F32),
            jax.ShapeDtypeStruct((layers, WIDE), F32),
            vector,
            vector,
            vector,
        ],
        compiler_params=params(),
        name="hand_out",
    )(lax.axis_index("batch").astype(jnp.int32).reshape(1), weight, up, small)


def send_first(halves):
    count = lax.axis_size("batch")

    def pairs(stream, bit):
        return [(2 * source + stream, 2 * flip(source, bit) + stream) for source in range(count)]

    axes = ("batch", "stream")
    return [
        lax.ppermute(halves[0], axes, pairs(0, 2) + pairs(1, 0)),
        lax.ppermute(halves[2], axes, pairs(1, 1)),
    ]


def shards(
    tokens, cotangent, branch_weight, branch_bias, up_weight, down_bias,
    norm_gain, norm_bias, freq_seeds, doc_starts,
):
    is_attention = lax.axis_index("stream") == 0
    length, width = tokens.shape
    rotary = tuple(jnp.asarray(table) for table in rotary_rows(length))
    biases = branch_bias[0].astype(F32).reshape(-1, 1, width)
    tables = lax.cond(
        is_attention,
        lambda: tuple(feature_tables(freq_seeds)),
        lambda: (
            jnp.zeros((LAYERS, QUADS, WIDE, WIDE), BF16),
            jnp.zeros((LAYERS, QUADS, WIDE, WIDE), BF16),
            jnp.zeros((LAYERS, QUADS, 1, WIDE), F32),
        ),
    )
    swap = [(0, 1), (1, 0)]

    def attention(layer, stream):
        return tuple(
            attention_forward(
                layer, stream, doc_starts, norm_gain, norm_bias, branch_weight, biases, tables,
                rotary,
            )
        )

    def feed_forward(layer, stream):
        return tuple(
            mlp_forward(
                layer, stream, norm_gain, norm_bias, up_weight, biases, branch_weight, down_bias
            )
        )

    count = lax.axis_size("batch")
    blocked = count == branch_weight.shape[2] // WIDE
    me = lax.axis_index("batch") if blocked else 0
    place = jnp.stack([jnp.asarray(bit_of(me, bit), jnp.int32) for bit in range(3)])

    part, *kept = lax.cond(
        is_attention,
        functools.partial(attention, 0, (tokens,)),
        functools.partial(feed_forward, 0, (tokens,)),
    )
    stream = (tokens, part, lax.ppermute(part, "stream", swap))

    def attention_ends():
        x, part, *back = attention_last(
            1, place, stream, doc_starts, norm_gain, norm_bias, branch_weight, biases, tables,
            rotary, cotangent,
        )
        return x, part, *flat_halves(*back)

    def feed_forward_ends():
        x, part, *back = mlp_last(
            1, place, stream, norm_gain, norm_bias, up_weight, biases, branch_weight, down_bias,
            cotangent,
        )
        return x, part, *flat_halves(*back)

    x1, part, part1, *halves1, bias1 = lax.cond(
        jnp.logical_not(is_attention), feed_forward_ends, attention_ends
    )
    stream = (x1, part, lax.ppermute(part, "stream", swap))

    def attention_back(layer, grad, stream):
        h, state, mixed = kept
        *result, part, a, b, c, d, bias = attention_backward(
            layer, place, doc_starts, grad, h, state, mixed, tables, rotary, branch_weight, stream
        )
        return *result, *flat_halves(part, a, b, c, d, bias)

    def feed_forward_back(layer, grad, stream):
        h, act, slope = kept
        *result, part, a, b, c, d, bias = mlp_backward(
            layer, place, grad, h, act, slope, branch_weight, up_weight, stream
        )
        return *result, *flat_halves(part, a, b, c, d, bias)

    def back(layer, grad, stream=()):
        *result, part, a, b, c, d, bias = lax.cond(
            is_attention,
            functools.partial(attention_back, layer, grad, stream),
            functools.partial(feed_forward_back, layer, grad, stream),
        )
        return *result, part, (a, b, c, d), bias

    def norm_back(layer, x, part, grad, kind):
        other = lax.ppermute(part, "stream", swap)
        return norm_backward(layer, x, part, other, grad, norm_gain, kind)

    if blocked:
        came = send_first(halves1)
    grad0, sums1 = norm_back(1, x1, part1, cotangent, BF16)
    result, part0, halves0, bias0 = back(0, grad0, stream)
    input_grad, sums0 = norm_back(0, tokens, part0, grad0, F32)
    if blocked:
        weight, up, small = finish(halves1, halves0, came, (bias0, bias1, sums1, sums0))
    else:
        weight, up = scatter_rows((halves0, halves1))
        small = lax.psum(jnp.concatenate([bias0, bias1, sums1, sums0]), "batch")
    index, rows = lax.axis_index("batch"), bias0.shape[0]
    each, own = branch_weight.shape[2] // count, width // count
    if blocked:
        weight, up, bias, down, gain, offset = hand_out(weight, up, small, rows, own)
    else:
        bias = lax.dynamic_slice_in_dim(
            small[: 2 * rows].reshape(LAYERS, -1), index * each, each, axis=1
        )
        sums = small[2 * rows :].reshape(LAYERS, 8, width)[::-1]
        sums = lax.dynamic_slice_in_dim(sums, index * own, own, axis=2)
        down, gain, offset = sums[:, 2], sums[:, 0], sums[:, 1]
    return result, input_grad, weight[None], bias[None], up, down, gain, offset


def scatter_rows(layers):
    weights, ups = [], []
    for sent, kept, sent_up, kept_up in layers:
        blocks = (-1,) + kept.shape[1:]
        wide, far = (4, 2) + kept.shape[1:], (2, 4) + kept.shape[1:]
        weight = jnp.where(
            lax.axis_index("stream") == 1,
            jnp.stack([kept.reshape(wide), sent.reshape(wide)], axis=2).reshape(blocks),
            jnp.stack([kept.reshape(far), sent.reshape(far)], axis=1).reshape(blocks),
        )
        weight = rows_of(weight)
        up = jnp.stack([kept_up.reshape(wide), sent_up.reshape(wide)], axis=1)
        up = rows_of(up.reshape(blocks))
        up = jnp.where(lax.axis_index("stream") == 1, up, 0.0)
        weights.append(lax.psum_scatter(weight, "batch", scatter_dimension=0, tiled=True))
        ups.append(lax.psum_scatter(up, ("batch", "stream"), scatter_dimension=0, tiled=True))
    return jnp.stack(weights), jnp.stack(ups)


def rows_of(blocks):
    return jnp.transpose(blocks, (0, 2, 1)).reshape(-1, blocks.shape[1])


def solution(mesh):
    placed = (
        P("batch", None),
        P("batch", None),
        P("stream", None, None, None),
        P("stream", None, None),
        P(),
        P(),
        P(),
        P(),
        P(),
        P("batch", None),
    )
    return jax.shard_map(
        shards,
        mesh=mesh,
        in_specs=placed,
        out_specs=(
            P("batch", None),
            P("batch", None),
            P("stream", None, "batch", None),
            P("stream", None, "batch"),
            P(None, ("batch", "stream"), None),
            P(None, "batch"),
            P(None, "batch"),
            P(None, "batch"),
        ),
        check_vma=False,
    )
```

```python
import functools
import math
from typing import NamedTuple

import jax
import jax.numpy as jnp
import numpy as np
from jax import lax
from jax.experimental import pallas as pl
from jax.experimental.pallas import tpu as pltpu
from jax.sharding import PartitionSpec as P

HEADS = 16
DH = 64
ROT = 16
FEAT = 64
LAYERS = 2
EPSILON = 1e-05
HIGH = lax.Precision.HIGHEST
F32 = jnp.float32
BF16 = jnp.bfloat16
WIDE = 256
PAIR = 128
QUADS = HEADS * DH // WIDE
PAIRS = HEADS * DH // PAIR
ROWS = 256
VMEM_LIMIT = 56 * 1024 * 1024


def params():
    return pltpu.CompilerParams(vmem_limit_bytes=VMEM_LIMIT)


def whole(shape):
    zeros = (0,) * len(shape)
    return pl.BlockSpec(shape, lambda *_: zeros, pipeline_mode=pl.Buffered(1))


def dot_nn(left, right):
    return lax.dot_general(left, right, (((1,), (0,)), ((), ())), preferred_element_type=F32)


def dot_tn(left, right):
    return lax.dot_general(left, right, (((0,), (0,)), ((), ())), preferred_element_type=F32)


def dot_nt(left, right):
    return lax.dot_general(left, right, (((1,), (1,)), ((), ())), preferred_element_type=F32)


def split(values):
    upper = values.astype(BF16)
    return upper, (values - upper.astype(F32)).astype(BF16)


def lane_index(rows, lanes):
    return lax.broadcasted_iota(jnp.int32, (rows, lanes), 1)


def row_index(rows, lanes):
    return lax.broadcasted_iota(jnp.int32, (rows, lanes), 0)


def cosine_block():
    samples = np.arange(DH, dtype=np.float64)
    angles = math.pi * (samples[None, :] + 0.5) * samples[:, None] / DH
    table = np.cos(angles) * math.sqrt(2.0 / DH)
    table[0] *= math.sqrt(0.5)
    return (table.T * DH ** (-0.25)).astype(np.float32)


def rotary_rows(length):
    position = np.arange(length, dtype=np.float32)
    inverse = (10000.0 ** (-np.arange(0, ROT, 2, dtype=np.float32) / ROT)).astype(np.float32)
    angles = position[:, None] * inverse[None, :]
    cosine, sine = np.cos(angles), np.sin(angles)
    rest = DH - ROT
    cosine_head = np.concatenate([cosine, cosine, np.ones((length, rest))], 1)
    sine_head = np.concatenate([-sine, sine, np.zeros((length, rest))], 1)
    repeat = PAIR // DH
    return (
        np.tile(cosine_head, (1, repeat)).astype(np.float32),
        np.tile(sine_head, (1, repeat)).astype(np.float32),
    )


def tables_kernel(seeds_ref, cosine_ref, upper_ref, lower_ref, weight_ref):
    feature = lane_index(DH, WIDE) % FEAT
    same_head = row_index(WIDE, WIDE) // DH == lane_index(WIDE, WIDE) // FEAT
    ones = jnp.where(same_head, 1.0, 0.0).astype(BF16)
    pick = (row_index(QUADS, WIDE) == lane_index(QUADS, WIDE) // FEAT).astype(BF16)
    cosine = cosine_ref[...]
    for group in range(QUADS):
        seeds = seeds_ref[0, group * QUADS : (group + 1) * QUADS].astype(F32).astype(BF16)
        seeds = dot_tn(seeds, pick).astype(jnp.int32)
        lattice = (feature * seeds) & (FEAT - 1)
        prob = (lattice.astype(F32) + 0.5) * (1.0 / FEAT)
        radius = jnp.sqrt(-2.0 * jnp.log(jnp.minimum(prob, 1.0 - prob)))
        above = 2.515517 + 0.802853 * radius + 0.010328 * radius * radius
        below = (
            1.0
            + 1.432788 * radius
            + 0.189269 * radius * radius
            + 0.001308 * radius * radius * radius
        )
        magnitude = radius - above / below
        omega = jnp.where(prob > 0.5, magnitude, -magnitude)
        project = jnp.dot(cosine, omega, precision=HIGH, preferred_element_type=F32)
        project = jnp.concatenate([project] * QUADS, axis=0)
        upper_ref[0, group], lower_ref[0, group] = split(jnp.where(same_head, project, 0.0))
        grown = jnp.exp(-0.5 / DH * jnp.sum(omega * omega, axis=0, keepdims=True))
        upper, rest = split(jnp.broadcast_to(grown, (8, WIDE)))
        total = dot_nn(upper, ones) + dot_nn(rest, ones)
        weight_ref[0, group] = FEAT * grown / total[:1]


def feature_tables(seeds):
    return pl.pallas_call(
        tables_kernel,
        grid=(LAYERS,),
        in_specs=[
            pl.BlockSpec((1, HEADS, DH), lambda l: (l, 0, 0)),
            whole((DH, DH)),
        ],
        out_specs=[
            pl.BlockSpec((1, QUADS, WIDE, WIDE), lambda l: (l, 0, 0, 0)),
            pl.BlockSpec((1, QUADS, WIDE, WIDE), lambda l: (l, 0, 0, 0)),
            pl.BlockSpec((1, QUADS, 1, WIDE), lambda l: (l, 0, 0, 0)),
        ],
        out_shape=[
            jax.ShapeDtypeStruct((LAYERS, QUADS, WIDE, WIDE), BF16),
            jax.ShapeDtypeStruct((LAYERS, QUADS, WIDE, WIDE), BF16),
            jax.ShapeDtypeStruct((LAYERS, QUADS, 1, WIDE), F32),
        ],
        compiler_params=params(),
        name="feature_tables",
    )(seeds, jnp.asarray(cosine_block()))


def turn(values, cosine, sine):
    lanes = values.shape[1]
    half = ROT // 2
    lane = lane_index(*values.shape) % DH
    swapped = jnp.where(
        lane < half, pltpu.roll(values, lanes - half, 1), pltpu.roll(values, half, 1)
    )
    return values * cosine + swapped * sine


def turn_back(values, cosine, sine):
    lanes = values.shape[1]
    half = ROT // 2
    lane = lane_index(*values.shape) % DH
    turned = values * sine
    swapped = jnp.where(
        lane < half, pltpu.roll(turned, lanes - half, 1), pltpu.roll(turned, half, 1)
    )
    return values * cosine + jnp.where(lane < ROT, swapped, 0.0)


def normalized(x_ref_rows, gain, offset):
    average = jnp.mean(x_ref_rows, -1, keepdims=True)
    centered = x_ref_rows - average
    variance = jnp.mean(centered * centered, -1, keepdims=True)
    return centered * lax.rsqrt(variance + EPSILON) * gain + offset


def start_layer(stream, x_ref, h_ref, gain_ref, offset_ref):
    length = h_ref.shape[0]
    step = min(256, length)

    @pl.loop(0, length // step)
    def _(index):
        rows = pl.ds(pl.multiple_of(index * step, step), step)
        values = stream[0][rows].astype(F32)
        if len(stream) > 1:
            values = values + (stream[1][rows] + stream[2][rows])
            x_ref[rows] = values
        h_ref[rows] = normalized(
            values, gain_ref[...].astype(F32), offset_ref[...].astype(F32)
        ).astype(BF16)


JOB = 256


def start_last_layer(stream, x_hbm, buffers, loads, stores, h_ref, gain_ref, offset_ref):
    gain, offset = gain_ref[...].astype(F32), offset_ref[...].astype(F32)
    jobs = h_ref.shape[0] // JOB

    def rows_at(index):
        return pl.ds(pl.multiple_of(index * JOB, JOB), JOB)

    def load(part, index):
        rows = rows_at(index)
        return pltpu.make_async_copy(
            stream[part].at[rows], buffers[part].at[rows], loads.at[part, index]
        )

    def store(index):
        rows = rows_at(index)
        return pltpu.make_async_copy(buffers[1].at[rows], x_hbm.at[rows], stores.at[index])

    @pl.loop(0, jobs)
    def _(index):
        for part in range(len(stream)):
            load(part, index).start()

    @pl.loop(0, jobs)
    def _(index):
        rows = rows_at(index)
        for part in range(len(stream)):
            load(part, index).wait()
        values = buffers[0][rows].astype(F32) + (buffers[1][rows] + buffers[2][rows])
        buffers[1][rows] = values
        store(index).start()
        h_ref[rows] = normalized(values, gain, offset).astype(BF16)

    @pl.loop(0, jobs)
    def _(index):
        store(index).wait()


def chunk_semaphores(length):
    return [
        pltpu.SemaphoreType.DMA((3, length // JOB)),
        pltpu.SemaphoreType.DMA((length // JOB,)),
    ]


def gelu_parts(units):
    below = 0.5 + 0.5 * lax.erf(units * math.sqrt(0.5))
    return below, jnp.exp(-0.5 * units * units) * (1.0 / math.sqrt(2.0 * math.pi))


FF_BLOCK = 1024
FF_ROWS = 512


def mlp_forward_kernel(layer, count, *refs):
    stream, refs = refs[:count], refs[count:]
    gain_ref, offset_ref, up_ref, bias_ref, down_ref, down_bias_ref = refs[:6]
    gain_ref, offset_ref, down_bias_ref = [
        ref.at[layer : layer + 1] for ref in (gain_ref, offset_ref, down_bias_ref)
    ]
    refs = refs[6:]
    x_ref = None
    if count > 1:
        x_ref, refs = refs[0], refs[1:]
    part_ref, h_ref, act_ref, slope_ref = refs
    step = pl.program_id(0)

    @pl.when(step == 0)
    def _():
        start_layer(stream, x_ref, h_ref, gain_ref, offset_ref)
        part_ref[...] = jnp.broadcast_to(down_bias_ref[...].astype(F32), part_ref.shape)

    for first in range(0, h_ref.shape[0], FF_ROWS):
        rows = slice(first, first + FF_ROWS)
        units = dot_nt(h_ref[rows], up_ref[0]) + bias_ref[0]
        below, density = gelu_parts(units)
        active = (units * below).astype(BF16)
        act_ref[0, rows] = active
        slope_ref[0, rows] = (below + units * density).astype(BF16)
        part_ref[rows] += dot_nn(active, down_ref[0, 0])


def plane_block(length, lanes):
    per_plane = 1024 // lanes
    return pl.BlockSpec((1, length, lanes), lambda j: (j // per_plane, 0, j % per_plane))


def mlp_forward(layer, stream, gain, offset, up, biases, down_weight, down_bias):
    length, width = stream[0].shape
    hidden = up.shape[1]
    blocks = hidden // FF_BLOCK
    state = jax.ShapeDtypeStruct((4, length, width), BF16)
    full = jax.ShapeDtypeStruct((length, width), F32)
    out_shape = [full, jax.ShapeDtypeStruct((length, width), BF16), state, state]
    out_specs = [whole((length, width)), whole((length, width))]
    out_specs += [plane_block(length, FF_BLOCK)] * 2
    if len(stream) > 1:
        out_shape, out_specs = [full] + out_shape, [whole((length, width))] + out_specs
    return pl.pallas_call(
        functools.partial(mlp_forward_kernel, layer, len(stream)),
        grid=(blocks,),
        in_specs=[whole((length, width))] * len(stream)
        + [
            whole((LAYERS, width)),
            whole((LAYERS, width)),
            pl.BlockSpec((1, FF_BLOCK, width), lambda j: (layer, j, 0)),
            pl.BlockSpec((1, 1, FF_BLOCK), lambda j: (layer * blocks + j, 0, 0)),
            pl.BlockSpec((1, 1, FF_BLOCK, width), lambda j: (0, layer, j, 0)),
            whole((LAYERS, width)),
        ],
        out_specs=out_specs,
        out_shape=out_shape,
        compiler_params=params(),
        name="mlp_forward",
    )(*stream, gain, offset, up, biases, down_weight, down_bias)


def add_stream(stream, result_ref):
    if stream:
        result_ref[...] = stream[0][...] + (stream[1][...] + stream[2][...])


def stream_specs(stream):
    specs = [
        pl.BlockSpec((part.shape[0] // 4, part.shape[1]), lambda j, *_: (j, 0)) for part in stream
    ]
    shapes = [jax.ShapeDtypeStruct(part.shape, F32) for part in stream[:1]]
    return specs, specs[:1], shapes


def mlp_backward_kernel(count, place_ref, *refs):
    stream, refs = refs[:count], refs[count:]
    grad_ref, h_ref, act_ref, slope_ref, down_ref, up_ref = refs[:6]
    result_ref, refs = (refs[6], refs[7:]) if count else (None, refs[6:])
    part_ref, along_x, kept_x, along_y, kept_y, bias_ref = refs[:6]
    grad_t, h_t, units = refs[6:]
    step = pl.program_id(0)
    add_stream(stream, result_ref)

    @pl.when(step == 0)
    def _():
        grad_t[...] = grad_ref[...].T
        h_t[...] = h_ref[...].T
        part_ref[...] = jnp.zeros_like(part_ref)

    bias = jnp.zeros((1, FF_BLOCK), F32)
    for first in range(0, h_ref.shape[0], ROWS):
        rows = slice(first, first + ROWS)
        grad_act = dot_nt(grad_ref[rows], down_ref[0, 0])
        grad_unit = (grad_act * slope_ref[0, rows].astype(F32)).astype(BF16)
        bias += jnp.sum(grad_unit.astype(F32), axis=0, keepdims=True)
        units[rows] = grad_unit
        part_ref[rows] += dot_nn(grad_unit, up_ref[0])
    bias_ref[pl.ds(step, 1)] = bias

    mlp_weights(
        place_ref, grad_t, h_t, act_ref.at[0], units, along_x, kept_x, along_y, kept_y
    )


def mlp_weights(place_ref, grad_t, h_t, act, units, along_x, kept_x, along_y, kept_y):
    def block(y, x):
        return pl.ds(pl.multiple_of((2 * y + x) * WIDE, WIDE), WIDE)

    near_x, near_y = place_ref[0], place_ref[1]

    @pl.loop(0, h_t.shape[0] // ROWS)
    def _(index):
        rows = pl.ds(pl.multiple_of(index * ROWS, ROWS), ROWS)

        @pl.loop(0, 2)
        def _(side):
            for target, x in ((along_x, 1 - near_x), (kept_x, near_x)):
                target[0, side, rows] = dot_nn(grad_t[rows], act[:, block(side, x)])
            for target, y in ((along_y, 1 - near_y), (kept_y, near_y)):
                target[0, side, rows] = dot_nn(h_t[rows], units[:, block(y, side)])


def mlp_last_kernel(layer, place_ref, *refs):
    stream, refs = refs[:3], refs[3:]
    gain_ref, offset_ref, up_ref, bias_ref, down_ref, down_bias_ref, grad_ref = refs[:7]
    gain_ref, offset_ref, down_bias_ref = [
        ref.at[layer : layer + 1] for ref in (gain_ref, offset_ref, down_bias_ref)
    ]
    x_hbm, part_ref, grad_part, along_x, kept_x, along_y, kept_y, bias_out = refs[7:15]
    h_ref, grad_t, h_t, act, units, loads, stores = refs[15:]
    step = pl.program_id(0)

    @pl.when(step == 0)
    def _():
        buffers = (act, part_ref, grad_part)
        start_last_layer(stream, x_hbm, buffers, loads, stores, h_ref, gain_ref, offset_ref)
        part_ref[...] = jnp.broadcast_to(down_bias_ref[...].astype(F32), part_ref.shape)
        grad_part[...] = jnp.zeros_like(grad_part)
        grad_t[...] = grad_ref[...].T
        h_t[...] = h_ref[...].T

    here = pl.ds(step, 1)
    bias_out[here] = jnp.zeros((1, FF_BLOCK), F32)

    @pl.loop(0, h_ref.shape[0] // ROWS)
    def _(index):
        rows = pl.ds(pl.multiple_of(index * ROWS, ROWS), ROWS)
        hidden = dot_nt(h_ref[rows], up_ref[0]) + bias_ref[0]
        below, density = gelu_parts(hidden)
        active = (hidden * below).astype(BF16)
        act[rows] = active
        part_ref[rows] += dot_nn(active, down_ref[0, 0])
        grad_act = dot_nt(grad_ref[rows], down_ref[0, 0])
        grad_unit = (grad_act * (below + hidden * density)).astype(BF16)
        bias_out[here] += jnp.sum(grad_unit.astype(F32), axis=0, keepdims=True)
        units[rows] = grad_unit
        grad_part[rows] += dot_nn(grad_unit, up_ref[0])
    mlp_weights(place_ref, grad_t, h_t, act, units, along_x, kept_x, along_y, kept_y)


def mlp_last(layer, place, stream, gain, offset, up, biases, down_weight, down_bias, grad):
    length, width = stream[0].shape
    blocks = up.shape[1] // FF_BLOCK
    full = jax.ShapeDtypeStruct((length, width), F32)
    pair = pl.BlockSpec((1, 2, width, WIDE), lambda j, *_: (j, 0, 0, 0))
    return pl.pallas_call(
        functools.partial(mlp_last_kernel, layer),
        grid_spec=pltpu.PrefetchScalarGridSpec(
            num_scalar_prefetch=1,
            grid=(blocks,),
            in_specs=[pl.BlockSpec(memory_space=pltpu.HBM)] * 3
            + [
                whole((LAYERS, width)),
                whole((LAYERS, width)),
                pl.BlockSpec((1, FF_BLOCK, width), lambda j, *_: (layer, j, 0)),
                pl.BlockSpec((1, 1, FF_BLOCK), lambda j, *_: (layer * blocks + j, 0, 0)),
                pl.BlockSpec((1, 1, FF_BLOCK, width), lambda j, *_: (0, layer, j, 0)),
                whole((LAYERS, width)),
                whole((length, width)),
            ],
            out_specs=[pl.BlockSpec(memory_space=pltpu.HBM)]
            + [whole((length, width))] * 2
            + [pair] * 4
            + [whole((blocks, FF_BLOCK))],
            scratch_shapes=[
                pltpu.VMEM((length, width), BF16),
                pltpu.VMEM((width, length), BF16),
                pltpu.VMEM((width, length), BF16),
                pltpu.VMEM((length, FF_BLOCK), BF16),
                pltpu.VMEM((length, FF_BLOCK), BF16),
            ]
            + chunk_semaphores(length),
        ),
        out_shape=[full, full, full]
        + halves_of(width, (4, 2, width, WIDE))
        + [jax.ShapeDtypeStruct((blocks, FF_BLOCK), F32)],
        compiler_params=params(),
        name="mlp_last",
    )(place, *stream, gain, offset, up, biases, down_weight, down_bias, grad)


def halves_of(width, weight):
    shapes = (weight,) * 2 + ((4, 2, width, WIDE),) * 2
    return [jax.ShapeDtypeStruct(shape, F32) for shape in shapes]


def flat_halves(part, sent, kept, sent_up, kept_up, bias):
    halves = [half.reshape((-1,) + half.shape[2:]) for half in (sent, kept, sent_up, kept_up)]
    return (part, *halves, bias)


def mlp_backward(layer, place, grad, h, act, slope, down_weight, up, stream=()):
    length, width = h.shape
    hidden = up.shape[1]
    blocks = hidden // FF_BLOCK
    pair = pl.BlockSpec((1, 2, width, WIDE), lambda j, *_: (j, 0, 0, 0))
    plane = pl.BlockSpec((1, length, FF_BLOCK), lambda j, *_: (j, 0, 0))
    stream_in, stream_out, stream_shape = stream_specs(stream)
    return pl.pallas_call(
        functools.partial(mlp_backward_kernel, len(stream)),
        grid_spec=pltpu.PrefetchScalarGridSpec(
            num_scalar_prefetch=1,
            grid=(blocks,),
            in_specs=stream_in
            + [
                whole((length, width)),
                whole((length, width)),
                plane,
                plane,
                pl.BlockSpec((1, 1, FF_BLOCK, width), lambda j, *_: (0, layer, j, 0)),
                pl.BlockSpec((1, FF_BLOCK, width), lambda j, *_: (layer, j, 0)),
            ],
            out_specs=stream_out
            + [whole((length, width))]
            + [pair] * 4
            + [whole((blocks, FF_BLOCK))],
            scratch_shapes=[
                pltpu.VMEM((width, length), BF16),
                pltpu.VMEM((width, length), BF16),
                pltpu.VMEM((length, FF_BLOCK), BF16),
            ],
        ),
        out_shape=stream_shape
        + [jax.ShapeDtypeStruct((length, width), F32)]
        + halves_of(width, (4, 2, width, WIDE))
        + [jax.ShapeDtypeStruct((blocks, FF_BLOCK), F32)],
        compiler_params=params(),
        name="mlp_backward",
    )(place, *stream, grad, h, act, slope, down_weight, up)


def head_sums(values, ones):
    upper, lower = split(values)
    return dot_nn(upper, ones) + dot_nn(lower, ones)


def same_head_ones():
    same = row_index(WIDE, WIDE) // DH == lane_index(WIDE, WIDE) // DH
    return jnp.where(same, 1.0, 0.0).astype(BF16)


def document_of(starts_ref, positions):
    return sum((starts_ref[0, i] <= positions).astype(jnp.int32) for i in range(starts_ref.shape[1]))


def write_mask(starts_ref, mask_ref, flipped):
    for first in range(0, mask_ref.shape[0], ROWS):
        lanes = lane_index(1, ROWS) + first
        own = row_index(ROWS, 1) + first
        order = (own <= lanes) if flipped else (lanes <= own)
        seen = (document_of(starts_ref, own) == document_of(starts_ref, lanes)) & order
        mask_ref[first : first + ROWS] = jnp.where(seen, 1.0, 0.0).astype(BF16)


def document_edges(starts_ref, length):
    edges = []
    for first in range(0, length, ROWS):
        rows = document_of(starts_ref, row_index(ROWS, 1) + first)
        here = document_of(starts_ref, first)
        later = document_of(starts_ref, first + ROWS)
        edges.append((rows == here, rows == later, here == later))
    return edges


def wide_rotary(cosine_ref, sine_ref, rows):
    return tuple(
        jnp.concatenate([ref[rows]] * (WIDE // PAIR), axis=1) for ref in (cosine_ref, sine_ref)
    )


def attend_heads(
    first_bias, starts_ref, weight_ref, bias_ref, upper_ref, lower_ref, scale_ref, cosine_ref,
    sine_ref, part_ref, h_ref, state_ref, mixed_ref, mask_ref,
):
    length = h_ref.shape[0]
    ones = same_head_ones()
    table_up, table_low = upper_ref[0, 0], lower_ref[0, 0]
    lanes_of_step = pl.ds(pl.multiple_of(pl.program_id(0) * WIDE, WIDE), WIDE)

    def features(values, rows):
        upper, lower = split(turn(values, *wide_rotary(cosine_ref, sine_ref, rows)))
        return dot_nn(upper, table_up) + (dot_nn(lower, table_up) + dot_nn(upper, table_low))

    for first in range(0, length, ROWS):
        rows = slice(first, first + ROWS)
        queries, keys, values = [
            dot_nt(h_ref[rows], weight_ref[0, 0, kind, 0])
            + bias_ref[first_bias + kind, :, lanes_of_step]
            for kind in range(3)
        ]
        state_ref[0, rows] = jnp.exp(features(queries, rows)).astype(BF16)
        logs = features(keys, rows) - (0.5 / math.sqrt(DH)) * head_sums(keys * keys, ones)
        state_ref[1, rows] = (scale_ref[0, 0] * jnp.exp(logs)).astype(BF16)
        state_ref[2, rows] = keys.astype(BF16)
        state_ref[3, rows] = values.astype(BF16)

    zero = jnp.zeros((), BF16)
    one = jnp.ones((), BF16)
    left = lane_index(ROWS, PAIR) < DH
    row, lane = row_index(PAIR, 2 * PAIR), lane_index(PAIR, 2 * PAIR)
    same = row // DH == lane // PAIR
    edges = document_edges(starts_ref, length)
    for pair in range(WIDE // PAIR):
        lanes = slice(pair * PAIR, (pair + 1) * PAIR)
        before = None
        for block, (same_first, same_next, goes_on) in enumerate(edges):
            rows = slice(block * ROWS, (block + 1) * ROWS)
            seen = mask_ref[rows] > zero
            queries, keys = state_ref[0, rows, lanes], state_ref[1, rows, lanes]
            values = [jnp.where(own, state_ref[3, rows, lanes], one) for own in (left, ~left)]
            if block > 0:
                earlier = dot_nn(queries, before.astype(BF16))
                earlier = jnp.where(same_first, earlier, 0.0)
            sums = []
            for head, own in enumerate((left, ~left)):
                scores = dot_nt(queries, jnp.where(own, keys, zero)).astype(BF16)
                total = dot_nn(jnp.where(seen, scores, zero), values[head])
                if block > 0:
                    total = total + earlier[:, head * PAIR : (head + 1) * PAIR]
                sums.append(total)
            if block + 1 < len(edges):
                kept = jnp.where(same_next, keys, zero)
                added = jnp.where(same, dot_tn(kept, jnp.concatenate(values, axis=1)), 0.0)
                if block > 0:
                    added = added + jnp.where(goes_on, before, 0.0)
                before = added
            numer = jnp.where(left, sums[0], sums[1])
            denom = jnp.where(left, pltpu.roll(sums[0], DH, 1), pltpu.roll(sums[1], DH, 1))
            inverse = 1.0 / denom
            mixed_ref[0, rows, lanes] = (numer * inverse).astype(BF16)
            mixed_ref[1, rows, lanes], mixed_ref[2, rows, lanes] = split(inverse)
    for first in range(0, length, ROWS):
        rows = slice(first, first + ROWS)
        part_ref[rows] += dot_nn(mixed_ref[0, rows], weight_ref[0, 0, 3, 0])


def attention_forward_kernel(layer, count, *refs):
    stream, refs = refs[:count], refs[count:]
    starts_ref, gain_ref, offset_ref, weight_ref, bias_ref = refs[:5]
    gain_ref, offset_ref = [ref.at[layer : layer + 1] for ref in (gain_ref, offset_ref)]
    first_bias = layer * (bias_ref.shape[0] // LAYERS)
    upper_ref, lower_ref, scale_ref, cosine_ref, sine_ref = refs[5:10]
    refs = refs[10:]
    x_ref = None
    if count > 1:
        x_ref, refs = refs[0], refs[1:]
    part_ref, h_ref, state_ref, mixed_ref, mask_ref = refs

    @pl.when(pl.program_id(0) == 0)
    def _():
        start_layer(stream, x_ref, h_ref, gain_ref, offset_ref)
        write_mask(starts_ref, mask_ref, False)
        part_ref[...] = jnp.broadcast_to(bias_ref[first_bias + 3], part_ref.shape)

    attend_heads(
        first_bias, starts_ref, weight_ref, bias_ref, upper_ref, lower_ref, scale_ref, cosine_ref,
        sine_ref, part_ref, h_ref, state_ref, mixed_ref, mask_ref,
    )


def kinds_of(weight):
    return weight.reshape(weight.shape[:2] + (4, QUADS, WIDE, weight.shape[3]))


def attention_forward(layer, stream, starts, gain, offset, weight, biases, tables, rotary):
    length, width = stream[0].shape
    full = jax.ShapeDtypeStruct((length, width), F32)
    state = jax.ShapeDtypeStruct((4, length, width), BF16)
    out_shape = [full, jax.ShapeDtypeStruct((length, width), BF16), state, state]
    four = pl.BlockSpec((4, length, WIDE), lambda g: (0, 0, g))
    out_specs = [whole((length, width)), whole((length, width)), four, four]
    if len(stream) > 1:
        out_shape, out_specs = [full] + out_shape, [whole((length, width))] + out_specs
    return pl.pallas_call(
        functools.partial(attention_forward_kernel, layer, len(stream)),
        grid=(QUADS,),
        in_specs=[whole((length, width))] * len(stream)
        + [
            pl.BlockSpec(memory_space=pltpu.SMEM),
            whole((LAYERS, width)),
            whole((LAYERS, width)),
            pl.BlockSpec((1, 1, 4, 1, WIDE, width), lambda g: (0, layer, 0, g, 0, 0)),
            whole((LAYERS * 4, 1, width)),
            pl.BlockSpec((1, 1, WIDE, WIDE), lambda g: (layer, g, 0, 0)),
            pl.BlockSpec((1, 1, WIDE, WIDE), lambda g: (layer, g, 0, 0)),
            pl.BlockSpec((1, 1, 1, WIDE), lambda g: (layer, g, 0, 0)),
            whole((length, PAIR)),
            whole((length, PAIR)),
        ],
        out_specs=out_specs,
        out_shape=out_shape,
        scratch_shapes=[pltpu.VMEM((length, ROWS), BF16)],
        compiler_params=params(),
        name="attention_forward",
    )(
        *stream, starts, gain, offset, kinds_of(weight),
        biases, *tables, *rotary,
    )


def attend_heads_back(
    place_ref, starts_ref, grad_ref, state_ref, mixed_ref, table_ref, cosine_ref, sine_ref,
    weight_ref, part_ref, along_z, kept_z, bias_ref, mask_ref, upright, numer_ref, feat_ref, flow,
):
    group = pl.program_id(0)
    length, width = grad_ref.shape
    row, lane = row_index(WIDE, WIDE), lane_index(WIDE, WIDE)
    partner = (row // PAIR == lane // PAIR) & (row // DH != lane // DH)
    partner = jnp.where(partner, 1.0, 0.0).astype(BF16)
    zero = jnp.zeros((), BF16)
    one = jnp.ones((), BF16)
    for first in range(0, length, ROWS):
        rows = slice(first, first + ROWS)
        grad = dot_nt(grad_ref[rows], weight_ref[0, 0, 3, 0]).astype(BF16).astype(F32)
        inverse = mixed_ref[1, rows].astype(F32) + mixed_ref[2, rows].astype(F32)
        scaled = grad * inverse
        upper, lower = split(-head_sums(scaled * mixed_ref[0, rows].astype(F32), partner))
        numer = scaled.astype(BF16)
        lane = lane_index(ROWS, WIDE)
        spare = jnp.where(lane % DH == 0, upper, jnp.where(lane % DH == 1, lower, zero))
        left = lane % PAIR < DH
        numer_ref[0, rows] = jnp.where(left, numer, spare)
        numer_ref[1, rows] = jnp.where(left, spare, numer)

    left = lane_index(ROWS, PAIR) < DH
    spare = jnp.where(lane_index(ROWS, PAIR) % DH < 2, one, zero)
    row, lane = row_index(2 * PAIR, PAIR), lane_index(2 * PAIR, PAIR)
    same = row // PAIR == lane // DH
    row, lane = row_index(PAIR, PAIR), lane_index(PAIR, PAIR)
    same_head = row // DH == lane // DH
    edges = document_edges(starts_ref, length)
    blocks = range(len(edges))

    def both(upper_and_lower, sums):
        upper, lower = split(sums)
        return dot_nn(upper_and_lower, upper) + dot_nn(upper_and_lower, lower)

    for pair in range(WIDE // PAIR):
        lanes = slice(pair * PAIR, (pair + 1) * PAIR)

        def rows_of_block(block):
            rows = slice(block * ROWS, (block + 1) * ROWS)
            numers = [numer_ref[head, rows, lanes] for head in range(2)]
            values = state_ref[3, rows, lanes]
            values = [jnp.where(own, values, spare) for own in (left, ~left)]
            return rows, state_ref[0, rows, lanes], state_ref[1, rows, lanes], values, numers

        before, after = {}, {}
        for block in blocks[1:]:
            rows, queries, keys, values, numers = rows_of_block(block - 1)
            _, same_next, goes_on = edges[block - 1]
            kept = jnp.where(same_next, keys, zero)
            added = jnp.where(same, dot_tn(jnp.concatenate(values, axis=1), kept), 0.0)
            if block > 1:
                added = added + jnp.where(goes_on, before[block - 1], 0.0)
            before[block] = added
        for block in blocks[::-1][:-1]:
            rows, queries, keys, values, numers = rows_of_block(block)
            same_first, _, goes_on = edges[block]
            kept = jnp.where(same_first, queries, zero)
            keys_sum = jnp.where(same, dot_tn(jnp.concatenate(numers, axis=1), kept), 0.0)
            values_sum = dot_tn(kept, jnp.where(left, numers[0], numers[1]))
            values_sum = jnp.where(same_head, values_sum, 0.0)
            if block + 1 < len(edges):
                keys_sum = keys_sum + jnp.where(goes_on, after[block + 1][0], 0.0)
                values_sum = values_sum + jnp.where(goes_on, after[block + 1][1], 0.0)
            after[block] = (keys_sum, values_sum)
        for block in blocks:
            rows, queries, keys, values, numers = rows_of_block(block)
            same_first, same_next, _ = edges[block]
            seen = mask_ref[rows] > zero
            numer = jnp.where(left, numers[0], numers[1])
            grads = []
            grad_query = None
            for head, own in enumerate((left, ~left)):
                own_keys = jnp.where(own, keys, zero)
                scores = dot_nt(own_keys, queries).astype(BF16)
                grad_value = dot_nn(jnp.where(seen, scores, zero), numer)
                grad_scores = dot_nt(values[head], numers[head]).astype(BF16)
                grad_scores = jnp.where(seen, grad_scores, zero)
                grads.append((grad_value, dot_nn(grad_scores, queries)))
                from_head = dot_tn(grad_scores, own_keys)
                grad_query = from_head if head == 0 else grad_query + from_head
            grad_value = jnp.where(left, grads[0][0], grads[1][0])
            grad_key = jnp.where(left, grads[0][1], grads[1][1])
            if block + 1 < len(edges):
                keys_sum, values_sum = after[block + 1]
                late = both(jnp.concatenate(values, axis=1), keys_sum)
                grad_key = grad_key + jnp.where(same_next, late, 0.0)
                late = dot_nn(keys, values_sum.astype(BF16))
                grad_value = grad_value + jnp.where(same_next, late, 0.0)
            if block > 0:
                early = both(jnp.concatenate(numers, axis=1), before[block])
                grad_query = grad_query + jnp.where(same_first, early, 0.0)
            flow[2, rows, lanes] = grad_value.astype(BF16)
            feat_ref[1, rows, lanes] = (grad_key * keys.astype(F32)).astype(BF16)
            feat_ref[0, rows, lanes] = (grad_query * queries.astype(F32)).astype(BF16)

    ones = same_head_ones()
    table = table_ref[0, 0]
    sums = [jnp.zeros((1, WIDE), F32)] * 3
    for first in range(0, length, ROWS):
        rows = slice(first, first + ROWS)
        cosine, sine = wide_rotary(cosine_ref, sine_ref, rows)
        flow[0, rows] = turn_back(dot_nt(feat_ref[0, rows], table), cosine, sine).astype(BF16)
        shrink = dot_nn(feat_ref[1, rows], ones) * (1.0 / math.sqrt(DH))
        turned = turn_back(dot_nt(feat_ref[1, rows], table), cosine, sine)
        flow[1, rows] = (turned - state_ref[2, rows].astype(F32) * shrink).astype(BF16)
        total = part_ref[rows]
        for kind in range(3):
            block = flow[kind, rows]
            sums[kind] = sums[kind] + jnp.sum(block.astype(F32), axis=0, keepdims=True)
            total = total + dot_nn(block, weight_ref[0, 0, kind, 0])
        part_ref[rows] = total
    for kind in range(3):
        bias_ref[kind : kind + 1] = sums[kind]
    lanes = pl.ds(pl.multiple_of(group * WIDE, WIDE), WIDE)
    bias_ref[3:4] = jnp.sum(grad_ref[:, lanes].astype(F32), axis=0, keepdims=True)
    flow[3] = mixed_ref[0]
    for first in range(0, width, ROWS):
        rows = slice(first, first + ROWS)
        for far in range(2):
            for target, near in ((along_z, 1 - place_ref[2]), (kept_z, place_ref[2])):
                kind = 2 * far + near
                target[far, 0, rows] = dot_nn(upright[kind // 3, rows], flow[kind])


def attention_backward_kernel(count, place_ref, *refs):
    stream, refs = refs[:count], refs[count:]
    starts_ref, grad_ref, h_ref, state_ref, mixed_ref, table_ref = refs[:6]
    cosine_ref, sine_ref, weight_ref = refs[6:9]
    result_ref, refs = (refs[9], refs[10:]) if count else (None, refs[9:])
    part_ref, along_z, kept_z, _, _, bias_ref = refs[:6]
    mask_ref, upright, numer_ref, feat_ref, flow = refs[6:]
    add_stream(stream, result_ref)

    @pl.when(pl.program_id(0) == 0)
    def _():
        write_mask(starts_ref, mask_ref, True)
        upright[0] = h_ref[...].T
        upright[1] = grad_ref[...].T
        part_ref[...] = jnp.zeros_like(part_ref)

    attend_heads_back(
        place_ref, starts_ref, grad_ref, state_ref, mixed_ref, table_ref, cosine_ref, sine_ref,
        weight_ref, part_ref, along_z, kept_z, bias_ref, mask_ref, upright, numer_ref, feat_ref,
        flow,
    )


def attention_backward(
    layer, place, starts, grad, h, state, mixed, tables, rotary, weight, stream=()
):
    _, length, width = state.shape
    four = pl.BlockSpec((4, length, WIDE), lambda g, *_: (0, 0, g))
    halves = pl.BlockSpec((2, 1, width, WIDE), lambda g, *_: (0, g, 0, 0))
    stream_in, stream_out, stream_shape = stream_specs(stream)
    return pl.pallas_call(
        functools.partial(attention_backward_kernel, len(stream)),
        grid_spec=pltpu.PrefetchScalarGridSpec(
            num_scalar_prefetch=1,
            grid=(QUADS,),
            in_specs=stream_in
            + [
                pl.BlockSpec(memory_space=pltpu.SMEM),
                whole((length, width)),
                whole((length, width)),
                four,
                four,
                pl.BlockSpec((1, 1, WIDE, WIDE), lambda g, *_: (layer, g, 0, 0)),
                whole((length, PAIR)),
                whole((length, PAIR)),
                pl.BlockSpec((1, 1, 4, 1, WIDE, width), lambda g, *_: (0, layer, 0, g, 0, 0)),
            ],
            out_specs=stream_out
            + [whole((length, width))]
            + [halves, halves]
            + [pl.BlockSpec(memory_space=pl.ANY)] * 2
            + [pl.BlockSpec((4, WIDE), lambda g, *_: (0, g))],
            scratch_shapes=[
                pltpu.VMEM((length, ROWS), BF16),
                pltpu.VMEM((2, width, length), BF16),
                pltpu.VMEM((2, length, WIDE), BF16),
                pltpu.VMEM((2, length, WIDE), BF16),
                pltpu.VMEM((4, length, WIDE), BF16),
            ],
        ),
        out_shape=stream_shape
        + [jax.ShapeDtypeStruct((length, width), F32)]
        + halves_of(width, (2, 4, width, WIDE))
        + [jax.ShapeDtypeStruct((4, width), F32)],
        compiler_params=params(),
        name="attention_backward",
    )(place, *stream, starts, grad, h, state, mixed, tables[0], *rotary, kinds_of(weight))


def attention_last_kernel(layer, place_ref, *refs):
    stream, refs = refs[:3], refs[3:]
    starts_ref, gain_ref, offset_ref, weight_ref, bias_ref = refs[:5]
    gain_ref, offset_ref = [ref.at[layer : layer + 1] for ref in (gain_ref, offset_ref)]
    first_bias = layer * (bias_ref.shape[0] // LAYERS)
    upper_ref, lower_ref, scale_ref, cosine_ref, sine_ref, grad_ref = refs[5:11]
    x_hbm, part_ref, grad_part, along_z, kept_z, _, _, bias_out = refs[11:19]
    h_ref, state_ref, mixed_ref, mask_ref, mask_back = refs[19:24]
    upright, numer_ref, feat_ref, flow, loads, stores = refs[24:]

    @pl.when(pl.program_id(0) == 0)
    def _():
        buffers = (upright.at[0], part_ref, grad_part)
        start_last_layer(stream, x_hbm, buffers, loads, stores, h_ref, gain_ref, offset_ref)
        write_mask(starts_ref, mask_ref, False)
        write_mask(starts_ref, mask_back, True)
        part_ref[...] = jnp.broadcast_to(bias_ref[first_bias + 3], part_ref.shape)
        grad_part[...] = jnp.zeros_like(grad_part)
        upright[0] = h_ref[...].T
        upright[1] = grad_ref[...].T

    attend_heads(
        first_bias, starts_ref, weight_ref, bias_ref, upper_ref, lower_ref, scale_ref, cosine_ref,
        sine_ref, part_ref, h_ref, state_ref, mixed_ref, mask_ref,
    )
    attend_heads_back(
        place_ref, starts_ref, grad_ref, state_ref, mixed_ref, upper_ref, cosine_ref, sine_ref,
        weight_ref, grad_part, along_z, kept_z, bias_out, mask_back, upright, numer_ref, feat_ref,
        flow,
    )


def attention_last(
    layer, place, stream, starts, gain, offset, weight, biases, tables, rotary, grad
):
    length, width = stream[0].shape
    full = jax.ShapeDtypeStruct((length, width), F32)
    halves = pl.BlockSpec((2, 1, width, WIDE), lambda g, *_: (0, g, 0, 0))
    return pl.pallas_call(
        functools.partial(attention_last_kernel, layer),
        grid_spec=pltpu.PrefetchScalarGridSpec(
            num_scalar_prefetch=1,
            grid=(QUADS,),
            in_specs=[pl.BlockSpec(memory_space=pltpu.HBM)] * 3
            + [
                pl.BlockSpec(memory_space=pltpu.SMEM),
                whole((LAYERS, width)),
                whole((LAYERS, width)),
                pl.BlockSpec((1, 1, 4, 1, WIDE, width), lambda g, *_: (0, layer, 0, g, 0, 0)),
                whole((LAYERS * 4, 1, width)),
                pl.BlockSpec((1, 1, WIDE, WIDE), lambda g, *_: (layer, g, 0, 0)),
                pl.BlockSpec((1, 1, WIDE, WIDE), lambda g, *_: (layer, g, 0, 0)),
                pl.BlockSpec((1, 1, 1, WIDE), lambda g, *_: (layer, g, 0, 0)),
                whole((length, PAIR)),
                whole((length, PAIR)),
                whole((length, width)),
            ],
            out_specs=[pl.BlockSpec(memory_space=pltpu.HBM)]
            + [whole((length, width))] * 2
            + [halves, halves]
            + [pl.BlockSpec(memory_space=pl.ANY)] * 2
            + [pl.BlockSpec((4, WIDE), lambda g, *_: (0, g))],
            scratch_shapes=[
                pltpu.VMEM((length, width), BF16),
                pltpu.VMEM((4, length, WIDE), BF16),
                pltpu.VMEM((3, length, WIDE), BF16),
                pltpu.VMEM((length, ROWS), BF16),
                pltpu.VMEM((length, ROWS), BF16),
                pltpu.VMEM((2, width, length), BF16),
                pltpu.VMEM((2, length, WIDE), BF16),
                pltpu.VMEM((2, length, WIDE), BF16),
                pltpu.VMEM((4, length, WIDE), BF16),
            ]
            + chunk_semaphores(length),
        ),
        out_shape=[full, full, full]
        + halves_of(width, (2, 4, width, WIDE))
        + [jax.ShapeDtypeStruct((4, width), F32)],
        compiler_params=params(),
        name="attention_last",
    )(
        place, *stream, starts, gain, offset, kinds_of(weight), biases, *tables, *rotary, grad
    )


def norm_gradient(values, incoming, grad, gain, sums_ref):
    average = jnp.mean(values, -1, keepdims=True)
    centered = values - average
    variance = jnp.mean(centered * centered, -1, keepdims=True)
    inverse = lax.rsqrt(variance + EPSILON)
    unit = centered * inverse
    grad_unit = incoming * gain
    first = jnp.mean(grad_unit, -1, keepdims=True)
    second = jnp.mean(grad_unit * unit, -1, keepdims=True)
    sums_ref[0:1] += jnp.sum(incoming * unit, axis=0, keepdims=True)
    sums_ref[1:2] += jnp.sum(incoming, axis=0, keepdims=True)
    sums_ref[2:3] += jnp.sum(grad, axis=0, keepdims=True)
    return grad + inverse * (grad_unit - first - unit * second)


def norm_backward_kernel(layer, x_ref, own_ref, other_ref, grad_ref, gain_ref, out_ref, sums_ref):
    @pl.when(pl.program_id(0) == 0)
    def _():
        sums_ref[...] = jnp.zeros_like(sums_ref)

    out = norm_gradient(
        x_ref[...].astype(F32),
        own_ref[...] + other_ref[...],
        grad_ref[...].astype(F32),
        gain_ref[layer : layer + 1].astype(F32),
        sums_ref,
    )
    out_ref[...] = out.astype(out_ref.dtype)


def norm_backward(layer, x, own, other, grad, gain, kind):
    length, width = own.shape
    block = pl.BlockSpec((ROWS, width), lambda i: (i, 0))
    return pl.pallas_call(
        functools.partial(norm_backward_kernel, layer),
        grid=(length // ROWS,),
        in_specs=[block, block, block, block, whole((LAYERS, width))],
        out_specs=[block, whole((8, width))],
        out_shape=[
            jax.ShapeDtypeStruct((length, width), kind),
            jax.ShapeDtypeStruct((8, width), F32),
        ],
        compiler_params=params(),
        name="norm_backward",
    )(x, own, other, grad, gain)


MESH = pl.DeviceIdType.MESH
UNIT = 16
SLOTS = 6
LAG = 2


class Flow(NamedTuple):
    order: tuple
    core: int
    is_up: int
    layer: int
    row: int
    units: int
    start: int
    place: int


def flows_of(width, layer, start):
    rows = width // 2
    kinds = (
        ((0, 1, 2, 3), 1, 0, 0, 0),
        ((1, 0, 2, 3), 1, 1, 0, 1),
        ((0, 1, 2, 3), 1, 0, 1, 2),
        ((1, 0, 2, 3), 1, 1, 1, 3),
        ((2, 0, 1, 3), 0, 0, 0, 0),
        ((2, 1, 0, 3), 0, 0, 1, 1),
    )
    return [
        Flow(order, core, is_up, layer, part * rows, rows // UNIT, start, 4 * layer + place)
        for order, core, is_up, part, place in kinds
    ]


def bit_of(index, bit):
    return (index // (1 << bit)) % 2


def flip(index, bit):
    return index + (1 << bit) * (1 - 2 * bit_of(index, bit))


def finish_kernel(
    bits, flows,
    kept_weight1, kept_up1, came_weight1, came_up1,
    kept_weight0, kept_up0, sent_weight0, sent_up0,
    bias0_ref, bias1_ref, sums1_ref, sums0_ref,
    weight_sum, up_out, small_out,
    up_sum, up_near, up_came,
    *scratch,
):
    stages = bits
    kept = ((kept_weight1, kept_up1), (kept_weight0, kept_up0))
    moved = ((came_weight1, came_up1), (sent_weight0, sent_up0))
    small_parts = (bias0_ref, bias1_ref, sums1_ref, sums0_ref)
    places = 1 + max(flow.place for flow in flows)
    held, scratch = scratch[: places * (stages + 1)], scratch[places * (stages + 1) :]
    held = [held[f * (stages + 1) : (f + 1) * (stages + 1)] for f in range(places)]
    small, small_came = scratch[: stages + 1], scratch[stages + 1 : 2 * stages + 1]
    load_sem, send_sem, recv_sem, credit, small_send, small_recv, near_send, near_recv = (
        scratch[2 * stages + 1 :]
    )
    me, core = lax.axis_index("batch"), lax.axis_index("stream")

    barrier = pltpu.get_barrier_semaphore()
    for bit in range(bits):
        pl.semaphore_signal(
            barrier, inc=1, device_id={"batch": flip(me, bit)}, device_id_type=MESH
        )
    pl.semaphore_signal(barrier, inc=1, device_id={"stream": 1 - core}, device_id_type=MESH)
    pl.semaphore_wait(barrier, bits + 1)

    small_start = 2
    turn_start = max(flow.start + flow.units for flow in flows if flow.layer == 1)
    turn_start += LAG * stages + 1

    def near_copy(layer):
        return pltpu.make_async_remote_copy(
            src_ref=up_near.at[layer],
            dst_ref=up_came.at[layer],
            send_sem=near_send.at[layer],
            recv_sem=near_recv.at[layer],
            device_id={"stream": 0},
            device_id_type=MESH,
        )

    def part_up(layer):
        @pl.when(core == 1)
        def _():
            up_near[layer] = up_sum[layer, :, : WIDE // 2]
            near_copy(layer).start()
            up_out[layer] = up_sum[layer, :, WIDE // 2 :]

    def small_copy(stage):
        return pltpu.make_async_remote_copy(
            src_ref=small[stage],
            dst_ref=small_came[stage],
            send_sem=small_send.at[stage],
            recv_sem=small_recv.at[stage],
            device_id={"batch": flip(me, stage)},
            device_id_type=MESH,
        )

    def small_step(stage):
        if stage == 0:
            row = 0
            for part in small_parts:
                small[0][row : row + part.shape[0]] = part[...]
                row += part.shape[0]
        else:
            small_copy(stage - 1).wait()
            small[stage][...] = small[stage - 1][...] + small_came[stage - 1][...]
        if stage < stages:
            small_copy(stage).start()
        else:
            small_out[...] = small[stage][...]

    def view(order, stage, mine):
        left = sorted(set(range(bits)) - set(order[:stage]), reverse=True)
        pick = bit_of(me, order[stage])
        pick = pick if mine else 1 - pick
        return tuple(pick if bit == order[stage] else slice(None) for bit in left)

    def remote(flow, stage, slot, source):
        place = flow.place
        return pltpu.make_async_remote_copy(
            src_ref=source,
            dst_ref=held[place][stage + 1].at[slot],
            send_sem=send_sem.at[place, stage, slot],
            recv_sem=recv_sem.at[place, stage, slot],
            device_id={"batch": flip(me, flow.order[stage])},
            device_id_type=MESH,
        )

    def sent_from(flow, stage, slot):
        if stage == 0:
            return held[flow.place][0].at[slot]
        return held[flow.place][stage].at[(slot,) + view(flow.order, stage, False)]

    def load(flow, slot, source):
        place = flow.place
        return pltpu.make_async_copy(source, held[place][0].at[slot], load_sem.at[place, slot])

    def load_came(flow, slot, source):
        return pltpu.make_async_copy(
            source, held[flow.place][1].at[slot], recv_sem.at[flow.place, 0, slot]
        )

    def return_credit(flow, stage, unit):
        if stage == 0 and flow.layer == 0:
            return

        @pl.when(unit + SLOTS < flow.units)
        def _():
            pl.semaphore_signal(
                credit.at[flow.place, stage],
                inc=1,
                device_id={"batch": flip(me, flow.order[stage])},
                device_id_type=MESH,
            )

    def take_credit(flow, stage, unit):
        @pl.when(unit >= SLOTS)
        def _():
            pl.semaphore_wait(credit.at[flow.place, stage], 1)

    def begin(flow, unit):
        slot = lax.rem(unit, SLOTS)
        at = (slice(None),) * (bits - 1)
        at += (pl.ds(pl.multiple_of(flow.row + unit * UNIT, UNIT), UNIT),)
        load(flow, slot, kept[flow.layer][flow.is_up].at[at]).start()
        source = moved[flow.layer][flow.is_up].at[at]
        if flow.layer == 0:
            load_came(flow, slot, source).start()
        else:
            take_credit(flow, 0, unit)
            remote(flow, 0, slot, source).start()

    def advance(flow, stage, unit):
        slot = lax.rem(unit, SLOTS)
        buffers, begun = held[flow.place], flow.layer == 0
        copy = remote(flow, stage - 1, slot, sent_from(flow, stage - 1, slot))
        if stage == 1 and begun:
            load_came(flow, slot, buffers[0].at[slot]).wait()
        else:
            copy.wait_recv()
        if stage == 1:
            load(flow, slot, buffers[1].at[slot]).wait()
            mine = buffers[0][slot]
        else:
            mine = buffers[stage - 1][(slot,) + view(flow.order, stage - 1, True)]
        value = buffers[stage][slot] + mine
        if stage < stages:
            buffers[stage][slot] = value
            take_credit(flow, stage, unit)
            remote(flow, stage, slot, sent_from(flow, stage, slot)).start()
        else:
            target = up_sum if flow.is_up else weight_sum
            at = pl.ds(pl.multiple_of(flow.row + unit * UNIT, UNIT), UNIT)
            target[flow.layer, at] = value
        if stage > 1 or not begun:
            copy.wait_send()
        if stage >= 2:
            return_credit(flow, stage - 2, unit)
        if stage == stages:
            return_credit(flow, stage - 1, unit)

    def within(flow, unit):
        return (unit >= 0) & (unit < flow.units) & (core == flow.core)

    def step(index, carry):
        for flow in flows:
            unit = index - flow.start
            pl.when(within(flow, unit))(functools.partial(begin, flow, unit))
        for stage in range(stages, 0, -1):
            for flow in flows:
                unit = index - flow.start - LAG * stage
                pl.when(within(flow, unit))(functools.partial(advance, flow, stage, unit))
        for stage in range(stages + 1):
            pl.when(index == small_start + 2 * stage)(functools.partial(small_step, stage))
        pl.when(index == turn_start)(functools.partial(part_up, 1))
        return carry

    last = max(flow.start + flow.units for flow in flows)
    lax.fori_loop(0, last + LAG * stages, step, 0)
    part_up(0)
    for layer in range(len(moved)):

        @pl.when(core == 0)
        def _():
            near_copy(layer).wait_recv()
            up_out[layer] = up_came[layer]

        @pl.when(core == 1)
        def _():
            near_copy(layer).wait_send()


def finish(last, first, came, smalls):
    width = last[0].shape[1]
    bits = 4
    split = (2,) * (bits - 1)
    flows = flows_of(width, 1, 0)
    flows += flows_of(width, 0, max(flow.start + flow.units for flow in flows))
    small = (sum(part.shape[0] for part in smalls), width)
    scratch = [
        pltpu.VMEM((2, width, WIDE), F32),
        pltpu.VMEM((2, width, WIDE // 2), F32),
        pltpu.VMEM((2, width, WIDE // 2), F32),
    ]
    places = 1 + max(flow.place for flow in flows)
    for _ in range(places):
        for stage in range(bits + 1):
            lead = (SLOTS,) + (2,) * (bits - 1 - max(stage - 1, 0))
            scratch.append(pltpu.VMEM(lead + (UNIT, WIDE), F32))
    scratch += [pltpu.VMEM(small, F32)] * (2 * bits + 1)
    scratch += [
        pltpu.SemaphoreType.DMA((places, SLOTS)),
        pltpu.SemaphoreType.DMA((places, bits, SLOTS)),
        pltpu.SemaphoreType.DMA((places, bits, SLOTS)),
        pltpu.SemaphoreType.REGULAR((places, bits)),
        pltpu.SemaphoreType.DMA((bits,)),
        pltpu.SemaphoreType.DMA((bits,)),
        pltpu.SemaphoreType.DMA((2,)),
        pltpu.SemaphoreType.DMA((2,)),
    ]
    large = [last[1], last[3], *came, first[1], first[3], first[0], first[2]]
    large = [array.reshape(split + array.shape[1:]) for array in large]
    return pl.pallas_call(
        functools.partial(finish_kernel, bits, flows),
        in_specs=[pl.BlockSpec(memory_space=pltpu.HBM)] * len(large)
        + [pl.BlockSpec(memory_space=pltpu.VMEM)] * len(smalls),
        out_specs=[pl.BlockSpec(memory_space=pltpu.VMEM)] * 3,
        out_shape=[
            jax.ShapeDtypeStruct((2, width, WIDE), F32),
            jax.ShapeDtypeStruct((2, width, WIDE // 2), F32),
            jax.ShapeDtypeStruct(small, F32),
        ],
        scratch_shapes=scratch,
        compiler_params=pltpu.CompilerParams(
            collective_id=0, has_side_effects=True, vmem_limit_bytes=VMEM_LIMIT
        ),
        name="finish",
    )(*large, *smalls)


def hand_out_kernel(
    rows, own, index_ref, weight_ref, up_ref, small_ref,
    weight_out, up_out, bias_out, down_out, gain_out, offset_out,
):
    index = index_ref[0]
    layers = weight_ref.shape[0]
    for layer in range(layers):
        weight_out[layer] = weight_ref[layers - 1 - layer].T
        up_out[layer] = up_ref[layers - 1 - layer].T
        per_row = small_ref.shape[1] // WIDE
        lanes = pl.ds(pl.multiple_of(lax.rem(index, per_row) * WIDE, WIDE), WIDE)
        row = pl.ds(layer * rows + index // per_row, 1)
        bias_out[layer : layer + 1] = small_ref[row, lanes]
        first = 2 * rows + 8 * (layers - 1 - layer)
        width = small_ref.shape[1]
        sums = pltpu.roll(small_ref[first : first + 8], lax.rem(width - index * own, width), 1)
        gain_out[layer : layer + 1] = sums[0:1, :own]
        offset_out[layer : layer + 1] = sums[1:2, :own]
        down_out[layer : layer + 1] = sums[2:3, :own]


def hand_out(weight, up, small, rows, own):
    layers, width, _ = weight.shape
    vector = jax.ShapeDtypeStruct((layers, own), F32)
    return pl.pallas_call(
        functools.partial(hand_out_kernel, rows, own),
        in_specs=[pl.BlockSpec(memory_space=pltpu.SMEM)]
        + [pl.BlockSpec(memory_space=pltpu.VMEM)] * 3,
        out_specs=[pl.BlockSpec(memory_space=pltpu.VMEM)] * 6,
        out_shape=[
            jax.ShapeDtypeStruct((layers, WIDE, width), F32),
            jax.ShapeDtypeStruct((layers, WIDE // 2, width), F32),
            jax.ShapeDtypeStruct((layers, WIDE), F32),
            vector,
            vector,
            vector,
        ],
        compiler_params=params(),
        name="hand_out",
    )(lax.axis_index("batch").astype(jnp.int32).reshape(1), weight, up, small)


def send_first(halves):
    count = lax.axis_size("batch")

    def pairs(stream, bit):
        return [(2 * source + stream, 2 * flip(source, bit) + stream) for source in range(count)]

    axes = ("batch", "stream")
    return [
        lax.ppermute(halves[0], axes, pairs(0, 2) + pairs(1, 0)),
        lax.ppermute(halves[2], axes, pairs(1, 1)),
    ]


def shards(
    tokens, cotangent, branch_weight, branch_bias, up_weight, down_bias,
    norm_gain, norm_bias, freq_seeds, doc_starts,
):
    is_attention = lax.axis_index("stream") == 0
    length, width = tokens.shape
    rotary = tuple(jnp.asarray(table) for table in rotary_rows(length))
    biases = branch_bias[0].astype(F32).reshape(-1, 1, width)
    tables = lax.cond(
        is_attention,
        lambda: tuple(feature_tables(freq_seeds)),
        lambda: (
            jnp.zeros((LAYERS, QUADS, WIDE, WIDE), BF16),
            jnp.zeros((LAYERS, QUADS, WIDE, WIDE), BF16),
            jnp.zeros((LAYERS, QUADS, 1, WIDE), F32),
        ),
    )
    swap = [(0, 1), (1, 0)]

    def attention(layer, stream):
        return tuple(
            attention_forward(
                layer, stream, doc_starts, norm_gain, norm_bias, branch_weight, biases, tables,
                rotary,
            )
        )

    def feed_forward(layer, stream):
        return tuple(
            mlp_forward(
                layer, stream, norm_gain, norm_bias, up_weight, biases, branch_weight, down_bias
            )
        )

    count = lax.axis_size("batch")
    blocked = count == branch_weight.shape[2] // WIDE
    me = lax.axis_index("batch") if blocked else 0
    place = jnp.stack([jnp.asarray(bit_of(me, bit), jnp.int32) for bit in range(3)])

    part, *kept = lax.cond(
        is_attention,
        functools.partial(attention, 0, (tokens,)),
        functools.partial(feed_forward, 0, (tokens,)),
    )
    stream = (tokens, part, lax.ppermute(part, "stream", swap))

    def attention_ends():
        x, part, *back = attention_last(
            1, place, stream, doc_starts, norm_gain, norm_bias, branch_weight, biases, tables,
            rotary, cotangent,
        )
        return x, part, *flat_halves(*back)

    def feed_forward_ends():
        x, part, *back = mlp_last(
            1, place, stream, norm_gain, norm_bias, up_weight, biases, branch_weight, down_bias,
            cotangent,
        )
        return x, part, *flat_halves(*back)

    x1, part, part1, *halves1, bias1 = lax.cond(
        jnp.logical_not(is_attention), feed_forward_ends, attention_ends
    )
    stream = (x1, part, lax.ppermute(part, "stream", swap))

    def attention_back(layer, grad, stream):
        h, state, mixed = kept
        *result, part, a, b, c, d, bias = attention_backward(
            layer, place, doc_starts, grad, h, state, mixed, tables, rotary, branch_weight, stream
        )
        return *result, *flat_halves(part, a, b, c, d, bias)

    def feed_forward_back(layer, grad, stream):
        h, act, slope = kept
        *result, part, a, b, c, d, bias = mlp_backward(
            layer, place, grad, h, act, slope, branch_weight, up_weight, stream
        )
        return *result, *flat_halves(part, a, b, c, d, bias)

    def back(layer, grad, stream=()):
        *result, part, a, b, c, d, bias = lax.cond(
            is_attention,
            functools.partial(attention_back, layer, grad, stream),
            functools.partial(feed_forward_back, layer, grad, stream),
        )
        return *result, part, (a, b, c, d), bias

    def norm_back(layer, x, part, grad, kind):
        other = lax.ppermute(part, "stream", swap)
        return norm_backward(layer, x, part, other, grad, norm_gain, kind)

    if blocked:
        came = send_first(halves1)
    grad0, sums1 = norm_back(1, x1, part1, cotangent, BF16)
    result, part0, halves0, bias0 = back(0, grad0, stream)
    input_grad, sums0 = norm_back(0, tokens, part0, grad0, F32)
    if blocked:
        weight, up, small = finish(halves1, halves0, came, (bias0, bias1, sums1, sums0))
    else:
        weight, up = scatter_rows((halves0, halves1))
        small = lax.psum(jnp.concatenate([bias0, bias1, sums1, sums0]), "batch")
    index, rows = lax.axis_index("batch"), bias0.shape[0]
    each, own = branch_weight.shape[2] // count, width // count
    if blocked:
        weight, up, bias, down, gain, offset = hand_out(weight, up, small, rows, own)
    else:
        bias = lax.dynamic_slice_in_dim(
            small[: 2 * rows].reshape(LAYERS, -1), index * each, each, axis=1
        )
        sums = small[2 * rows :].reshape(LAYERS, 8, width)[::-1]
        sums = lax.dynamic_slice_in_dim(sums, index * own, own, axis=2)
        down, gain, offset = sums[:, 2], sums[:, 0], sums[:, 1]
    return result, input_grad, weight[None], bias[None], up, down, gain, offset


def scatter_rows(layers):
    weights, ups = [], []
    for sent, kept, sent_up, kept_up in layers:
        blocks = (-1,) + kept.shape[1:]
        wide, far = (4, 2) + kept.shape[1:], (2, 4) + kept.shape[1:]
        weight = jnp.where(
            lax.axis_index("stream") == 1,
            jnp.stack([kept.reshape(wide), sent.reshape(wide)], axis=2).reshape(blocks),
            jnp.stack([kept.reshape(far), sent.reshape(far)], axis=1).reshape(blocks),
        )
        weight = rows_of(weight)
        up = jnp.stack([kept_up.reshape(wide), sent_up.reshape(wide)], axis=1)
        up = rows_of(up.reshape(blocks))
        up = jnp.where(lax.axis_index("stream") == 1, up, 0.0)
        weights.append(lax.psum_scatter(weight, "batch", scatter_dimension=0, tiled=True))
        ups.append(lax.psum_scatter(up, ("batch", "stream"), scatter_dimension=0, tiled=True))
    return jnp.stack(weights), jnp.stack(ups)


def rows_of(blocks):
    return jnp.transpose(blocks, (0, 2, 1)).reshape(-1, blocks.shape[1])


def solution(mesh):
    placed = (
        P("batch", None),
        P("batch", None),
        P("stream", None, None, None),
        P("stream", None, None),
        P(),
        P(),
        P(),
        P(),
        P(),
        P("batch", None),
    )
    return jax.shard_map(
        shards,
        mesh=mesh,
        in_specs=placed,
        out_specs=(
            P("batch", None),
            P("batch", None),
            P("stream", None, "batch", None),
            P("stream", None, "batch"),
            P(None, ("batch", "stream"), None),
            P(None, "batch"),
            P(None, "batch"),
            P(None, "batch"),
        ),
        check_vma=False,
    )
```

```python
import functools
import math
from typing import NamedTuple

import jax
import jax.numpy as jnp
import numpy as np
from jax import lax
from jax.experimental import pallas as pl
from jax.experimental.pallas import tpu as pltpu
from jax.sharding import PartitionSpec as P

HEADS = 16
DH = 64
ROT = 16
FEAT = 64
LAYERS = 2
EPSILON = 1e-05
HIGH = lax.Precision.HIGHEST
F32 = jnp.float32
BF16 = jnp.bfloat16
WIDE = 256
PAIR = 128
QUADS = HEADS * DH // WIDE
PAIRS = HEADS * DH // PAIR
ROWS = 256
VMEM_LIMIT = 56 * 1024 * 1024


def params():
    return pltpu.CompilerParams(vmem_limit_bytes=VMEM_LIMIT)


def whole(shape):
    zeros = (0,) * len(shape)
    return pl.BlockSpec(shape, lambda *_: zeros, pipeline_mode=pl.Buffered(1))


def dot_nn(left, right):
    return lax.dot_general(left, right, (((1,), (0,)), ((), ())), preferred_element_type=F32)


def dot_tn(left, right):
    return lax.dot_general(left, right, (((0,), (0,)), ((), ())), preferred_element_type=F32)


def dot_nt(left, right):
    return lax.dot_general(left, right, (((1,), (1,)), ((), ())), preferred_element_type=F32)


def split(values):
    upper = values.astype(BF16)
    return upper, (values - upper.astype(F32)).astype(BF16)


def lane_index(rows, lanes):
    return lax.broadcasted_iota(jnp.int32, (rows, lanes), 1)


def row_index(rows, lanes):
    return lax.broadcasted_iota(jnp.int32, (rows, lanes), 0)


def cosine_block():
    samples = np.arange(DH, dtype=np.float64)
    angles = math.pi * (samples[None, :] + 0.5) * samples[:, None] / DH
    table = np.cos(angles) * math.sqrt(2.0 / DH)
    table[0] *= math.sqrt(0.5)
    return (table.T * DH ** (-0.25)).astype(np.float32)


def rotary_rows(length):
    position = np.arange(length, dtype=np.float32)
    inverse = (10000.0 ** (-np.arange(0, ROT, 2, dtype=np.float32) / ROT)).astype(np.float32)
    angles = position[:, None] * inverse[None, :]
    cosine, sine = np.cos(angles), np.sin(angles)
    rest = DH - ROT
    cosine_head = np.concatenate([cosine, cosine, np.ones((length, rest))], 1)
    sine_head = np.concatenate([-sine, sine, np.zeros((length, rest))], 1)
    repeat = PAIR // DH
    return (
        np.tile(cosine_head, (1, repeat)).astype(np.float32),
        np.tile(sine_head, (1, repeat)).astype(np.float32),
    )


def tables_kernel(seeds_ref, cosine_ref, upper_ref, lower_ref, weight_ref):
    feature = lane_index(DH, WIDE) % FEAT
    same_head = row_index(WIDE, WIDE) // DH == lane_index(WIDE, WIDE) // FEAT
    ones = jnp.where(same_head, 1.0, 0.0).astype(BF16)
    pick = (row_index(QUADS, WIDE) == lane_index(QUADS, WIDE) // FEAT).astype(BF16)
    cosine = cosine_ref[...]
    for group in range(QUADS):
        seeds = seeds_ref[0, group * QUADS : (group + 1) * QUADS].astype(F32).astype(BF16)
        seeds = dot_tn(seeds, pick).astype(jnp.int32)
        lattice = (feature * seeds) & (FEAT - 1)
        prob = (lattice.astype(F32) + 0.5) * (1.0 / FEAT)
        radius = jnp.sqrt(-2.0 * jnp.log(jnp.minimum(prob, 1.0 - prob)))
        above = 2.515517 + 0.802853 * radius + 0.010328 * radius * radius
        below = (
            1.0
            + 1.432788 * radius
            + 0.189269 * radius * radius
            + 0.001308 * radius * radius * radius
        )
        magnitude = radius - above / below
        omega = jnp.where(prob > 0.5, magnitude, -magnitude)
        project = jnp.dot(cosine, omega, precision=HIGH, preferred_element_type=F32)
        project = jnp.concatenate([project] * QUADS, axis=0)
        upper_ref[0, group], lower_ref[0, group] = split(jnp.where(same_head, project, 0.0))
        grown = jnp.exp(-0.5 / DH * jnp.sum(omega * omega, axis=0, keepdims=True))
        upper, rest = split(jnp.broadcast_to(grown, (8, WIDE)))
        total = dot_nn(upper, ones) + dot_nn(rest, ones)
        weight_ref[0, group] = FEAT * grown / total[:1]


def feature_tables(seeds):
    return pl.pallas_call(
        tables_kernel,
        grid=(1,),
        in_specs=[
            pl.BlockSpec((1, HEADS, DH), lambda l: (l, 0, 0)),
            whole((DH, DH)),
        ],
        out_specs=[
            pl.BlockSpec((1, QUADS, WIDE, WIDE), lambda l: (l, 0, 0, 0)),
            pl.BlockSpec((1, QUADS, WIDE, WIDE), lambda l: (l, 0, 0, 0)),
            pl.BlockSpec((1, QUADS, 1, WIDE), lambda l: (l, 0, 0, 0)),
        ],
        out_shape=[
            jax.ShapeDtypeStruct((1, QUADS, WIDE, WIDE), BF16),
            jax.ShapeDtypeStruct((1, QUADS, WIDE, WIDE), BF16),
            jax.ShapeDtypeStruct((1, QUADS, 1, WIDE), F32),
        ],
        compiler_params=params(),
        name="feature_tables",
    )(seeds, jnp.asarray(cosine_block()))


def turn(values, cosine, sine):
    lanes = values.shape[1]
    half = ROT // 2
    lane = lane_index(*values.shape) % DH
    swapped = jnp.where(
        lane < half, pltpu.roll(values, lanes - half, 1), pltpu.roll(values, half, 1)
    )
    return values * cosine + swapped * sine


def turn_back(values, cosine, sine):
    lanes = values.shape[1]
    half = ROT // 2
    lane = lane_index(*values.shape) % DH
    turned = values * sine
    swapped = jnp.where(
        lane < half, pltpu.roll(turned, lanes - half, 1), pltpu.roll(turned, half, 1)
    )
    return values * cosine + jnp.where(lane < ROT, swapped, 0.0)


def normalized(x_ref_rows, gain, offset):
    average = jnp.mean(x_ref_rows, -1, keepdims=True)
    centered = x_ref_rows - average
    variance = jnp.mean(centered * centered, -1, keepdims=True)
    return centered * lax.rsqrt(variance + EPSILON) * gain + offset


def start_layer(stream, x_ref, h_ref, gain_ref, offset_ref):
    length = h_ref.shape[0]
    step = min(256, length)

    @pl.loop(0, length // step)
    def _(index):
        rows = pl.ds(pl.multiple_of(index * step, step), step)
        values = stream[0][rows].astype(F32)
        if len(stream) > 1:
            values = values + (stream[1][rows] + stream[2][rows])
            x_ref[rows] = values
        h_ref[rows] = normalized(
            values, gain_ref[...].astype(F32), offset_ref[...].astype(F32)
        ).astype(BF16)


JOB = 256


def start_last_layer(stream, x_hbm, buffers, loads, stores, h_ref, gain_ref, offset_ref):
    gain, offset = gain_ref[...].astype(F32), offset_ref[...].astype(F32)
    jobs = h_ref.shape[0] // JOB

    def rows_at(index):
        return pl.ds(pl.multiple_of(index * JOB, JOB), JOB)

    def load(part, index):
        rows = rows_at(index)
        return pltpu.make_async_copy(
            stream[part].at[rows], buffers[part].at[rows], loads.at[part, index]
        )

    def store(index):
        rows = rows_at(index)
        return pltpu.make_async_copy(buffers[1].at[rows], x_hbm.at[rows], stores.at[index])

    @pl.loop(0, jobs)
    def _(index):
        for part in range(len(stream)):
            load(part, index).start()

    @pl.loop(0, jobs)
    def _(index):
        rows = rows_at(index)
        for part in range(len(stream)):
            load(part, index).wait()
        values = buffers[0][rows].astype(F32) + (buffers[1][rows] + buffers[2][rows])
        buffers[1][rows] = values
        store(index).start()
        h_ref[rows] = normalized(values, gain, offset).astype(BF16)

    @pl.loop(0, jobs)
    def _(index):
        store(index).wait()


def chunk_semaphores(length):
    return [
        pltpu.SemaphoreType.DMA((3, length // JOB)),
        pltpu.SemaphoreType.DMA((length // JOB,)),
    ]


def gelu_parts(units):
    below = 0.5 + 0.5 * lax.erf(units * math.sqrt(0.5))
    return below, jnp.exp(-0.5 * units * units) * (1.0 / math.sqrt(2.0 * math.pi))


FF_BLOCK = 1024
FF_ROWS = 512


def mlp_forward_kernel(layer, count, *refs):
    stream, refs = refs[:count], refs[count:]
    gain_ref, offset_ref, up_ref, bias_ref, down_ref, down_bias_ref = refs[:6]
    gain_ref, offset_ref, down_bias_ref = [
        ref.at[layer : layer + 1] for ref in (gain_ref, offset_ref, down_bias_ref)
    ]
    refs = refs[6:]
    x_ref = None
    if count > 1:
        x_ref, refs = refs[0], refs[1:]
    part_ref, h_ref, act_ref, slope_ref = refs
    step = pl.program_id(0)

    @pl.when(step == 0)
    def _():
        start_layer(stream, x_ref, h_ref, gain_ref, offset_ref)
        part_ref[...] = jnp.broadcast_to(down_bias_ref[...].astype(F32), part_ref.shape)

    for first in range(0, h_ref.shape[0], FF_ROWS):
        rows = slice(first, first + FF_ROWS)
        units = dot_nt(h_ref[rows], up_ref[0]) + bias_ref[0]
        below, density = gelu_parts(units)
        active = (units * below).astype(BF16)
        act_ref[0, rows] = active
        slope_ref[0, rows] = (below + units * density).astype(BF16)
        part_ref[rows] += dot_nn(active, down_ref[0, 0])


def plane_block(length, lanes):
    per_plane = 1024 // lanes
    return pl.BlockSpec((1, length, lanes), lambda j: (j // per_plane, 0, j % per_plane))


def mlp_forward(layer, stream, gain, offset, up, biases, down_weight, down_bias):
    length, width = stream[0].shape
    hidden = up.shape[1]
    blocks = hidden // FF_BLOCK
    state = jax.ShapeDtypeStruct((4, length, width), BF16)
    full = jax.ShapeDtypeStruct((length, width), F32)
    out_shape = [full, jax.ShapeDtypeStruct((length, width), BF16), state, state]
    out_specs = [whole((length, width)), whole((length, width))]
    out_specs += [plane_block(length, FF_BLOCK)] * 2
    if len(stream) > 1:
        out_shape, out_specs = [full] + out_shape, [whole((length, width))] + out_specs
    return pl.pallas_call(
        functools.partial(mlp_forward_kernel, layer, len(stream)),
        grid=(blocks,),
        in_specs=[whole((length, width))] * len(stream)
        + [
            whole((LAYERS, width)),
            whole((LAYERS, width)),
            pl.BlockSpec((1, FF_BLOCK, width), lambda j: (layer, j, 0)),
            pl.BlockSpec((1, 1, FF_BLOCK), lambda j: (layer * blocks + j, 0, 0)),
            pl.BlockSpec((1, 1, FF_BLOCK, width), lambda j: (0, layer, j, 0)),
            whole((LAYERS, width)),
        ],
        out_specs=out_specs,
        out_shape=out_shape,
        compiler_params=params(),
        name="mlp_forward",
    )(*stream, gain, offset, up, biases, down_weight, down_bias)


def add_stream(stream, result_ref):
    if stream:
        result_ref[...] = stream[0][...] + (stream[1][...] + stream[2][...])


def stream_specs(stream):
    specs = [
        pl.BlockSpec((part.shape[0] // 4, part.shape[1]), lambda j, *_: (j, 0)) for part in stream
    ]
    shapes = [jax.ShapeDtypeStruct(part.shape, F32) for part in stream[:1]]
    return specs, specs[:1], shapes


def mlp_backward_kernel(count, place_ref, *refs):
    stream, refs = refs[:count], refs[count:]
    grad_ref, h_ref, act_ref, slope_ref, down_ref, up_ref = refs[:6]
    result_ref, refs = (refs[6], refs[7:]) if count else (None, refs[6:])
    part_ref, along_x, kept_x, along_y, kept_y, bias_ref = refs[:6]
    grad_t, h_t, units = refs[6:]
    step = pl.program_id(0)
    add_stream(stream, result_ref)

    @pl.when(step == 0)
    def _():
        grad_t[...] = grad_ref[...].T
        h_t[...] = h_ref[...].T
        part_ref[...] = jnp.zeros_like(part_ref)

    bias = jnp.zeros((1, FF_BLOCK), F32)
    for first in range(0, h_ref.shape[0], ROWS):
        rows = slice(first, first + ROWS)
        grad_act = dot_nt(grad_ref[rows], down_ref[0, 0])
        grad_unit = (grad_act * slope_ref[0, rows].astype(F32)).astype(BF16)
        bias += jnp.sum(grad_unit.astype(F32), axis=0, keepdims=True)
        units[rows] = grad_unit
        part_ref[rows] += dot_nn(grad_unit, up_ref[0])
    bias_ref[pl.ds(step, 1)] = bias

    mlp_weights(
        place_ref, grad_t, h_t, act_ref.at[0], units, along_x, kept_x, along_y, kept_y
    )


def mlp_weights(place_ref, grad_t, h_t, act, units, along_x, kept_x, along_y, kept_y):
    def block(y, x):
        return pl.ds(pl.multiple_of((2 * y + x) * WIDE, WIDE), WIDE)

    near_x, near_y = place_ref[0], place_ref[1]

    @pl.loop(0, h_t.shape[0] // ROWS)
    def _(index):
        rows = pl.ds(pl.multiple_of(index * ROWS, ROWS), ROWS)

        @pl.loop(0, 2)
        def _(side):
            for target, x in ((along_x, 1 - near_x), (kept_x, near_x)):
                target[0, side, rows] = dot_nn(grad_t[rows], act[:, block(side, x)])
            for target, y in ((along_y, 1 - near_y), (kept_y, near_y)):
                target[0, side, rows] = dot_nn(h_t[rows], units[:, block(y, side)])


def mlp_last_kernel(layer, place_ref, *refs):
    stream, refs = refs[:3], refs[3:]
    gain_ref, offset_ref, up_ref, bias_ref, down_ref, down_bias_ref, grad_ref = refs[:7]
    gain_ref, offset_ref, down_bias_ref = [
        ref.at[layer : layer + 1] for ref in (gain_ref, offset_ref, down_bias_ref)
    ]
    x_hbm, part_ref, grad_part, along_x, kept_x, along_y, kept_y, bias_out = refs[7:15]
    h_ref, grad_t, h_t, act, units, loads, stores = refs[15:]
    step = pl.program_id(0)

    @pl.when(step == 0)
    def _():
        buffers = (act, part_ref, grad_part)
        start_last_layer(stream, x_hbm, buffers, loads, stores, h_ref, gain_ref, offset_ref)
        part_ref[...] = jnp.broadcast_to(down_bias_ref[...].astype(F32), part_ref.shape)
        grad_part[...] = jnp.zeros_like(grad_part)
        grad_t[...] = grad_ref[...].T
        h_t[...] = h_ref[...].T

    here = pl.ds(step, 1)
    bias_out[here] = jnp.zeros((1, FF_BLOCK), F32)

    @pl.loop(0, h_ref.shape[0] // ROWS)
    def _(index):
        rows = pl.ds(pl.multiple_of(index * ROWS, ROWS), ROWS)
        hidden = dot_nt(h_ref[rows], up_ref[0]) + bias_ref[0]
        below, density = gelu_parts(hidden)
        active = (hidden * below).astype(BF16)
        act[rows] = active
        part_ref[rows] += dot_nn(active, down_ref[0, 0])
        grad_act = dot_nt(grad_ref[rows], down_ref[0, 0])
        grad_unit = (grad_act * (below + hidden * density)).astype(BF16)
        bias_out[here] += jnp.sum(grad_unit.astype(F32), axis=0, keepdims=True)
        units[rows] = grad_unit
        grad_part[rows] += dot_nn(grad_unit, up_ref[0])
    mlp_weights(place_ref, grad_t, h_t, act, units, along_x, kept_x, along_y, kept_y)


def mlp_last(layer, place, stream, gain, offset, up, biases, down_weight, down_bias, grad):
    length, width = stream[0].shape
    blocks = up.shape[1] // FF_BLOCK
    full = jax.ShapeDtypeStruct((length, width), F32)
    pair = pl.BlockSpec((1, 2, width, WIDE), lambda j, *_: (j, 0, 0, 0))
    return pl.pallas_call(
        functools.partial(mlp_last_kernel, layer),
        grid_spec=pltpu.PrefetchScalarGridSpec(
            num_scalar_prefetch=1,
            grid=(blocks,),
            in_specs=[pl.BlockSpec(memory_space=pltpu.HBM)] * 3
            + [
                whole((LAYERS, width)),
                whole((LAYERS, width)),
                pl.BlockSpec((1, FF_BLOCK, width), lambda j, *_: (layer, j, 0)),
                pl.BlockSpec((1, 1, FF_BLOCK), lambda j, *_: (layer * blocks + j, 0, 0)),
                pl.BlockSpec((1, 1, FF_BLOCK, width), lambda j, *_: (0, layer, j, 0)),
                whole((LAYERS, width)),
                whole((length, width)),
            ],
            out_specs=[pl.BlockSpec(memory_space=pltpu.HBM)]
            + [whole((length, width))] * 2
            + [pair] * 4
            + [whole((blocks, FF_BLOCK))],
            scratch_shapes=[
                pltpu.VMEM((length, width), BF16),
                pltpu.VMEM((width, length), BF16),
                pltpu.VMEM((width, length), BF16),
                pltpu.VMEM((length, FF_BLOCK), BF16),
                pltpu.VMEM((length, FF_BLOCK), BF16),
            ]
            + chunk_semaphores(length),
        ),
        out_shape=[full, full, full]
        + halves_of(width, (4, 2, width, WIDE))
        + [jax.ShapeDtypeStruct((blocks, FF_BLOCK), F32)],
        compiler_params=params(),
        name="mlp_last",
    )(place, *stream, gain, offset, up, biases, down_weight, down_bias, grad)


def halves_of(width, weight):
    shapes = (weight,) * 2 + ((4, 2, width, WIDE),) * 2
    return [jax.ShapeDtypeStruct(shape, F32) for shape in shapes]


def flat_halves(part, sent, kept, sent_up, kept_up, bias):
    halves = [half.reshape((-1,) + half.shape[2:]) for half in (sent, kept, sent_up, kept_up)]
    return (part, *halves, bias)


def mlp_backward(layer, place, grad, h, act, slope, down_weight, up, stream=()):
    length, width = h.shape
    hidden = up.shape[1]
    blocks = hidden // FF_BLOCK
    pair = pl.BlockSpec((1, 2, width, WIDE), lambda j, *_: (j, 0, 0, 0))
    plane = pl.BlockSpec((1, length, FF_BLOCK), lambda j, *_: (j, 0, 0))
    stream_in, stream_out, stream_shape = stream_specs(stream)
    return pl.pallas_call(
        functools.partial(mlp_backward_kernel, len(stream)),
        grid_spec=pltpu.PrefetchScalarGridSpec(
            num_scalar_prefetch=1,
            grid=(blocks,),
            in_specs=stream_in
            + [
                whole((length, width)),
                whole((length, width)),
                plane,
                plane,
                pl.BlockSpec((1, 1, FF_BLOCK, width), lambda j, *_: (0, layer, j, 0)),
                pl.BlockSpec((1, FF_BLOCK, width), lambda j, *_: (layer, j, 0)),
            ],
            out_specs=stream_out
            + [whole((length, width))]
            + [pair] * 4
            + [whole((blocks, FF_BLOCK))],
            scratch_shapes=[
                pltpu.VMEM((width, length), BF16),
                pltpu.VMEM((width, length), BF16),
                pltpu.VMEM((length, FF_BLOCK), BF16),
            ],
        ),
        out_shape=stream_shape
        + [jax.ShapeDtypeStruct((length, width), F32)]
        + halves_of(width, (4, 2, width, WIDE))
        + [jax.ShapeDtypeStruct((blocks, FF_BLOCK), F32)],
        compiler_params=params(),
        name="mlp_backward",
    )(place, *stream, grad, h, act, slope, down_weight, up)


def head_sums(values, ones):
    upper, lower = split(values)
    return dot_nn(upper, ones) + dot_nn(lower, ones)


def same_head_ones():
    same = row_index(WIDE, WIDE) // DH == lane_index(WIDE, WIDE) // DH
    return jnp.where(same, 1.0, 0.0).astype(BF16)


def document_of(starts_ref, positions):
    return sum((starts_ref[0, i] <= positions).astype(jnp.int32) for i in range(starts_ref.shape[1]))


def write_mask(starts_ref, mask_ref, flipped):
    for first in range(0, mask_ref.shape[0], ROWS):
        lanes = lane_index(1, ROWS) + first
        own = row_index(ROWS, 1) + first
        order = (own <= lanes) if flipped else (lanes <= own)
        seen = (document_of(starts_ref, own) == document_of(starts_ref, lanes)) & order
        mask_ref[first : first + ROWS] = jnp.where(seen, 1.0, 0.0).astype(BF16)


def document_edges(starts_ref, length):
    edges = []
    for first in range(0, length, ROWS):
        rows = document_of(starts_ref, row_index(ROWS, 1) + first)
        here = document_of(starts_ref, first)
        later = document_of(starts_ref, first + ROWS)
        edges.append((rows == here, rows == later, here == later))
    return edges


def wide_rotary(cosine_ref, sine_ref, rows):
    return tuple(
        jnp.concatenate([ref[rows]] * (WIDE // PAIR), axis=1) for ref in (cosine_ref, sine_ref)
    )


def attend_heads(
    first_bias, starts_ref, weight_ref, bias_ref, upper_ref, lower_ref, scale_ref, cosine_ref,
    sine_ref, part_ref, h_ref, state_ref, mixed_ref, mask_ref,
):
    length = h_ref.shape[0]
    ones = same_head_ones()
    table_up, table_low = upper_ref[0, 0], lower_ref[0, 0]
    lanes_of_step = pl.ds(pl.multiple_of(pl.program_id(0) * WIDE, WIDE), WIDE)

    def features(values, rows):
        upper, lower = split(turn(values, *wide_rotary(cosine_ref, sine_ref, rows)))
        return dot_nn(upper, table_up) + (dot_nn(lower, table_up) + dot_nn(upper, table_low))

    for first in range(0, length, ROWS):
        rows = slice(first, first + ROWS)
        queries, keys, values = [
            dot_nt(h_ref[rows], weight_ref[0, 0, kind, 0])
            + bias_ref[first_bias + kind, :, lanes_of_step]
            for kind in range(3)
        ]
        state_ref[0, rows] = jnp.exp(features(queries, rows)).astype(BF16)
        logs = features(keys, rows) - (0.5 / math.sqrt(DH)) * head_sums(keys * keys, ones)
        state_ref[1, rows] = (scale_ref[0, 0] * jnp.exp(logs)).astype(BF16)
        state_ref[2, rows] = keys.astype(BF16)
        state_ref[3, rows] = values.astype(BF16)

    zero = jnp.zeros((), BF16)
    one = jnp.ones((), BF16)
    left = lane_index(ROWS, PAIR) < DH
    row, lane = row_index(PAIR, 2 * PAIR), lane_index(PAIR, 2 * PAIR)
    same = row // DH == lane // PAIR
    edges = document_edges(starts_ref, length)
    for pair in range(WIDE // PAIR):
        lanes = slice(pair * PAIR, (pair + 1) * PAIR)
        before = None
        for block, (same_first, same_next, goes_on) in enumerate(edges):
            rows = slice(block * ROWS, (block + 1) * ROWS)
            seen = mask_ref[rows] > zero
            queries, keys = state_ref[0, rows, lanes], state_ref[1, rows, lanes]
            values = [jnp.where(own, state_ref[3, rows, lanes], one) for own in (left, ~left)]
            if block > 0:
                earlier = dot_nn(queries, before.astype(BF16))
                earlier = jnp.where(same_first, earlier, 0.0)
            sums = []
            for head, own in enumerate((left, ~left)):
                scores = dot_nt(queries, jnp.where(own, keys, zero)).astype(BF16)
                total = dot_nn(jnp.where(seen, scores, zero), values[head])
                if block > 0:
                    total = total + earlier[:, head * PAIR : (head + 1) * PAIR]
                sums.append(total)
            if block + 1 < len(edges):
                kept = jnp.where(same_next, keys, zero)
                added = jnp.where(same, dot_tn(kept, jnp.concatenate(values, axis=1)), 0.0)
                if block > 0:
                    added = added + jnp.where(goes_on, before, 0.0)
                before = added
            numer = jnp.where(left, sums[0], sums[1])
            denom = jnp.where(left, pltpu.roll(sums[0], DH, 1), pltpu.roll(sums[1], DH, 1))
            inverse = 1.0 / denom
            mixed_ref[0, rows, lanes] = (numer * inverse).astype(BF16)
            mixed_ref[1, rows, lanes], mixed_ref[2, rows, lanes] = split(inverse)
    for first in range(0, length, ROWS):
        rows = slice(first, first + ROWS)
        part_ref[rows] += dot_nn(mixed_ref[0, rows], weight_ref[0, 0, 3, 0])


def attention_forward_kernel(layer, count, *refs):
    stream, refs = refs[:count], refs[count:]
    starts_ref, gain_ref, offset_ref, weight_ref, bias_ref = refs[:5]
    gain_ref, offset_ref = [ref.at[layer : layer + 1] for ref in (gain_ref, offset_ref)]
    first_bias = layer * (bias_ref.shape[0] // LAYERS)
    upper_ref, lower_ref, scale_ref, cosine_ref, sine_ref = refs[5:10]
    refs = refs[10:]
    x_ref = None
    if count > 1:
        x_ref, refs = refs[0], refs[1:]
    part_ref, h_ref, state_ref, mixed_ref, mask_ref = refs

    @pl.when(pl.program_id(0) == 0)
    def _():
        start_layer(stream, x_ref, h_ref, gain_ref, offset_ref)
        write_mask(starts_ref, mask_ref, False)
        part_ref[...] = jnp.broadcast_to(bias_ref[first_bias + 3], part_ref.shape)

    attend_heads(
        first_bias, starts_ref, weight_ref, bias_ref, upper_ref, lower_ref, scale_ref, cosine_ref,
        sine_ref, part_ref, h_ref, state_ref, mixed_ref, mask_ref,
    )


def kinds_of(weight):
    return weight.reshape(weight.shape[:2] + (4, QUADS, WIDE, weight.shape[3]))


def attention_forward(layer, stream, starts, gain, offset, weight, biases, tables, rotary):
    length, width = stream[0].shape
    full = jax.ShapeDtypeStruct((length, width), F32)
    state = jax.ShapeDtypeStruct((4, length, width), BF16)
    out_shape = [full, jax.ShapeDtypeStruct((length, width), BF16), state, state]
    four = pl.BlockSpec((4, length, WIDE), lambda g: (0, 0, g))
    out_specs = [whole((length, width)), whole((length, width)), four, four]
    if len(stream) > 1:
        out_shape, out_specs = [full] + out_shape, [whole((length, width))] + out_specs
    return pl.pallas_call(
        functools.partial(attention_forward_kernel, layer, len(stream)),
        grid=(QUADS,),
        in_specs=[whole((length, width))] * len(stream)
        + [
            pl.BlockSpec(memory_space=pltpu.SMEM),
            whole((LAYERS, width)),
            whole((LAYERS, width)),
            pl.BlockSpec((1, 1, 4, 1, WIDE, width), lambda g: (0, layer, 0, g, 0, 0)),
            whole((LAYERS * 4, 1, width)),
            pl.BlockSpec((1, 1, WIDE, WIDE), lambda g: (layer, g, 0, 0)),
            pl.BlockSpec((1, 1, WIDE, WIDE), lambda g: (layer, g, 0, 0)),
            pl.BlockSpec((1, 1, 1, WIDE), lambda g: (layer, g, 0, 0)),
            whole((length, PAIR)),
            whole((length, PAIR)),
        ],
        out_specs=out_specs,
        out_shape=out_shape,
        scratch_shapes=[pltpu.VMEM((length, ROWS), BF16)],
        compiler_params=params(),
        name="attention_forward",
    )(
        *stream, starts, gain, offset, kinds_of(weight),
        biases, *tables, *rotary,
    )


def attend_heads_back(
    place_ref, starts_ref, grad_ref, state_ref, mixed_ref, table_ref, cosine_ref, sine_ref,
    weight_ref, part_ref, along_z, kept_z, bias_ref, mask_ref, upright, numer_ref, feat_ref, flow,
    mixed_grad=None,
):
    group = pl.program_id(0)
    length, width = grad_ref.shape
    row, lane = row_index(WIDE, WIDE), lane_index(WIDE, WIDE)
    partner = (row // PAIR == lane // PAIR) & (row // DH != lane // DH)
    partner = jnp.where(partner, 1.0, 0.0).astype(BF16)
    zero = jnp.zeros((), BF16)
    one = jnp.ones((), BF16)
    for first in range(0, length, ROWS):
        rows = slice(first, first + ROWS)
        if mixed_grad is None:
            grad = dot_nt(grad_ref[rows], weight_ref[0, 0, 3, 0]).astype(BF16).astype(F32)
        else:
            grad = mixed_grad[rows].astype(F32)
        inverse = mixed_ref[1, rows].astype(F32) + mixed_ref[2, rows].astype(F32)
        scaled = grad * inverse
        upper, lower = split(-head_sums(scaled * mixed_ref[0, rows].astype(F32), partner))
        numer = scaled.astype(BF16)
        lane = lane_index(ROWS, WIDE)
        spare = jnp.where(lane % DH == 0, upper, jnp.where(lane % DH == 1, lower, zero))
        left = lane % PAIR < DH
        numer_ref[0, rows] = jnp.where(left, numer, spare)
        numer_ref[1, rows] = jnp.where(left, spare, numer)

    left = lane_index(ROWS, PAIR) < DH
    spare = jnp.where(lane_index(ROWS, PAIR) % DH < 2, one, zero)
    row, lane = row_index(2 * PAIR, PAIR), lane_index(2 * PAIR, PAIR)
    same = row // PAIR == lane // DH
    row, lane = row_index(PAIR, PAIR), lane_index(PAIR, PAIR)
    same_head = row // DH == lane // DH
    edges = document_edges(starts_ref, length)
    blocks = range(len(edges))

    def both(upper_and_lower, sums):
        upper, lower = split(sums)
        return dot_nn(upper_and_lower, upper) + dot_nn(upper_and_lower, lower)

    for pair in range(WIDE // PAIR):
        lanes = slice(pair * PAIR, (pair + 1) * PAIR)

        def rows_of_block(block):
            rows = slice(block * ROWS, (block + 1) * ROWS)
            numers = [numer_ref[head, rows, lanes] for head in range(2)]
            values = state_ref[3, rows, lanes]
            values = [jnp.where(own, values, spare) for own in (left, ~left)]
            return rows, state_ref[0, rows, lanes], state_ref[1, rows, lanes], values, numers

        before, after = {}, {}
        for block in blocks[1:]:
            rows, queries, keys, values, numers = rows_of_block(block - 1)
            _, same_next, goes_on = edges[block - 1]
            kept = jnp.where(same_next, keys, zero)
            added = jnp.where(same, dot_tn(jnp.concatenate(values, axis=1), kept), 0.0)
            if block > 1:
                added = added + jnp.where(goes_on, before[block - 1], 0.0)
            before[block] = added
        for block in blocks[::-1][:-1]:
            rows, queries, keys, values, numers = rows_of_block(block)
            same_first, _, goes_on = edges[block]
            kept = jnp.where(same_first, queries, zero)
            keys_sum = jnp.where(same, dot_tn(jnp.concatenate(numers, axis=1), kept), 0.0)
            values_sum = dot_tn(kept, jnp.where(left, numers[0], numers[1]))
            values_sum = jnp.where(same_head, values_sum, 0.0)
            if block + 1 < len(edges):
                keys_sum = keys_sum + jnp.where(goes_on, after[block + 1][0], 0.0)
                values_sum = values_sum + jnp.where(goes_on, after[block + 1][1], 0.0)
            after[block] = (keys_sum, values_sum)
        for block in blocks:
            rows, queries, keys, values, numers = rows_of_block(block)
            same_first, same_next, _ = edges[block]
            seen = mask_ref[rows] > zero
            numer = jnp.where(left, numers[0], numers[1])
            grads = []
            grad_query = None
            for head, own in enumerate((left, ~left)):
                own_keys = jnp.where(own, keys, zero)
                scores = dot_nt(own_keys, queries).astype(BF16)
                grad_value = dot_nn(jnp.where(seen, scores, zero), numer)
                grad_scores = dot_nt(values[head], numers[head]).astype(BF16)
                grad_scores = jnp.where(seen, grad_scores, zero)
                grads.append((grad_value, dot_nn(grad_scores, queries)))
                from_head = dot_tn(grad_scores, own_keys)
                grad_query = from_head if head == 0 else grad_query + from_head
            grad_value = jnp.where(left, grads[0][0], grads[1][0])
            grad_key = jnp.where(left, grads[0][1], grads[1][1])
            if block + 1 < len(edges):
                keys_sum, values_sum = after[block + 1]
                late = both(jnp.concatenate(values, axis=1), keys_sum)
                grad_key = grad_key + jnp.where(same_next, late, 0.0)
                late = dot_nn(keys, values_sum.astype(BF16))
                grad_value = grad_value + jnp.where(same_next, late, 0.0)
            if block > 0:
                early = both(jnp.concatenate(numers, axis=1), before[block])
                grad_query = grad_query + jnp.where(same_first, early, 0.0)
            flow[2, rows, lanes] = grad_value.astype(BF16)
            feat_ref[1, rows, lanes] = (grad_key * keys.astype(F32)).astype(BF16)
            feat_ref[0, rows, lanes] = (grad_query * queries.astype(F32)).astype(BF16)

    ones = same_head_ones()
    table = table_ref[0, 0]
    sums = [jnp.zeros((1, WIDE), F32)] * 3
    for first in range(0, length, ROWS):
        rows = slice(first, first + ROWS)
        cosine, sine = wide_rotary(cosine_ref, sine_ref, rows)
        flow[0, rows] = turn_back(dot_nt(feat_ref[0, rows], table), cosine, sine).astype(BF16)
        shrink = dot_nn(feat_ref[1, rows], ones) * (1.0 / math.sqrt(DH))
        turned = turn_back(dot_nt(feat_ref[1, rows], table), cosine, sine)
        flow[1, rows] = (turned - state_ref[2, rows].astype(F32) * shrink).astype(BF16)
        total = part_ref[rows]
        for kind in range(3):
            block = flow[kind, rows]
            sums[kind] = sums[kind] + jnp.sum(block.astype(F32), axis=0, keepdims=True)
            total = total + dot_nn(block, weight_ref[0, 0, kind, 0])
        part_ref[rows] = total
    for kind in range(3):
        bias_ref[kind : kind + 1] = sums[kind]
    lanes = pl.ds(pl.multiple_of(group * WIDE, WIDE), WIDE)
    bias_ref[3:4] = jnp.sum(grad_ref[:, lanes].astype(F32), axis=0, keepdims=True)
    flow[3] = mixed_ref[0]
    for first in range(0, width, ROWS):
        rows = slice(first, first + ROWS)
        for far in range(2):
            for target, near in ((along_z, 1 - place_ref[2]), (kept_z, place_ref[2])):
                kind = 2 * far + near
                target[far, 0, rows] = dot_nn(upright[kind // 3, rows], flow[kind])


def attention_backward_kernel(count, place_ref, *refs):
    stream, refs = refs[:count], refs[count:]
    starts_ref, grad_ref, h_ref, state_ref, mixed_ref, table_ref = refs[:6]
    cosine_ref, sine_ref, weight_ref = refs[6:9]
    result_ref, refs = (refs[9], refs[10:]) if count else (None, refs[9:])
    part_ref, along_z, kept_z, _, _, bias_ref = refs[:6]
    mask_ref, upright, numer_ref, feat_ref, flow = refs[6:]
    add_stream(stream, result_ref)

    @pl.when(pl.program_id(0) == 0)
    def _():
        write_mask(starts_ref, mask_ref, True)
        upright[0] = h_ref[...].T
        upright[1] = grad_ref[...].T
        part_ref[...] = jnp.zeros_like(part_ref)

    attend_heads_back(
        place_ref, starts_ref, grad_ref, state_ref, mixed_ref, table_ref, cosine_ref, sine_ref,
        weight_ref, part_ref, along_z, kept_z, bias_ref, mask_ref, upright, numer_ref, feat_ref,
        flow,
    )


def attention_backward(
    layer, place, starts, grad, h, state, mixed, tables, rotary, weight, stream=()
):
    _, length, width = state.shape
    four = pl.BlockSpec((4, length, WIDE), lambda g, *_: (0, 0, g))
    halves = pl.BlockSpec((2, 1, width, WIDE), lambda g, *_: (0, g, 0, 0))
    stream_in, stream_out, stream_shape = stream_specs(stream)
    return pl.pallas_call(
        functools.partial(attention_backward_kernel, len(stream)),
        grid_spec=pltpu.PrefetchScalarGridSpec(
            num_scalar_prefetch=1,
            grid=(QUADS,),
            in_specs=stream_in
            + [
                pl.BlockSpec(memory_space=pltpu.SMEM),
                whole((length, width)),
                whole((length, width)),
                four,
                four,
                pl.BlockSpec((1, 1, WIDE, WIDE), lambda g, *_: (layer, g, 0, 0)),
                whole((length, PAIR)),
                whole((length, PAIR)),
                pl.BlockSpec((1, 1, 4, 1, WIDE, width), lambda g, *_: (0, layer, 0, g, 0, 0)),
            ],
            out_specs=stream_out
            + [whole((length, width))]
            + [halves, halves]
            + [pl.BlockSpec(memory_space=pl.ANY)] * 2
            + [pl.BlockSpec((4, WIDE), lambda g, *_: (0, g))],
            scratch_shapes=[
                pltpu.VMEM((length, ROWS), BF16),
                pltpu.VMEM((2, width, length), BF16),
                pltpu.VMEM((2, length, WIDE), BF16),
                pltpu.VMEM((2, length, WIDE), BF16),
                pltpu.VMEM((4, length, WIDE), BF16),
            ],
        ),
        out_shape=stream_shape
        + [jax.ShapeDtypeStruct((length, width), F32)]
        + halves_of(width, (2, 4, width, WIDE))
        + [jax.ShapeDtypeStruct((4, width), F32)],
        compiler_params=params(),
        name="attention_backward",
    )(place, *stream, starts, grad, h, state, mixed, tables[0], *rotary, kinds_of(weight))


def attention_last_kernel(layer, place_ref, *refs):
    stream, refs = refs[:3], refs[3:]
    starts_ref, gain_ref, offset_ref, weight_ref, bias_ref = refs[:5]
    gain_ref, offset_ref = [ref.at[layer : layer + 1] for ref in (gain_ref, offset_ref)]
    first_bias = layer * (bias_ref.shape[0] // LAYERS)
    upper_ref, lower_ref, scale_ref, cosine_ref, sine_ref, grad_ref = refs[5:11]
    mixed_grad, grad_t = refs[11:13]
    x_hbm, part_ref, grad_part, along_z, kept_z, _, _, bias_out = refs[13:21]
    h_ref, state_ref, mixed_ref, mask_ref, mask_back = refs[21:26]
    upright, numer_ref, feat_ref, flow, turned, loads, stores = refs[26:]

    @pl.when(pl.program_id(0) == 0)
    def _():
        buffers = (upright.at[0], part_ref, grad_part)
        copy = pltpu.make_async_copy(grad_t, upright.at[1], turned)
        copy.start()
        start_last_layer(stream, x_hbm, buffers, loads, stores, h_ref, gain_ref, offset_ref)
        write_mask(starts_ref, mask_ref, False)
        write_mask(starts_ref, mask_back, True)
        part_ref[...] = jnp.broadcast_to(bias_ref[first_bias + 3], part_ref.shape)
        grad_part[...] = jnp.zeros_like(grad_part)
        upright[0] = h_ref[...].T
        copy.wait()

    attend_heads(
        first_bias, starts_ref, weight_ref, bias_ref, upper_ref, lower_ref, scale_ref, cosine_ref,
        sine_ref, part_ref, h_ref, state_ref, mixed_ref, mask_ref,
    )
    attend_heads_back(
        place_ref, starts_ref, grad_ref, state_ref, mixed_ref, upper_ref, cosine_ref, sine_ref,
        weight_ref, grad_part, along_z, kept_z, bias_out, mask_back, upright, numer_ref, feat_ref,
        flow, mixed_grad,
    )


def attention_last(
    layer, place, stream, starts, gain, offset, weight, biases, tables, rotary, grad, mixed_grad,
    grad_t,
):
    length, width = stream[0].shape
    full = jax.ShapeDtypeStruct((length, width), F32)
    halves = pl.BlockSpec((2, 1, width, WIDE), lambda g, *_: (0, g, 0, 0))
    return pl.pallas_call(
        functools.partial(attention_last_kernel, layer),
        grid_spec=pltpu.PrefetchScalarGridSpec(
            num_scalar_prefetch=1,
            grid=(QUADS,),
            in_specs=[pl.BlockSpec(memory_space=pltpu.HBM)] * 3
            + [
                pl.BlockSpec(memory_space=pltpu.SMEM),
                whole((LAYERS, width)),
                whole((LAYERS, width)),
                pl.BlockSpec((1, 1, 4, 1, WIDE, width), lambda g, *_: (0, layer, 0, g, 0, 0)),
                whole((LAYERS * 4, 1, width)),
                pl.BlockSpec((1, 1, WIDE, WIDE), lambda g, *_: (0, g, 0, 0)),
                pl.BlockSpec((1, 1, WIDE, WIDE), lambda g, *_: (0, g, 0, 0)),
                pl.BlockSpec((1, 1, 1, WIDE), lambda g, *_: (0, g, 0, 0)),
                whole((length, PAIR)),
                whole((length, PAIR)),
                whole((length, width)),
                pl.BlockSpec((length, WIDE), lambda g, *_: (0, g)),
                pl.BlockSpec(memory_space=pltpu.HBM),
            ],
            out_specs=[pl.BlockSpec(memory_space=pltpu.HBM)]
            + [whole((length, width))] * 2
            + [halves, halves]
            + [pl.BlockSpec(memory_space=pl.ANY)] * 2
            + [pl.BlockSpec((4, WIDE), lambda g, *_: (0, g))],
            scratch_shapes=[
                pltpu.VMEM((length, width), BF16),
                pltpu.VMEM((4, length, WIDE), BF16),
                pltpu.VMEM((3, length, WIDE), BF16),
                pltpu.VMEM((length, ROWS), BF16),
                pltpu.VMEM((length, ROWS), BF16),
                pltpu.VMEM((2, width, length), BF16),
                pltpu.VMEM((2, length, WIDE), BF16),
                pltpu.VMEM((2, length, WIDE), BF16),
                pltpu.VMEM((4, length, WIDE), BF16),
                pltpu.SemaphoreType.DMA,
            ]
            + chunk_semaphores(length),
        ),
        out_shape=[full, full, full]
        + halves_of(width, (2, 4, width, WIDE))
        + [jax.ShapeDtypeStruct((4, width), F32)],
        compiler_params=params(),
        name="attention_last",
    )(
        place, *stream, starts, gain, offset, kinds_of(weight), biases, *tables, *rotary, grad,
        mixed_grad, grad_t,
    )


def unread(shapes):
    def kernel(*refs):
        del refs

    return tuple(
        pl.pallas_call(
            kernel,
            out_specs=[pl.BlockSpec(memory_space=pl.ANY)] * len(shapes),
            out_shape=list(shapes),
            name="unread",
        )()
    )


def prepare_kernel(part_ref, grad_ref, weight_ref, mixed_grad, grad_t):
    del part_ref
    mixed_grad[...] = dot_nt(grad_ref[...], weight_ref[0, 0]).astype(BF16)

    @pl.when(pl.program_id(0) == 0)
    def _():
        grad_t[...] = grad_ref[...].T


def prepare(layer, part, grad, weight):
    length, width = grad.shape
    lanes = width // 2
    return pl.pallas_call(
        prepare_kernel,
        grid=(width // lanes,),
        in_specs=[
            pl.BlockSpec(memory_space=pltpu.HBM),
            whole((length, width)),
            pl.BlockSpec((1, 1, lanes, width), lambda j: (0, layer, 6 + j, 0)),
        ],
        out_specs=[pl.BlockSpec((length, lanes), lambda j: (0, j)), whole((width, length))],
        out_shape=[
            jax.ShapeDtypeStruct((length, width), BF16),
            jax.ShapeDtypeStruct((width, length), BF16),
        ],
        compiler_params=params(),
        name="prepare",
    )(part, grad, weight)


def norm_gradient(values, incoming, grad, gain, sums_ref):
    average = jnp.mean(values, -1, keepdims=True)
    centered = values - average
    variance = jnp.mean(centered * centered, -1, keepdims=True)
    inverse = lax.rsqrt(variance + EPSILON)
    unit = centered * inverse
    grad_unit = incoming * gain
    first = jnp.mean(grad_unit, -1, keepdims=True)
    second = jnp.mean(grad_unit * unit, -1, keepdims=True)
    sums_ref[0:1] += jnp.sum(incoming * unit, axis=0, keepdims=True)
    sums_ref[1:2] += jnp.sum(incoming, axis=0, keepdims=True)
    sums_ref[2:3] += jnp.sum(grad, axis=0, keepdims=True)
    return grad + inverse * (grad_unit - first - unit * second)


def norm_backward_kernel(layer, x_ref, own_ref, other_ref, grad_ref, gain_ref, out_ref, sums_ref):
    @pl.when(pl.program_id(0) == 0)
    def _():
        sums_ref[...] = jnp.zeros_like(sums_ref)

    out = norm_gradient(
        x_ref[...].astype(F32),
        own_ref[...] + other_ref[...],
        grad_ref[...].astype(F32),
        gain_ref[layer : layer + 1].astype(F32),
        sums_ref,
    )
    out_ref[...] = out.astype(out_ref.dtype)


def norm_backward(layer, x, own, other, grad, gain, kind):
    length, width = own.shape
    block = pl.BlockSpec((ROWS, width), lambda i: (i, 0))
    return pl.pallas_call(
        functools.partial(norm_backward_kernel, layer),
        grid=(length // ROWS,),
        in_specs=[block, block, block, block, whole((LAYERS, width))],
        out_specs=[block, whole((8, width))],
        out_shape=[
            jax.ShapeDtypeStruct((length, width), kind),
            jax.ShapeDtypeStruct((8, width), F32),
        ],
        compiler_params=params(),
        name="norm_backward",
    )(x, own, other, grad, gain)


MESH = pl.DeviceIdType.MESH
UNIT = 16
SLOTS = 6
LAG = 2


class Flow(NamedTuple):
    order: tuple
    core: int
    is_up: int
    layer: int
    row: int
    units: int
    start: int
    place: int


def flows_of(width, layer, start):
    rows = width // 2
    kinds = (
        ((0, 1, 2, 3), 1, 0, 0, 0),
        ((1, 0, 2, 3), 1, 1, 0, 1),
        ((0, 1, 2, 3), 1, 0, 1, 2),
        ((1, 0, 2, 3), 1, 1, 1, 3),
        ((2, 0, 1, 3), 0, 0, 0, 0),
        ((2, 1, 0, 3), 0, 0, 1, 1),
    )
    return [
        Flow(order, core, is_up, layer, part * rows, rows // UNIT, start, 4 * layer + place)
        for order, core, is_up, part, place in kinds
    ]


def bit_of(index, bit):
    return (index // (1 << bit)) % 2


def flip(index, bit):
    return index + (1 << bit) * (1 - 2 * bit_of(index, bit))


def finish_kernel(
    bits, flows,
    kept_weight1, kept_up1, came_weight1, came_up1,
    kept_weight0, kept_up0, sent_weight0, sent_up0,
    bias0_ref, bias1_ref, sums1_ref, sums0_ref,
    weight_sum, up_out, small_out,
    up_sum, up_near, up_came,
    *scratch,
):
    stages = bits
    kept = ((kept_weight1, kept_up1), (kept_weight0, kept_up0))
    moved = ((came_weight1, came_up1), (sent_weight0, sent_up0))
    small_parts = (bias0_ref, bias1_ref, sums1_ref, sums0_ref)
    places = 1 + max(flow.place for flow in flows)
    held, scratch = scratch[: places * (stages + 1)], scratch[places * (stages + 1) :]
    held = [held[f * (stages + 1) : (f + 1) * (stages + 1)] for f in range(places)]
    small, small_came = scratch[: stages + 1], scratch[stages + 1 : 2 * stages + 1]
    load_sem, send_sem, recv_sem, credit, small_send, small_recv, near_send, near_recv = (
        scratch[2 * stages + 1 :]
    )
    me, core = lax.axis_index("batch"), lax.axis_index("stream")

    barrier = pltpu.get_barrier_semaphore()
    for bit in range(bits):
        pl.semaphore_signal(
            barrier, inc=1, device_id={"batch": flip(me, bit)}, device_id_type=MESH
        )
    pl.semaphore_signal(barrier, inc=1, device_id={"stream": 1 - core}, device_id_type=MESH)
    pl.semaphore_wait(barrier, bits + 1)

    small_start = 2
    turn_start = max(flow.start + flow.units for flow in flows if flow.layer == 1)
    turn_start += LAG * stages + 1

    def near_copy(layer):
        return pltpu.make_async_remote_copy(
            src_ref=up_near.at[layer],
            dst_ref=up_came.at[layer],
            send_sem=near_send.at[layer],
            recv_sem=near_recv.at[layer],
            device_id={"stream": 0},
            device_id_type=MESH,
        )

    def part_up(layer):
        @pl.when(core == 1)
        def _():
            up_near[layer] = up_sum[layer, :, : WIDE // 2]
            near_copy(layer).start()
            up_out[layer] = up_sum[layer, :, WIDE // 2 :]

    def small_copy(stage):
        return pltpu.make_async_remote_copy(
            src_ref=small[stage],
            dst_ref=small_came[stage],
            send_sem=small_send.at[stage],
            recv_sem=small_recv.at[stage],
            device_id={"batch": flip(me, stage)},
            device_id_type=MESH,
        )

    def small_step(stage):
        if stage == 0:
            row = 0
            for part in small_parts:
                small[0][row : row + part.shape[0]] = part[...]
                row += part.shape[0]
        else:
            small_copy(stage - 1).wait()
            small[stage][...] = small[stage - 1][...] + small_came[stage - 1][...]
        if stage < stages:
            small_copy(stage).start()
        else:
            small_out[...] = small[stage][...]

    def view(order, stage, mine):
        left = sorted(set(range(bits)) - set(order[:stage]), reverse=True)
        pick = bit_of(me, order[stage])
        pick = pick if mine else 1 - pick
        return tuple(pick if bit == order[stage] else slice(None) for bit in left)

    def remote(flow, stage, slot, source):
        place = flow.place
        return pltpu.make_async_remote_copy(
            src_ref=source,
            dst_ref=held[place][stage + 1].at[slot],
            send_sem=send_sem.at[place, stage, slot],
            recv_sem=recv_sem.at[place, stage, slot],
            device_id={"batch": flip(me, flow.order[stage])},
            device_id_type=MESH,
        )

    def sent_from(flow, stage, slot):
        if stage == 0:
            return held[flow.place][0].at[slot]
        return held[flow.place][stage].at[(slot,) + view(flow.order, stage, False)]

    def load(flow, slot, source):
        place = flow.place
        return pltpu.make_async_copy(source, held[place][0].at[slot], load_sem.at[place, slot])

    def load_came(flow, slot, source):
        return pltpu.make_async_copy(
            source, held[flow.place][1].at[slot], recv_sem.at[flow.place, 0, slot]
        )

    def return_credit(flow, stage, unit):
        if stage == 0 and flow.layer == 0:
            return

        @pl.when(unit + SLOTS < flow.units)
        def _():
            pl.semaphore_signal(
                credit.at[flow.place, stage],
                inc=1,
                device_id={"batch": flip(me, flow.order[stage])},
                device_id_type=MESH,
            )

    def take_credit(flow, stage, unit):
        @pl.when(unit >= SLOTS)
        def _():
            pl.semaphore_wait(credit.at[flow.place, stage], 1)

    def begin(flow, unit):
        slot = lax.rem(unit, SLOTS)
        at = (slice(None),) * (bits - 1)
        at += (pl.ds(pl.multiple_of(flow.row + unit * UNIT, UNIT), UNIT),)
        load(flow, slot, kept[flow.layer][flow.is_up].at[at]).start()
        source = moved[flow.layer][flow.is_up].at[at]
        if flow.layer == 0:
            load_came(flow, slot, source).start()
        else:
            take_credit(flow, 0, unit)
            remote(flow, 0, slot, source).start()

    def advance(flow, stage, unit):
        slot = lax.rem(unit, SLOTS)
        buffers, begun = held[flow.place], flow.layer == 0
        copy = remote(flow, stage - 1, slot, sent_from(flow, stage - 1, slot))
        if stage == 1 and begun:
            load_came(flow, slot, buffers[0].at[slot]).wait()
        else:
            copy.wait_recv()
        if stage == 1:
            load(flow, slot, buffers[1].at[slot]).wait()
            mine = buffers[0][slot]
        else:
            mine = buffers[stage - 1][(slot,) + view(flow.order, stage - 1, True)]
        value = buffers[stage][slot] + mine
        if stage < stages:
            buffers[stage][slot] = value
            take_credit(flow, stage, unit)
            remote(flow, stage, slot, sent_from(flow, stage, slot)).start()
        else:
            target = up_sum if flow.is_up else weight_sum
            at = pl.ds(pl.multiple_of(flow.row + unit * UNIT, UNIT), UNIT)
            target[flow.layer, at] = value
        if stage > 1 or not begun:
            copy.wait_send()
        if stage >= 2:
            return_credit(flow, stage - 2, unit)
        if stage == stages:
            return_credit(flow, stage - 1, unit)

    def within(flow, unit):
        return (unit >= 0) & (unit < flow.units) & (core == flow.core)

    def step(index, carry):
        for flow in flows:
            unit = index - flow.start
            pl.when(within(flow, unit))(functools.partial(begin, flow, unit))
        for stage in range(stages, 0, -1):
            for flow in flows:
                unit = index - flow.start - LAG * stage
                pl.when(within(flow, unit))(functools.partial(advance, flow, stage, unit))
        for stage in range(stages + 1):
            pl.when(index == small_start + 2 * stage)(functools.partial(small_step, stage))
        pl.when(index == turn_start)(functools.partial(part_up, 1))
        return carry

    last = max(flow.start + flow.units for flow in flows)
    lax.fori_loop(0, last + LAG * stages, step, 0)
    part_up(0)
    for layer in range(len(moved)):

        @pl.when(core == 0)
        def _():
            near_copy(layer).wait_recv()
            up_out[layer] = up_came[layer]

        @pl.when(core == 1)
        def _():
            near_copy(layer).wait_send()


def finish(last, first, came, smalls):
    width = last[0].shape[1]
    bits = 4
    split = (2,) * (bits - 1)
    flows = flows_of(width, 1, 0)
    flows += flows_of(width, 0, max(flow.start + flow.units for flow in flows))
    small = (sum(part.shape[0] for part in smalls), width)
    scratch = [
        pltpu.VMEM((2, width, WIDE), F32),
        pltpu.VMEM((2, width, WIDE // 2), F32),
        pltpu.VMEM((2, width, WIDE // 2), F32),
    ]
    places = 1 + max(flow.place for flow in flows)
    for _ in range(places):
        for stage in range(bits + 1):
            lead = (SLOTS,) + (2,) * (bits - 1 - max(stage - 1, 0))
            scratch.append(pltpu.VMEM(lead + (UNIT, WIDE), F32))
    scratch += [pltpu.VMEM(small, F32)] * (2 * bits + 1)
    scratch += [
        pltpu.SemaphoreType.DMA((places, SLOTS)),
        pltpu.SemaphoreType.DMA((places, bits, SLOTS)),
        pltpu.SemaphoreType.DMA((places, bits, SLOTS)),
        pltpu.SemaphoreType.REGULAR((places, bits)),
        pltpu.SemaphoreType.DMA((bits,)),
        pltpu.SemaphoreType.DMA((bits,)),
        pltpu.SemaphoreType.DMA((2,)),
        pltpu.SemaphoreType.DMA((2,)),
    ]
    large = [last[1], last[3], *came, first[1], first[3], first[0], first[2]]
    large = [array.reshape(split + array.shape[1:]) for array in large]
    return pl.pallas_call(
        functools.partial(finish_kernel, bits, flows),
        in_specs=[pl.BlockSpec(memory_space=pltpu.HBM)] * len(large)
        + [pl.BlockSpec(memory_space=pltpu.VMEM)] * len(smalls),
        out_specs=[pl.BlockSpec(memory_space=pltpu.VMEM)] * 3,
        out_shape=[
            jax.ShapeDtypeStruct((2, width, WIDE), F32),
            jax.ShapeDtypeStruct((2, width, WIDE // 2), F32),
            jax.ShapeDtypeStruct(small, F32),
        ],
        scratch_shapes=scratch,
        compiler_params=pltpu.CompilerParams(
            collective_id=0, has_side_effects=True, vmem_limit_bytes=VMEM_LIMIT
        ),
        name="finish",
    )(*large, *smalls)


def hand_out_kernel(
    rows, own, index_ref, weight_ref, up_ref, small_ref,
    weight_out, up_out, bias_out, down_out, gain_out, offset_out,
):
    index = index_ref[0]
    layers = weight_ref.shape[0]
    for layer in range(layers):
        weight_out[layer] = weight_ref[layers - 1 - layer].T
        up_out[layer] = up_ref[layers - 1 - layer].T
        per_row = small_ref.shape[1] // WIDE
        lanes = pl.ds(pl.multiple_of(lax.rem(index, per_row) * WIDE, WIDE), WIDE)
        row = pl.ds(layer * rows + index // per_row, 1)
        bias_out[layer : layer + 1] = small_ref[row, lanes]
        first = 2 * rows + 8 * (layers - 1 - layer)
        width = small_ref.shape[1]
        sums = pltpu.roll(small_ref[first : first + 8], lax.rem(width - index * own, width), 1)
        gain_out[layer : layer + 1] = sums[0:1, :own]
        offset_out[layer : layer + 1] = sums[1:2, :own]
        down_out[layer : layer + 1] = sums[2:3, :own]


def hand_out(weight, up, small, rows, own):
    layers, width, _ = weight.shape
    vector = jax.ShapeDtypeStruct((layers, own), F32)
    return pl.pallas_call(
        functools.partial(hand_out_kernel, rows, own),
        in_specs=[pl.BlockSpec(memory_space=pltpu.SMEM)]
        + [pl.BlockSpec(memory_space=pltpu.VMEM)] * 3,
        out_specs=[pl.BlockSpec(memory_space=pltpu.VMEM)] * 6,
        out_shape=[
            jax.ShapeDtypeStruct((layers, WIDE, width), F32),
            jax.ShapeDtypeStruct((layers, WIDE // 2, width), F32),
            jax.ShapeDtypeStruct((layers, WIDE), F32),
            vector,
            vector,
            vector,
        ],
        compiler_params=params(),
        name="hand_out",
    )(lax.axis_index("batch").astype(jnp.int32).reshape(1), weight, up, small)


def send_first(halves):
    count = lax.axis_size("batch")

    def pairs(stream, bit):
        return [(2 * source + stream, 2 * flip(source, bit) + stream) for source in range(count)]

    axes = ("batch", "stream")
    return [
        lax.ppermute(halves[0], axes, pairs(0, 2) + pairs(1, 0)),
        lax.ppermute(halves[2], axes, pairs(1, 1)),
    ]


def shards(
    tokens, cotangent, branch_weight, branch_bias, up_weight, down_bias,
    norm_gain, norm_bias, freq_seeds, doc_starts,
):
    is_attention = lax.axis_index("stream") == 0
    length, width = tokens.shape
    rotary = tuple(jnp.asarray(table) for table in rotary_rows(length))
    biases = branch_bias[0].astype(F32).reshape(-1, 1, width)

    def tables_of(layer):
        return tuple(feature_tables(freq_seeds[layer : layer + 1]))

    wide = jax.ShapeDtypeStruct((1, QUADS, WIDE, WIDE), BF16)
    none = (wide, wide, jax.ShapeDtypeStruct((1, QUADS, 1, WIDE), F32))
    square = jax.ShapeDtypeStruct((length, width), BF16)

    def no_tables():
        return unread(none)

    tables = lax.cond(is_attention, lambda: tables_of(0), no_tables)
    swap = [(0, 1), (1, 0)]

    def attention(layer, stream):
        return tuple(
            attention_forward(
                layer, stream, doc_starts, norm_gain, norm_bias, branch_weight, biases, tables,
                rotary,
            )
        )

    def feed_forward(layer, stream):
        return tuple(
            mlp_forward(
                layer, stream, norm_gain, norm_bias, up_weight, biases, branch_weight, down_bias
            )
        )

    count = lax.axis_size("batch")
    blocked = count == branch_weight.shape[2] // WIDE
    me = lax.axis_index("batch") if blocked else 0
    place = jnp.stack([jnp.asarray(bit_of(me, bit), jnp.int32) for bit in range(3)])

    part, *kept = lax.cond(
        is_attention,
        functools.partial(attention, 0, (tokens,)),
        functools.partial(feed_forward, 0, (tokens,)),
    )
    stream = (tokens, part, lax.ppermute(part, "stream", swap))

    def ready():
        return *tables_of(1), *prepare(1, part, cotangent, branch_weight)

    def not_ready():
        return unread(none + (square, jax.ShapeDtypeStruct((width, length), BF16)))

    *tables1, mixed_grad, grad_t = lax.cond(is_attention, ready, not_ready)

    def attention_ends():
        x, part, *back = attention_last(
            1, place, stream, doc_starts, norm_gain, norm_bias, branch_weight, biases, tables1,
            rotary, cotangent, mixed_grad, grad_t,
        )
        return x, part, *flat_halves(*back)

    def feed_forward_ends():
        x, part, *back = mlp_last(
            1, place, stream, norm_gain, norm_bias, up_weight, biases, branch_weight, down_bias,
            cotangent,
        )
        return x, part, *flat_halves(*back)

    x1, part, part1, *halves1, bias1 = lax.cond(
        jnp.logical_not(is_attention), feed_forward_ends, attention_ends
    )
    def attention_back(layer, grad, stream):
        h, state, mixed = kept
        *result, part, a, b, c, d, bias = attention_backward(
            layer, place, doc_starts, grad, h, state, mixed, tables, rotary, branch_weight, stream
        )
        return *result, *flat_halves(part, a, b, c, d, bias)

    def feed_forward_back(layer, grad, stream):
        h, act, slope = kept
        *result, part, a, b, c, d, bias = mlp_backward(
            layer, place, grad, h, act, slope, branch_weight, up_weight, stream
        )
        return *result, *flat_halves(part, a, b, c, d, bias)

    def back(layer, grad, stream=()):
        *result, part, a, b, c, d, bias = lax.cond(
            is_attention,
            functools.partial(attention_back, layer, grad, stream),
            functools.partial(feed_forward_back, layer, grad, stream),
        )
        return *result, part, (a, b, c, d), bias

    def norm_back(layer, x, part, grad, kind):
        other = lax.ppermute(part, "stream", swap)
        return norm_backward(layer, x, part, other, grad, norm_gain, kind)

    if blocked:
        came = send_first(halves1)
    grad0, sums1 = norm_back(1, x1, part1, cotangent, BF16)
    stream = (x1, part, lax.ppermute(part, "stream", swap))
    result, part0, halves0, bias0 = back(0, grad0, stream)
    input_grad, sums0 = norm_back(0, tokens, part0, grad0, F32)
    if blocked:
        weight, up, small = finish(halves1, halves0, came, (bias0, bias1, sums1, sums0))
    else:
        weight, up = scatter_rows((halves0, halves1))
        small = lax.psum(jnp.concatenate([bias0, bias1, sums1, sums0]), "batch")
    index, rows = lax.axis_index("batch"), bias0.shape[0]
    each, own = branch_weight.shape[2] // count, width // count
    if blocked:
        weight, up, bias, down, gain, offset = hand_out(weight, up, small, rows, own)
    else:
        bias = lax.dynamic_slice_in_dim(
            small[: 2 * rows].reshape(LAYERS, -1), index * each, each, axis=1
        )
        sums = small[2 * rows :].reshape(LAYERS, 8, width)[::-1]
        sums = lax.dynamic_slice_in_dim(sums, index * own, own, axis=2)
        down, gain, offset = sums[:, 2], sums[:, 0], sums[:, 1]
    return result, input_grad, weight[None], bias[None], up, down, gain, offset


def scatter_rows(layers):
    weights, ups = [], []
    for sent, kept, sent_up, kept_up in layers:
        blocks = (-1,) + kept.shape[1:]
        wide, far = (4, 2) + kept.shape[1:], (2, 4) + kept.shape[1:]
        weight = jnp.where(
            lax.axis_index("stream") == 1,
            jnp.stack([kept.reshape(wide), sent.reshape(wide)], axis=2).reshape(blocks),
            jnp.stack([kept.reshape(far), sent.reshape(far)], axis=1).reshape(blocks),
        )
        weight = rows_of(weight)
        up = jnp.stack([kept_up.reshape(wide), sent_up.reshape(wide)], axis=1)
        up = rows_of(up.reshape(blocks))
        up = jnp.where(lax.axis_index("stream") == 1, up, 0.0)
        weights.append(lax.psum_scatter(weight, "batch", scatter_dimension=0, tiled=True))
        ups.append(lax.psum_scatter(up, ("batch", "stream"), scatter_dimension=0, tiled=True))
    return jnp.stack(weights), jnp.stack(ups)


def rows_of(blocks):
    return jnp.transpose(blocks, (0, 2, 1)).reshape(-1, blocks.shape[1])


def solution(mesh):
    placed = (
        P("batch", None),
        P("batch", None),
        P("stream", None, None, None),
        P("stream", None, None),
        P(),
        P(),
        P(),
        P(),
        P(),
        P("batch", None),
    )
    return jax.shard_map(
        shards,
        mesh=mesh,
        in_specs=placed,
        out_specs=(
            P("batch", None),
            P("batch", None),
            P("stream", None, "batch", None),
            P("stream", None, "batch"),
            P(None, ("batch", "stream"), None),
            P(None, "batch"),
            P(None, "batch"),
            P(None, "batch"),
        ),
        check_vma=False,
    )
```
